32 devices in a mesh: dp: 2 (over y), row: 4 (over x, core), col: 4 (over z).
Axes of the slice: x: 2, y: 2, z: 4, core: 2. Of those that a mesh axis runs over, the one named last changes fastest.
Arguments:
- inputs: bfloat16 [8, 1536, 768], P(('dp', 'col'), 'row'), may hold values from -6 to 6
- cotangent: bfloat16 [8, 1536, 768], P(('dp', 'col'), 'row'), may hold values from -6 to 6
- routes: int32 [8, 1536, 2], P(('dp', 'col'), 'row'), may hold values from 0 to 7, all different within a row; in each aligned block of 384 rows (0 to 383, 384 to 767, ..., all dimensions but the last counted through in order) at most 144 rows name the same one
- buckets: int32 [1152], replicated, may hold values from 0 to 31, as said below
- norm_gains: bfloat16 [4, 768], P(None, ('row', 'col')), may hold values from 0.25 to 1.75
- attn_qkv: bfloat16 [2, 768, 2304], P(None, ('row', 'col')), may hold values from -0.21875 to 0.21875
- attn_out: bfloat16 [2, 768, 768], P(None, ('row', 'col')), may hold values from -0.875 to 0.875
- rel_bias: bfloat16 [2, 32, 12], P(None, ('row', 'col')), may hold values from -4 to 4
- mlp_in: bfloat16 [768, 3072], P(('row', 'col')), may hold values from -0.21875 to 0.21875
- mlp_out: bfloat16 [3072, 768], P(('row', 'col')), may hold values from -0.109375 to 0.109375
- router: bfloat16 [768, 8], P(('row', 'col')), may hold values from -0.15625 to 0.15625
- expert_in: bfloat16 [8, 768, 3072], P(('dp', 'col'), None, 'row'), may hold values from -0.21875 to 0.21875
- expert_out: bfloat16 [8, 3072, 768], P(('dp', 'col'), 'row'), may hold values from -0.109375 to 0.109375
Outputs:
- output: float32 [8, 1536, 768], P(('dp', 'col'), 'row')
- input_grad: float32 [8, 1536, 768], P(('dp', 'col'), 'row')
- grad_norm_gains: float32 [4, 768], P(None, ('row', 'col'))
- grad_attn_qkv: float32 [2, 768, 2304], P(None, ('row', 'col'))
- grad_attn_out: float32 [2, 768, 768], P(None, ('row', 'col'))
- grad_rel_bias: float32 [2, 32, 12], P(None, ('row', 'col'))
- grad_mlp_in: float32 [768, 3072], P(('row', 'col'))
- grad_mlp_out: float32 [3072, 768], P(('row', 'col'))
- grad_router: float32 [768, 8], P(('row', 'col'))
- grad_expert_in: float32 [8, 768, 3072], P(('dp', 'col'), None, 'row')
- grad_expert_out: float32 [8, 3072, 768], P(('dp', 'col'), 'row')
The draws below stay inside these ranges and needn't reach their ends.
Inputs may be any that keep to these rules, and one draw needn't show every extreme that they name: `routes`: each row names two different experts; among the 384 rows of one block no expert is named more than 144 times, a bound that some block reaches. `buckets`: non-decreasing in the distance; 0 at distance 0 and 31 at distance 1152 - 1.
All inputs are finite; a program needn't handle non-finite values.
Results may differ from the reference program's by a relative error of at most 0.029.
Values may be sent and summed in bfloat16 or wider, within the bound.
A program may use at most 320 MiB of HBM per device.

```python
import math
import jax
import jax.numpy as jnp
import numpy as np
from jax import lax

D = 768
HEADS = 12
HDIM = 64
FF = 3072
BUCKETS = 32
PLEN = 1024
CLEN = 128
PROMPTS = 1
CONT_DEV = 1
TOK_DEV = 384
TOK_SET = 1536
SETS = 8
EXPERTS = 8
CAP = 144
DIST = 1152
N_ROW = 4


def draw_buckets(key, part):
    key = jax.random.fold_in(key, 7)
    levels = jax.random.randint(key, (PLEN + CLEN,), 0, BUCKETS)
    ordered = jnp.sort(levels)
    ordered = ordered.at[0].set(0).at[PLEN + CLEN - 1].set(BUCKETS - 1)
    return ordered.astype(jnp.int32)


def steps_of(own_key, extent, shards, smallest, top_value):
    level = 1.0
    for dim, parts in shards:
        heights = jax.random.uniform(jax.random.fold_in(jax.random.fold_in(own_key, 6), dim), (parts,), jnp.float32, smallest / len(shards), top_value / len(shards))
        level = level * jnp.repeat(jnp.exp(heights), extent[dim] // parts).reshape((-1,) + (1,) * (len(extent) - 1 - dim))
    return level


def deal_out(own_key, own, number, rows, count, top, reach, slope):
    ranking = jax.random.permutation(own_key, count)
    crowded, ordinary = load_shares(count, rows * top, reach, slope, True), load_shares(count, rows * top, reach, slope, False)
    places = jnp.arange(count)

    def named(lengths, offset_by):
        used = int((lengths > 0).sum())
        fixed = max(1, used // 4)
        shifted = fixed + (places - fixed + offset_by * (used - fixed)) % max(1, count - fixed)
        return jnp.zeros((count,), jnp.int32).at[ranking[jnp.where(places < fixed, places, shifted)]].set(jnp.asarray(lengths, jnp.int32))

    lengths = jnp.where(number % 4 == 0, named(crowded, number // 4), named(ordinary, number - number // 4 - 1))
    mixed = jax.random.permutation(jax.random.fold_in(own, 3), count)
    donor, sink = mixed[0:count // 2 * 2:2], mixed[1:count // 2 * 2:2]
    room = jnp.minimum(lengths[donor] - 1, reach - lengths[sink]) // 2
    room = jnp.where((donor == ranking[0]) | (sink == ranking[0]) | (lengths[sink] == 0), 0, jnp.maximum(room, 0))
    shifted = jax.random.randint(jax.random.fold_in(own, 4), (count // 2,), 0, 1 << 20) % (room + 1)
    lengths = lengths.at[donor].add(-shifted).at[sink].add(shifted)
    members = jnp.searchsorted(jnp.cumsum(lengths), jnp.arange(rows * top), side="right").astype(jnp.int32)
    table = members.reshape(top, rows).T
    table = table[jax.random.permutation(jax.random.fold_in(own, 1), rows)]
    offset_by = jax.random.randint(jax.random.fold_in(own, 2), (rows, 1), 0, top)
    return jnp.take_along_axis(table, (jnp.arange(top)[None, :] + offset_by) % top, axis=1)


def load_shares(number_of, total, reach, lean, full):
    portions = [(1 << 20) // math.isqrt(rank ** lean) + 1 for rank in range(1, number_of + 1)]
    largest = reach if full else min(reach, max(-(-total // number_of), total * portions[0] // sum(portions)))
    least = 1 if total - largest >= number_of - 1 else 0
    given, spare = [largest] + [least] * (number_of - 1), total - largest - least * (number_of - 1)
    while spare > 0:
        movable = [i for i in range(1, number_of) if given[i] < largest] or [i for i in range(1, number_of) if given[i] < reach]
        mass, remaining = sum([portions[i] for i in movable]), spare
        for i in movable:
            more = min(reach - given[i], max(1, remaining * portions[i] // mass), spare)
            given[i] = given[i] + more
            spare = spare - more
    return np.array(given)


def scatter_about(key, extent, scale, reach, shards=(), kind=jnp.bfloat16):
    level = steps_of(key, extent, shards, -0.22, 0.18) if shards else 1.0
    entries = jax.random.normal(key, extent, jnp.float32) * scale * level
    return jnp.minimum(jnp.maximum(entries, -reach), reach).astype(kind)


def setup_inputs(seed: int = 0) -> dict:
    splits = jax.random.split(jax.random.key(seed), 14)
    inputs = scatter_about(splits[0], (SETS, TOK_SET, D), 1.0, 6.0, ((0, 8), (1, 4)))
    cotangent = scatter_about(splits[1], (SETS, TOK_SET, D), 1.0, 6.0, ((0, 8), (1, 4)))
    routes_keys = jax.random.split(jax.random.fold_in(splits[2], 1), SETS * TOK_SET // TOK_DEV)
    routes_turns = jax.random.permutation(jax.random.fold_in(splits[2], 3), SETS * TOK_SET // TOK_DEV)
    routes = jax.vmap(lambda own, number: deal_out(jax.random.fold_in(splits[2], 2), own, number, TOK_DEV, EXPERTS, 2, CAP, 1))(routes_keys, routes_turns).reshape((SETS, TOK_SET, 2))
    buckets = draw_buckets(jax.random.fold_in(splits[13], 71), 0)
    norm_gains = jnp.clip(1.0 + 0.15 * jax.random.normal(splits[4], (4, D), jnp.float32), 0.25, 1.75).astype(jnp.bfloat16)
    attn_qkv = scatter_about(splits[5], (2, D, 3 * D), D ** -0.5, 0.21875, ((1, 16),))
    attn_out = scatter_about(splits[6], (2, D, D), (D // 16) ** -0.5, 0.875, ((1, 16),))
    rel_bias = scatter_about(splits[7], (2, BUCKETS, HEADS), 1.0, 4.0, ((1, 16),))
    mlp_in = scatter_about(splits[8], (D, FF), D ** -0.5, 0.21875, ((0, 16),))
    mlp_out = scatter_about(splits[9], (FF, D), FF ** -0.5, 0.109375, ((0, 16),))
    router = scatter_about(splits[10], (D, EXPERTS), (2 * D) ** -0.5, 0.15625, ((0, 16),))
    expert_in = scatter_about(splits[11], (EXPERTS, D, FF), D ** -0.5, 0.21875, ((0, 8), (2, 4)))
    expert_out = scatter_about(splits[12], (EXPERTS, FF, D), FF ** -0.5, 0.109375, ((0, 8), (1, 4)))
    return {"inputs": inputs, "cotangent": cotangent, "routes": routes, "buckets": buckets, "norm_gains": norm_gains, "attn_qkv": attn_qkv, "attn_out": attn_out, "rel_bias": rel_bias, "mlp_in": mlp_in, "mlp_out": mlp_out, "router": router, "expert_in": expert_in, "expert_out": expert_out}


@jax.custom_vjp
def low(v):
    return lax.optimization_barrier(v.astype(jnp.bfloat16)).astype(jnp.float32)

@jax.custom_vjp
def low_back(v):
    return v

def low_keep(v):
    return (low(v), None)

def low_pass(kept, grad):
    return (grad,)

def back_keep(v):
    return (v, None)

def back_low(kept, grad):
    return (low(grad),)
low.defvjp(low_keep, low_pass)
low_back.defvjp(back_keep, back_low)
EPS = 1e-06
CURVE = 0.7978845608028654
HIGH = lax.Precision.HIGHEST

def norm_rows(values, gain):
    center = values - lax.optimization_barrier(jnp.mean(values, -1, keepdims=True))
    spread = lax.optimization_barrier(jnp.mean(center * center, -1, keepdims=True))
    return center * lax.rsqrt(spread + EPS) * gain

def gelu(values):
    return 0.5 * values * (1.0 + jnp.tanh(CURVE * (values + 0.044715 * values * values * values)))

def softmax_rows(scores):
    top = lax.optimization_barrier(jnp.max(scores, -1, keepdims=True))
    raised = jnp.exp(scores - top)
    return raised / lax.optimization_barrier(jnp.sum(raised, -1, keepdims=True))

def product(left, right):
    return jnp.dot(left, right, precision=HIGH)

def heads_of(block):
    return block.reshape(block.shape[:-1] + (HEADS, HDIM))

def attend(query, keys, values, bias, mask):
    raw = jnp.einsum('bqhe,bkhe->bhqk', query, keys, precision=HIGH) * HDIM ** (-0.5)
    raw = raw + jnp.transpose(bias, (2, 0, 1))[None]
    scores = low_back(jnp.where(mask[None, None], raw, -1e+30))
    probs = low(softmax_rows(scores))
    return jnp.einsum('bhqk,bkhe->bqhe', probs, values, precision=HIGH)

def attention_layer(state, gain, weight_in, weight_out, rel, conts, buckets):
    pslice = PLEN // N_ROW
    normed = low(norm_rows(state, gain))
    projected = low(low_back(product(normed, weight_in)))
    blocks = projected.reshape(N_ROW, TOK_DEV, 3 * D)
    prompt = blocks[:, :PROMPTS * pslice].reshape(N_ROW, PROMPTS, pslice, 3 * D)
    prompt = jnp.transpose(prompt, (1, 0, 2, 3)).reshape(PROMPTS, PLEN, 3 * D)
    cont = blocks[:, PROMPTS * pslice:].reshape(N_ROW * CONT_DEV, CLEN, 3 * D)
    prompt_query = heads_of(prompt[..., :D])
    prompt_keys = heads_of(prompt[..., D:2 * D])
    prompt_values = heads_of(prompt[..., 2 * D:])
    cont_query = heads_of(cont[..., :D])
    cont_keys = heads_of(cont[..., D:2 * D])
    cont_values = heads_of(cont[..., 2 * D:])
    key_pos = jnp.arange(PLEN, dtype=jnp.int32)
    prompt_dist = key_pos[:, None] - key_pos[None, :]
    prompt_bias = jnp.take(rel, jnp.take(buckets, jnp.clip(prompt_dist, 0, DIST - 1), axis=0), axis=0)
    prompt_mix = attend(prompt_query, prompt_keys, prompt_values, prompt_bias, prompt_dist >= 0)
    own_pos = jnp.arange(CLEN, dtype=jnp.int32)
    cont_dist = jnp.concatenate([PLEN + own_pos[:, None] - key_pos[None, :], own_pos[:, None] - own_pos[None, :]], 1)
    cont_bias = jnp.take(rel, jnp.take(buckets, jnp.clip(cont_dist, 0, DIST - 1), axis=0), axis=0)
    all_keys = jnp.concatenate([jnp.take(prompt_keys, conts, axis=0), cont_keys], 1)
    all_values = jnp.concatenate([jnp.take(prompt_values, conts, axis=0), cont_values], 1)
    cont_mix = attend(cont_query, all_keys, all_values, cont_bias, cont_dist >= 0)
    prompt_mix = jnp.transpose(prompt_mix.reshape(PROMPTS, N_ROW, pslice, D), (1, 0, 2, 3))
    prompt_mix = prompt_mix.reshape(N_ROW, PROMPTS * pslice, D)
    cont_mix = cont_mix.reshape(N_ROW, CONT_DEV * CLEN, D)
    mixed = jnp.concatenate([prompt_mix, cont_mix], 1).reshape(TOK_SET, D)
    mixed = low(low_back(mixed))
    return state + low_back(product(mixed, weight_out))

def dense_layer(state, gain, weight_in, weight_out):
    normed = low(norm_rows(state, gain))
    hidden = low_back(product(normed, weight_in))
    active = low(gelu(hidden))
    return state + low_back(product(active, weight_out))

def expert_layer(state, gain, route_weight, first, second, routes):
    normed = low(norm_rows(state, gain))
    logits = low_back(product(normed, route_weight))
    levels = jnp.arange(EXPERTS, dtype=jnp.int32)
    choose = (routes[:, :, None] == levels[None, None, :]).astype(jnp.float32)
    gates = softmax_rows(lax.optimization_barrier(jnp.sum(choose * logits[:, None, :], -1)))
    flat = routes.reshape(-1)
    hits = (flat[:, None] == levels[None, :]).astype(jnp.int32)
    rank = lax.optimization_barrier(jnp.sum((jnp.cumsum(hits, 0) - 1) * hits, 1))
    slots = N_ROW * CAP
    place = flat * slots + rank
    source = jnp.zeros((EXPERTS * slots,), jnp.int32).at[place].set(jnp.arange(flat.shape[0], dtype=jnp.int32) + 1)
    copies = low_back(jnp.repeat(normed, 2, axis=0))
    filled = (source > 0)[:, None]
    buffer = jnp.where(filled, jnp.take(copies, jnp.maximum(source - 1, 0), axis=0), 0.0)
    buffer = buffer.reshape(EXPERTS, slots, D)
    hidden = low_back(jnp.einsum('ecd,edf->ecf', buffer, first, precision=HIGH))
    active = low(gelu(hidden))
    result = low(low_back(jnp.einsum('ecf,efd->ecd', active, second, precision=HIGH)))
    back = jnp.take(result.reshape(EXPERTS * slots, D), place, axis=0).reshape(TOK_SET, 2, D)
    return state + lax.optimization_barrier(jnp.sum(gates[:, :, None] * back, 1))

def block_pass(state, gains, qkv_w, out_w, rel, dense_in, dense_out, route_w, first, second, routes, conts, buckets):
    state = attention_layer(state, gains[0], qkv_w[0], out_w[0], rel[0], conts, buckets)
    state = dense_layer(state, gains[1], dense_in, dense_out)
    state = attention_layer(state, gains[2], qkv_w[1], out_w[1], rel[1], conts, buckets)
    return expert_layer(state, gains[3], route_w, first, second, routes)

def reference(inputs, cotangent, routes, buckets, norm_gains, attn_qkv, attn_out, rel_bias, mlp_in, mlp_out, router, expert_in, expert_out):
    weights = (norm_gains.astype(jnp.float32), attn_qkv.astype(jnp.float32), attn_out.astype(jnp.float32), rel_bias.astype(jnp.float32), mlp_in.astype(jnp.float32), mlp_out.astype(jnp.float32), router.astype(jnp.float32), expert_in.astype(jnp.float32), expert_out.astype(jnp.float32))
    conts = jnp.zeros((N_ROW * CONT_DEV,), jnp.int32)

    def one_set(totals, item):
        rows, upstream, route_set = item

        def forward(state, gains, qkv_w, out_w, rel, dense_in, dense_out, route_w, first, second):
            return block_pass(state, gains, qkv_w, out_w, rel, dense_in, dense_out, route_w, first, second, route_set, conts, buckets)
        result, pull = jax.vjp(forward, rows.astype(jnp.float32), *weights)
        grads = pull(upstream.astype(jnp.float32))
        totals = tuple((total + grad for total, grad in zip(totals, grads[1:])))
        return (totals, (result, grads[0]))
    zeros = tuple((jnp.zeros(weight.shape, jnp.float32) for weight in weights))
    totals, (results, input_grads) = lax.scan(one_set, zeros, (inputs, cotangent, routes))
    return (results, input_grads, totals[0], totals[1], totals[2], totals[3], totals[4], totals[5], totals[6], totals[7], totals[8])
```

```python
import functools

import jax
import jax.numpy as jnp
from jax import lax
from jax.experimental import pallas as pl
from jax.experimental.pallas import tpu as pltpu
from jax.sharding import PartitionSpec as P

D = 768
HEADS = 12
HDIM = 64
FF = 3072
BUCKETS = 32
PLEN = 1024
CLEN = 128
KEYS = PLEN + CLEN
WRAP = KEYS + 128
STRIP = 2 * PLEN
NEG = -1e30
EPS = 1e-06
CURVE = 0.7978845608028654
CUBE = 0.044715
HIGH = lax.Precision.HIGHEST
F32 = jnp.float32
LOW = jnp.bfloat16
MIB = 1 << 20


def dot_low(left, right):
    return jnp.dot(left, right, preferred_element_type=F32)


def dot_back(left, right):
    return lax.dot_general(left, right, (((1,), (1,)), ((), ())), preferred_element_type=F32)


def dot_over(left, right):
    return lax.dot_general(left, right, (((0,), (0,)), ((), ())), preferred_element_type=F32)


def normalise(values):
    center = values - jnp.mean(values, -1, keepdims=True)
    scale = lax.rsqrt(jnp.mean(center * center, -1, keepdims=True) + EPS)
    return center * scale, scale


def norm_rows(values, gain):
    return normalise(values)[0] * gain


def norm_back(values, gain, upstream):
    unit, scale = normalise(values)
    pulled = upstream * gain
    shift = jnp.mean(pulled, -1, keepdims=True)
    along = jnp.mean(pulled * unit, -1, keepdims=True)
    return (pulled - shift - unit * along) * scale, jnp.sum(upstream * unit, 0, keepdims=True)


def gelu_parts(values):
    square = values * values
    bend = jnp.tanh(CURVE * (values + CUBE * square * values))
    half = 0.5 * (1.0 + bend)
    slope = half + 0.5 * values * (1.0 - bend * bend) * (CURVE + 3.0 * CURVE * CUBE * square)
    return values * half, slope


def gelu(values):
    return 0.5 * values * (1.0 + jnp.tanh(CURVE * (values + CUBE * values * values * values)))


def params(mib, steps=1):
    return pltpu.CompilerParams(
        vmem_limit_bytes=mib * MIB, dimension_semantics=("arbitrary",) * steps
    )


def whole(shape):
    return pl.BlockSpec(shape, lambda *_: (0,) * len(shape))


def bias_table(buckets, rel):
    place = jnp.arange(WRAP, dtype=jnp.int32)
    dist = jnp.where(place <= PLEN, PLEN - place, PLEN + WRAP - place)
    read = (place <= PLEN) | (place > KEYS)
    index = jnp.take(buckets, jnp.clip(dist, 0, KEYS - 1), axis=0)
    hot = ((index[:, None] == jnp.arange(BUCKETS)[None, :]) & read[:, None]).astype(LOW)
    floor = jnp.where(read, 0.0, NEG).astype(F32)
    return hot, floor


def fill_strip(strip, table, head):
    @pl.when(pl.program_id(0) == 0)
    def _():
        strip[:, KEYS:] = jnp.full((128, STRIP - KEYS), NEG, F32)

    line = jnp.broadcast_to(table[pl.ds(head, 1), :], (128, WRAP))
    strip[:, :KEYS] = pltpu.roll(line, 0, 1, stride=1, stride_axis=0)[:, :KEYS]


def tiles_of(pslice):
    places = []
    for tile in range(pslice // 128):
        start = PLEN - (lax.axis_index("row") * pslice + tile * 128)
        places.append((tile * 128, pl.ds(pl.multiple_of(start, 128), PLEN), PLEN))
    places.append((pslice, pl.ds(0, KEYS), KEYS))
    return places


def attend_kernel(pslice, query, keys, values, table, mixed, total, strip, raw, weights):
    pair = pl.program_id(0)
    lane = lax.broadcasted_iota(jnp.int32, (1, 128), 1)

    @pl.when(pair == 0)
    def _():
        weights[:pslice, PLEN:] = jnp.zeros((pslice, CLEN), LOW)

    for half in range(2):
        mine = (lane < HDIM) if half == 0 else (lane >= HDIM)
        fill_strip(strip, table, 2 * pair + half)
        part = jnp.where(mine, query[...], 0) * HDIM ** (-0.5)
        raw[...] = dot_back(part.astype(LOW), keys[...])
        for row, place, count in tiles_of(pslice):
            rows = pl.ds(row, 128)
            scores = raw[rows, :count] + strip[:, place]
            top = jnp.max(scores, -1, keepdims=True)
            raised = jnp.exp(scores - top)
            summed = jnp.sum(raised, -1, keepdims=True)
            weights[rows, :count] = (raised * (1.0 / summed)).astype(LOW)
            log_total = jnp.broadcast_to(top + jnp.log(summed), (128, 128))
            if half == 0:
                total[rows, :] = log_total
            else:
                total[rows, :] = jnp.where(mine, log_total, total[rows, :])
        result = dot_low(weights[...], values[...]).astype(LOW)
        if half == 0:
            mixed[...] = result
        else:
            mixed[...] = jnp.where(mine, result, mixed[...])


def attend_forward(query, keys, values, table):
    tokens = query.shape[0]
    pslice = tokens - CLEN
    block = lambda rows: pl.BlockSpec((rows, 128), lambda i: (0, i))
    return pl.pallas_call(
        functools.partial(attend_kernel, pslice),
        grid=(HEADS // 2,),
        out_shape=(
            jax.ShapeDtypeStruct((tokens, D), LOW),
            jax.ShapeDtypeStruct((tokens, D), F32),
        ),
        in_specs=[block(tokens), block(KEYS), block(KEYS), whole(table.shape)],
        out_specs=(block(tokens), block(tokens)),
        scratch_shapes=[
            pltpu.VMEM((128, STRIP), F32),
            pltpu.VMEM((tokens, KEYS), F32),
            pltpu.VMEM((tokens, KEYS), LOW),
        ],
        compiler_params=params(32),
    )(query, keys, values, table)


def attend_back_kernel(
    pslice,
    query,
    keys,
    values,
    table,
    total,
    grad_mixed,
    grad_query,
    grad_keys,
    grad_values,
    grad_table,
    strip,
    raw,
    pulled,
    probs,
    grads,
    folded,
    sum_keys,
    sum_values,
):
    pair = pl.program_id(0)
    lane = lax.broadcasted_iota(jnp.int32, (1, 128), 1)
    across = lax.broadcasted_iota(jnp.int32, (128, 128), 0)
    along = lax.broadcasted_iota(jnp.int32, (128, 128), 1)
    mirror = (across + along == 127).astype(LOW)

    @pl.when(pair == 0)
    def _():
        probs[:pslice, PLEN:] = jnp.zeros((pslice, CLEN), LOW)
        grads[:pslice, PLEN:] = jnp.zeros((pslice, CLEN), LOW)

    for half in range(2):
        mine = (lane < HDIM) if half == 0 else (lane >= HDIM)
        fill_strip(strip, table, 2 * pair + half)
        part = (jnp.where(mine, query[...], 0) * HDIM ** (-0.5)).astype(LOW)
        upstream = jnp.where(mine, grad_mixed[...], 0).astype(LOW)
        raw[...] = dot_back(part, keys[...])
        pulled[...] = dot_back(upstream, values[...])
        folded[...] = jnp.zeros_like(folded)
        for row, place, count in tiles_of(pslice):
            rows = pl.ds(row, 128)
            log_total = total[rows, half * HDIM : half * HDIM + 1]
            chance = jnp.exp(raw[rows, :count] + strip[:, place] - log_total)
            product = chance * pulled[rows, :count]
            centre = jnp.sum(product, -1, keepdims=True)
            slope = (product - chance * centre).astype(LOW)
            probs[rows, :count] = chance.astype(LOW)
            grads[rows, :count] = slope
            folded[:, place] += dot_low(mirror, slope)
        result = dot_low(grads[...], keys[...]) * HDIM ** (-0.5)
        if half == 0:
            grad_query[...] = result.astype(LOW)
            sum_keys[...] = dot_over(part, grads[...])
            sum_values[...] = dot_over(upstream, probs[...])
        else:
            grad_query[...] = jnp.where(mine, result.astype(LOW), grad_query[...])
            sum_keys[...] += dot_over(part, grads[...])
            sum_values[...] += dot_over(upstream, probs[...])
        turned = pltpu.roll(folded[:, :WRAP], WRAP - 127, 1, stride=1, stride_axis=0)
        grad_table[pl.ds(2 * pair + half, 1), :] = jnp.sum(turned, 0, keepdims=True)
    grad_keys[...] = sum_keys[...].T.astype(LOW)
    grad_values[...] = sum_values[...].T.astype(LOW)


def attend_backward(query, keys, values, table, total, grad_mixed):
    tokens = query.shape[0]
    pslice = tokens - CLEN
    block = lambda rows: pl.BlockSpec((rows, 128), lambda i: (0, i))
    return pl.pallas_call(
        functools.partial(attend_back_kernel, pslice),
        grid=(HEADS // 2,),
        out_shape=(
            jax.ShapeDtypeStruct((tokens, D), LOW),
            jax.ShapeDtypeStruct((KEYS, D), LOW),
            jax.ShapeDtypeStruct((KEYS, D), LOW),
            jax.ShapeDtypeStruct(table.shape, F32),
        ),
        in_specs=[
            block(tokens),
            block(KEYS),
            block(KEYS),
            whole(table.shape),
            block(tokens),
            block(tokens),
        ],
        out_specs=(block(tokens), block(KEYS), block(KEYS), whole(table.shape)),
        scratch_shapes=[
            pltpu.VMEM((128, STRIP), F32),
            pltpu.VMEM((tokens, KEYS), F32),
            pltpu.VMEM((tokens, KEYS), F32),
            pltpu.VMEM((tokens, KEYS), LOW),
            pltpu.VMEM((tokens, KEYS), LOW),
            pltpu.VMEM((128, STRIP), F32),
            pltpu.VMEM((128, KEYS), F32),
            pltpu.VMEM((128, KEYS), F32),
        ],
        compiler_params=params(32),
    )(query, keys, values, table, total, grad_mixed)


def mlp_forward_kernel(state, gain, first, second, result, normed):
    step = pl.program_id(0)

    @pl.when(step == 0)
    def _():
        normed[...] = norm_rows(state[...], gain[...]).astype(LOW)
        result[...] = state[...]

    active = gelu(dot_low(normed[...], first[...])).astype(LOW)
    result[...] += dot_low(active, second[...])


def mlp_forward(state, gain, first, second):
    tokens = state.shape[0]
    part = 768
    return pl.pallas_call(
        mlp_forward_kernel,
        grid=(FF // part,),
        out_shape=(
            jax.ShapeDtypeStruct((tokens, D), F32),
            jax.ShapeDtypeStruct((tokens, D), LOW),
        ),
        in_specs=[
            whole((tokens, D)),
            whole((1, D)),
            pl.BlockSpec((D, part), lambda i: (0, i)),
            pl.BlockSpec((part, D), lambda i: (i, 0)),
        ],
        out_specs=(whole((tokens, D)), whole((tokens, D))),
        compiler_params=params(32),
    )(state, gain, first, second)


def mlp_backward_kernel(
    grad_next, state, normed, gain, first, second, result, grad_gain, grad_first, grad_second, low, total
):
    step = pl.program_id(0)

    @pl.when(step == 0)
    def _():
        low[...] = grad_next[...].astype(LOW)
        total[...] = jnp.zeros_like(total)

    active, slope = gelu_parts(dot_low(normed[...], first[...]))
    grad_hidden = (slope * dot_back(low[...], second[...])).astype(LOW)
    grad_second[...] = dot_over(active.astype(LOW), low[...]).astype(LOW)
    grad_first[...] = dot_over(normed[...], grad_hidden).astype(LOW)
    total[...] += dot_back(grad_hidden, first[...])

    @pl.when(step == pl.num_programs(0) - 1)
    def _():
        grad_state, grad_line = norm_back(state[...], gain[...], total[...])
        result[...] = grad_next[...] + grad_state
        grad_gain[...] = grad_line


def mlp_backward(grad_next, state, normed, gain, first, second):
    tokens = state.shape[0]
    part = 768
    return pl.pallas_call(
        mlp_backward_kernel,
        grid=(FF // part,),
        out_shape=(
            jax.ShapeDtypeStruct((tokens, D), F32),
            jax.ShapeDtypeStruct((1, D), F32),
            jax.ShapeDtypeStruct((D, FF), LOW),
            jax.ShapeDtypeStruct((FF, D), LOW),
        ),
        in_specs=[
            whole((tokens, D)),
            whole((tokens, D)),
            whole((tokens, D)),
            whole((1, D)),
            pl.BlockSpec((D, part), lambda i: (0, i)),
            pl.BlockSpec((part, D), lambda i: (i, 0)),
        ],
        out_specs=(
            whole((tokens, D)),
            whole((1, D)),
            pl.BlockSpec((D, part), lambda i: (0, i)),
            pl.BlockSpec((part, D), lambda i: (i, 0)),
        ),
        scratch_shapes=[pltpu.VMEM((tokens, D), LOW), pltpu.VMEM((tokens, D), F32)],
        compiler_params=params(48),
    )(grad_next, state, normed, gain, first, second)


def expert_kernel(
    rows, cotangent, gate, first, second, result, grad_rows, grad_gate, grad_first, grad_second, upstream, total, back
):
    step = pl.program_id(0)

    @pl.when(step == 0)
    def _():
        upstream[...] = (gate[:, :1] * cotangent[...].astype(F32)).astype(LOW)
        total[...] = jnp.zeros_like(total)
        back[...] = jnp.zeros_like(back)

    active, slope = gelu_parts(dot_low(rows[...], first[...]))
    active = active.astype(LOW)
    total[...] += dot_low(active, second[...])
    grad_hidden = (slope * dot_back(upstream[...], second[...])).astype(LOW)
    grad_second[...] = dot_over(active, upstream[...]).astype(LOW)
    grad_first[...] = dot_over(rows[...], grad_hidden).astype(LOW)
    back[...] += dot_back(grad_hidden, first[...])

    @pl.when(step == pl.num_programs(0) - 1)
    def _():
        low = total[...].astype(LOW)
        result[...] = low
        grad_rows[...] = back[...].astype(LOW)
        reach = jnp.sum(cotangent[...].astype(F32) * low.astype(F32), -1, keepdims=True)
        grad_gate[...] = jnp.broadcast_to(reach, grad_gate.shape)


def expert_pass(rows, cotangent, gate, first, second):
    count = rows.shape[0]
    shards, _, width = first.shape
    part = 256
    split = width // part
    inner = pl.BlockSpec((None, D, part), lambda i: (i // split, 0, i % split))
    outer = pl.BlockSpec((None, part, D), lambda i: (i // split, i % split, 0))
    return pl.pallas_call(
        expert_kernel,
        grid=(shards * split,),
        out_shape=(
            jax.ShapeDtypeStruct((count, D), LOW),
            jax.ShapeDtypeStruct((count, D), LOW),
            jax.ShapeDtypeStruct((count, 128), F32),
            jax.ShapeDtypeStruct(first.shape, LOW),
            jax.ShapeDtypeStruct(second.shape, LOW),
        ),
        in_specs=[whole((count, D)), whole((count, D)), whole((count, 128)), inner, outer],
        out_specs=(whole((count, D)), whole((count, D)), whole((count, 128)), inner, outer),
        scratch_shapes=[
            pltpu.VMEM((count, D), LOW),
            pltpu.VMEM((count, D), F32),
            pltpu.VMEM((count, D), F32),
        ],
        compiler_params=params(56),
    )(rows, cotangent, gate, first, second)


def split_low(values):
    high = values.astype(LOW)
    rest = values - high.astype(F32)
    middle = rest.astype(LOW)
    return high, middle, (rest - middle.astype(F32)).astype(LOW)


def exchange(block):
    return lax.all_to_all(block, ("dp", "col"), split_axis=0, concat_axis=0, tiled=True)


def attention_forward(state, gain, others, weight_in, weight_out, table, raw_others):
    tokens = state.shape[0]
    pslice = tokens - CLEN
    normed = norm_rows(state, gain).astype(LOW)
    if others is None:
        shared = lax.all_gather(normed[:pslice], "row", axis=0, tiled=True)
    else:
        shared = norm_rows(others.astype(F32), gain).astype(LOW)
    read = jnp.concatenate([shared, normed[pslice:]], 0)
    query = dot_low(normed, weight_in[:, :D]).astype(LOW)
    keys = dot_low(read, weight_in[:, D : 2 * D]).astype(LOW)
    values = dot_low(read, weight_in[:, 2 * D :]).astype(LOW)
    mixed, total = attend_forward(query, keys, values, table)
    return state + dot_low(mixed, weight_out), (state, normed, read, query, keys, values, mixed, total)


def attention_backward(grad_next, stash, gain, weight_in, weight_out, table, hot):
    state, normed, read, query, keys, values, mixed, total = stash
    pslice = state.shape[0] - CLEN
    branch = grad_next.astype(LOW)
    grad_out = dot_over(mixed, branch).astype(LOW)
    grad_mixed = dot_back(branch, weight_out).astype(LOW)
    grad_query, grad_keys, grad_values, grad_table = attend_backward(
        query, keys, values, table, total, grad_mixed
    )
    grad_in = jnp.concatenate(
        [dot_over(normed, grad_query), dot_over(read, grad_keys), dot_over(read, grad_values)], 1
    ).astype(LOW)
    grad_read = dot_back(grad_keys, weight_in[:, D : 2 * D]) + dot_back(
        grad_values, weight_in[:, 2 * D :]
    )
    own = lax.psum_scatter(
        grad_read[:PLEN].astype(LOW), "row", scatter_dimension=0, tiled=True
    ).astype(F32)
    grad_normed = dot_back(grad_query, weight_in[:, :D]) + jnp.concatenate(
        [own, grad_read[PLEN:]], 0
    )
    grad_state, grad_gain = norm_back(state, gain, grad_normed)
    grad_rel = jnp.dot(grad_table[:HEADS], hot.astype(F32), precision=HIGH).T
    return grad_next + grad_state, grad_in, grad_out, grad_rel, grad_gain


def on_device(
    inputs,
    cotangent,
    routes,
    buckets,
    norm_gains,
    attn_qkv,
    attn_out,
    rel_bias,
    mlp_in,
    mlp_out,
    router,
    expert_in,
    expert_out,
):
    grid = ("row", "col")
    places = lax.axis_size(grid)
    experts = lax.axis_size(("dp", "col"))
    tokens = inputs.shape[1]
    pslice = tokens - CLEN
    capacity = max(2, 3 * tokens // experts)

    small = [norm_gains.reshape(-1), rel_bias.reshape(-1), router.reshape(-1)]
    cuts = [part.shape[0] for part in small]
    packed = jnp.concatenate(small)
    packed = jnp.pad(packed, (0, -packed.shape[0] % 1024)).reshape(-1, 128)
    packed = lax.all_gather(packed, grid, axis=0, tiled=False).reshape(places, -1)
    gains = packed[:, : cuts[0]].reshape(places, 4, -1).transpose(1, 0, 2).reshape(4, 1, D).astype(F32)
    rel = packed[:, cuts[0] : cuts[0] + cuts[1]].reshape(places, 2, -1, HEADS)
    rel = rel.transpose(1, 0, 2, 3).reshape(2, BUCKETS, HEADS)
    route_w = packed[:, cuts[0] + cuts[1] : sum(cuts)].reshape(D, experts)

    qkv = [lax.all_gather(attn_qkv[i], grid, axis=0, tiled=True) for i in range(2)]
    out = [lax.all_gather(attn_out[i], grid, axis=0, tiled=True) for i in range(2)]
    dense_in = lax.all_gather(mlp_in, grid, axis=0, tiled=True)
    dense_out = lax.all_gather(mlp_out, grid, axis=0, tiled=True)
    first = lax.all_gather(expert_in[0], "row", axis=0, tiled=False)
    second = lax.all_gather(expert_out[0], "row", axis=0, tiled=False)

    hot, floor = bias_table(buckets, rel)
    tables = [
        jnp.pad(dot_low(rel[i].T, hot.T) + floor[None], ((0, 16 - HEADS), (0, 0))) for i in range(2)
    ]

    flat = routes[0].reshape(-1)
    levels = jnp.arange(experts, dtype=jnp.int32)
    choose = (routes[0][:, :, None] == levels[None, None, :]).astype(F32)
    hits = (flat[:, None] == levels[None, :]).astype(LOW)
    before = jnp.arange(2 * tokens)
    before = (before[:, None] > before[None, :]).astype(LOW)
    rank = jnp.sum(dot_low(before, hits) * hits.astype(F32), 1).astype(jnp.int32)
    place = (flat * capacity + rank).reshape(tokens, 2)
    slots = jnp.arange(experts * capacity, dtype=jnp.int32)
    picks = [(place[:, k][:, None] == slots[None, :]).astype(LOW) for k in range(2)]
    both = picks[0] + picks[1]
    sent_cotangent = dot_over(both, cotangent[0]).astype(LOW).reshape(experts, capacity, D)
    far_cotangent = exchange(sent_cotangent).reshape(experts * capacity, D)

    state0 = inputs[0].astype(F32)
    shared0 = lax.all_gather(inputs[0, :pslice], "row", axis=0, tiled=True)
    state1, stash1 = attention_forward(state0, gains[0], shared0, qkv[0], out[0], tables[0], None)
    state2, normed1 = mlp_forward(state1, gains[1], dense_in, dense_out)
    state3, stash3 = attention_forward(state2, gains[2], None, qkv[1], out[1], tables[1], None)

    normed3 = norm_rows(state3, gains[3]).astype(LOW)
    logits = dot_low(normed3, route_w)
    picked = jnp.sum(choose * logits[:, None, :], -1)
    raised = jnp.exp(picked - jnp.max(picked, -1, keepdims=True))
    gates = raised / jnp.sum(raised, -1, keepdims=True)
    parts = [split_low(gates[:, k]) for k in range(2)]
    spread = [
        dot_over(picks[k], jnp.pad(jnp.stack(parts[k], 1), ((0, 0), (0, 125)))) for k in range(2)
    ]
    sent = jnp.concatenate([dot_over(both, normed3), spread[0] + spread[1]], 1).astype(LOW)
    received = exchange(sent.reshape(experts, capacity, D + 128)).reshape(experts * capacity, D + 128)
    far_gate = jnp.sum(received[:, D : D + 3].astype(F32), 1, keepdims=True)
    far_gate = jnp.broadcast_to(far_gate, (experts * capacity, 128))
    result, grad_rows, grad_gate, grad_first, grad_second = expert_pass(
        received[:, :D], far_cotangent, far_gate, first, second
    )
    reach = jnp.pad(jnp.stack(split_low(grad_gate[:, 0]), 1), ((0, 0), (0, 125)))
    returned = exchange(
        jnp.concatenate([grad_rows, reach], 1).reshape(experts, capacity, D + 128)
    ).reshape(experts * capacity, D + 128)
    outcome = exchange(result.reshape(experts, capacity, D)).reshape(experts * capacity, D)
    output = state3 + sum(gates[:, k : k + 1] * dot_low(picks[k], outcome) for k in range(2))

    grad_gates = jnp.stack(
        [jnp.sum(dot_low(picks[k], returned[:, D:]), 1) for k in range(2)], 1
    )
    grad_picked = gates * (grad_gates - jnp.sum(gates * grad_gates, -1, keepdims=True))
    grad_logits = jnp.sum(choose * grad_picked[:, :, None], 1).astype(LOW)
    grad_route = dot_over(normed3, grad_logits)
    grad_normed3 = dot_low(both, returned[:, :D]) + dot_back(grad_logits, route_w)
    upstream = cotangent[0].astype(F32)
    grad_state3, gain_last = norm_back(state3, gains[3], grad_normed3)
    grad3 = upstream + grad_state3
    own_first = lax.psum_scatter(grad_first, "row", scatter_dimension=0, tiled=False)
    own_second = lax.psum_scatter(grad_second, "row", scatter_dimension=0, tiled=False)

    grad2, qkv_late, out_late, rel_late, gain_third = attention_backward(
        grad3, stash3, gains[2], qkv[1], out[1], tables[1], hot
    )
    grad1, gain_second, dense_grad_in, dense_grad_out = mlp_backward(
        grad2, state1, normed1, gains[1], dense_in, dense_out
    )
    grad0, qkv_early, out_early, rel_early, gain_first = attention_backward(
        grad1, stash1, gains[0], qkv[0], out[0], tables[0], hot
    )

    def share(block):
        block = lax.psum_scatter(block.astype(LOW), grid, scatter_dimension=0, tiled=True)
        return lax.psum(block, "dp").astype(F32)

    gain_grads = jnp.concatenate([gain_first, gain_second, gain_third, gain_last], 0)
    gain_grads = gain_grads.reshape(4, places, -1).transpose(1, 0, 2).reshape(places, -1)
    rel_grads = jnp.stack([rel_early, rel_late]).reshape(2, places, -1, HEADS)
    rel_grads = rel_grads.transpose(1, 0, 2, 3).reshape(places, -1)
    packed = jnp.concatenate([gain_grads, rel_grads, grad_route.reshape(places, -1)], 1)
    packed = jnp.pad(packed, ((0, 0), (0, -packed.shape[1] % 1024))).reshape(-1, 128)
    packed = share(packed).reshape(-1)
    gain_share = packed[: cuts[0]].reshape(4, -1)
    rel_share = packed[cuts[0] : cuts[0] + cuts[1]].reshape(2, -1, HEADS)
    route_share = packed[cuts[0] + cuts[1] : sum(cuts)].reshape(-1, experts)
    return (
        output[None],
        grad0[None],
        gain_share,
        jnp.stack([share(qkv_early), share(qkv_late)]),
        jnp.stack([share(out_early), share(out_late)]),
        rel_share,
        share(dense_grad_in),
        share(dense_grad_out),
        route_share,
        own_first.astype(F32)[None],
        own_second.astype(F32)[None],
    )


def solution(mesh):
    in_specs = (
        P(("dp", "col"), "row", None),
        P(("dp", "col"), "row", None),
        P(("dp", "col"), "row", None),
        P(),
        P(None, ("row", "col")),
        P(None, ("row", "col"), None),
        P(None, ("row", "col"), None),
        P(None, ("row", "col"), None),
        P(("row", "col"), None),
        P(("row", "col"), None),
        P(("row", "col"), None),
        P(("dp", "col"), None, "row"),
        P(("dp", "col"), "row", None),
    )
    out_specs = (
        P(("dp", "col"), "row", None),
        P(("dp", "col"), "row", None),
        P(None, ("row", "col")),
        P(None, ("row", "col"), None),
        P(None, ("row", "col"), None),
        P(None, ("row", "col"), None),
        P(("row", "col"), None),
        P(("row", "col"), None),
        P(("row", "col"), None),
        P(("dp", "col"), None, "row"),
        P(("dp", "col"), "row", None),
    )
    return jax.shard_map(
        on_device, mesh=mesh, in_specs=in_specs, out_specs=out_specs, check_vma=False
    )
```

```python
import functools

import jax
import jax.numpy as jnp
from jax import lax
from jax.experimental import pallas as pl
from jax.experimental.pallas import tpu as pltpu
from jax.sharding import PartitionSpec as P

D = 768
HEADS = 12
HDIM = 64
FF = 3072
BUCKETS = 32
PLEN = 1024
CLEN = 128
KEYS = PLEN + CLEN
WRAP = KEYS + 128
STRIP = 2 * PLEN
NEG = -1e30
EPS = 1e-06
CURVE = 0.7978845608028654
CUBE = 0.044715
HIGH = lax.Precision.HIGHEST
F32 = jnp.float32
LOW = jnp.bfloat16
MIB = 1 << 20


def dot_low(left, right):
    return jnp.dot(left, right, preferred_element_type=F32)


def dot_back(left, right):
    return lax.dot_general(left, right, (((1,), (1,)), ((), ())), preferred_element_type=F32)


def dot_over(left, right):
    return lax.dot_general(left, right, (((0,), (0,)), ((), ())), preferred_element_type=F32)


def normalise(values):
    center = values - jnp.mean(values, -1, keepdims=True)
    scale = lax.rsqrt(jnp.mean(center * center, -1, keepdims=True) + EPS)
    return center * scale, scale


def norm_rows(values, gain):
    return normalise(values)[0] * gain


def norm_back(values, gain, upstream):
    unit, scale = normalise(values)
    pulled = upstream * gain
    shift = jnp.mean(pulled, -1, keepdims=True)
    along = jnp.mean(pulled * unit, -1, keepdims=True)
    return (pulled - shift - unit * along) * scale, jnp.sum(upstream * unit, 0, keepdims=True)


def gelu_parts(values):
    square = values * values
    bend = jnp.tanh(CURVE * (values + CUBE * square * values))
    half = 0.5 * (1.0 + bend)
    slope = half + 0.5 * values * (1.0 - bend * bend) * (CURVE + 3.0 * CURVE * CUBE * square)
    return values * half, slope


def gelu(values):
    return 0.5 * values * (1.0 + jnp.tanh(CURVE * (values + CUBE * values * values * values)))


def params(mib, steps=1):
    return pltpu.CompilerParams(
        vmem_limit_bytes=mib * MIB, dimension_semantics=("arbitrary",) * steps
    )


def whole(shape):
    return pl.BlockSpec(shape, lambda *_: (0,) * len(shape))


MESH = pl.DeviceIdType.MESH


class Remote:
    def __init__(self, src, dst, send, recv, index, device):
        self.parts = (src, dst, send, recv, index, device)

    def described(self):
        src, dst, send, recv, index, device = self.parts
        return pltpu.make_async_remote_copy(
            src_ref=src,
            dst_ref=dst,
            send_sem=send.at[index],
            recv_sem=recv.at[index],
            device_id=device,
            device_id_type=MESH,
        )

    def start(self):
        self.described().start()

    def wait_recv(self):
        self.described().wait_recv()

    def wait_send(self):
        self.described().wait_send()


def remote(src, dst, send, recv, index, **device):
    return Remote(src, dst, send, recv, index, device)


def neighbours():
    row, dp = lax.axis_index("row"), lax.axis_index("dp")
    across = lax.rem(row + 2, 4)
    core = row + 1 - 2 * lax.rem(row, 2)
    return row, across, core, dp + 1 - 2 * lax.rem(dp, 2)


class Gather:
    def __init__(self, shape, split, cols):
        self.shape, self.split, self.cols = shape, split, cols
        self.result = jax.ShapeDtypeStruct((4, cols) + shape, LOW)
        count = 4 * cols - 1 + (4 * cols - 2 if split else 0)
        self.scratch = [
            pltpu.SemaphoreType.DMA((count + 2 * cols,)),
            pltpu.SemaphoreType.DMA((count + 2 * cols,)),
            pltpu.SemaphoreType.DMA((1,)),
        ]

    def copies(self, src, dst, send, recv, local):
        cols = self.cols
        row, across, core, plane = neighbours()
        col, dp = lax.axis_index("col"), lax.axis_index("dp")
        half = self.shape[0] // 2
        part = pl.ds(lax.rem(dp, 2) * half, half) if self.split else slice(None)
        rest = pl.ds((1 - lax.rem(dp, 2)) * half, half)
        number = [0]

        def make(source, target, **device):
            number[0] += 1
            return remote(source, target, send, recv, number[0] - 1, **device)

        def piece(where, step, which):
            view = dst.at[where, lax.rem(col - step + cols, cols)]
            return view if which == slice(None) else view.at[which]

        own = src if not self.split else src.at[part]
        out = {}
        out["local"] = pltpu.make_async_copy(src, dst.at[row, col], local.at[0])
        out["z"] = [
            make(own, piece(row, 0, part), col=lax.rem(col + step, cols)) for step in range(1, cols)
        ]
        out["x"] = [make(own, piece(row, 0, part), row=across)]
        out["x"] += [
            make(piece(row, step, part), piece(row, step, part), row=across)
            for step in range(1, cols)
        ]
        out["core own"] = make(src, dst.at[row, col], row=core)
        out["core z"] = [
            make(piece(row, step, part), piece(row, step, part), row=core) for step in range(1, cols)
        ]
        out["core x"] = [
            make(piece(across, step, part), piece(across, step, part), row=core)
            for step in range(cols)
        ]
        if self.split:
            out["y z"] = [
                make(piece(row, step, part), piece(row, step, part), dp=plane)
                for step in range(1, cols)
            ]
            out["y x"] = [
                make(piece(across, step, part), piece(across, step, part), dp=plane)
                for step in range(cols)
            ]
            out["core y z"] = [
                make(piece(row, step, rest), piece(row, step, rest), row=core)
                for step in range(1, cols)
            ]
            out["core y x"] = [
                make(piece(across, step, rest), piece(across, step, rest), row=core)
                for step in range(cols)
            ]
        return out

    def peers(self):
        cols, col = self.cols, lax.axis_index("col")
        row, across, core, plane = neighbours()
        found = {(0, step): dict(col=lax.rem(col + step, cols)) for step in range(1, cols)}
        found.update(across=dict(row=across), core=dict(row=core))
        if self.split:
            found[(1, 0)] = dict(dp=plane)
        return found

    def phase(self, number, *refs):
        out = self.copies(*refs)
        if number == 0:
            out["local"].start()
            for copy in out["z"]:
                copy.start()
            out["x"][0].start()
            out["core own"].start()
        elif number == 1:
            for step in self.order():
                out["z"][step - 1].wait_recv()
                out["x"][step].start()
                if self.split:
                    out["y z"][step - 1].start()
                out["core z"][step - 1].start()
        elif number == 2:
            for step in [0] + self.order():
                out["x"][step].wait_recv()
                if self.split:
                    out["y x"][step].start()
                out["core x"][step].start()
        elif number == 3 and self.split:
            for step in self.order():
                out["y z"][step - 1].wait_recv()
                out["core y z"][step - 1].start()
            for step in [0] + self.order():
                out["y x"][step].wait_recv()
                out["core y x"][step].start()
        elif number == 4:
            out["local"].wait()
            late = [out["core own"]] + out["core z"] + out["core x"]
            if self.split:
                late += out["core y z"] + out["core y x"]
            for copy in late:
                copy.wait_recv()
            early = out["z"] + out["x"] + late
            if self.split:
                early += out["y z"] + out["y x"]
            for copy in early:
                copy.wait_send()

    def order(self):
        steps = list(range(1, self.cols))
        return sorted(steps, key=lambda step: min(step, self.cols - step))


class Rows:
    def __init__(self, shape):
        self.result = jax.ShapeDtypeStruct((4,) + shape, LOW)
        self.scratch = [
            pltpu.SemaphoreType.DMA((3,)),
            pltpu.SemaphoreType.DMA((3,)),
            pltpu.SemaphoreType.DMA((1,)),
        ]

    def peers(self):
        row, across, core, plane = neighbours()
        return dict(across=dict(row=across), core=dict(row=core))

    def phase(self, number, src, dst, send, recv, local):
        row, across, core, plane = neighbours()
        own = pltpu.make_async_copy(src, dst.at[row], local.at[0])
        far = remote(src, dst.at[row], send, recv, 0, row=across)
        near = remote(src, dst.at[row], send, recv, 1, row=core)
        on = remote(dst.at[across], dst.at[across], send, recv, 2, row=core)
        if number == 0:
            own.start()
            far.start()
            near.start()
        elif number == 2:
            far.wait_recv()
            on.start()
        elif number == 4:
            own.wait()
            near.wait_recv()
            on.wait_recv()
            for copy in (far, near, on):
                copy.wait_send()


class Swap:
    def __init__(self, shape, planes, cols):
        self.planes, self.cols, self.count = planes, cols, planes * cols
        self.result = jax.ShapeDtypeStruct((self.count,) + shape, LOW)
        self.scratch = [
            pltpu.SemaphoreType.DMA((self.count - 1,)),
            pltpu.SemaphoreType.DMA((self.count - 1,)),
            pltpu.SemaphoreType.DMA((1,)),
        ]

    def peers(self):
        dp, col = lax.axis_index("dp"), lax.axis_index("col")
        steps = [(a, b) for a in range(self.planes) for b in range(self.cols) if a or b]
        return {
            (a, b): dict(dp=lax.rem(dp + a, self.planes), col=lax.rem(col + b, self.cols))
            for a, b in steps
        }

    def phase(self, number, src, dst, send, recv, local):
        if number not in (0, 4):
            return
        me = lax.axis_index("dp") * self.cols + lax.axis_index("col")
        own = pltpu.make_async_copy(src.at[me], dst.at[me], local.at[0])
        copies = [
            remote(src.at[to["dp"] * self.cols + to["col"]], dst.at[me], send, recv, index, **to)
            for index, to in enumerate(self.peers().values())
        ]
        if number == 0:
            own.start()
            for copy in copies:
                copy.start()
        else:
            own.wait()
            for copy in copies:
                copy.wait_recv()
            for copy in copies:
                copy.wait_send()


def greet(flows):
    barrier = pltpu.get_barrier_semaphore()
    devices = {}
    for flow in flows:
        devices.update(flow.peers())
    for device in devices.values():
        pl.semaphore_signal(barrier, inc=1, device_id=device, device_id_type=MESH)
    pl.semaphore_wait(barrier, len(devices))


def carry(body, flows, marks, grid, in_specs, out_specs, out_shape, scratch_shapes, mib, name):
    inputs, outputs, extras = len(in_specs), len(out_specs), len(scratch_shapes)
    steps = grid[0]
    hbm = pl.BlockSpec(memory_space=pl.ANY)

    def kernel(*refs):
        refs = list(refs)
        take = lambda count: [refs.pop(0) for _ in range(count)]
        own_in, sources = take(inputs), take(len(flows))
        own_out, results = take(outputs), take(len(flows))
        own_extra = take(extras)
        packs = [
            [source, result] + take(3) for source, result in zip(sources, results)
        ]
        step = pl.program_id(0)

        def phase(number):
            for flow, pack in zip(flows, packs):
                flow.phase(number, *pack)

        @pl.when(step == 0)
        def _():
            greet(flows)
            phase(0)

        for number, mark in enumerate(marks):
            if mark < steps:
                pl.when(step == mark)(functools.partial(phase, number + 1))
        if body is not None:
            body(*own_in, *own_out, *own_extra)

        @pl.when(step == steps - 1)
        def _():
            for number, mark in enumerate(marks):
                if mark >= steps:
                    phase(number + 1)
            phase(4)

    def call(*args):
        return pl.pallas_call(
            kernel,
            grid=grid,
            out_shape=tuple(out_shape) + tuple(flow.result for flow in flows),
            in_specs=list(in_specs) + [hbm] * len(flows),
            out_specs=tuple(out_specs) + (hbm,) * len(flows),
            scratch_shapes=list(scratch_shapes) + [s for flow in flows for s in flow.scratch],
            compiler_params=pltpu.CompilerParams(
                vmem_limit_bytes=mib * MIB,
                dimension_semantics=("arbitrary",),
                collective_id=name,
                has_side_effects=True,
            ),
        )(*args)

    return call


def bias_table(buckets, rel):
    place = jnp.arange(WRAP, dtype=jnp.int32)
    dist = jnp.where(place <= PLEN, PLEN - place, PLEN + WRAP - place)
    read = (place <= PLEN) | (place > KEYS)
    index = jnp.take(buckets, jnp.clip(dist, 0, KEYS - 1), axis=0)
    hot = ((index[:, None] == jnp.arange(BUCKETS)[None, :]) & read[:, None]).astype(LOW)
    floor = jnp.where(read, 0.0, NEG).astype(F32)
    return hot, floor


def fill_strip(strip, table, head):
    @pl.when(pl.program_id(0) == 0)
    def _():
        strip[:, KEYS:] = jnp.full((128, STRIP - KEYS), NEG, F32)

    line = jnp.broadcast_to(table[pl.ds(head, 1), :], (128, WRAP))
    strip[:, :KEYS] = pltpu.roll(line, 0, 1, stride=1, stride_axis=0)[:, :KEYS]


def tiles_of(pslice):
    places = []
    for tile in range(pslice // 128):
        start = PLEN - (lax.axis_index("row") * pslice + tile * 128)
        places.append((tile * 128, pl.ds(pl.multiple_of(start, 128), PLEN), PLEN))
    places.append((pslice, pl.ds(0, KEYS), KEYS))
    return places


def attend_kernel(pslice, query, keys, values, table, mixed, total, strip, raw, weights):
    pair = pl.program_id(0)
    lane = lax.broadcasted_iota(jnp.int32, (1, 128), 1)

    @pl.when(pair == 0)
    def _():
        weights[:pslice, PLEN:] = jnp.zeros((pslice, CLEN), LOW)

    for half in range(2):
        mine = (lane < HDIM) if half == 0 else (lane >= HDIM)
        fill_strip(strip, table, 2 * pair + half)
        part = jnp.where(mine, query[...], 0) * HDIM ** (-0.5)
        raw[...] = dot_back(part.astype(LOW), keys[...])
        for row, place, count in tiles_of(pslice):
            rows = pl.ds(row, 128)
            scores = raw[rows, :count] + strip[:, place]
            top = jnp.max(scores, -1, keepdims=True)
            raised = jnp.exp(scores - top)
            summed = jnp.sum(raised, -1, keepdims=True)
            weights[rows, :count] = (raised * (1.0 / summed)).astype(LOW)
            log_total = jnp.broadcast_to(top + jnp.log(summed), (128, 128))
            if half == 0:
                total[rows, :] = log_total
            else:
                total[rows, :] = jnp.where(mine, log_total, total[rows, :])
        result = dot_low(weights[...], values[...]).astype(LOW)
        if half == 0:
            mixed[...] = result
        else:
            mixed[...] = jnp.where(mine, result, mixed[...])


def attend_forward(query, keys, values, table, flows=(), marks=(), sources=(), name=None):
    tokens = query.shape[0]
    pslice = tokens - CLEN
    block = lambda rows: pl.BlockSpec((rows, 128), lambda i: (0, i))
    shapes = dict(
        grid=(HEADS // 2,),
        out_shape=(
            jax.ShapeDtypeStruct((tokens, D), LOW),
            jax.ShapeDtypeStruct((tokens, D), F32),
        ),
        in_specs=[block(tokens), block(KEYS), block(KEYS), whole(table.shape)],
        out_specs=(block(tokens), block(tokens)),
        scratch_shapes=[
            pltpu.VMEM((128, STRIP), F32),
            pltpu.VMEM((tokens, KEYS), F32),
            pltpu.VMEM((tokens, KEYS), LOW),
        ],
    )
    body = functools.partial(attend_kernel, pslice)
    if flows:
        call = carry(body, flows, marks, mib=32, name=name, **shapes)
    else:
        call = pl.pallas_call(body, compiler_params=params(32), **shapes)
    return call(query, keys, values, table, *sources)


def attend_back_kernel(
    pslice,
    query,
    keys,
    values,
    table,
    total,
    grad_mixed,
    grad_query,
    grad_keys,
    grad_values,
    grad_table,
    strip,
    raw,
    pulled,
    probs,
    grads,
    folded,
    sum_keys,
    sum_values,
):
    pair = pl.program_id(0)
    lane = lax.broadcasted_iota(jnp.int32, (1, 128), 1)
    across = lax.broadcasted_iota(jnp.int32, (128, 128), 0)
    along = lax.broadcasted_iota(jnp.int32, (128, 128), 1)
    mirror = (across + along == 127).astype(LOW)

    @pl.when(pair == 0)
    def _():
        probs[:pslice, PLEN:] = jnp.zeros((pslice, CLEN), LOW)
        grads[:pslice, PLEN:] = jnp.zeros((pslice, CLEN), LOW)

    for half in range(2):
        mine = (lane < HDIM) if half == 0 else (lane >= HDIM)
        fill_strip(strip, table, 2 * pair + half)
        part = (jnp.where(mine, query[...], 0) * HDIM ** (-0.5)).astype(LOW)
        upstream = jnp.where(mine, grad_mixed[...], 0).astype(LOW)
        raw[...] = dot_back(part, keys[...])
        pulled[...] = dot_back(upstream, values[...])
        folded[...] = jnp.zeros_like(folded)
        for row, place, count in tiles_of(pslice):
            rows = pl.ds(row, 128)
            log_total = total[rows, half * HDIM : half * HDIM + 1]
            chance = jnp.exp(raw[rows, :count] + strip[:, place] - log_total)
            product = chance * pulled[rows, :count]
            centre = jnp.sum(product, -1, keepdims=True)
            slope = (product - chance * centre).astype(LOW)
            probs[rows, :count] = chance.astype(LOW)
            grads[rows, :count] = slope
            folded[:, place] += dot_low(mirror, slope)
        result = dot_low(grads[...], keys[...]) * HDIM ** (-0.5)
        if half == 0:
            grad_query[...] = result.astype(LOW)
            sum_keys[...] = dot_over(part, grads[...])
            sum_values[...] = dot_over(upstream, probs[...])
        else:
            grad_query[...] = jnp.where(mine, result.astype(LOW), grad_query[...])
            sum_keys[...] += dot_over(part, grads[...])
            sum_values[...] += dot_over(upstream, probs[...])
        turned = pltpu.roll(folded[:, :WRAP], WRAP - 127, 1, stride=1, stride_axis=0)
        grad_table[pl.ds(2 * pair + half, 1), :] = jnp.sum(turned, 0, keepdims=True)
    grad_keys[...] = sum_keys[...].T.astype(LOW)
    grad_values[...] = sum_values[...].T.astype(LOW)


def attend_backward(query, keys, values, table, total, grad_mixed):
    tokens = query.shape[0]
    pslice = tokens - CLEN
    block = lambda rows: pl.BlockSpec((rows, 128), lambda i: (0, i))
    return pl.pallas_call(
        functools.partial(attend_back_kernel, pslice),
        grid=(HEADS // 2,),
        out_shape=(
            jax.ShapeDtypeStruct((tokens, D), LOW),
            jax.ShapeDtypeStruct((KEYS, D), LOW),
            jax.ShapeDtypeStruct((KEYS, D), LOW),
            jax.ShapeDtypeStruct(table.shape, F32),
        ),
        in_specs=[
            block(tokens),
            block(KEYS),
            block(KEYS),
            whole(table.shape),
            block(tokens),
            block(tokens),
        ],
        out_specs=(block(tokens), block(KEYS), block(KEYS), whole(table.shape)),
        scratch_shapes=[
            pltpu.VMEM((128, STRIP), F32),
            pltpu.VMEM((tokens, KEYS), F32),
            pltpu.VMEM((tokens, KEYS), F32),
            pltpu.VMEM((tokens, KEYS), LOW),
            pltpu.VMEM((tokens, KEYS), LOW),
            pltpu.VMEM((128, STRIP), F32),
            pltpu.VMEM((128, KEYS), F32),
            pltpu.VMEM((128, KEYS), F32),
        ],
        compiler_params=params(32),
    )(query, keys, values, table, total, grad_mixed)


def mlp_forward_kernel(state, gain, first, second, result, normed):
    step = pl.program_id(0)

    @pl.when(step == 0)
    def _():
        normed[...] = norm_rows(state[...], gain[...]).astype(LOW)
        result[...] = state[...]

    active = gelu(dot_low(normed[...], first[...])).astype(LOW)
    result[...] += dot_low(active, second[...])


def mlp_forward(state, gain, first, second):
    tokens = state.shape[0]
    part = 768
    return pl.pallas_call(
        mlp_forward_kernel,
        grid=(FF // part,),
        out_shape=(
            jax.ShapeDtypeStruct((tokens, D), F32),
            jax.ShapeDtypeStruct((tokens, D), LOW),
        ),
        in_specs=[
            whole((tokens, D)),
            whole((1, D)),
            pl.BlockSpec((D, part), lambda i: (0, i)),
            pl.BlockSpec((part, D), lambda i: (i, 0)),
        ],
        out_specs=(whole((tokens, D)), whole((tokens, D))),
        compiler_params=params(32),
    )(state, gain, first, second)


def mlp_backward_kernel(
    grad_next, state, normed, gain, first, second, result, grad_gain, grad_first, grad_second, low, total
):
    step = pl.program_id(0)

    @pl.when(step == 0)
    def _():
        low[...] = grad_next[...].astype(LOW)
        total[...] = jnp.zeros_like(total)

    active, slope = gelu_parts(dot_low(normed[...], first[...]))
    grad_hidden = (slope * dot_back(low[...], second[...])).astype(LOW)
    grad_second[...] = dot_over(active.astype(LOW), low[...]).astype(LOW)
    grad_first[...] = dot_over(normed[...], grad_hidden).astype(LOW)
    total[...] += dot_back(grad_hidden, first[...])

    @pl.when(step == pl.num_programs(0) - 1)
    def _():
        grad_state, grad_line = norm_back(state[...], gain[...], total[...])
        result[...] = grad_next[...] + grad_state
        grad_gain[...] = grad_line


def mlp_backward(grad_next, state, normed, gain, first, second):
    tokens = state.shape[0]
    part = 768
    return pl.pallas_call(
        mlp_backward_kernel,
        grid=(FF // part,),
        out_shape=(
            jax.ShapeDtypeStruct((tokens, D), F32),
            jax.ShapeDtypeStruct((1, D), F32),
            jax.ShapeDtypeStruct((D, FF), LOW),
            jax.ShapeDtypeStruct((FF, D), LOW),
        ),
        in_specs=[
            whole((tokens, D)),
            whole((tokens, D)),
            whole((tokens, D)),
            whole((1, D)),
            pl.BlockSpec((D, part), lambda i: (0, i)),
            pl.BlockSpec((part, D), lambda i: (i, 0)),
        ],
        out_specs=(
            whole((tokens, D)),
            whole((1, D)),
            pl.BlockSpec((D, part), lambda i: (0, i)),
            pl.BlockSpec((part, D), lambda i: (i, 0)),
        ),
        scratch_shapes=[pltpu.VMEM((tokens, D), LOW), pltpu.VMEM((tokens, D), F32)],
        compiler_params=params(48),
    )(grad_next, state, normed, gain, first, second)


def expert_kernel(
    rows, cotangent, gate, first, second, result, grad_rows, grad_gate, grad_first, grad_second, upstream, total, back
):
    step = pl.program_id(0)

    @pl.when(step == 0)
    def _():
        upstream[...] = (gate[:, :1] * cotangent[...].astype(F32)).astype(LOW)
        total[...] = jnp.zeros_like(total)
        back[...] = jnp.zeros_like(back)

    active, slope = gelu_parts(dot_low(rows[...], first[...]))
    active = active.astype(LOW)
    total[...] += dot_low(active, second[...])
    grad_hidden = (slope * dot_back(upstream[...], second[...])).astype(LOW)
    grad_second[...] = dot_over(active, upstream[...]).astype(LOW)
    grad_first[...] = dot_over(rows[...], grad_hidden).astype(LOW)
    back[...] += dot_back(grad_hidden, first[...])

    @pl.when(step == pl.num_programs(0) - 1)
    def _():
        low = total[...].astype(LOW)
        result[...] = low
        grad_rows[...] = back[...].astype(LOW)
        reach = jnp.sum(cotangent[...].astype(F32) * low.astype(F32), -1, keepdims=True)
        grad_gate[...] = jnp.broadcast_to(reach, grad_gate.shape)


def expert_pass(rows, cotangent, gate, first, second):
    count = rows.shape[0]
    shards, _, width = first.shape
    part = 256
    split = width // part
    inner = pl.BlockSpec((None, D, part), lambda i: (i // split, 0, i % split))
    outer = pl.BlockSpec((None, part, D), lambda i: (i // split, i % split, 0))
    return pl.pallas_call(
        expert_kernel,
        grid=(shards * split,),
        out_shape=(
            jax.ShapeDtypeStruct((count, D), LOW),
            jax.ShapeDtypeStruct((count, D), LOW),
            jax.ShapeDtypeStruct((count, 128), F32),
            jax.ShapeDtypeStruct(first.shape, LOW),
            jax.ShapeDtypeStruct(second.shape, LOW),
        ),
        in_specs=[whole((count, D)), whole((count, D)), whole((count, 128)), inner, outer],
        out_specs=(whole((count, D)), whole((count, D)), whole((count, 128)), inner, outer),
        scratch_shapes=[
            pltpu.VMEM((count, D), LOW),
            pltpu.VMEM((count, D), F32),
            pltpu.VMEM((count, D), F32),
        ],
        compiler_params=params(56),
    )(rows, cotangent, gate, first, second)


def split_low(values):
    high = values.astype(LOW)
    rest = values - high.astype(F32)
    middle = rest.astype(LOW)
    return high, middle, (rest - middle.astype(F32)).astype(LOW)


def exchange(block):
    return lax.all_to_all(block, ("dp", "col"), split_axis=0, concat_axis=0, tiled=True)


def attention_forward(state, gain, others, weight_in, weight_out, table, raw_others):
    tokens = state.shape[0]
    pslice = tokens - CLEN
    normed = norm_rows(state, gain).astype(LOW)
    if others is None:
        shared = lax.all_gather(normed[:pslice], "row", axis=0, tiled=True)
    else:
        shared = norm_rows(others.astype(F32), gain).astype(LOW)
    read = jnp.concatenate([shared, normed[pslice:]], 0)
    query = dot_low(normed, weight_in[:, :D]).astype(LOW)
    keys = dot_low(read, weight_in[:, D : 2 * D]).astype(LOW)
    values = dot_low(read, weight_in[:, 2 * D :]).astype(LOW)
    mixed, total = attend_forward(query, keys, values, table)
    return state + dot_low(mixed, weight_out), (state, normed, read, query, keys, values, mixed, total)


def attention_backward(grad_next, stash, gain, weight_in, weight_out, table, hot):
    state, normed, read, query, keys, values, mixed, total = stash
    pslice = state.shape[0] - CLEN
    branch = grad_next.astype(LOW)
    grad_out = dot_over(mixed, branch).astype(LOW)
    grad_mixed = dot_back(branch, weight_out).astype(LOW)
    grad_query, grad_keys, grad_values, grad_table = attend_backward(
        query, keys, values, table, total, grad_mixed
    )
    grad_in = jnp.concatenate(
        [dot_over(normed, grad_query), dot_over(read, grad_keys), dot_over(read, grad_values)], 1
    ).astype(LOW)
    grad_read = dot_back(grad_keys, weight_in[:, D : 2 * D]) + dot_back(
        grad_values, weight_in[:, 2 * D :]
    )
    own = lax.psum_scatter(
        grad_read[:PLEN].astype(LOW), "row", scatter_dimension=0, tiled=True
    ).astype(F32)
    grad_normed = dot_back(grad_query, weight_in[:, :D]) + jnp.concatenate(
        [own, grad_read[PLEN:]], 0
    )
    grad_state, grad_gain = norm_back(state, gain, grad_normed)
    grad_rel = jnp.dot(grad_table[:HEADS], hot.astype(F32), precision=HIGH).T
    return grad_next + grad_state, grad_in, grad_out, grad_rel, grad_gain


def general(
    inputs,
    cotangent,
    routes,
    buckets,
    norm_gains,
    attn_qkv,
    attn_out,
    rel_bias,
    mlp_in,
    mlp_out,
    router,
    expert_in,
    expert_out,
):
    grid = ("row", "col")
    places = lax.axis_size(grid)
    experts = lax.axis_size(("dp", "col"))
    tokens = inputs.shape[1]
    pslice = tokens - CLEN
    capacity = max(2, 3 * tokens // experts)

    small = [norm_gains.reshape(-1), rel_bias.reshape(-1), router.reshape(-1)]
    cuts = [part.shape[0] for part in small]
    packed = jnp.concatenate(small)
    packed = jnp.pad(packed, (0, -packed.shape[0] % 1024)).reshape(-1, 128)
    packed = lax.all_gather(packed, grid, axis=0, tiled=False).reshape(places, -1)
    gains = packed[:, : cuts[0]].reshape(places, 4, -1).transpose(1, 0, 2).reshape(4, 1, D).astype(F32)
    rel = packed[:, cuts[0] : cuts[0] + cuts[1]].reshape(places, 2, -1, HEADS)
    rel = rel.transpose(1, 0, 2, 3).reshape(2, BUCKETS, HEADS)
    route_w = packed[:, cuts[0] + cuts[1] : sum(cuts)].reshape(D, experts)

    qkv = [lax.all_gather(attn_qkv[i], grid, axis=0, tiled=True) for i in range(2)]
    out = [lax.all_gather(attn_out[i], grid, axis=0, tiled=True) for i in range(2)]
    dense_in = lax.all_gather(mlp_in, grid, axis=0, tiled=True)
    dense_out = lax.all_gather(mlp_out, grid, axis=0, tiled=True)
    first = lax.all_gather(expert_in[0], "row", axis=0, tiled=False)
    second = lax.all_gather(expert_out[0], "row", axis=0, tiled=False)

    hot, floor = bias_table(buckets, rel)
    tables = [
        jnp.pad(dot_low(rel[i].T, hot.T) + floor[None], ((0, 16 - HEADS), (0, 0))) for i in range(2)
    ]

    flat = routes[0].reshape(-1)
    levels = jnp.arange(experts, dtype=jnp.int32)
    choose = (routes[0][:, :, None] == levels[None, None, :]).astype(F32)
    hits = (flat[:, None] == levels[None, :]).astype(LOW)
    before = jnp.arange(2 * tokens)
    before = (before[:, None] > before[None, :]).astype(LOW)
    rank = jnp.sum(dot_low(before, hits) * hits.astype(F32), 1).astype(jnp.int32)
    place = (flat * capacity + rank).reshape(tokens, 2)
    slots = jnp.arange(experts * capacity, dtype=jnp.int32)
    picks = [(place[:, k][:, None] == slots[None, :]).astype(LOW) for k in range(2)]
    both = picks[0] + picks[1]
    sent_cotangent = dot_over(both, cotangent[0]).astype(LOW).reshape(experts, capacity, D)
    far_cotangent = exchange(sent_cotangent).reshape(experts * capacity, D)

    state0 = inputs[0].astype(F32)
    shared0 = lax.all_gather(inputs[0, :pslice], "row", axis=0, tiled=True)
    state1, stash1 = attention_forward(state0, gains[0], shared0, qkv[0], out[0], tables[0], None)
    state2, normed1 = mlp_forward(state1, gains[1], dense_in, dense_out)
    state3, stash3 = attention_forward(state2, gains[2], None, qkv[1], out[1], tables[1], None)

    normed3 = norm_rows(state3, gains[3]).astype(LOW)
    logits = dot_low(normed3, route_w)
    picked = jnp.sum(choose * logits[:, None, :], -1)
    raised = jnp.exp(picked - jnp.max(picked, -1, keepdims=True))
    gates = raised / jnp.sum(raised, -1, keepdims=True)
    parts = [split_low(gates[:, k]) for k in range(2)]
    spread = [
        dot_over(picks[k], jnp.pad(jnp.stack(parts[k], 1), ((0, 0), (0, 125)))) for k in range(2)
    ]
    sent = jnp.concatenate([dot_over(both, normed3), spread[0] + spread[1]], 1).astype(LOW)
    received = exchange(sent.reshape(experts, capacity, D + 128)).reshape(experts * capacity, D + 128)
    far_gate = jnp.sum(received[:, D : D + 3].astype(F32), 1, keepdims=True)
    far_gate = jnp.broadcast_to(far_gate, (experts * capacity, 128))
    result, grad_rows, grad_gate, grad_first, grad_second = expert_pass(
        received[:, :D], far_cotangent, far_gate, first, second
    )
    reach = jnp.pad(jnp.stack(split_low(grad_gate[:, 0]), 1), ((0, 0), (0, 125)))
    returned = exchange(
        jnp.concatenate([grad_rows, reach], 1).reshape(experts, capacity, D + 128)
    ).reshape(experts * capacity, D + 128)
    outcome = exchange(result.reshape(experts, capacity, D)).reshape(experts * capacity, D)
    output = state3 + sum(gates[:, k : k + 1] * dot_low(picks[k], outcome) for k in range(2))

    grad_gates = jnp.stack(
        [jnp.sum(dot_low(picks[k], returned[:, D:]), 1) for k in range(2)], 1
    )
    grad_picked = gates * (grad_gates - jnp.sum(gates * grad_gates, -1, keepdims=True))
    grad_logits = jnp.sum(choose * grad_picked[:, :, None], 1).astype(LOW)
    grad_route = dot_over(normed3, grad_logits)
    grad_normed3 = dot_low(both, returned[:, :D]) + dot_back(grad_logits, route_w)
    upstream = cotangent[0].astype(F32)
    grad_state3, gain_last = norm_back(state3, gains[3], grad_normed3)
    grad3 = upstream + grad_state3
    own_first = lax.psum_scatter(grad_first, "row", scatter_dimension=0, tiled=False)
    own_second = lax.psum_scatter(grad_second, "row", scatter_dimension=0, tiled=False)

    grad2, qkv_late, out_late, rel_late, gain_third = attention_backward(
        grad3, stash3, gains[2], qkv[1], out[1], tables[1], hot
    )
    grad1, gain_second, dense_grad_in, dense_grad_out = mlp_backward(
        grad2, state1, normed1, gains[1], dense_in, dense_out
    )
    grad0, qkv_early, out_early, rel_early, gain_first = attention_backward(
        grad1, stash1, gains[0], qkv[0], out[0], tables[0], hot
    )

    def share(block):
        block = lax.psum_scatter(block.astype(LOW), grid, scatter_dimension=0, tiled=True)
        return lax.psum(block, "dp").astype(F32)

    gain_grads = jnp.concatenate([gain_first, gain_second, gain_third, gain_last], 0)
    gain_grads = gain_grads.reshape(4, places, -1).transpose(1, 0, 2).reshape(places, -1)
    rel_grads = jnp.stack([rel_early, rel_late]).reshape(2, places, -1, HEADS)
    rel_grads = rel_grads.transpose(1, 0, 2, 3).reshape(places, -1)
    packed = jnp.concatenate([gain_grads, rel_grads, grad_route.reshape(places, -1)], 1)
    packed = jnp.pad(packed, ((0, 0), (0, -packed.shape[1] % 1024))).reshape(-1, 128)
    packed = share(packed).reshape(-1)
    gain_share = packed[: cuts[0]].reshape(4, -1)
    rel_share = packed[cuts[0] : cuts[0] + cuts[1]].reshape(2, -1, HEADS)
    route_share = packed[cuts[0] + cuts[1] : sum(cuts)].reshape(-1, experts)
    return (
        output[None],
        grad0[None],
        gain_share,
        jnp.stack([share(qkv_early), share(qkv_late)]),
        jnp.stack([share(out_early), share(out_late)]),
        rel_share,
        share(dense_grad_in),
        share(dense_grad_out),
        route_share,
        own_first.astype(F32)[None],
        own_second.astype(F32)[None],
    )


def mlp_up_kernel(state, gain, first, second, result, normed):
    step = pl.program_id(0)

    @pl.when(step == 0)
    def _():
        normed[...] = norm_rows(state[...], gain[...]).astype(LOW)
        result[...] = state[...]

    active = gelu(dot_low(normed[...], first[...].reshape(D, D))).astype(LOW)
    result[...] += dot_low(active, second[...].reshape(D, D))


def mlp_blocks(cols, piece):
    return (
        pl.BlockSpec((4, cols, None, piece, D), lambda i: (0, 0, 4 + i, 0, 0)),
        pl.BlockSpec((None, cols, 4, piece, D), lambda i: (i, 0, 0, 0, 0)),
    )


def mlp_up(state, gain, dense, flows, marks, sources, name):
    tokens = state.shape[0]
    _, cols, _, piece, _ = dense.shape
    return carry(
        mlp_up_kernel,
        flows,
        marks,
        grid=(4,),
        out_shape=(
            jax.ShapeDtypeStruct((tokens, D), F32),
            jax.ShapeDtypeStruct((tokens, D), LOW),
        ),
        in_specs=[whole((tokens, D)), whole((1, D)), *mlp_blocks(cols, piece)],
        out_specs=(whole((tokens, D)), whole((tokens, D))),
        scratch_shapes=[],
        mib=32,
        name=name,
    )(state, gain, dense, dense, *sources)


def mlp_down_kernel(
    grad_next, state, normed, gain, first, second, result, grad_gain, grad_first, grad_second, low, total
):
    step = pl.program_id(0)

    @pl.when(step == 0)
    def _():
        low[...] = grad_next[...].astype(LOW)
        total[...] = jnp.zeros_like(total)

    inner, outer = first[...].reshape(D, D), second[...].reshape(D, D)
    active, slope = gelu_parts(dot_low(normed[...], inner))
    grad_hidden = (slope * dot_back(low[...], outer)).astype(LOW)
    grad_second[...] = dot_over(active.astype(LOW), low[...]).astype(LOW).reshape(grad_second.shape)
    grad_first[...] = dot_over(normed[...], grad_hidden).astype(LOW).reshape(grad_first.shape)
    total[...] += dot_back(grad_hidden, inner)

    @pl.when(step == pl.num_programs(0) - 1)
    def _():
        grad_state, grad_line = norm_back(state[...], gain[...], total[...])
        result[...] = grad_next[...] + grad_state
        grad_gain[...] = grad_line


def mlp_down(grad_next, state, normed, gain, dense):
    tokens = state.shape[0]
    _, cols, _, piece, _ = dense.shape
    share = jax.ShapeDtypeStruct((4, cols, 4, piece, D), LOW)
    return pl.pallas_call(
        mlp_down_kernel,
        grid=(4,),
        out_shape=(
            jax.ShapeDtypeStruct((tokens, D), F32),
            jax.ShapeDtypeStruct((1, D), F32),
            share,
            share,
        ),
        in_specs=[
            whole((tokens, D)),
            whole((tokens, D)),
            whole((tokens, D)),
            whole((1, D)),
            *mlp_blocks(cols, piece),
        ],
        out_specs=(
            whole((tokens, D)),
            whole((1, D)),
            pl.BlockSpec((4, cols, None, piece, D), lambda i: (0, 0, i, 0, 0)),
            pl.BlockSpec((None, cols, 4, piece, D), lambda i: (i, 0, 0, 0, 0)),
        ),
        scratch_shapes=[pltpu.VMEM((tokens, D), LOW), pltpu.VMEM((tokens, D), F32)],
        compiler_params=params(48),
    )(grad_next, state, normed, gain, dense, dense)


CORE = [(0, 1), (1, 0), (2, 3), (3, 2)]
ACROSS = [(0, 2), (2, 0), (1, 3), (3, 1)]


def pick(block, index, axis=0):
    return lax.dynamic_index_in_dim(block, index, axis, keepdims=False)


def added(left, right):
    return (left.astype(F32) + right.astype(F32)).astype(LOW)


def reduce_row(block):
    row = lax.axis_index("row")
    x, core = row // 2, row % 2
    block = block.reshape((2, 2) + block.shape[1:])
    mine = added(pick(block, core, 1), lax.ppermute(pick(block, 1 - core, 1), "row", CORE))
    return pick(mine, x).astype(F32) + lax.ppermute(pick(mine, 1 - x), "row", ACROSS).astype(F32)


def reduce_shares(block):
    row, col, dp = lax.axis_index("row"), lax.axis_index("col"), lax.axis_index("dp")
    cols, planes = lax.axis_size("col"), lax.axis_size("dp")
    x, core = row // 2, row % 2
    swap = [(i, i + 1 - 2 * (i % 2)) for i in range(planes)]
    half = block.shape[2] // 2
    block = block.reshape((2, 2) + block.shape[1:])
    mine = added(pick(block, core, 1), lax.ppermute(pick(block, 1 - core, 1), "row", CORE))
    cut = lambda which: lax.dynamic_slice_in_dim(mine, which * half, half, 2)
    mine = added(cut(dp % 2), lax.ppermute(cut(1 - dp % 2), "dp", swap))
    mine = added(pick(mine, x), lax.ppermute(pick(mine, 1 - x), "row", ACROSS))
    total = pick(mine, col).astype(F32)
    for step in range(1, cols):
        shift = [(i, (i + step) % cols) for i in range(cols)]
        total = total + lax.ppermute(pick(mine, (col + step) % cols), "col", shift).astype(F32)
    total = total.astype(LOW)
    other = lax.ppermute(total, "dp", swap)
    both = jnp.stack([total, other])
    return jnp.concatenate([pick(both, dp % 2), pick(both, 1 - dp % 2)], 0).astype(F32)


def attention_up(state, normed, shared, weights, table, flows, marks, sources, name):
    tokens = state.shape[0]
    pslice = tokens - CLEN
    parts = [weights[:, :, i].reshape(D, D) for i in range(4)]
    read = jnp.concatenate([shared, normed[pslice:]], 0)
    query = dot_low(normed, parts[0]).astype(LOW)
    keys = dot_low(read, parts[1]).astype(LOW)
    values = dot_low(read, parts[2]).astype(LOW)
    mixed, total, *moved = attend_forward(query, keys, values, table, flows, marks, sources, name)
    stash = (state, normed, read, query, keys, values, mixed, total, parts)
    return state + dot_low(mixed, parts[3]), stash, moved


def attention_down(grad_next, stash, gain, table, hot, shape):
    state, normed, read, query, keys, values, mixed, total, parts = stash
    pslice = state.shape[0] - CLEN
    branch = grad_next.astype(LOW)
    grad_out = dot_over(mixed, branch)
    grad_mixed = dot_back(branch, parts[3]).astype(LOW)
    grad_query, grad_keys, grad_values, grad_table = attend_backward(
        query, keys, values, table, total, grad_mixed
    )
    grads = [dot_over(normed, grad_query), dot_over(read, grad_keys), dot_over(read, grad_values)]
    grads = jnp.stack([grad.astype(LOW).reshape(shape) for grad in grads + [grad_out]], 2)
    grad_read = dot_back(grad_keys, parts[1]) + dot_back(grad_values, parts[2])
    own = reduce_row(grad_read[:PLEN].astype(LOW).reshape(4, pslice, D))
    grad_normed = dot_back(grad_query, parts[0]) + jnp.concatenate([own, grad_read[PLEN:]], 0)
    grad_state, grad_gain = norm_back(state, gain, grad_normed)
    grad_rel = jnp.dot(grad_table[:HEADS], hot.astype(F32), precision=HIGH).T
    return grad_next + grad_state, grads, grad_rel, grad_gain


def tiled(
    inputs,
    cotangent,
    routes,
    buckets,
    norm_gains,
    attn_qkv,
    attn_out,
    rel_bias,
    mlp_in,
    mlp_out,
    router,
    expert_in,
    expert_out,
):
    grid = ("row", "col")
    places = lax.axis_size(grid)
    cols, planes = lax.axis_size("col"), lax.axis_size("dp")
    experts = planes * cols
    tokens = inputs.shape[1]
    pslice = tokens - CLEN
    capacity = max(2, 3 * tokens // experts)
    piece = D // places

    small = [norm_gains.reshape(-1), rel_bias.reshape(-1), router.reshape(-1)]
    cuts = [part.shape[0] for part in small]
    packed = jnp.concatenate(small)
    packed = jnp.pad(packed, (0, -packed.shape[0] % 2048)).reshape(1, -1, 128)

    def pieces(*blocks):
        return jnp.concatenate(
            [block.reshape(piece, -1, D).transpose(1, 0, 2) for block in blocks], 0
        )

    def laid(block):
        return block.reshape(-1, piece, D)

    attn = [pieces(attn_qkv[i], attn_out[i]) for i in range(2)]
    dense = jnp.concatenate([laid(mlp_out), pieces(mlp_in)], 0)

    early = [
        Gather(packed.shape, False, cols),
        Gather((2, piece, D), False, cols),
        Gather((2, piece, D), True, cols),
        Rows((pslice, D)),
    ]
    packed, attn_a, attn_b, shared0 = carry(
        None, early, (1, 1, 1), (1,), [], [], [], [], 32, 1
    )(packed, attn[0][:2], attn[0][2:], inputs[0, :pslice])
    weights0 = jnp.concatenate([attn_a, attn_b], 2)
    packed = packed.reshape(places, -1)
    gains = packed[:, : cuts[0]].reshape(places, 4, -1).transpose(1, 0, 2).reshape(4, 1, D).astype(F32)
    rel = packed[:, cuts[0] : cuts[0] + cuts[1]].reshape(places, 2, -1, HEADS)
    rel = rel.transpose(1, 0, 2, 3).reshape(2, BUCKETS, HEADS)
    route_w = packed[:, cuts[0] + cuts[1] : sum(cuts)].reshape(D, experts)

    hot, floor = bias_table(buckets, rel)
    tables = [
        jnp.pad(dot_low(rel[i].T, hot.T) + floor[None], ((0, 16 - HEADS), (0, 0))) for i in range(2)
    ]

    flat = routes[0].reshape(-1)
    levels = jnp.arange(experts, dtype=jnp.int32)
    choose = (routes[0][:, :, None] == levels[None, None, :]).astype(F32)
    hits = (flat[:, None] == levels[None, :]).astype(LOW)
    before = jnp.arange(2 * tokens)
    before = (before[:, None] > before[None, :]).astype(LOW)
    rank = jnp.sum(dot_low(before, hits) * hits.astype(F32), 1).astype(jnp.int32)
    place = (flat * capacity + rank).reshape(tokens, 2)
    slots = jnp.arange(experts * capacity, dtype=jnp.int32)
    picks = [(place[:, k][:, None] == slots[None, :]).astype(LOW) for k in range(2)]
    both = picks[0] + picks[1]
    sent_cotangent = dot_over(both, cotangent[0]).astype(LOW).reshape(experts, capacity, D)

    state0 = inputs[0].astype(F32)
    normed0 = norm_rows(state0, gains[0]).astype(LOW)
    shared0 = norm_rows(shared0.reshape(PLEN, D).astype(F32), gains[0]).astype(LOW)
    state1, stash1, (dense, first) = attention_up(
        state0,
        normed0,
        shared0,
        weights0,
        tables[0],
        [Gather(dense.shape, True, cols), Rows(expert_in.shape[1:])],
        (2, 4, 6),
        (dense, expert_in[0]),
        2,
    )
    state2, normed1, weights1 = mlp_up(
        state1, gains[1], dense, [Gather(attn[1].shape, True, cols)], (2, 3, 4), (attn[1],), 3
    )
    normed2 = norm_rows(state2, gains[2]).astype(LOW)
    shared2 = lax.all_gather(normed2[:pslice], "row", axis=0, tiled=True)
    state3, stash3, (second, far_cotangent) = attention_up(
        state2,
        normed2,
        shared2,
        weights1,
        tables[1],
        [Rows(expert_out.shape[1:]), Swap((capacity, D), planes, cols)],
        (2, 4, 6),
        (expert_out[0], sent_cotangent),
        4,
    )
    far_cotangent = far_cotangent.reshape(experts * capacity, D)

    normed3 = norm_rows(state3, gains[3]).astype(LOW)
    logits = dot_low(normed3, route_w)
    picked = jnp.sum(choose * logits[:, None, :], -1)
    raised = jnp.exp(picked - jnp.max(picked, -1, keepdims=True))
    gates = raised / jnp.sum(raised, -1, keepdims=True)
    parts = [split_low(gates[:, k]) for k in range(2)]
    spread = [
        dot_over(picks[k], jnp.pad(jnp.stack(parts[k], 1), ((0, 0), (0, 125)))) for k in range(2)
    ]
    sent = jnp.concatenate([dot_over(both, normed3), spread[0] + spread[1]], 1).astype(LOW)
    received = exchange(sent.reshape(experts, capacity, D + 128)).reshape(experts * capacity, D + 128)
    far_gate = jnp.sum(received[:, D : D + 3].astype(F32), 1, keepdims=True)
    far_gate = jnp.broadcast_to(far_gate, (experts * capacity, 128))
    result, grad_rows, grad_gate, grad_first, grad_second = expert_pass(
        received[:, :D], far_cotangent, far_gate, first, second
    )
    reach = jnp.pad(jnp.stack(split_low(grad_gate[:, 0]), 1), ((0, 0), (0, 125)))
    returned = exchange(
        jnp.concatenate([grad_rows, reach], 1).reshape(experts, capacity, D + 128)
    ).reshape(experts * capacity, D + 128)
    outcome = exchange(result.reshape(experts, capacity, D)).reshape(experts * capacity, D)
    output = state3 + sum(gates[:, k : k + 1] * dot_low(picks[k], outcome) for k in range(2))

    grad_gates = jnp.stack(
        [jnp.sum(dot_low(picks[k], returned[:, D:]), 1) for k in range(2)], 1
    )
    grad_picked = gates * (grad_gates - jnp.sum(gates * grad_gates, -1, keepdims=True))
    grad_logits = jnp.sum(choose * grad_picked[:, :, None], 1).astype(LOW)
    grad_route = dot_over(normed3, grad_logits)
    grad_normed3 = dot_low(both, returned[:, :D]) + dot_back(grad_logits, route_w)
    upstream = cotangent[0].astype(F32)
    grad_state3, gain_last = norm_back(state3, gains[3], grad_normed3)
    grad3 = upstream + grad_state3
    own_first = reduce_row(grad_first)
    own_second = reduce_row(grad_second)

    shape = (4, cols, piece, D)
    grad2, late, rel_late, gain_third = attention_down(
        grad3, stash3, gains[2], tables[1], hot, shape
    )
    late = reduce_shares(late)
    grad1, gain_second, dense_first, dense_second = mlp_down(
        grad2, state1, normed1, gains[1], dense
    )
    dense_share = reduce_shares(jnp.concatenate([dense_second, dense_first], 2))
    grad0, early, rel_early, gain_first = attention_down(
        grad1, stash1, gains[0], tables[0], hot, shape
    )
    early = reduce_shares(early)

    gain_grads = jnp.concatenate([gain_first, gain_second, gain_third, gain_last], 0)
    gain_grads = gain_grads.reshape(4, places, -1).transpose(1, 0, 2).reshape(places, -1)
    rel_grads = jnp.stack([rel_early, rel_late]).reshape(2, places, -1, HEADS)
    rel_grads = rel_grads.transpose(1, 0, 2, 3).reshape(places, -1)
    packed = jnp.concatenate([gain_grads, rel_grads, grad_route.reshape(places, -1)], 1)
    packed = jnp.pad(packed, ((0, 0), (0, -packed.shape[1] % 2048))).astype(LOW)
    packed = reduce_shares(packed.reshape(4, cols, 2, -1, 128)).reshape(-1)
    gain_share = packed[: cuts[0]].reshape(4, -1)
    rel_share = packed[cuts[0] : cuts[0] + cuts[1]].reshape(2, -1, HEADS)
    route_share = packed[cuts[0] + cuts[1] : sum(cuts)].reshape(-1, experts)

    def unpieced(block):
        return block.transpose(1, 0, 2).reshape(piece, -1)

    return (
        output[None],
        grad0[None],
        gain_share,
        jnp.stack([unpieced(early[:3]), unpieced(late[:3])]),
        jnp.stack([early[3], late[3]]),
        rel_share,
        unpieced(dense_share[4:]),
        dense_share[:4].reshape(-1, D),
        route_share,
        own_first[None],
        own_second[None],
    )


def solution(mesh):
    in_specs = (
        P(("dp", "col"), "row", None),
        P(("dp", "col"), "row", None),
        P(("dp", "col"), "row", None),
        P(),
        P(None, ("row", "col")),
        P(None, ("row", "col"), None),
        P(None, ("row", "col"), None),
        P(None, ("row", "col"), None),
        P(("row", "col"), None),
        P(("row", "col"), None),
        P(("row", "col"), None),
        P(("dp", "col"), None, "row"),
        P(("dp", "col"), "row", None),
    )
    out_specs = (
        P(("dp", "col"), "row", None),
        P(("dp", "col"), "row", None),
        P(None, ("row", "col")),
        P(None, ("row", "col"), None),
        P(None, ("row", "col"), None),
        P(None, ("row", "col"), None),
        P(("row", "col"), None),
        P(("row", "col"), None),
        P(("row", "col"), None),
        P(("dp", "col"), None, "row"),
        P(("dp", "col"), "row", None),
    )
    sizes = dict(mesh.shape)
    piece = D // (sizes["row"] * sizes["col"])
    capacity = 3 * (PLEN // sizes["row"] + CLEN) // (sizes["dp"] * sizes["col"])
    whole_tiles = sizes["row"] == 4 and sizes["dp"] == 2 and piece % 16 == 0 and capacity % 16 == 0
    return jax.shard_map(
        tiled if whole_tiles else general, mesh=mesh, in_specs=in_specs, out_specs=out_specs, check_vma=False
    )
```

```python
import functools

import jax
import jax.numpy as jnp
from jax import lax
from jax.experimental import pallas as pl
from jax.experimental.pallas import tpu as pltpu
from jax.sharding import PartitionSpec as P

D = 768
HEADS = 12
HDIM = 64
FF = 3072
BUCKETS = 32
PLEN = 1024
CLEN = 128
KEYS = PLEN + CLEN
WRAP = KEYS + 128
STRIP = 2 * PLEN
NEG = -1e30
EPS = 1e-06
CURVE = 0.7978845608028654
CUBE = 0.044715
HIGH = lax.Precision.HIGHEST
F32 = jnp.float32
LOW = jnp.bfloat16
MIB = 1 << 20


def dot_low(left, right):
    return jnp.dot(left, right, preferred_element_type=F32)


def dot_back(left, right):
    return lax.dot_general(left, right, (((1,), (1,)), ((), ())), preferred_element_type=F32)


def dot_over(left, right):
    return lax.dot_general(left, right, (((0,), (0,)), ((), ())), preferred_element_type=F32)


def normalise(values):
    center = values - jnp.mean(values, -1, keepdims=True)
    scale = lax.rsqrt(jnp.mean(center * center, -1, keepdims=True) + EPS)
    return center * scale, scale


def norm_rows(values, gain):
    return normalise(values)[0] * gain


def norm_back(values, gain, upstream):
    unit, scale = normalise(values)
    pulled = upstream * gain
    shift = jnp.mean(pulled, -1, keepdims=True)
    along = jnp.mean(pulled * unit, -1, keepdims=True)
    return (pulled - shift - unit * along) * scale, jnp.sum(upstream * unit, 0, keepdims=True)


def gelu_parts(values):
    square = values * values
    bend = jnp.tanh(CURVE * (values + CUBE * square * values))
    half = 0.5 * (1.0 + bend)
    slope = half + 0.5 * values * (1.0 - bend * bend) * (CURVE + 3.0 * CURVE * CUBE * square)
    return values * half, slope


def gelu(values):
    return 0.5 * values * (1.0 + jnp.tanh(CURVE * (values + CUBE * values * values * values)))


def params(mib, steps=1):
    return pltpu.CompilerParams(
        vmem_limit_bytes=mib * MIB, dimension_semantics=("arbitrary",) * steps
    )


def whole(shape):
    return pl.BlockSpec(shape, lambda *_: (0,) * len(shape))


MESH = pl.DeviceIdType.MESH


class Remote:
    def __init__(self, src, dst, send, recv, index, device):
        self.parts = (src, dst, send, recv, index, device)

    def described(self):
        src, dst, send, recv, index, device = self.parts
        return pltpu.make_async_remote_copy(
            src_ref=src,
            dst_ref=dst,
            send_sem=send.at[index],
            recv_sem=recv.at[index],
            device_id=device,
            device_id_type=MESH,
        )

    def start(self):
        self.described().start()

    def wait_recv(self):
        self.described().wait_recv()

    def wait_send(self):
        self.described().wait_send()


def remote(src, dst, send, recv, index, **device):
    return Remote(src, dst, send, recv, index, device)


def neighbours():
    row, dp = lax.axis_index("row"), lax.axis_index("dp")
    across = lax.rem(row + 2, 4)
    core = row + 1 - 2 * lax.rem(row, 2)
    return row, across, core, dp + 1 - 2 * lax.rem(dp, 2)


class Within:
    def __init__(self, src, dst, sem):
        self.parts = (src, dst, sem)

    def start(self):
        pltpu.make_async_copy(*self.parts).start()

    def wait(self):
        pltpu.make_async_copy(*self.parts).wait()


class Gather:
    phases = 5
    take = None

    def __init__(self, shape, split, cols):
        self.shape, self.split, self.cols = shape, split, cols
        self.spec = pl.BlockSpec(memory_space=pl.ANY)
        self.result = jax.ShapeDtypeStruct((4, cols) + shape, LOW)
        count = 4 * cols - 1 + (4 * cols - 2 if split else 0)
        self.scratch = [
            pltpu.SemaphoreType.DMA((count + 2 * cols,)),
            pltpu.SemaphoreType.DMA((count + 2 * cols,)),
            pltpu.SemaphoreType.DMA((1,)),
        ]

    def copies(self, src, dst, send, recv, local):
        cols = self.cols
        row, across, core, plane = neighbours()
        col, dp = lax.axis_index("col"), lax.axis_index("dp")
        half = self.shape[0] // 2
        part = pl.ds(lax.rem(dp, 2) * half, half) if self.split else slice(None)
        rest = pl.ds((1 - lax.rem(dp, 2)) * half, half)
        number = [0]

        def make(source, target, **device):
            number[0] += 1
            return remote(source, target, send, recv, number[0] - 1, **device)

        def piece(where, step, which):
            view = dst.at[where, lax.rem(col - step + cols, cols)]
            return view if which == slice(None) else view.at[which]

        own = src if not self.split else src.at[part]
        out = {}
        out["local"] = Within(src, dst.at[row, col], local.at[0])
        out["z"] = [
            make(own, piece(row, 0, part), col=lax.rem(col + step, cols)) for step in range(1, cols)
        ]
        out["x"] = [make(own, piece(row, 0, part), row=across)]
        out["x"] += [
            make(piece(row, step, part), piece(row, step, part), row=across)
            for step in range(1, cols)
        ]
        out["core own"] = make(src, dst.at[row, col], row=core)
        out["core z"] = [
            make(piece(row, step, part), piece(row, step, part), row=core) for step in range(1, cols)
        ]
        out["core x"] = [
            make(piece(across, step, part), piece(across, step, part), row=core)
            for step in range(cols)
        ]
        if self.split:
            out["y z"] = [
                make(piece(row, step, part), piece(row, step, part), dp=plane)
                for step in range(1, cols)
            ]
            out["y x"] = [
                make(piece(across, step, part), piece(across, step, part), dp=plane)
                for step in range(cols)
            ]
            out["core y z"] = [
                make(piece(row, step, rest), piece(row, step, rest), row=core)
                for step in range(1, cols)
            ]
            out["core y x"] = [
                make(piece(across, step, rest), piece(across, step, rest), row=core)
                for step in range(cols)
            ]
        return out

    def peers(self):
        cols, col = self.cols, lax.axis_index("col")
        row, across, core, plane = neighbours()
        found = {(0, step): dict(col=lax.rem(col + step, cols)) for step in range(1, cols)}
        found.update(across=dict(row=across), core=dict(row=core))
        if self.split:
            found[(1, 0)] = dict(dp=plane)
        return found

    def phase(self, number, *refs):
        out = self.copies(*refs)
        if number == 0:
            out["local"].start()
            for copy in out["z"]:
                copy.start()
            out["x"][0].start()
            out["core own"].start()
        elif number == 1:
            for step in self.order():
                out["z"][step - 1].wait_recv()
                out["x"][step].start()
                if self.split:
                    out["y z"][step - 1].start()
                out["core z"][step - 1].start()
        elif number == 2:
            for step in [0] + self.order():
                out["x"][step].wait_recv()
                if self.split:
                    out["y x"][step].start()
                out["core x"][step].start()
        elif number == 3 and self.split:
            for step in self.order():
                out["y z"][step - 1].wait_recv()
                out["core y z"][step - 1].start()
            for step in [0] + self.order():
                out["y x"][step].wait_recv()
                out["core y x"][step].start()
        elif number == 4:
            out["local"].wait()
            late = [out["core own"]] + out["core z"] + out["core x"]
            if self.split:
                late += out["core y z"] + out["core y x"]
            for copy in late:
                copy.wait_recv()
            early = out["z"] + out["x"] + late
            if self.split:
                early += out["y z"] + out["y x"]
            for copy in early:
                copy.wait_send()

    def order(self):
        steps = list(range(1, self.cols))
        return sorted(steps, key=lambda step: min(step, self.cols - step))


class Rows:
    phases = 3

    def __init__(self, shape, take=None):
        self.take = take
        self.result = jax.ShapeDtypeStruct((4,) + shape, LOW)
        self.spec = pl.BlockSpec(memory_space=pl.ANY)
        self.scratch = [
            pltpu.SemaphoreType.DMA((3,)),
            pltpu.SemaphoreType.DMA((3,)),
            pltpu.SemaphoreType.DMA((1,)),
        ]

    def peers(self):
        row, across, core, plane = neighbours()
        return dict(across=dict(row=across), core=dict(row=core))

    def phase(self, number, src, dst, send, recv, local):
        row, across, core, plane = neighbours()
        own = Within(src, dst.at[row], local.at[0])
        far = remote(src, dst.at[row], send, recv, 0, row=across)
        near = remote(src, dst.at[row], send, recv, 1, row=core)
        on = remote(dst.at[across], dst.at[across], send, recv, 2, row=core)
        if number == 0:
            own.start()
            far.start()
            near.start()
        elif number == 1:
            far.wait_recv()
            on.start()
        else:
            own.wait()
            near.wait_recv()
            on.wait_recv()
            for copy in (far, near, on):
                copy.wait_send()


SLOTS = [(a, b) for b in range(4) for a in range(2)]


def slot_device(slot):
    a, b = SLOTS[slot]
    dp, col = lax.axis_index("dp"), lax.axis_index("col")
    flipped = (col, col + 1 - 2 * lax.rem(col, 2), lax.rem(col + 2, 4), 3 - col)[b]
    device = {}
    if a:
        device["dp"] = 1 - dp
    if b:
        device["col"] = flipped
    return device


class Swap:
    phases = 2

    def __init__(self, shape, take=None):
        self.take = take
        self.result = jax.ShapeDtypeStruct((len(SLOTS),) + shape, LOW)
        self.spec = pl.BlockSpec(memory_space=pl.ANY)
        self.scratch = [
            pltpu.SemaphoreType.DMA((len(SLOTS),)),
            pltpu.SemaphoreType.DMA((len(SLOTS),)),
            pltpu.SemaphoreType.DMA((1,)),
        ]

    def peers(self):
        return {SLOTS[slot]: slot_device(slot) for slot in range(1, len(SLOTS))}

    def phase(self, number, src, dst, send, recv, local):
        own = Within(src.at[0], dst.at[0], local.at[0])
        copies = [
            remote(src.at[slot], dst.at[slot], send, recv, slot, **slot_device(slot))
            for slot in range(1, len(SLOTS))
        ]
        if number == 0:
            for copy in copies:
                copy.start()
            own.start()
        else:
            own.wait()
            for copy in copies:
                copy.wait_recv()
            for copy in copies:
                copy.wait_send()


def each(count, body):
    lax.fori_loop(0, count, lambda index, carried: (body(index), carried)[1], 0)


class Reduce:
    def __init__(self, shape, ops, cols=1, first=0, take=None, keep=False):
        self.ops, self.cols, self.first, self.take, self.keep = ops, cols, first, take, keep
        self.count = shape[0]
        self.part = shape[0] // 2 if "y" in ops else shape[0]
        self.phases = len(ops) + 1
        self.result = jax.ShapeDtypeStruct(shape, F32)
        self.spec = whole(shape)
        tail = shape[1:]
        buffers = {"core": [(2, cols, self.count), (2, cols, self.count)]}
        if "y" in ops:
            buffers["y"] = [(2, cols, self.part)]
        buffers["x"] = [(cols, self.part)]
        if "z" in ops:
            buffers["z"] = [(cols - 1, self.part), (self.part,)]
            buffers["end"] = [(self.part,)]
        self.names = list(buffers)
        self.lengths = [len(buffers[name]) for name in self.names]
        self.scratch = [pltpu.VMEM(lead + tail, LOW) for name in self.names for lead in buffers[name]]
        self.scratch += [
            pltpu.SemaphoreType.DMA((8,)),
            pltpu.SemaphoreType.DMA((8,)),
            pltpu.SemaphoreType.DMA((2,)),
        ]

    def peers(self):
        row, across, core, plane = neighbours()
        found = dict(across=dict(row=across), core=dict(row=core))
        if "z" in self.ops:
            for slot in (1, 2, 4, 6):
                found[SLOTS[slot]] = slot_device(slot)
        return found

    def phase(self, number, src, out, *scratch):
        scratch = list(scratch)
        held = {
            name: [scratch.pop(0) for _ in range(length)]
            for name, length in zip(self.names, self.lengths)
        }
        send, recv, local = scratch
        row, across, core, plane = neighbours()
        x, c = row // 2, lax.rem(row, 2)
        dp, col = lax.axis_index("dp"), lax.axis_index("col")
        total, near = held["core"]
        span = pl.ds(self.first, self.count)
        start = dp * self.part if "y" in self.ops else 0
        part, rest = pl.ds(start, self.part), pl.ds((1 - dp) * self.part, self.part)
        loads = [
            Within(src.at[2 * i + c, :, span], total.at[i], local.at[i])
            for i in range(2)
        ]

        def copies(op):
            if op == "core":
                return [
                    remote(src.at[2 * i + 1 - c, :, span], near.at[i], send, recv, i, row=core)
                    for i in range(2)
                ]
            if op == "y":
                return [remote(total.at[:, :, rest], held["y"][0], send, recv, 2, dp=plane)]
            if op == "x":
                return [remote(total.at[1 - x, :, part], held["x"][0], send, recv, 3, row=across)]
            if op == "z":
                found = []
                for b in (2, 3, 1):
                    device = slot_device(2 * b)
                    view = total.at[x, device["col"], part]
                    found.append(remote(view, held["z"][0].at[b - 1], send, recv, 3 + b, **device))
                return found
            return [remote(held["z"][1], held["end"][0], send, recv, 7, dp=plane)]

        wide = lambda value: value.astype(F32)
        count, cols, size = self.count, self.cols, self.part
        if number > 0:
            op = self.ops[number - 1]
            if op == "core":
                for load in loads:
                    load.wait()
            for copy in copies(op):
                copy.wait_recv()
            if op == "core":

                def add(i):
                    at = (i // (cols * count), lax.rem(i // count, cols), lax.rem(i, count))
                    total[at] = (wide(total[at]) + wide(near[at])).astype(LOW)

                each(2 * cols * count, add)
            elif op == "y":

                def add(i):
                    at = (i // (cols * size), lax.rem(i // size, cols))
                    k = lax.rem(i, size)
                    kept = at + (start + k,)
                    total[kept] = (wide(total[kept]) + wide(held["y"][0][at + (k,)])).astype(LOW)

                each(2 * cols * size, add)
            elif op == "x":

                def add(i):
                    z, k = i // size, lax.rem(i, size)
                    value = wide(total[x, z, start + k]) + wide(held["x"][0][z, k])
                    if number == len(self.ops):
                        out[k] = value
                    else:
                        total[x, z, start + k] = value.astype(LOW)

                each(cols * size, add)
            elif op == "z":

                def add(k):
                    value = wide(total[x, col, start + k])
                    for b in range(cols - 1):
                        value = value + wide(held["z"][0][b, k])
                    held["z"][1][k] = value.astype(LOW)

                each(size, add)
            else:

                def add(k):
                    mine, other = wide(held["z"][1][k]), wide(held["end"][0][k])
                    if op == "sum":
                        out[k] = mine + other
                    else:
                        out[start + k] = mine
                        out[(1 - dp) * size + k] = other

                each(size, add)
        if number < len(self.ops):
            op = self.ops[number]
            if op == "core":
                for load in loads:
                    load.start()
            for copy in copies(op):
                copy.start()
        else:
            for op in self.ops:
                for copy in copies(op):
                    copy.wait_send()


def greet(flows):
    barrier = pltpu.get_barrier_semaphore()
    devices = {}
    for flow in flows:
        devices.update(flow.peers())
    for device in devices.values():
        pl.semaphore_signal(barrier, inc=1, device_id=device, device_id_type=MESH)
    pl.semaphore_wait(barrier, len(devices))


LATE = 99


def carry(body, moves, grid, in_specs, out_specs, out_shape, scratch_shapes, mib, name, after=None):
    inputs, outputs, extras = len(in_specs), len(out_specs), len(scratch_shapes)
    steps = grid[0]
    hbm = pl.BlockSpec(memory_space=pl.ANY)
    flows = [flow for flow, _ in moves]
    given = [flow for flow in flows if flow.take is None]
    shown = [flow for flow in flows if not getattr(flow, "keep", False)]

    def kernel(*refs):
        refs = list(refs)
        take = lambda count: [refs.pop(0) for _ in range(count)]
        own_in = take(inputs)
        sources = {flow: refs.pop(0) for flow in given}
        own_out = take(outputs)
        results = {flow: refs.pop(0) for flow in shown}
        own_extra = take(extras)
        packs = {}
        for flow in flows:
            if flow not in results:
                results[flow] = refs.pop(0)
            if flow not in sources:
                sources[flow] = flow.take(own_out, own_extra)
            packs[flow] = [sources[flow], results[flow]] + take(len(flow.scratch))
        step = pl.program_id(0)

        def run(mark):
            for number in range(max(flow.phases for flow in flows)):
                for flow, marks in moves:
                    if number < flow.phases and marks[number] == mark:
                        flow.phase(number, *packs[flow])

        for mark in range(steps):
            if mark == 0 or any(mark in marks for _, marks in moves):

                @pl.when(step == mark)
                def _():
                    if mark == 0:
                        greet(flows)
                    run(mark)

        if body is not None:
            body(*own_in, *own_out, *own_extra)

        @pl.when(step == steps - 1)
        def _():
            run(LATE)
            if after is not None:
                after(own_in, own_out, own_extra, [results[flow] for flow in flows])

    scratch = list(scratch_shapes)
    for flow in flows:
        if flow not in shown:
            scratch.append(pltpu.VMEM(flow.result.shape, flow.result.dtype))
        scratch += flow.scratch

    def call(*args):
        return pl.pallas_call(
            kernel,
            grid=grid,
            out_shape=tuple(out_shape) + tuple(flow.result for flow in shown),
            in_specs=list(in_specs) + [hbm] * len(given),
            out_specs=tuple(out_specs) + tuple(flow.spec for flow in shown),
            scratch_shapes=scratch,
            compiler_params=pltpu.CompilerParams(
                vmem_limit_bytes=mib * MIB,
                dimension_semantics=("arbitrary",),
                collective_id=name,
                has_side_effects=True,
            ),
        )(*args)

    return call


def bias_table(buckets, rel):
    place = jnp.arange(WRAP, dtype=jnp.int32)
    dist = jnp.where(place <= PLEN, PLEN - place, PLEN + WRAP - place)
    read = (place <= PLEN) | (place > KEYS)
    index = jnp.take(buckets, jnp.clip(dist, 0, KEYS - 1), axis=0)
    hot = ((index[:, None] == jnp.arange(BUCKETS)[None, :]) & read[:, None]).astype(LOW)
    floor = jnp.where(read, 0.0, NEG).astype(F32)
    return hot, floor


def fill_strip(strip, table, head):
    @pl.when(pl.program_id(0) == 0)
    def _():
        strip[:, KEYS:] = jnp.full((128, STRIP - KEYS), NEG, F32)

    line = jnp.broadcast_to(table[pl.ds(head, 1), :], (128, WRAP))
    strip[:, :KEYS] = pltpu.roll(line, 0, 1, stride=1, stride_axis=0)[:, :KEYS]


def tiles_of(pslice):
    places = []
    for tile in range(pslice // 128):
        start = PLEN - (lax.axis_index("row") * pslice + tile * 128)
        places.append((tile * 128, pl.ds(pl.multiple_of(start, 128), PLEN), PLEN))
    places.append((pslice, pl.ds(0, KEYS), KEYS))
    return places


def attend_kernel(pslice, query, keys, values, table, mixed, total, strip, raw, weights):
    pair = pl.program_id(0)
    lane = lax.broadcasted_iota(jnp.int32, (1, 128), 1)

    @pl.when(pair == 0)
    def _():
        weights[:pslice, PLEN:] = jnp.zeros((pslice, CLEN), LOW)

    for half in range(2):
        mine = (lane < HDIM) if half == 0 else (lane >= HDIM)
        fill_strip(strip, table, 2 * pair + half)
        part = jnp.where(mine, query[...], 0) * HDIM ** (-0.5)
        raw[...] = dot_back(part.astype(LOW), keys[...])
        for row, place, count in tiles_of(pslice):
            rows = pl.ds(row, 128)
            scores = raw[rows, :count] + strip[:, place]
            top = jnp.max(scores, -1, keepdims=True)
            raised = jnp.exp(scores - top)
            summed = jnp.sum(raised, -1, keepdims=True)
            weights[rows, :count] = (raised * (1.0 / summed)).astype(LOW)
            log_total = jnp.broadcast_to(top + jnp.log(summed), (128, 128))
            if half == 0:
                total[rows, :] = log_total
            else:
                total[rows, :] = jnp.where(mine, log_total, total[rows, :])
        result = dot_low(weights[...], values[...]).astype(LOW)
        if half == 0:
            mixed[...] = result
        else:
            mixed[...] = jnp.where(mine, result, mixed[...])


def attend_forward(query, keys, values, table):
    tokens = query.shape[0]
    pslice = tokens - CLEN
    block = lambda rows: pl.BlockSpec((rows, 128), lambda i: (0, i))
    return pl.pallas_call(
        functools.partial(attend_kernel, pslice),
        grid=(HEADS // 2,),
        out_shape=(
            jax.ShapeDtypeStruct((tokens, D), LOW),
            jax.ShapeDtypeStruct((tokens, D), F32),
        ),
        in_specs=[block(tokens), block(KEYS), block(KEYS), whole(table.shape)],
        out_specs=(block(tokens), block(tokens)),
        scratch_shapes=[
            pltpu.VMEM((128, STRIP), F32),
            pltpu.VMEM((tokens, KEYS), F32),
            pltpu.VMEM((tokens, KEYS), LOW),
        ],
        compiler_params=params(32),
    )(query, keys, values, table)


def attend_back_kernel(
    pslice,
    query,
    keys,
    values,
    table,
    total,
    grad_mixed,
    grad_query,
    grad_keys,
    grad_values,
    grad_table,
    strip,
    raw,
    pulled,
    probs,
    grads,
    folded,
    sum_keys,
    sum_values,
):
    pair = pl.program_id(0)
    lane = lax.broadcasted_iota(jnp.int32, (1, 128), 1)
    across = lax.broadcasted_iota(jnp.int32, (128, 128), 0)
    along = lax.broadcasted_iota(jnp.int32, (128, 128), 1)
    mirror = (across + along == 127).astype(LOW)

    @pl.when(pair == 0)
    def _():
        probs[:pslice, PLEN:] = jnp.zeros((pslice, CLEN), LOW)
        grads[:pslice, PLEN:] = jnp.zeros((pslice, CLEN), LOW)

    for half in range(2):
        mine = (lane < HDIM) if half == 0 else (lane >= HDIM)
        fill_strip(strip, table, 2 * pair + half)
        part = (jnp.where(mine, query[...], 0) * HDIM ** (-0.5)).astype(LOW)
        upstream = jnp.where(mine, grad_mixed[...], 0).astype(LOW)
        raw[...] = dot_back(part, keys[...])
        pulled[...] = dot_back(upstream, values[...])
        folded[...] = jnp.zeros_like(folded)
        for row, place, count in tiles_of(pslice):
            rows = pl.ds(row, 128)
            log_total = total[rows, half * HDIM : half * HDIM + 1]
            chance = jnp.exp(raw[rows, :count] + strip[:, place] - log_total)
            product = chance * pulled[rows, :count]
            centre = jnp.sum(product, -1, keepdims=True)
            slope = (product - chance * centre).astype(LOW)
            probs[rows, :count] = chance.astype(LOW)
            grads[rows, :count] = slope
            folded[:, place] += dot_low(mirror, slope)
        result = dot_low(grads[...], keys[...]) * HDIM ** (-0.5)
        if half == 0:
            grad_query[...] = result.astype(LOW)
            sum_keys[...] = dot_over(part, grads[...])
            sum_values[...] = dot_over(upstream, probs[...])
        else:
            grad_query[...] = jnp.where(mine, result.astype(LOW), grad_query[...])
            sum_keys[...] += dot_over(part, grads[...])
            sum_values[...] += dot_over(upstream, probs[...])
        turned = pltpu.roll(folded[:, :WRAP], WRAP - 127, 1, stride=1, stride_axis=0)
        grad_table[pl.ds(2 * pair + half, 1), :] = jnp.sum(turned, 0, keepdims=True)
    grad_keys[...] = sum_keys[...].T.astype(LOW)
    grad_values[...] = sum_values[...].T.astype(LOW)


def attend_backward(query, keys, values, table, total, grad_mixed):
    tokens = query.shape[0]
    pslice = tokens - CLEN
    block = lambda rows: pl.BlockSpec((rows, 128), lambda i: (0, i))
    return pl.pallas_call(
        functools.partial(attend_back_kernel, pslice),
        grid=(HEADS // 2,),
        out_shape=(
            jax.ShapeDtypeStruct((tokens, D), LOW),
            jax.ShapeDtypeStruct((KEYS, D), LOW),
            jax.ShapeDtypeStruct((KEYS, D), LOW),
            jax.ShapeDtypeStruct(table.shape, F32),
        ),
        in_specs=[
            block(tokens),
            block(KEYS),
            block(KEYS),
            whole(table.shape),
            block(tokens),
            block(tokens),
        ],
        out_specs=(block(tokens), block(KEYS), block(KEYS), whole(table.shape)),
        scratch_shapes=[
            pltpu.VMEM((128, STRIP), F32),
            pltpu.VMEM((tokens, KEYS), F32),
            pltpu.VMEM((tokens, KEYS), F32),
            pltpu.VMEM((tokens, KEYS), LOW),
            pltpu.VMEM((tokens, KEYS), LOW),
            pltpu.VMEM((128, STRIP), F32),
            pltpu.VMEM((128, KEYS), F32),
            pltpu.VMEM((128, KEYS), F32),
        ],
        compiler_params=params(32),
    )(query, keys, values, table, total, grad_mixed)


def mlp_forward_kernel(state, gain, first, second, result, normed):
    step = pl.program_id(0)

    @pl.when(step == 0)
    def _():
        normed[...] = norm_rows(state[...], gain[...]).astype(LOW)
        result[...] = state[...]

    active = gelu(dot_low(normed[...], first[...])).astype(LOW)
    result[...] += dot_low(active, second[...])


def mlp_forward(state, gain, first, second):
    tokens = state.shape[0]
    part = 768
    return pl.pallas_call(
        mlp_forward_kernel,
        grid=(FF // part,),
        out_shape=(
            jax.ShapeDtypeStruct((tokens, D), F32),
            jax.ShapeDtypeStruct((tokens, D), LOW),
        ),
        in_specs=[
            whole((tokens, D)),
            whole((1, D)),
            pl.BlockSpec((D, part), lambda i: (0, i)),
            pl.BlockSpec((part, D), lambda i: (i, 0)),
        ],
        out_specs=(whole((tokens, D)), whole((tokens, D))),
        compiler_params=params(32),
    )(state, gain, first, second)


def mlp_backward_kernel(
    grad_next, state, normed, gain, first, second, result, grad_gain, grad_first, grad_second, low, total
):
    step = pl.program_id(0)

    @pl.when(step == 0)
    def _():
        low[...] = grad_next[...].astype(LOW)
        total[...] = jnp.zeros_like(total)

    active, slope = gelu_parts(dot_low(normed[...], first[...]))
    grad_hidden = (slope * dot_back(low[...], second[...])).astype(LOW)
    grad_second[...] = dot_over(active.astype(LOW), low[...]).astype(LOW)
    grad_first[...] = dot_over(normed[...], grad_hidden).astype(LOW)
    total[...] += dot_back(grad_hidden, first[...])

    @pl.when(step == pl.num_programs(0) - 1)
    def _():
        grad_state, grad_line = norm_back(state[...], gain[...], total[...])
        result[...] = grad_next[...] + grad_state
        grad_gain[...] = grad_line


def mlp_backward(grad_next, state, normed, gain, first, second):
    tokens = state.shape[0]
    part = 768
    return pl.pallas_call(
        mlp_backward_kernel,
        grid=(FF // part,),
        out_shape=(
            jax.ShapeDtypeStruct((tokens, D), F32),
            jax.ShapeDtypeStruct((1, D), F32),
            jax.ShapeDtypeStruct((D, FF), LOW),
            jax.ShapeDtypeStruct((FF, D), LOW),
        ),
        in_specs=[
            whole((tokens, D)),
            whole((tokens, D)),
            whole((tokens, D)),
            whole((1, D)),
            pl.BlockSpec((D, part), lambda i: (0, i)),
            pl.BlockSpec((part, D), lambda i: (i, 0)),
        ],
        out_specs=(
            whole((tokens, D)),
            whole((1, D)),
            pl.BlockSpec((D, part), lambda i: (0, i)),
            pl.BlockSpec((part, D), lambda i: (i, 0)),
        ),
        scratch_shapes=[pltpu.VMEM((tokens, D), LOW), pltpu.VMEM((tokens, D), F32)],
        compiler_params=params(48),
    )(grad_next, state, normed, gain, first, second)


def expert_kernel(
    rows, cotangent, gate, first, second, result, grad_rows, grad_gate, grad_first, grad_second, upstream, total, back
):
    step = pl.program_id(0)

    @pl.when(step == 0)
    def _():
        upstream[...] = (gate[:, :1] * cotangent[...].astype(F32)).astype(LOW)
        total[...] = jnp.zeros_like(total)
        back[...] = jnp.zeros_like(back)

    active, slope = gelu_parts(dot_low(rows[...], first[...]))
    active = active.astype(LOW)
    total[...] += dot_low(active, second[...])
    grad_hidden = (slope * dot_back(upstream[...], second[...])).astype(LOW)
    grad_second[...] = dot_over(active, upstream[...]).astype(LOW)
    grad_first[...] = dot_over(rows[...], grad_hidden).astype(LOW)
    back[...] += dot_back(grad_hidden, first[...])

    @pl.when(step == pl.num_programs(0) - 1)
    def _():
        low = total[...].astype(LOW)
        result[...] = low
        grad_rows[...] = back[...].astype(LOW)
        reach = jnp.sum(cotangent[...].astype(F32) * low.astype(F32), -1, keepdims=True)
        grad_gate[...] = jnp.broadcast_to(reach, grad_gate.shape)


def expert_pass(rows, cotangent, gate, first, second):
    count = rows.shape[0]
    shards, _, width = first.shape
    part = 256
    split = width // part
    inner = pl.BlockSpec((None, D, part), lambda i: (i // split, 0, i % split))
    outer = pl.BlockSpec((None, part, D), lambda i: (i // split, i % split, 0))
    return pl.pallas_call(
        expert_kernel,
        grid=(shards * split,),
        out_shape=(
            jax.ShapeDtypeStruct((count, D), LOW),
            jax.ShapeDtypeStruct((count, D), LOW),
            jax.ShapeDtypeStruct((count, 128), F32),
            jax.ShapeDtypeStruct(first.shape, LOW),
            jax.ShapeDtypeStruct(second.shape, LOW),
        ),
        in_specs=[whole((count, D)), whole((count, D)), whole((count, 128)), inner, outer],
        out_specs=(whole((count, D)), whole((count, D)), whole((count, 128)), inner, outer),
        scratch_shapes=[
            pltpu.VMEM((count, D), LOW),
            pltpu.VMEM((count, D), F32),
            pltpu.VMEM((count, D), F32),
        ],
        compiler_params=params(56),
    )(rows, cotangent, gate, first, second)


def split_low(values):
    high = values.astype(LOW)
    rest = values - high.astype(F32)
    middle = rest.astype(LOW)
    return high, middle, (rest - middle.astype(F32)).astype(LOW)


def exchange(block):
    return lax.all_to_all(block, ("dp", "col"), split_axis=0, concat_axis=0, tiled=True)


def attention_forward(state, gain, others, weight_in, weight_out, table, raw_others):
    tokens = state.shape[0]
    pslice = tokens - CLEN
    normed = norm_rows(state, gain).astype(LOW)
    if others is None:
        shared = lax.all_gather(normed[:pslice], "row", axis=0, tiled=True)
    else:
        shared = norm_rows(others.astype(F32), gain).astype(LOW)
    read = jnp.concatenate([shared, normed[pslice:]], 0)
    query = dot_low(normed, weight_in[:, :D]).astype(LOW)
    keys = dot_low(read, weight_in[:, D : 2 * D]).astype(LOW)
    values = dot_low(read, weight_in[:, 2 * D :]).astype(LOW)
    mixed, total = attend_forward(query, keys, values, table)
    return state + dot_low(mixed, weight_out), (state, normed, read, query, keys, values, mixed, total)


def attention_backward(grad_next, stash, gain, weight_in, weight_out, table, hot):
    state, normed, read, query, keys, values, mixed, total = stash
    pslice = state.shape[0] - CLEN
    branch = grad_next.astype(LOW)
    grad_out = dot_over(mixed, branch).astype(LOW)
    grad_mixed = dot_back(branch, weight_out).astype(LOW)
    grad_query, grad_keys, grad_values, grad_table = attend_backward(
        query, keys, values, table, total, grad_mixed
    )
    grad_in = jnp.concatenate(
        [dot_over(normed, grad_query), dot_over(read, grad_keys), dot_over(read, grad_values)], 1
    ).astype(LOW)
    grad_read = dot_back(grad_keys, weight_in[:, D : 2 * D]) + dot_back(
        grad_values, weight_in[:, 2 * D :]
    )
    own = lax.psum_scatter(
        grad_read[:PLEN].astype(LOW), "row", scatter_dimension=0, tiled=True
    ).astype(F32)
    grad_normed = dot_back(grad_query, weight_in[:, :D]) + jnp.concatenate(
        [own, grad_read[PLEN:]], 0
    )
    grad_state, grad_gain = norm_back(state, gain, grad_normed)
    grad_rel = jnp.dot(grad_table[:HEADS], hot.astype(F32), precision=HIGH).T
    return grad_next + grad_state, grad_in, grad_out, grad_rel, grad_gain


def general(
    inputs,
    cotangent,
    routes,
    buckets,
    norm_gains,
    attn_qkv,
    attn_out,
    rel_bias,
    mlp_in,
    mlp_out,
    router,
    expert_in,
    expert_out,
):
    grid = ("row", "col")
    places = lax.axis_size(grid)
    experts = lax.axis_size(("dp", "col"))
    tokens = inputs.shape[1]
    pslice = tokens - CLEN
    capacity = max(2, 3 * tokens // experts)

    small = [norm_gains.reshape(-1), rel_bias.reshape(-1), router.reshape(-1)]
    cuts = [part.shape[0] for part in small]
    packed = jnp.concatenate(small)
    packed = jnp.pad(packed, (0, -packed.shape[0] % 1024)).reshape(-1, 128)
    packed = lax.all_gather(packed, grid, axis=0, tiled=False).reshape(places, -1)
    gains = packed[:, : cuts[0]].reshape(places, 4, -1).transpose(1, 0, 2).reshape(4, 1, D).astype(F32)
    rel = packed[:, cuts[0] : cuts[0] + cuts[1]].reshape(places, 2, -1, HEADS)
    rel = rel.transpose(1, 0, 2, 3).reshape(2, BUCKETS, HEADS)
    route_w = packed[:, cuts[0] + cuts[1] : sum(cuts)].reshape(D, experts)

    qkv = [lax.all_gather(attn_qkv[i], grid, axis=0, tiled=True) for i in range(2)]
    out = [lax.all_gather(attn_out[i], grid, axis=0, tiled=True) for i in range(2)]
    dense_in = lax.all_gather(mlp_in, grid, axis=0, tiled=True)
    dense_out = lax.all_gather(mlp_out, grid, axis=0, tiled=True)
    first = lax.all_gather(expert_in[0], "row", axis=0, tiled=False)
    second = lax.all_gather(expert_out[0], "row", axis=0, tiled=False)

    hot, floor = bias_table(buckets, rel)
    tables = [
        jnp.pad(dot_low(rel[i].T, hot.T) + floor[None], ((0, 16 - HEADS), (0, 0))) for i in range(2)
    ]

    flat = routes[0].reshape(-1)
    levels = jnp.arange(experts, dtype=jnp.int32)
    choose = (routes[0][:, :, None] == levels[None, None, :]).astype(F32)
    hits = (flat[:, None] == levels[None, :]).astype(LOW)
    before = jnp.arange(2 * tokens)
    before = (before[:, None] > before[None, :]).astype(LOW)
    rank = jnp.sum(dot_low(before, hits) * hits.astype(F32), 1).astype(jnp.int32)
    place = (flat * capacity + rank).reshape(tokens, 2)
    slots = jnp.arange(experts * capacity, dtype=jnp.int32)
    picks = [(place[:, k][:, None] == slots[None, :]).astype(LOW) for k in range(2)]
    both = picks[0] + picks[1]
    sent_cotangent = dot_over(both, cotangent[0]).astype(LOW).reshape(experts, capacity, D)
    far_cotangent = exchange(sent_cotangent).reshape(experts * capacity, D)

    state0 = inputs[0].astype(F32)
    shared0 = lax.all_gather(inputs[0, :pslice], "row", axis=0, tiled=True)
    state1, stash1 = attention_forward(state0, gains[0], shared0, qkv[0], out[0], tables[0], None)
    state2, normed1 = mlp_forward(state1, gains[1], dense_in, dense_out)
    state3, stash3 = attention_forward(state2, gains[2], None, qkv[1], out[1], tables[1], None)

    normed3 = norm_rows(state3, gains[3]).astype(LOW)
    logits = dot_low(normed3, route_w)
    picked = jnp.sum(choose * logits[:, None, :], -1)
    raised = jnp.exp(picked - jnp.max(picked, -1, keepdims=True))
    gates = raised / jnp.sum(raised, -1, keepdims=True)
    parts = [split_low(gates[:, k]) for k in range(2)]
    spread = [
        dot_over(picks[k], jnp.pad(jnp.stack(parts[k], 1), ((0, 0), (0, 125)))) for k in range(2)
    ]
    sent = jnp.concatenate([dot_over(both, normed3), spread[0] + spread[1]], 1).astype(LOW)
    received = exchange(sent.reshape(experts, capacity, D + 128)).reshape(experts * capacity, D + 128)
    far_gate = jnp.sum(received[:, D : D + 3].astype(F32), 1, keepdims=True)
    far_gate = jnp.broadcast_to(far_gate, (experts * capacity, 128))
    result, grad_rows, grad_gate, grad_first, grad_second = expert_pass(
        received[:, :D], far_cotangent, far_gate, first, second
    )
    reach = jnp.pad(jnp.stack(split_low(grad_gate[:, 0]), 1), ((0, 0), (0, 125)))
    returned = exchange(
        jnp.concatenate([grad_rows, reach], 1).reshape(experts, capacity, D + 128)
    ).reshape(experts * capacity, D + 128)
    outcome = exchange(result.reshape(experts, capacity, D)).reshape(experts * capacity, D)
    output = state3 + sum(gates[:, k : k + 1] * dot_low(picks[k], outcome) for k in range(2))

    grad_gates = jnp.stack(
        [jnp.sum(dot_low(picks[k], returned[:, D:]), 1) for k in range(2)], 1
    )
    grad_picked = gates * (grad_gates - jnp.sum(gates * grad_gates, -1, keepdims=True))
    grad_logits = jnp.sum(choose * grad_picked[:, :, None], 1).astype(LOW)
    grad_route = dot_over(normed3, grad_logits)
    grad_normed3 = dot_low(both, returned[:, :D]) + dot_back(grad_logits, route_w)
    upstream = cotangent[0].astype(F32)
    grad_state3, gain_last = norm_back(state3, gains[3], grad_normed3)
    grad3 = upstream + grad_state3
    own_first = lax.psum_scatter(grad_first, "row", scatter_dimension=0, tiled=False)
    own_second = lax.psum_scatter(grad_second, "row", scatter_dimension=0, tiled=False)

    grad2, qkv_late, out_late, rel_late, gain_third = attention_backward(
        grad3, stash3, gains[2], qkv[1], out[1], tables[1], hot
    )
    grad1, gain_second, dense_grad_in, dense_grad_out = mlp_backward(
        grad2, state1, normed1, gains[1], dense_in, dense_out
    )
    grad0, qkv_early, out_early, rel_early, gain_first = attention_backward(
        grad1, stash1, gains[0], qkv[0], out[0], tables[0], hot
    )

    def share(block):
        block = lax.psum_scatter(block.astype(LOW), grid, scatter_dimension=0, tiled=True)
        return lax.psum(block, "dp").astype(F32)

    gain_grads = jnp.concatenate([gain_first, gain_second, gain_third, gain_last], 0)
    gain_grads = gain_grads.reshape(4, places, -1).transpose(1, 0, 2).reshape(places, -1)
    rel_grads = jnp.stack([rel_early, rel_late]).reshape(2, places, -1, HEADS)
    rel_grads = rel_grads.transpose(1, 0, 2, 3).reshape(places, -1)
    packed = jnp.concatenate([gain_grads, rel_grads, grad_route.reshape(places, -1)], 1)
    packed = jnp.pad(packed, ((0, 0), (0, -packed.shape[1] % 1024))).reshape(-1, 128)
    packed = share(packed).reshape(-1)
    gain_share = packed[: cuts[0]].reshape(4, -1)
    rel_share = packed[cuts[0] : cuts[0] + cuts[1]].reshape(2, -1, HEADS)
    route_share = packed[cuts[0] + cuts[1] : sum(cuts)].reshape(-1, experts)
    return (
        output[None],
        grad0[None],
        gain_share,
        jnp.stack([share(qkv_early), share(qkv_late)]),
        jnp.stack([share(out_early), share(out_late)]),
        rel_share,
        share(dense_grad_in),
        share(dense_grad_out),
        route_share,
        own_first.astype(F32)[None],
        own_second.astype(F32)[None],
    )


def once(shape):
    return pl.BlockSpec(shape, lambda *_: (0,) * len(shape), pipeline_mode=pl.Buffered(1))


def head_block(cols, piece, index):
    return pl.BlockSpec((4, cols, None, piece, 128), lambda i: (0, 0, index, 0, i))


def outer_block(cols, piece):
    return pl.BlockSpec(
        (4, cols, None, piece, D), lambda i: (0, 0, 1, 0, 0), pipeline_mode=pl.Buffered(1)
    )


def up_kernel(
    raw_rows,
    pslice,
    state,
    own,
    shared,
    gain,
    table,
    wq,
    wk,
    wv,
    wo,
    result,
    normed,
    read,
    query,
    keys,
    values,
    mixed,
    total,
    strip,
    raw,
    weights,
    outer,
):
    pair = pl.program_id(0)
    lane = lax.broadcasted_iota(jnp.int32, (1, 128), 1)

    @pl.when(pair == 0)
    def _():
        weights[:pslice, PLEN:] = jnp.zeros((pslice, CLEN), LOW)
        outer[...] = wo[...].reshape(D, D)
        result[...] = state[...].astype(F32)
        if raw_rows:
            normed[...] = norm_rows(own[...].astype(F32), gain[...]).astype(LOW)
            for i in range(PLEN // pslice):
                rows = pl.ds(i * pslice, pslice)
                read[rows, :] = norm_rows(shared[i].astype(F32), gain[...]).astype(LOW)
        else:
            normed[...] = own[...]
            for i in range(PLEN // pslice):
                read[pl.ds(i * pslice, pslice), :] = shared[i]
        read[PLEN:, :] = normed[pslice:, :]

    query[...] = dot_low(normed[...], wq[...].reshape(D, 128)).astype(LOW)
    both = jnp.concatenate([wk[...].reshape(D, 128), wv[...].reshape(D, 128)], 1)
    both = dot_low(read[...], both).astype(LOW)
    keys[...] = both[:, :128]
    values[...] = both[:, 128:]

    for half in range(2):
        mine = (lane < HDIM) if half == 0 else (lane >= HDIM)
        fill_strip(strip, table, 2 * pair + half)
        part = jnp.where(mine, query[...], 0) * HDIM ** (-0.5)
        raw[...] = dot_back(part.astype(LOW), keys[...])
        for row, place, count in tiles_of(pslice):
            rows = pl.ds(row, 128)
            scores = raw[rows, :count] + strip[:, place]
            top = jnp.max(scores, -1, keepdims=True)
            raised = jnp.exp(scores - top)
            summed = jnp.sum(raised, -1, keepdims=True)
            weights[rows, :count] = (raised * (1.0 / summed)).astype(LOW)
            log_total = jnp.broadcast_to(top + jnp.log(summed), (128, 128))
            if half == 0:
                total[rows, :] = log_total
            else:
                total[rows, :] = jnp.where(mine, log_total, total[rows, :])
        part = dot_low(weights[...], values[...]).astype(LOW)
        if half == 0:
            mixed[...] = part
        else:
            mixed[...] = jnp.where(mine, part, mixed[...])
    result[...] += dot_low(mixed[...], outer[pl.ds(pl.multiple_of(pair * 128, 128), 128), :])


def attention_up(state, own, shared, raw_rows, gain, table, inner, output, moves, sources, name):
    tokens = own.shape[0]
    pslice = tokens - CLEN
    _, cols, _, piece, _ = inner.shape
    block = lambda rows: pl.BlockSpec((rows, 128), lambda i: (0, i))
    low = lambda rows: jax.ShapeDtypeStruct((rows, D), LOW)
    result, normed, read, query, keys, values, mixed, total, *moved = carry(
        functools.partial(up_kernel, raw_rows, pslice),
        moves,
        grid=(HEADS // 2,),
        out_shape=(
            jax.ShapeDtypeStruct((tokens, D), F32),
            low(tokens),
            low(KEYS),
            low(tokens),
            low(KEYS),
            low(KEYS),
            low(tokens),
            jax.ShapeDtypeStruct((tokens, D), F32),
        ),
        in_specs=[
            once((tokens, D)),
            once((tokens, D)),
            once(shared.shape),
            once((1, D)),
            once(table.shape),
            head_block(cols, piece, 0),
            head_block(cols, piece, 1),
            head_block(cols, piece, 0),
            outer_block(cols, piece),
        ],
        out_specs=(
            whole((tokens, D)),
            whole((tokens, D)),
            whole((KEYS, D)),
            block(tokens),
            block(KEYS),
            block(KEYS),
            block(tokens),
            block(tokens),
        ),
        scratch_shapes=[
            pltpu.VMEM((128, STRIP), F32),
            pltpu.VMEM((tokens, KEYS), F32),
            pltpu.VMEM((tokens, KEYS), LOW),
            pltpu.VMEM((D, D), LOW),
        ],
        mib=48,
        name=name,
    )(state, own, shared, gain, table, inner, inner, output, output, *sources)
    return result, (normed, read, query, keys, values, mixed, total, inner, output), moved


def slide_sum(grid):
    rows = grid.shape[0]
    while rows > 8:
        rows = rows // 2
        grid = grid[:rows] + pltpu.roll(grid[rows:], WRAP - rows, 1)
    for step in (4, 2, 1):
        grid = grid + pltpu.roll(pltpu.roll(grid, 8 - step, 0), WRAP - step, 1)
    return grid[:1]


def down_kernel(
    pslice,
    grad_next,
    state,
    gain,
    normed,
    read,
    query,
    keys,
    values,
    mixed,
    total,
    table,
    wq,
    wk,
    wv,
    wo,
    result,
    grad_gain,
    grads,
    grad_table,
    low,
    outer,
    grad_outer,
    sum_own,
    sum_read,
    spill,
    strip,
    raw,
    pulled,
    probs,
    slopes,
    folded,
    sum_keys,
    sum_values,
):
    pair = pl.program_id(0)
    lane = lax.broadcasted_iota(jnp.int32, (1, 128), 1)
    here = pl.ds(pl.multiple_of(pair * 128, 128), 128)

    @pl.when(pair == 0)
    def _():
        probs[:pslice, PLEN:] = jnp.zeros((pslice, CLEN), LOW)
        slopes[:pslice, PLEN:] = jnp.zeros((pslice, CLEN), LOW)
        low[...] = grad_next[...].astype(LOW)
        outer[...] = wo[...].reshape(D, D)
        sum_own[...] = jnp.zeros_like(sum_own)
        sum_read[...] = jnp.zeros_like(sum_read)

    grad_outer[here, :] = dot_over(mixed[...], low[...]).astype(LOW)
    grad_mixed = dot_back(low[...], outer[here, :]).astype(LOW)
    for half in range(2):
        mine = (lane < HDIM) if half == 0 else (lane >= HDIM)
        fill_strip(strip, table, 2 * pair + half)
        part = (jnp.where(mine, query[...], 0) * HDIM ** (-0.5)).astype(LOW)
        upstream = jnp.where(mine, grad_mixed, 0).astype(LOW)
        raw[...] = dot_back(part, keys[...])
        pulled[...] = dot_back(upstream, values[...])
        folded[...] = jnp.zeros_like(folded)
        for row, place, count in tiles_of(pslice):
            rows = pl.ds(row, 128)
            log_total = total[rows, half * HDIM : half * HDIM + 1]
            chance = jnp.exp(raw[rows, :count] + strip[:, place] - log_total)
            product = chance * pulled[rows, :count]
            centre = jnp.sum(product, -1, keepdims=True)
            slope = (product - chance * centre).astype(LOW)
            probs[rows, :count] = chance.astype(LOW)
            slopes[rows, :count] = slope
            folded[:, place] += slope.astype(F32)
        step = (dot_low(slopes[...], keys[...]) * HDIM ** (-0.5)).astype(LOW)
        if half == 0:
            grad_query = step
            sum_keys[...] = dot_over(part, slopes[...])
            sum_values[...] = dot_over(upstream, probs[...])
        else:
            grad_query = jnp.where(mine, step, grad_query)
            sum_keys[...] += dot_over(part, slopes[...])
            sum_values[...] += dot_over(upstream, probs[...])
        grad_table[pl.ds(2 * pair + half, 1), :] = slide_sum(folded[:, :WRAP])

    shape = grads.shape[:2] + grads.shape[3:4] + (128,)

    def keep(index, turned):
        grads[:, :, index, :, here] = turned.T.astype(LOW).reshape(shape)

    keep(0, dot_over(grad_query, normed[...]))
    keep(1, dot_low(sum_keys[...].astype(LOW), read[...]))
    keep(2, dot_low(sum_values[...].astype(LOW), read[...]))
    sum_own[...] += dot_back(grad_query, wq[...].reshape(D, 128))
    pairs = jnp.concatenate([sum_keys[...].T, sum_values[...].T], 1).astype(LOW)
    both = jnp.concatenate([wk[...].reshape(D, 128), wv[...].reshape(D, 128)], 1)
    sum_read[...] += dot_back(pairs, both)

    @pl.when(pair == pl.num_programs(0) - 1)
    def _():
        grads[:, :, 3] = grad_outer[...].reshape(shape[:3] + (D,))
        spill[...] = sum_read[:PLEN, :].astype(LOW).reshape(spill.shape)


def down_after(pslice, own_in, own_out, extras, results):
    grad_next, state, gain = own_in[:3]
    result, grad_gain = own_out[:2]
    sum_own, sum_read = extras[3:5]
    shift = (pl.program_id(0) - (pl.num_programs(0) - 1)) * 8
    lines = 0.0
    for row, count in ((0, pslice), (pslice, CLEN)):
        rows = pl.ds(pl.multiple_of(row + shift, 8), count)
        if row == 0:
            more = results[0][...].reshape(pslice, D)
        else:
            more = sum_read[pl.ds(pl.multiple_of(PLEN + shift, 8), CLEN), :]
        grad_state, line = norm_back(state[rows, :].astype(F32), gain[...], sum_own[rows, :] + more)
        result[rows, :] = grad_next[rows, :] + grad_state
        lines = lines + line
    grad_gain[...] = lines


def attention_down(grad_next, state, gain, stash, table, moves, sources, name):
    normed, read, query, keys, values, mixed, total, inner, output = stash
    tokens = normed.shape[0]
    pslice = tokens - CLEN
    _, cols, _, piece, _ = inner.shape
    block = lambda rows: pl.BlockSpec((rows, 128), lambda i: (0, i))
    rows = Reduce(
        (pslice // 16, 16, D), ("core", "x"), take=lambda outs, extras: extras[5], keep=True
    )
    return carry(
        functools.partial(down_kernel, pslice),
        [(rows, (LATE,) * 3)] + moves,
        grid=(HEADS // 2,),
        out_shape=(
            jax.ShapeDtypeStruct((tokens, D), F32),
            jax.ShapeDtypeStruct((1, D), F32),
            jax.ShapeDtypeStruct((4, cols, 4, piece, D), LOW),
            jax.ShapeDtypeStruct(table.shape, F32),
        ),
        in_specs=[
            once((tokens, D)),
            once((tokens, D)),
            once((1, D)),
            once((tokens, D)),
            once((KEYS, D)),
            block(tokens),
            block(KEYS),
            block(KEYS),
            block(tokens),
            block(tokens),
            once(table.shape),
            head_block(cols, piece, 0),
            head_block(cols, piece, 1),
            head_block(cols, piece, 0),
            outer_block(cols, piece),
        ],
        out_specs=(
            whole((tokens, D)),
            whole((1, D)),
            whole((4, cols, 4, piece, D)),
            whole(table.shape),
        ),
        scratch_shapes=[
            pltpu.VMEM((tokens, D), LOW),
            pltpu.VMEM((D, D), LOW),
            pltpu.VMEM((D, D), LOW),
            pltpu.VMEM((tokens, D), F32),
            pltpu.VMEM((KEYS, D), F32),
            pltpu.VMEM((4, 1, pslice // 16, 16, D), LOW),
            pltpu.VMEM((128, STRIP), F32),
            pltpu.VMEM((tokens, KEYS), F32),
            pltpu.VMEM((tokens, KEYS), F32),
            pltpu.VMEM((tokens, KEYS), LOW),
            pltpu.VMEM((tokens, KEYS), LOW),
            pltpu.VMEM((128, STRIP), F32),
            pltpu.VMEM((128, KEYS), F32),
            pltpu.VMEM((128, KEYS), F32),
        ],
        mib=60,
        name=name,
        after=functools.partial(down_after, pslice),
    )(
        grad_next,
        state,
        gain,
        normed,
        read,
        query,
        keys,
        values,
        mixed,
        total,
        table,
        inner,
        inner,
        output,
        output,
        *sources,
    )


def mlp_up_kernel(state, gain, gain_next, first, second, result, normed, normed_next):
    step = pl.program_id(0)

    @pl.when(step == 0)
    def _():
        normed[...] = norm_rows(state[...], gain[...]).astype(LOW)
        result[...] = state[...]

    active = gelu(dot_low(normed[...], first[...].reshape(D, D))).astype(LOW)
    result[...] += dot_low(active, second[...].reshape(D, D))

    @pl.when(step == pl.num_programs(0) - 1)
    def _():
        normed_next[...] = norm_rows(result[...], gain_next[...]).astype(LOW)


def mlp_blocks(cols, piece):
    return (
        pl.BlockSpec((4, cols, None, piece, D), lambda i: (0, 0, 4 + i, 0, 0)),
        pl.BlockSpec((None, cols, 4, piece, D), lambda i: (i, 0, 0, 0, 0)),
    )


def mlp_up(state, gain, gain_next, dense, moves, sources, name):
    tokens = state.shape[0]
    pslice = tokens - CLEN
    _, cols, _, piece, _ = dense.shape
    rows = Rows((pslice, D), take=lambda outs, extras: outs[2].at[pl.ds(0, pslice)])
    return carry(
        mlp_up_kernel,
        [(rows, (LATE,) * 3)] + moves,
        grid=(4,),
        out_shape=(
            jax.ShapeDtypeStruct((tokens, D), F32),
            jax.ShapeDtypeStruct((tokens, D), LOW),
            jax.ShapeDtypeStruct((tokens, D), LOW),
        ),
        in_specs=[once((tokens, D)), once((1, D)), once((1, D)), *mlp_blocks(cols, piece)],
        out_specs=(whole((tokens, D)),) * 3,
        scratch_shapes=[],
        mib=32,
        name=name,
    )(state, gain, gain_next, dense, dense, *sources)


def mlp_down_kernel(
    grad_next, state, normed, gain, first, second, result, grad_gain, grad_first, grad_second, low, total
):
    step = pl.program_id(0)

    @pl.when(step == 0)
    def _():
        low[...] = grad_next[...].astype(LOW)
        total[...] = jnp.zeros_like(total)

    inner, outer = first[...].reshape(D, D), second[...].reshape(D, D)
    active, slope = gelu_parts(dot_low(normed[...], inner))
    grad_hidden = (slope * dot_back(low[...], outer)).astype(LOW)
    grad_second[...] = dot_over(active.astype(LOW), low[...]).astype(LOW).reshape(grad_second.shape)
    grad_first[...] = dot_over(normed[...], grad_hidden).astype(LOW).reshape(grad_first.shape)
    total[...] += dot_back(grad_hidden, inner)

    @pl.when(step == pl.num_programs(0) - 1)
    def _():
        grad_state, grad_line = norm_back(state[...], gain[...], total[...])
        result[...] = grad_next[...] + grad_state
        grad_gain[...] = grad_line


def mlp_down(grad_next, state, normed, gain, dense, moves, sources, name):
    tokens = state.shape[0]
    _, cols, _, piece, _ = dense.shape
    share = jax.ShapeDtypeStruct((4, cols, 4, piece, D), LOW)
    return carry(
        mlp_down_kernel,
        moves,
        grid=(4,),
        out_shape=(
            jax.ShapeDtypeStruct((tokens, D), F32),
            jax.ShapeDtypeStruct((1, D), F32),
            share,
            share,
        ),
        in_specs=[
            once((tokens, D)),
            once((tokens, D)),
            once((tokens, D)),
            once((1, D)),
            *mlp_blocks(cols, piece),
        ],
        out_specs=(
            whole((tokens, D)),
            whole((1, D)),
            pl.BlockSpec((4, cols, None, piece, D), lambda i: (0, 0, i, 0, 0)),
            pl.BlockSpec((None, cols, 4, piece, D), lambda i: (i, 0, 0, 0, 0)),
        ),
        scratch_shapes=[pltpu.VMEM((tokens, D), LOW), pltpu.VMEM((tokens, D), F32)],
        mib=60,
        name=name,
    )(grad_next, state, normed, gain, dense, dense, *sources)


def routed_kernel(
    sent,
    sent_gates,
    sent_cotangent,
    first,
    second,
    outcome,
    returned,
    reach,
    grad_first,
    grad_second,
    rows,
    gates,
    cotangent,
    inner,
    outer,
    active_all,
    hidden_all,
    upstream,
    back,
    back_reach,
    turned,
    sum_up,
    sum_down,
    held,
    row_send,
    row_recv,
    gate_send,
    gate_recv,
    back_send,
    back_recv,
    reach_send,
    reach_recv,
    local,
    store,
):
    capacity = rows.shape[1]
    barrier = pltpu.get_barrier_semaphore()
    others = range(1, len(SLOTS))
    for slot in others:
        pl.semaphore_signal(barrier, inc=1, device_id=slot_device(slot), device_id_type=MESH)
    loads = [
        Within(sent.at[0], rows.at[0], local.at[0]),
        Within(sent_gates.at[0], gates.at[0], local.at[1]),
        Within(sent_cotangent, cotangent, local.at[2]),
        Within(first, inner, local.at[3]),
        Within(second, outer, local.at[4]),
    ]
    for load in loads:
        load.start()
    pl.semaphore_wait(barrier, len(others))

    def there(slot):
        device = slot_device(slot)
        return (
            remote(sent_gates.at[slot], gates.at[slot], gate_send, gate_recv, slot, **device),
            remote(sent.at[slot], rows.at[slot], row_send, row_recv, slot, **device),
        )

    def home(slot):
        device = slot_device(slot)
        return (
            remote(back_reach.at[slot], reach.at[slot], reach_send, reach_recv, slot, **device),
            remote(back.at[slot], returned.at[slot], back_send, back_recv, slot, **device),
        )

    own_home = [
        Within(back_reach.at[0], reach.at[0], local.at[5]),
        Within(back.at[0], returned.at[0], local.at[6]),
    ]
    for slot in (4, 5, 1, 6, 7, 2, 3):
        for copy in there(slot):
            copy.start()
    for load in loads:
        load.wait()
    ones = jnp.ones((8, D), F32)
    count = 2 * capacity
    for b in (0, 2, 1, 3):
        for a in range(2):
            slot = 2 * b + a
            if slot:
                for copy in there(slot):
                    copy.wait_recv()
            gate = gates[slot].T[:capacity, :1]
            at = pl.ds(slot * capacity, capacity)
            upstream[at, :] = (gate * cotangent[slot].astype(F32)).astype(LOW)
        both = pl.ds(2 * b * capacity, count)
        block = rows[2 * b : 2 * b + 2].reshape(count, D)
        sum_up[...] = jnp.zeros_like(sum_up)
        sum_down[...] = jnp.zeros_like(sum_down)

        def part(j):
            active, slope = gelu_parts(dot_low(block, inner[j]))
            active = active.astype(LOW)
            active_all[j, both, :] = active
            sum_up[...] += dot_low(active, outer[j])
            hidden = (slope * dot_back(upstream[both, :], outer[j])).astype(LOW)
            hidden_all[j, both, :] = hidden
            sum_down[...] += dot_back(hidden, inner[j])

        each(4, part)
        back[2 * b : 2 * b + 2] = sum_down[...].astype(LOW).reshape(2, capacity, D)
        outcome[2 * b : 2 * b + 2] = sum_up[...].astype(LOW).reshape(2, capacity, D)
        for a in range(2):
            slot = 2 * b + a
            met = cotangent[slot].astype(F32) * outcome[slot].astype(F32)
            line = lax.dot_general(
                ones, met, (((1,), (1,)), ((), ())), precision=HIGH, preferred_element_type=F32
            )
            back_reach[slot] = jnp.pad(line, ((0, 0), (0, back_reach.shape[2] - capacity)))
            if slot:
                for copy in home(slot):
                    copy.start()
            else:
                for copy in own_home:
                    copy.start()
    turned[...] = rows[...].reshape(len(SLOTS) * capacity, D).T

    def stored(j, side):
        return (
            Within(held.at[side, 0], grad_first.at[j], store.at[side, 0]),
            Within(held.at[side, 1], grad_second.at[j], store.at[side, 1]),
        )

    def weigh(j):
        side = lax.rem(j, 2)

        @pl.when(j >= 2)
        def _():
            for copy in stored(j - 2, side):
                copy.wait()

        held[side, 0] = dot_low(turned[...], hidden_all[j]).astype(LOW)
        held[side, 1] = dot_over(active_all[j], upstream[...]).astype(LOW)
        for copy in stored(j, side):
            copy.start()

    each(4, weigh)
    for j in (2, 3):
        for copy in stored(j, j % 2):
            copy.wait()
    for copy in own_home:
        copy.wait()
    for slot in (4, 5, 1, 6, 7, 2, 3):
        for copy in home(slot):
            copy.wait_recv()
    for slot in (4, 5, 1, 6, 7, 2, 3):
        for copy in there(slot) + home(slot):
            copy.wait_send()


def routed(sent, gates, cotangent, first, second, name):
    slots, capacity, _ = sent.shape
    hbm = pl.BlockSpec(memory_space=pl.ANY)
    count = slots * capacity
    low = jax.ShapeDtypeStruct(sent.shape, LOW)
    share = jax.ShapeDtypeStruct(first.shape, LOW)
    pairs = [pltpu.SemaphoreType.DMA((slots,)) for _ in range(8)]
    return pl.pallas_call(
        routed_kernel,
        out_shape=(low, low, jax.ShapeDtypeStruct(gates.shape, F32), share, share),
        in_specs=[hbm] * 5,
        out_specs=(pl.BlockSpec(memory_space=pltpu.VMEM), hbm, hbm, hbm, hbm),
        scratch_shapes=[
            pltpu.VMEM(sent.shape, LOW),
            pltpu.VMEM(gates.shape, F32),
            pltpu.VMEM(sent.shape, LOW),
            pltpu.VMEM(first.shape, LOW),
            pltpu.VMEM(second.shape, LOW),
            pltpu.VMEM((4, count, D), LOW),
            pltpu.VMEM((4, count, D), LOW),
            pltpu.VMEM((count, D), LOW),
            pltpu.VMEM(sent.shape, LOW),
            pltpu.VMEM(gates.shape, F32),
            pltpu.VMEM((D, count), LOW),
            pltpu.VMEM((2 * capacity, D), F32),
            pltpu.VMEM((2 * capacity, D), F32),
            pltpu.VMEM((2, 2, D, D), LOW),
            *pairs,
            pltpu.SemaphoreType.DMA((7,)),
            pltpu.SemaphoreType.DMA((2, 2)),
        ],
        compiler_params=pltpu.CompilerParams(
            vmem_limit_bytes=60 * MIB, collective_id=name, has_side_effects=True
        ),
    )(sent, gates, cotangent, first, second)


def tiled(
    inputs,
    cotangent,
    routes,
    buckets,
    norm_gains,
    attn_qkv,
    attn_out,
    rel_bias,
    mlp_in,
    mlp_out,
    router,
    expert_in,
    expert_out,
):
    grid = ("row", "col")
    places = lax.axis_size(grid)
    cols, planes = lax.axis_size("col"), lax.axis_size("dp")
    experts = planes * cols
    tokens = inputs.shape[1]
    pslice = tokens - CLEN
    capacity = 3 * tokens // experts
    piece = D // places

    small = [norm_gains.reshape(-1), rel_bias.reshape(-1), router.reshape(-1)]
    cuts = [part.shape[0] for part in small]
    packed = jnp.concatenate(small)
    packed = jnp.pad(packed, (0, -packed.shape[0] % 2048)).reshape(1, -1, 128)

    def pieces(*blocks):
        return jnp.concatenate(
            [block.reshape(piece, -1, D).transpose(1, 0, 2) for block in blocks], 0
        )

    attn = [pieces(attn_qkv[i], attn_out[i]) for i in range(2)]
    dense = jnp.concatenate([mlp_out.reshape(-1, piece, D), pieces(mlp_in)], 0)

    pair = (2, piece, D)
    early = (0, LATE, LATE, LATE, LATE)
    packed, inner0, output0, shared0 = carry(
        None,
        [
            (Gather(packed.shape, False, cols), early),
            (Gather(pair, False, cols), early),
            (Gather(pair, True, cols), early),
            (Rows((pslice, D)), (0, LATE, LATE)),
        ],
        (1,),
        [],
        [],
        [],
        [],
        32,
        1,
    )(packed, attn[0][:2], attn[0][2:], inputs[0, :pslice])
    packed = packed.reshape(places, -1)
    gains = packed[:, : cuts[0]].reshape(places, 4, -1).transpose(1, 0, 2).reshape(4, 1, D).astype(F32)
    rel = packed[:, cuts[0] : cuts[0] + cuts[1]].reshape(places, 2, -1, HEADS)
    rel = rel.transpose(1, 0, 2, 3).reshape(2, BUCKETS, HEADS)
    route_w = packed[:, cuts[0] + cuts[1] : sum(cuts)].reshape(D, experts)

    gap = jnp.full((WRAP - KEYS,), -1, jnp.int32)
    index = jnp.concatenate([jnp.flip(buckets[: PLEN + 1]), gap, jnp.flip(buckets[PLEN + 1 :])])
    hot = (jnp.arange(BUCKETS, dtype=jnp.int32)[:, None] == index[None, :]).astype(LOW)
    floor = jnp.where(index < 0, NEG, 0.0).astype(F32)
    tables = [
        jnp.pad(dot_over(rel[i], hot) + floor[None], ((0, 16 - HEADS), (0, 0))) for i in range(2)
    ]

    flat = routes[0].reshape(-1)
    levels = jnp.arange(experts, dtype=jnp.int32)
    choose = (routes[0][:, :, None] == levels[None, None, :]).astype(F32)
    flipped_plane = (flat // cols) ^ lax.axis_index("dp")
    flipped_col = (flat % cols) ^ lax.axis_index("col")
    slot = 2 * flipped_col + flipped_plane
    hits = (slot[:, None] == levels[None, :]).astype(LOW)
    before = jnp.arange(2 * tokens)
    before = (before[:, None] > before[None, :]).astype(LOW)
    rank = jnp.sum(dot_low(before, hits) * hits.astype(F32), 1).astype(jnp.int32)
    place = (slot * capacity + rank).reshape(tokens, 2)
    spots = jnp.arange(experts * capacity, dtype=jnp.int32)
    picks = [(place[:, k][:, None] == spots[None, :]).astype(LOW) for k in range(2)]
    both = picks[0] + picks[1]
    sent_cotangent = dot_over(both, cotangent[0]).astype(LOW).reshape(experts, capacity, D)

    state1, stash1, (dense, first) = attention_up(
        inputs[0],
        inputs[0],
        shared0,
        True,
        gains[0],
        tables[0],
        inner0,
        output0,
        [
            (Gather(dense.shape, True, cols), (0, 2, 4, LATE, LATE)),
            (Rows(expert_in.shape[1:]), (0, 4, LATE)),
        ],
        (dense, expert_in[0]),
        2,
    )
    state2, normed1, normed2, shared2, inner1, output1 = mlp_up(
        state1,
        gains[1],
        gains[2],
        dense,
        [(Gather(pair, True, cols), (0, 2, LATE, LATE, LATE))] * 1
        + [(Gather(pair, True, cols), (0, 2, LATE, LATE, LATE))],
        (attn[1][:2], attn[1][2:]),
        3,
    )
    state3, stash3, (second, far_cotangent) = attention_up(
        state2,
        normed2,
        shared2,
        False,
        gains[2],
        tables[1],
        inner1,
        output1,
        [
            (Rows(expert_out.shape[1:]), (0, 4, LATE)),
            (Swap((capacity, D)), (0, LATE)),
        ],
        (expert_out[0], sent_cotangent),
        4,
    )

    normed3 = norm_rows(state3, gains[3]).astype(LOW)
    logits = dot_low(normed3, route_w)
    picked = jnp.sum(choose * logits[:, None, :], -1)
    raised = jnp.exp(picked - jnp.max(picked, -1, keepdims=True))
    gates = raised / jnp.sum(raised, -1, keepdims=True)
    line = sum(dot_over(jnp.stack(split_low(gates[:, k]), 1), picks[k]) for k in range(2))
    line = jnp.sum(line, 0).reshape(experts, 1, capacity)
    line = jnp.pad(line, ((0, 0), (0, 7), (0, -capacity % 128)))
    sent = dot_over(both, normed3).astype(LOW).reshape(experts, capacity, D)
    outcome, returned, reach, grad_first, grad_second = routed(
        sent, line, far_cotangent, first, second, 5
    )
    returned = returned.reshape(experts * capacity, D)
    reach = jnp.stack(split_low(reach[:, 0, :capacity].reshape(-1)), 1)
    grad_gates = jnp.stack([jnp.sum(dot_low(picks[k], reach), 1) for k in range(2)], 1)
    grad_picked = gates * (grad_gates - jnp.sum(gates * grad_gates, -1, keepdims=True))
    grad_logits = jnp.sum(choose * grad_picked[:, :, None], 1).astype(LOW)
    grad_route = dot_over(normed3, grad_logits)
    grad_normed3 = dot_low(both, returned) + dot_back(grad_logits, route_w)
    grad_state3, gain_last = norm_back(state3, gains[3], grad_normed3)
    grad3 = cotangent[0].astype(F32) + grad_state3

    laid = (4, 1, places, piece, D)
    expert_sum = lambda: Reduce((places, piece, D), ("core", "x"))
    halves = ("core", "y", "x", "z", "swap")
    plain = ("core", "x", "z", "sum")
    grad2, gain_third, late, table_late, own_first, outcome = attention_down(
        grad3,
        state2,
        gains[2],
        stash3,
        tables[1],
        [(expert_sum(), (0, 1, LATE)), (Swap((capacity, D)), (0, LATE))],
        (grad_first.reshape(laid), outcome),
        6,
    )
    outcome = outcome.reshape(experts * capacity, D)
    output = state3 + sum(gates[:, k : k + 1] * dot_low(picks[k], outcome) for k in range(2))
    grad1, gain_second, dense_first, dense_second, own_second, late_a, late_b = mlp_down(
        grad2,
        state1,
        normed1,
        gains[1],
        dense,
        [
            (expert_sum(), (0, 1, LATE)),
            (Reduce(pair, plain, cols), (0, 1, 3, LATE, LATE)),
            (Reduce(pair, halves, cols, first=2), (0, 1, 3, LATE, LATE, LATE)),
        ],
        (grad_second.reshape(laid), late, late),
        7,
    )
    quad = (4, piece, D)
    grad0, gain_first, early, table_early, own_inner, own_outer = attention_down(
        grad1,
        inputs[0],
        gains[0],
        stash1,
        tables[0],
        [
            (Reduce(quad, halves, cols), (0, 1, 3, 5, LATE, LATE)),
            (Reduce(quad, plain, cols), (0, 1, 3, 5, LATE)),
        ],
        (dense_first, dense_second),
        8,
    )

    def rel_grad(table):
        return lax.dot_general(
            hot.astype(F32),
            table[:HEADS],
            (((1,), (1,)), ((), ())),
            precision=HIGH,
            preferred_element_type=F32,
        )

    gain_grads = jnp.concatenate([gain_first, gain_second, gain_third, gain_last], 0)
    gain_grads = gain_grads.reshape(4, places, -1).transpose(1, 0, 2).reshape(places, -1)
    rel_grads = jnp.stack([rel_grad(table_early), rel_grad(table_late)])
    rel_grads = rel_grads.reshape(2, places, -1, HEADS).transpose(1, 0, 2, 3).reshape(places, -1)
    packed = jnp.concatenate([gain_grads, rel_grads, grad_route.reshape(places, -1)], 1)
    packed = jnp.pad(packed, ((0, 0), (0, -packed.shape[1] % 2048))).astype(LOW)
    packed = packed.reshape(4, cols, 1, -1, 128)
    early_a, early_b, packed = carry(
        None,
        [
            (Reduce(pair, plain, cols), (0,) + (LATE,) * 4),
            (Reduce(pair, halves, cols, first=2), (0,) + (LATE,) * 5),
            (Reduce(packed.shape[2:], plain, cols), (0,) + (LATE,) * 4),
        ],
        (1,),
        [],
        [],
        [],
        [],
        32,
        9,
    )(early, early, packed)
    packed = packed.reshape(-1)
    gain_share = packed[: cuts[0]].reshape(4, -1)
    rel_share = packed[cuts[0] : cuts[0] + cuts[1]].reshape(2, -1, HEADS)
    route_share = packed[cuts[0] + cuts[1] : sum(cuts)].reshape(-1, experts)

    def joined(*blocks):
        return jnp.concatenate([block[i] for block in blocks for i in range(block.shape[0])], 1)

    return (
        output[None],
        grad0[None],
        gain_share,
        jnp.stack([joined(early_a, early_b[:1]), joined(late_a, late_b[:1])]),
        jnp.stack([early_b[1], late_b[1]]),
        rel_share,
        joined(own_inner),
        own_outer.reshape(-1, D),
        route_share,
        own_first.reshape(1, D, D),
        own_second.reshape(1, D, D),
    )


def solution(mesh):
    in_specs = (
        P(("dp", "col"), "row", None),
        P(("dp", "col"), "row", None),
        P(("dp", "col"), "row", None),
        P(),
        P(None, ("row", "col")),
        P(None, ("row", "col"), None),
        P(None, ("row", "col"), None),
        P(None, ("row", "col"), None),
        P(("row", "col"), None),
        P(("row", "col"), None),
        P(("row", "col"), None),
        P(("dp", "col"), None, "row"),
        P(("dp", "col"), "row", None),
    )
    out_specs = (
        P(("dp", "col"), "row", None),
        P(("dp", "col"), "row", None),
        P(None, ("row", "col")),
        P(None, ("row", "col"), None),
        P(None, ("row", "col"), None),
        P(None, ("row", "col"), None),
        P(("row", "col"), None),
        P(("row", "col"), None),
        P(("row", "col"), None),
        P(("dp", "col"), None, "row"),
        P(("dp", "col"), "row", None),
    )
    sizes = dict(mesh.shape)
    piece = D // (sizes["row"] * sizes["col"])
    capacity = 3 * (PLEN // sizes["row"] + CLEN) // (sizes["dp"] * sizes["col"])
    whole_tiles = (sizes["dp"], sizes["row"], sizes["col"]) == (2, 4, 4) and piece % 16 == 0 and capacity % 16 == 0
    return jax.shard_map(
        tiled if whole_tiles else general, mesh=mesh, in_specs=in_specs, out_specs=out_specs, check_vma=False
    )
```

```python
import functools

import jax
import jax.numpy as jnp
from jax import lax
from jax.experimental import pallas as pl
from jax.experimental.pallas import tpu as pltpu
from jax.sharding import PartitionSpec as P

D = 768
HEADS = 12
HDIM = 64
FF = 3072
BUCKETS = 32
PLEN = 1024
CLEN = 128
KEYS = PLEN + CLEN
WRAP = KEYS + 128
STRIP = 2 * PLEN
NEG = -1e30
EPS = 1e-06
CURVE = 0.7978845608028654
CUBE = 0.044715
HIGH = lax.Precision.HIGHEST
F32 = jnp.float32
LOW = jnp.bfloat16
MIB = 1 << 20


def dot_low(left, right):
    return jnp.dot(left, right, preferred_element_type=F32)


def dot_back(left, right):
    return lax.dot_general(left, right, (((1,), (1,)), ((), ())), preferred_element_type=F32)


def dot_over(left, right):
    return lax.dot_general(left, right, (((0,), (0,)), ((), ())), preferred_element_type=F32)


def normalise(values):
    center = values - jnp.mean(values, -1, keepdims=True)
    scale = lax.rsqrt(jnp.mean(center * center, -1, keepdims=True) + EPS)
    return center * scale, scale


def norm_rows(values, gain):
    return normalise(values)[0] * gain


def norm_back(values, gain, upstream):
    unit, scale = normalise(values)
    pulled = upstream * gain
    shift = jnp.mean(pulled, -1, keepdims=True)
    along = jnp.mean(pulled * unit, -1, keepdims=True)
    return (pulled - shift - unit * along) * scale, jnp.sum(upstream * unit, 0, keepdims=True)


def gelu_parts(values):
    square = values * values
    bend = jnp.tanh(CURVE * (values + CUBE * square * values))
    half = 0.5 * (1.0 + bend)
    slope = half + 0.5 * values * (1.0 - bend * bend) * (CURVE + 3.0 * CURVE * CUBE * square)
    return values * half, slope


def gelu(values):
    return 0.5 * values * (1.0 + jnp.tanh(CURVE * (values + CUBE * values * values * values)))


def params(mib, steps=1):
    return pltpu.CompilerParams(
        vmem_limit_bytes=mib * MIB, dimension_semantics=("arbitrary",) * steps
    )


def whole(shape):
    return pl.BlockSpec(shape, lambda *_: (0,) * len(shape))


MESH = pl.DeviceIdType.MESH


class Remote:
    def __init__(self, src, dst, send, recv, index, device):
        self.parts = (src, dst, send, recv, index, device)

    def described(self):
        src, dst, send, recv, index, device = self.parts
        return pltpu.make_async_remote_copy(
            src_ref=src,
            dst_ref=dst,
            send_sem=send.at[index],
            recv_sem=recv.at[index],
            device_id=device,
            device_id_type=MESH,
        )

    def start(self):
        self.described().start()

    def wait_recv(self):
        self.described().wait_recv()

    def wait_send(self):
        self.described().wait_send()


def remote(src, dst, send, recv, index, **device):
    return Remote(src, dst, send, recv, index, device)


def neighbours():
    row, dp = lax.axis_index("row"), lax.axis_index("dp")
    across = lax.rem(row + 2, 4)
    core = row + 1 - 2 * lax.rem(row, 2)
    return row, across, core, dp + 1 - 2 * lax.rem(dp, 2)


class Within:
    def __init__(self, src, dst, sem):
        self.parts = (src, dst, sem)

    def start(self):
        pltpu.make_async_copy(*self.parts).start()

    def wait(self):
        pltpu.make_async_copy(*self.parts).wait()


class Gather:
    phases = 5

    def __init__(self, shape, split, cols, span=None, into=None, take=None):
        self.shape, self.split, self.cols, self.take, self.into = shape, split, cols, take, into
        self.span = (0, shape[-1]) if span is None else span
        self.spec = pl.BlockSpec(memory_space=pl.ANY)
        self.result = jax.ShapeDtypeStruct((4, cols) + shape, LOW)
        count = 4 * cols - 1 + (4 * cols - 2 if split else 0)
        self.scratch = [
            pltpu.SemaphoreType.DMA((count + 2 * cols,)),
            pltpu.SemaphoreType.DMA((count + 2 * cols,)),
            pltpu.SemaphoreType.DMA((1,)),
        ]

    def copies(self, src, dst, send, recv, local):
        cols = self.cols
        row, across, core, plane = neighbours()
        col, dp = lax.axis_index("col"), lax.axis_index("dp")
        first, width = self.span
        half = width // 2
        lead = (slice(None),) * (len(self.shape) - 1)
        full = lead + (pl.ds(first, width),)
        mine = pl.multiple_of(first + dp * half, 128)
        others = pl.multiple_of(first + (1 - dp) * half, 128)
        part = lead + (pl.ds(mine, half),) if self.split else full
        rest = lead + (pl.ds(others, half),)
        number = [0]

        def make(source, target, **device):
            number[0] += 1
            return remote(source, target, send, recv, number[0] - 1, **device)

        def piece(where, step, which):
            return dst.at[where, lax.rem(col - step + cols, cols)].at[which]

        own = src.at[part]
        out = {}
        out["local"] = Within(src.at[full], piece(row, 0, full), local.at[0])
        out["z"] = [
            make(own, piece(row, 0, part), col=lax.rem(col + step, cols)) for step in range(1, cols)
        ]
        out["x"] = [make(own, piece(row, 0, part), row=across)]
        out["x"] += [
            make(piece(row, step, part), piece(row, step, part), row=across)
            for step in range(1, cols)
        ]
        out["core own"] = make(src.at[full], piece(row, 0, full), row=core)
        out["core z"] = [
            make(piece(row, step, part), piece(row, step, part), row=core) for step in range(1, cols)
        ]
        out["core x"] = [
            make(piece(across, step, part), piece(across, step, part), row=core)
            for step in range(cols)
        ]
        if self.split:
            out["y z"] = [
                make(piece(row, step, part), piece(row, step, part), dp=plane)
                for step in range(1, cols)
            ]
            out["y x"] = [
                make(piece(across, step, part), piece(across, step, part), dp=plane)
                for step in range(cols)
            ]
            out["core y z"] = [
                make(piece(row, step, rest), piece(row, step, rest), row=core)
                for step in range(1, cols)
            ]
            out["core y x"] = [
                make(piece(across, step, rest), piece(across, step, rest), row=core)
                for step in range(cols)
            ]
        return out

    def peers(self):
        cols, col = self.cols, lax.axis_index("col")
        row, across, core, plane = neighbours()
        found = {(0, step): dict(col=lax.rem(col + step, cols)) for step in range(1, cols)}
        found.update(across=dict(row=across), core=dict(row=core))
        if self.split:
            found[(1, 0)] = dict(dp=plane)
        return found

    def phase(self, number, *refs):
        out = self.copies(*refs)
        if number == 0:
            out["local"].start()
            for copy in out["z"]:
                copy.start()
            out["x"][0].start()
            out["core own"].start()
        elif number == 1:
            for step in self.order():
                out["z"][step - 1].wait_recv()
                out["x"][step].start()
                if self.split:
                    out["y z"][step - 1].start()
                out["core z"][step - 1].start()
        elif number == 2:
            for step in [0] + self.order():
                out["x"][step].wait_recv()
                if self.split:
                    out["y x"][step].start()
                out["core x"][step].start()
        elif number == 3 and self.split:
            for step in self.order():
                out["y z"][step - 1].wait_recv()
                out["core y z"][step - 1].start()
            for step in [0] + self.order():
                out["y x"][step].wait_recv()
                out["core y x"][step].start()
        elif number == 4:
            out["local"].wait()
            late = [out["core own"]] + out["core z"] + out["core x"]
            if self.split:
                late += out["core y z"] + out["core y x"]
            for copy in late:
                copy.wait_recv()
            early = out["z"] + out["x"] + late
            if self.split:
                early += out["y z"] + out["y x"]
            for copy in early:
                copy.wait_send()

    def order(self):
        steps = list(range(1, self.cols))
        return sorted(steps, key=lambda step: min(step, self.cols - step))


class Rows:
    phases = 3

    def __init__(self, shape, take=None):
        self.take = take
        self.result = jax.ShapeDtypeStruct((4,) + shape, LOW)
        self.spec = pl.BlockSpec(memory_space=pl.ANY)
        self.scratch = [
            pltpu.SemaphoreType.DMA((3,)),
            pltpu.SemaphoreType.DMA((3,)),
            pltpu.SemaphoreType.DMA((1,)),
        ]

    def peers(self):
        row, across, core, plane = neighbours()
        return dict(across=dict(row=across), core=dict(row=core))

    def phase(self, number, src, dst, send, recv, local):
        row, across, core, plane = neighbours()
        own = Within(src, dst.at[row], local.at[0])
        far = remote(src, dst.at[row], send, recv, 0, row=across)
        near = remote(src, dst.at[row], send, recv, 1, row=core)
        on = remote(dst.at[across], dst.at[across], send, recv, 2, row=core)
        if number == 0:
            own.start()
            far.start()
            near.start()
        elif number == 1:
            far.wait_recv()
            on.start()
        else:
            own.wait()
            near.wait_recv()
            on.wait_recv()
            for copy in (far, near, on):
                copy.wait_send()


SLOTS = [(a, b) for b in range(4) for a in range(2)]


def slot_device(slot):
    a, b = SLOTS[slot]
    dp, col = lax.axis_index("dp"), lax.axis_index("col")
    flipped = (col, col + 1 - 2 * lax.rem(col, 2), lax.rem(col + 2, 4), 3 - col)[b]
    device = {}
    if a:
        device["dp"] = 1 - dp
    if b:
        device["col"] = flipped
    return device


class Swap:
    phases = 2

    def __init__(self, shape, take=None):
        self.take = take
        self.result = jax.ShapeDtypeStruct((len(SLOTS),) + shape, LOW)
        self.spec = pl.BlockSpec(memory_space=pl.ANY)
        self.scratch = [
            pltpu.SemaphoreType.DMA((len(SLOTS),)),
            pltpu.SemaphoreType.DMA((len(SLOTS),)),
            pltpu.SemaphoreType.DMA((1,)),
        ]

    def peers(self):
        return {SLOTS[slot]: slot_device(slot) for slot in range(1, len(SLOTS))}

    def phase(self, number, src, dst, send, recv, local):
        own = Within(src.at[0], dst.at[0], local.at[0])
        copies = [
            remote(src.at[slot], dst.at[slot], send, recv, slot, **slot_device(slot))
            for slot in range(1, len(SLOTS))
        ]
        if number == 0:
            for copy in copies:
                copy.start()
            own.start()
        else:
            own.wait()
            for copy in copies:
                copy.wait_recv()
            for copy in copies:
                copy.wait_send()


def each(count, body):
    lax.fori_loop(0, count, lambda index, carried: (body(index), carried)[1], 0)


class Reduce:
    def __init__(self, shape, ops, cols=1, first=0, take=None, keep=False):
        self.ops, self.cols, self.first, self.take, self.keep = ops, cols, first, take, keep
        self.count, tail = shape[0], shape[1:]
        self.part = self.count // 2 if "y" in ops else self.count
        self.phases = len(ops) + 1
        self.lead = 1 if ops[0] == "z" else 2
        ends = {
            "y": ((2, cols, self.part), LOW),
            "x": ((cols, self.part), LOW) if cols > 1 else ((self.part,), F32),
            "sum": ((self.part,), F32),
            "swap": ((2 * self.part,), F32),
        }
        lead, kind = ends[ops[-1]]
        self.result = jax.ShapeDtypeStruct(lead + tail, kind)
        self.spec = once(self.result.shape)
        full = (self.lead, cols, self.count)
        buffers = {"total": [full]}
        if "core" in ops and take is None:
            buffers["near"] = [full]
        if "y" in ops:
            buffers["y"] = [(2, cols, self.part)]
        if "x" in ops:
            buffers["x"] = [(cols, self.part)]
        if "z" in ops:
            buffers["z"] = [(cols - 1, self.part), (self.part,)]
            buffers["end"] = [(self.part,)]
        self.names = list(buffers)
        self.lengths = [len(buffers[name]) for name in self.names]
        self.scratch = [pltpu.VMEM(lead + tail, LOW) for name in self.names for lead in buffers[name]]
        self.scratch += [
            pltpu.SemaphoreType.DMA((8,)),
            pltpu.SemaphoreType.DMA((8,)),
            pltpu.SemaphoreType.DMA((2,)),
        ]

    def peers(self):
        row, across, core, plane = neighbours()
        found = {}
        if "core" in self.ops:
            found["core"] = dict(row=core)
        if "x" in self.ops:
            found["across"] = dict(row=across)
        slots = (2, 4, 6) if "z" in self.ops else ()
        if {"y", "sum", "swap"} & set(self.ops):
            slots += (1,)
        for slot in slots:
            found[SLOTS[slot]] = slot_device(slot)
        return found

    def phase(self, number, src, out, *scratch):
        scratch = list(scratch)
        held = {
            name: [scratch.pop(0) for _ in range(length)]
            for name, length in zip(self.names, self.lengths)
        }
        send, recv, local = scratch
        row, across, core, plane = neighbours()
        x, c = row // 2, lax.rem(row, 2)
        if self.ops[0] == "z":
            x = 0
        dp, col = lax.axis_index("dp"), lax.axis_index("col")
        total = held["total"][0]
        span = pl.ds(self.first, self.count)
        start = dp * self.part if "y" in self.ops else 0
        part, rest = pl.ds(start, self.part), pl.ds((1 - dp) * self.part, self.part)
        if self.take is not None:
            loads = []
        elif self.ops[0] == "core":
            loads = [Within(src.at[2 * i + c, :, span], total.at[i], local.at[i]) for i in range(2)]
        elif self.ops[0] == "z":
            loads = [Within(src.at[:, span], total.at[0], local.at[0])]
        else:
            loads = [Within(src.at[:, :, span], total, local.at[0])]

        def copies(op):
            if op == "core":
                near = held["near"][0] if self.take is None else total
                return [
                    remote(src.at[2 * i + 1 - c, :, span], near.at[i], send, recv, i, row=core)
                    for i in range(2)
                ]
            if op == "y":
                return [remote(total.at[:, :, rest], held["y"][0], send, recv, 2, dp=plane)]
            if op == "x":
                return [remote(total.at[1 - x, :, part], held["x"][0], send, recv, 3, row=across)]
            if op == "z":
                found = []
                for b in (2, 3, 1):
                    device = slot_device(2 * b)
                    view = total.at[x, device["col"], part]
                    found.append(remote(view, held["z"][0].at[b - 1], send, recv, 3 + b, **device))
                return found
            return [remote(held["z"][1], held["end"][0], send, recv, 7, dp=plane)]

        wide = lambda value: value.astype(F32)
        count, cols, size = self.count, self.cols, self.part
        if number > 0:
            op = self.ops[number - 1]
            last = number == len(self.ops)
            if op == "core":
                for load in loads:
                    load.wait()
            for copy in copies(op):
                copy.wait_recv()
            if op == "core":

                def add(i):
                    at = (i // (cols * count), lax.rem(i // count, cols), lax.rem(i, count))
                    if self.take is None:
                        more = held["near"][0][at]
                    else:
                        more = src[2 * at[0] + c, at[1], self.first + at[2]]
                    total[at] = (wide(total[at]) + wide(more)).astype(LOW)

                each(2 * cols * count, add)
            elif op == "y":

                def add(i):
                    at = (i // (cols * size), lax.rem(i // size, cols))
                    k = lax.rem(i, size)
                    kept = at + (start + k,)
                    value = wide(total[kept]) + wide(held["y"][0][at + (k,)])
                    if last:
                        out[at + (k,)] = value.astype(LOW)
                    else:
                        total[kept] = value.astype(LOW)

                each(2 * cols * size, add)
            elif op == "x":

                def add(i):
                    z, k = i // size, lax.rem(i, size)
                    value = wide(total[x, z, start + k]) + wide(held["x"][0][z, k])
                    if last and cols == 1:
                        out[k] = value
                    elif last:
                        out[z, k] = value.astype(LOW)
                    else:
                        total[x, z, start + k] = value.astype(LOW)

                each(cols * size, add)
            elif op == "z":

                def add(k):
                    value = wide(total[x, col, start + k])
                    for b in range(cols - 1):
                        value = value + wide(held["z"][0][b, k])
                    held["z"][1][k] = value.astype(LOW)

                each(size, add)
            else:

                def add(k):
                    mine, other = wide(held["z"][1][k]), wide(held["end"][0][k])
                    if op == "sum":
                        out[k] = mine + other
                    else:
                        out[dp * size + k] = mine
                        out[(1 - dp) * size + k] = other

                each(size, add)
        if number < len(self.ops):
            op = self.ops[number]
            if number == 0:
                for load in loads:
                    load.start()
                if op != "core":
                    for load in loads:
                        load.wait()
            for copy in copies(op):
                copy.start()
        else:
            for op in self.ops:
                for copy in copies(op):
                    copy.wait_send()


class CoreSum:
    phases = 6

    def __init__(self, shape, cols, take):
        self.take, self.cols = take, cols
        self.result = jax.ShapeDtypeStruct((2, cols, 8) + shape, LOW)
        self.spec = once(self.result.shape)
        self.scratch = [
            pltpu.VMEM(self.result.shape, LOW),
            pltpu.SemaphoreType.DMA((10,)),
            pltpu.SemaphoreType.DMA((10,)),
        ]

    def peers(self):
        row, across, core, plane = neighbours()
        return dict(core=dict(row=core))

    def phase(self, number, src, out, near, send, recv):
        row, across, core, plane = neighbours()
        c = lax.rem(row, 2)

        def inner(j, i):
            at = (slice(None), 4 + j)
            view = src.at[2 * i + 1 - c].at[at]
            return remote(view, near.at[i].at[at], send, recv, 2 * j + i, row=core)

        def outer(i):
            at = (slice(None), pl.ds(0, 4))
            view = src.at[2 * i + 1 - c].at[at]
            return remote(view, near.at[i].at[at], send, recv, 8 + i, row=core)

        def begin(j):
            for i in range(2):
                inner(j, i).start()
            if j % 2 == 1:
                outer(j // 2).start()

        def add(i, z, k):
            out[i, z, k] = (src[2 * i + c, z, k].astype(F32) + near[i, z, k].astype(F32)).astype(LOW)

        def end(j):
            for i in range(2):
                inner(j, i).wait_recv()
            each(2 * self.cols, lambda n: add(n // self.cols, lax.rem(n, self.cols), 4 + j))
            if j % 2 == 1:
                outer(j // 2).wait_recv()
                each(4 * self.cols, lambda n: add(j // 2, n // 4, lax.rem(n, 4)))

        if 1 <= number <= 4:
            begin(number - 1)
        if number in (3, 4):
            end(number - 3)
        if number == 5:
            end(2)
            end(3)
            for j in range(4):
                for i in range(2):
                    inner(j, i).wait_send()
            for i in range(2):
                outer(i).wait_send()


class Total:
    phases = 5

    def __init__(self, shape, take=None):
        self.take = take
        self.result = jax.ShapeDtypeStruct(shape, F32)
        self.spec = once(shape)
        self.scratch = [
            pltpu.VMEM((4,) + shape, LOW),
            pltpu.VMEM((6,) + shape, LOW),
            pltpu.SemaphoreType.DMA((6,)),
            pltpu.SemaphoreType.DMA((6,)),
            pltpu.SemaphoreType.DMA((1,)),
        ]

    def peers(self):
        row, across, core, plane = neighbours()
        found = dict(across=dict(row=across), core=dict(row=core))
        for slot in (1, 2, 4, 6):
            found[SLOTS[slot]] = slot_device(slot)
        return found

    def phase(self, number, src, out, mine, other, send, recv, local):
        row, across, core, plane = neighbours()
        hops = [[dict(row=core)], [dict(row=across)], [dict(dp=plane)]]
        hops.append([slot_device(2 * b) for b in (1, 2, 3)])

        def copies(hop):
            return [
                remote(mine.at[hop], other.at[hop + i], send, recv, hop + i, **device)
                for i, device in enumerate(hops[hop])
            ]

        if number == 0:
            load = Within(src, mine.at[0], local.at[0])
            load.start()
            load.wait()
        else:
            value = mine[number - 1].astype(F32)
            for i, copy in enumerate(copies(number - 1)):
                copy.wait_recv()
                value = value + other[number - 1 + i].astype(F32)
            if number < 4:
                mine[number] = value.astype(LOW)
            else:
                out[...] = value
        if number < 4:
            for copy in copies(number):
                copy.start()
        else:
            for hop in range(4):
                for copy in copies(hop):
                    copy.wait_send()


def greet(flows):
    barrier = pltpu.get_barrier_semaphore()
    devices = {}
    for flow in flows:
        devices.update(flow.peers())
    for device in devices.values():
        pl.semaphore_signal(barrier, inc=1, device_id=device, device_id_type=MESH)
    pl.semaphore_wait(barrier, len(devices))


LATE = 99


def layer(flow, index):
    flow.view = lambda ref: ref.at[index]
    return flow


def carry(body, moves, grid, in_specs, out_specs, out_shape, scratch_shapes, mib, name, after=None):
    inputs, outputs, extras = len(in_specs), len(out_specs), len(scratch_shapes)
    steps = grid[0]
    hbm = pl.BlockSpec(memory_space=pl.ANY)
    flows = [flow for flow, _ in moves]
    given = [flow for flow in flows if flow.take is None]
    shared = [flow for flow in flows if getattr(flow, "into", None) is not None]
    kept = [flow for flow in flows if getattr(flow, "keep", False)]
    shown = [flow for flow in flows if flow not in shared and flow not in kept]

    def kernel(*refs):
        refs = list(refs)
        take = lambda count: [refs.pop(0) for _ in range(count)]
        own_in = take(inputs)
        sources = {flow: refs.pop(0) for flow in given}
        own_out = take(outputs)
        results = {flow: refs.pop(0) for flow in shown}
        own_extra = take(extras)
        packs = {}
        for flow in flows:
            if flow in kept:
                results[flow] = refs.pop(0)
            elif flow in shared:
                results[flow] = results[flow.into]
            if flow not in sources:
                sources[flow] = flow.take(own_out, own_extra)
            source_of = getattr(flow, "view", None)
            if source_of is not None:
                sources[flow] = source_of(sources[flow])
            packs[flow] = [sources[flow], results[flow]] + take(len(flow.scratch))
        step = pl.program_id(0)

        def run(low, high):
            plan = []
            for index, (flow, marks) in enumerate(moves):
                for number in range(flow.phases):
                    if low <= marks[number] < high:
                        call = functools.partial(flow.phase, number, *packs[flow])
                        plan.append((marks[number], number, index, call))
            if after is not None and low <= after[0] < high:
                call = functools.partial(
                    after[1], own_in, own_out, own_extra, [results[flow] for flow in flows]
                )
                plan.append((after[0], 0, len(moves), call))
            for entry in sorted(plan, key=lambda entry: entry[:3]):
                entry[3]()

        for mark in range(steps):
            if mark == 0 or any(mark <= at < mark + 1 for _, marks in moves for at in marks):

                @pl.when(step == mark)
                def _():
                    if mark == 0:
                        greet(flows)
                    run(mark, mark + 1)

        if body is not None:
            body(*own_in, *own_out, *own_extra)

        @pl.when(step == steps - 1)
        def _():
            run(LATE - 1, LATE + 100)

    scratch = list(scratch_shapes)
    for flow in flows:
        if flow in kept:
            scratch.append(pltpu.VMEM(flow.result.shape, flow.result.dtype))
        scratch += flow.scratch

    def call(*args):
        return pl.pallas_call(
            kernel,
            grid=grid,
            out_shape=tuple(out_shape) + tuple(flow.result for flow in shown),
            in_specs=list(in_specs) + [hbm] * len(given),
            out_specs=tuple(out_specs) + tuple(flow.spec for flow in shown),
            scratch_shapes=scratch,
            compiler_params=pltpu.CompilerParams(
                vmem_limit_bytes=mib * MIB,
                dimension_semantics=("arbitrary",),
                collective_id=name,
                has_side_effects=True,
            ),
        )(*args)

    return call


def bias_table(buckets, rel):
    place = jnp.arange(WRAP, dtype=jnp.int32)
    dist = jnp.where(place <= PLEN, PLEN - place, PLEN + WRAP - place)
    read = (place <= PLEN) | (place > KEYS)
    index = jnp.take(buckets, jnp.clip(dist, 0, KEYS - 1), axis=0)
    hot = ((index[:, None] == jnp.arange(BUCKETS)[None, :]) & read[:, None]).astype(LOW)
    floor = jnp.where(read, 0.0, NEG).astype(F32)
    return hot, floor


def fill_strip(strip, table, head):
    @pl.when(pl.program_id(0) == 0)
    def _():
        strip[:, KEYS:] = jnp.full((128, STRIP - KEYS), NEG, F32)

    line = jnp.broadcast_to(table[pl.ds(head, 1), :], (128, WRAP))
    strip[:, :KEYS] = pltpu.roll(line, 0, 1, stride=1, stride_axis=0)[:, :KEYS]


def tiles_of(pslice):
    places = []
    for tile in range(pslice // 128):
        start = PLEN - (lax.axis_index("row") * pslice + tile * 128)
        places.append((tile * 128, pl.ds(pl.multiple_of(start, 128), PLEN), PLEN))
    places.append((pslice, pl.ds(0, KEYS), KEYS))
    return places


def attend_kernel(pslice, query, keys, values, table, mixed, total, strip, raw, weights):
    pair = pl.program_id(0)
    lane = lax.broadcasted_iota(jnp.int32, (1, 128), 1)

    @pl.when(pair == 0)
    def _():
        weights[:pslice, PLEN:] = jnp.zeros((pslice, CLEN), LOW)

    for half in range(2):
        mine = (lane < HDIM) if half == 0 else (lane >= HDIM)
        fill_strip(strip, table, 2 * pair + half)
        part = jnp.where(mine, query[...], 0) * HDIM ** (-0.5)
        raw[...] = dot_back(part.astype(LOW), keys[...])
        for row, place, count in tiles_of(pslice):
            rows = pl.ds(row, 128)
            scores = raw[rows, :count] + strip[:, place]
            top = jnp.max(scores, -1, keepdims=True)
            raised = jnp.exp(scores - top)
            summed = jnp.sum(raised, -1, keepdims=True)
            weights[rows, :count] = (raised * (1.0 / summed)).astype(LOW)
            log_total = jnp.broadcast_to(top + jnp.log(summed), (128, 128))
            if half == 0:
                total[rows, :] = log_total
            else:
                total[rows, :] = jnp.where(mine, log_total, total[rows, :])
        result = dot_low(weights[...], values[...]).astype(LOW)
        if half == 0:
            mixed[...] = result
        else:
            mixed[...] = jnp.where(mine, result, mixed[...])


def attend_forward(query, keys, values, table):
    tokens = query.shape[0]
    pslice = tokens - CLEN
    block = lambda rows: pl.BlockSpec((rows, 128), lambda i: (0, i))
    return pl.pallas_call(
        functools.partial(attend_kernel, pslice),
        grid=(HEADS // 2,),
        out_shape=(
            jax.ShapeDtypeStruct((tokens, D), LOW),
            jax.ShapeDtypeStruct((tokens, D), F32),
        ),
        in_specs=[block(tokens), block(KEYS), block(KEYS), whole(table.shape)],
        out_specs=(block(tokens), block(tokens)),
        scratch_shapes=[
            pltpu.VMEM((128, STRIP), F32),
            pltpu.VMEM((tokens, KEYS), F32),
            pltpu.VMEM((tokens, KEYS), LOW),
        ],
        compiler_params=params(32),
    )(query, keys, values, table)


def attend_back_kernel(
    pslice,
    query,
    keys,
    values,
    table,
    total,
    grad_mixed,
    grad_query,
    grad_keys,
    grad_values,
    grad_table,
    strip,
    raw,
    pulled,
    probs,
    grads,
    folded,
    sum_keys,
    sum_values,
):
    pair = pl.program_id(0)
    lane = lax.broadcasted_iota(jnp.int32, (1, 128), 1)
    across = lax.broadcasted_iota(jnp.int32, (128, 128), 0)
    along = lax.broadcasted_iota(jnp.int32, (128, 128), 1)
    mirror = (across + along == 127).astype(LOW)

    @pl.when(pair == 0)
    def _():
        probs[:pslice, PLEN:] = jnp.zeros((pslice, CLEN), LOW)
        grads[:pslice, PLEN:] = jnp.zeros((pslice, CLEN), LOW)

    for half in range(2):
        mine = (lane < HDIM) if half == 0 else (lane >= HDIM)
        fill_strip(strip, table, 2 * pair + half)
        part = (jnp.where(mine, query[...], 0) * HDIM ** (-0.5)).astype(LOW)
        upstream = jnp.where(mine, grad_mixed[...], 0).astype(LOW)
        raw[...] = dot_back(part, keys[...])
        pulled[...] = dot_back(upstream, values[...])
        folded[...] = jnp.zeros_like(folded)
        for row, place, count in tiles_of(pslice):
            rows = pl.ds(row, 128)
            log_total = total[rows, half * HDIM : half * HDIM + 1]
            chance = jnp.exp(raw[rows, :count] + strip[:, place] - log_total)
            product = chance * pulled[rows, :count]
            centre = jnp.sum(product, -1, keepdims=True)
            slope = (product - chance * centre).astype(LOW)
            probs[rows, :count] = chance.astype(LOW)
            grads[rows, :count] = slope
            folded[:, place] += dot_low(mirror, slope)
        result = dot_low(grads[...], keys[...]) * HDIM ** (-0.5)
        if half == 0:
            grad_query[...] = result.astype(LOW)
            sum_keys[...] = dot_over(part, grads[...])
            sum_values[...] = dot_over(upstream, probs[...])
        else:
            grad_query[...] = jnp.where(mine, result.astype(LOW), grad_query[...])
            sum_keys[...] += dot_over(part, grads[...])
            sum_values[...] += dot_over(upstream, probs[...])
        turned = pltpu.roll(folded[:, :WRAP], WRAP - 127, 1, stride=1, stride_axis=0)
        grad_table[pl.ds(2 * pair + half, 1), :] = jnp.sum(turned, 0, keepdims=True)
    grad_keys[...] = sum_keys[...].T.astype(LOW)
    grad_values[...] = sum_values[...].T.astype(LOW)


def attend_backward(query, keys, values, table, total, grad_mixed):
    tokens = query.shape[0]
    pslice = tokens - CLEN
    block = lambda rows: pl.BlockSpec((rows, 128), lambda i: (0, i))
    return pl.pallas_call(
        functools.partial(attend_back_kernel, pslice),
        grid=(HEADS // 2,),
        out_shape=(
            jax.ShapeDtypeStruct((tokens, D), LOW),
            jax.ShapeDtypeStruct((KEYS, D), LOW),
            jax.ShapeDtypeStruct((KEYS, D), LOW),
            jax.ShapeDtypeStruct(table.shape, F32),
        ),
        in_specs=[
            block(tokens),
            block(KEYS),
            block(KEYS),
            whole(table.shape),
            block(tokens),
            block(tokens),
        ],
        out_specs=(block(tokens), block(KEYS), block(KEYS), whole(table.shape)),
        scratch_shapes=[
            pltpu.VMEM((128, STRIP), F32),
            pltpu.VMEM((tokens, KEYS), F32),
            pltpu.VMEM((tokens, KEYS), F32),
            pltpu.VMEM((tokens, KEYS), LOW),
            pltpu.VMEM((tokens, KEYS), LOW),
            pltpu.VMEM((128, STRIP), F32),
            pltpu.VMEM((128, KEYS), F32),
            pltpu.VMEM((128, KEYS), F32),
        ],
        compiler_params=params(32),
    )(query, keys, values, table, total, grad_mixed)


def mlp_forward_kernel(state, gain, first, second, result, normed):
    step = pl.program_id(0)

    @pl.when(step == 0)
    def _():
        normed[...] = norm_rows(state[...], gain[...]).astype(LOW)
        result[...] = state[...]

    active = gelu(dot_low(normed[...], first[...])).astype(LOW)
    result[...] += dot_low(active, second[...])


def mlp_forward(state, gain, first, second):
    tokens = state.shape[0]
    part = 768
    return pl.pallas_call(
        mlp_forward_kernel,
        grid=(FF // part,),
        out_shape=(
            jax.ShapeDtypeStruct((tokens, D), F32),
            jax.ShapeDtypeStruct((tokens, D), LOW),
        ),
        in_specs=[
            whole((tokens, D)),
            whole((1, D)),
            pl.BlockSpec((D, part), lambda i: (0, i)),
            pl.BlockSpec((part, D), lambda i: (i, 0)),
        ],
        out_specs=(whole((tokens, D)), whole((tokens, D))),
        compiler_params=params(32),
    )(state, gain, first, second)


def mlp_backward_kernel(
    grad_next, state, normed, gain, first, second, result, grad_gain, grad_first, grad_second, low, total
):
    step = pl.program_id(0)

    @pl.when(step == 0)
    def _():
        low[...] = grad_next[...].astype(LOW)
        total[...] = jnp.zeros_like(total)

    active, slope = gelu_parts(dot_low(normed[...], first[...]))
    grad_hidden = (slope * dot_back(low[...], second[...])).astype(LOW)
    grad_second[...] = dot_over(active.astype(LOW), low[...]).astype(LOW)
    grad_first[...] = dot_over(normed[...], grad_hidden).astype(LOW)
    total[...] += dot_back(grad_hidden, first[...])

    @pl.when(step == pl.num_programs(0) - 1)
    def _():
        grad_state, grad_line = norm_back(state[...], gain[...], total[...])
        result[...] = grad_next[...] + grad_state
        grad_gain[...] = grad_line


def mlp_backward(grad_next, state, normed, gain, first, second):
    tokens = state.shape[0]
    part = 768
    return pl.pallas_call(
        mlp_backward_kernel,
        grid=(FF // part,),
        out_shape=(
            jax.ShapeDtypeStruct((tokens, D), F32),
            jax.ShapeDtypeStruct((1, D), F32),
            jax.ShapeDtypeStruct((D, FF), LOW),
            jax.ShapeDtypeStruct((FF, D), LOW),
        ),
        in_specs=[
            whole((tokens, D)),
            whole((tokens, D)),
            whole((tokens, D)),
            whole((1, D)),
            pl.BlockSpec((D, part), lambda i: (0, i)),
            pl.BlockSpec((part, D), lambda i: (i, 0)),
        ],
        out_specs=(
            whole((tokens, D)),
            whole((1, D)),
            pl.BlockSpec((D, part), lambda i: (0, i)),
            pl.BlockSpec((part, D), lambda i: (i, 0)),
        ),
        scratch_shapes=[pltpu.VMEM((tokens, D), LOW), pltpu.VMEM((tokens, D), F32)],
        compiler_params=params(48),
    )(grad_next, state, normed, gain, first, second)


def expert_kernel(
    rows, cotangent, gate, first, second, result, grad_rows, grad_gate, grad_first, grad_second, upstream, total, back
):
    step = pl.program_id(0)

    @pl.when(step == 0)
    def _():
        upstream[...] = (gate[:, :1] * cotangent[...].astype(F32)).astype(LOW)
        total[...] = jnp.zeros_like(total)
        back[...] = jnp.zeros_like(back)

    active, slope = gelu_parts(dot_low(rows[...], first[...]))
    active = active.astype(LOW)
    total[...] += dot_low(active, second[...])
    grad_hidden = (slope * dot_back(upstream[...], second[...])).astype(LOW)
    grad_second[...] = dot_over(active, upstream[...]).astype(LOW)
    grad_first[...] = dot_over(rows[...], grad_hidden).astype(LOW)
    back[...] += dot_back(grad_hidden, first[...])

    @pl.when(step == pl.num_programs(0) - 1)
    def _():
        low = total[...].astype(LOW)
        result[...] = low
        grad_rows[...] = back[...].astype(LOW)
        reach = jnp.sum(cotangent[...].astype(F32) * low.astype(F32), -1, keepdims=True)
        grad_gate[...] = jnp.broadcast_to(reach, grad_gate.shape)


def expert_pass(rows, cotangent, gate, first, second):
    count = rows.shape[0]
    shards, _, width = first.shape
    part = 256
    split = width // part
    inner = pl.BlockSpec((None, D, part), lambda i: (i // split, 0, i % split))
    outer = pl.BlockSpec((None, part, D), lambda i: (i // split, i % split, 0))
    return pl.pallas_call(
        expert_kernel,
        grid=(shards * split,),
        out_shape=(
            jax.ShapeDtypeStruct((count, D), LOW),
            jax.ShapeDtypeStruct((count, D), LOW),
            jax.ShapeDtypeStruct((count, 128), F32),
            jax.ShapeDtypeStruct(first.shape, LOW),
            jax.ShapeDtypeStruct(second.shape, LOW),
        ),
        in_specs=[whole((count, D)), whole((count, D)), whole((count, 128)), inner, outer],
        out_specs=(whole((count, D)), whole((count, D)), whole((count, 128)), inner, outer),
        scratch_shapes=[
            pltpu.VMEM((count, D), LOW),
            pltpu.VMEM((count, D), F32),
            pltpu.VMEM((count, D), F32),
        ],
        compiler_params=params(56),
    )(rows, cotangent, gate, first, second)


def split_low(values):
    high = values.astype(LOW)
    rest = values - high.astype(F32)
    middle = rest.astype(LOW)
    return high, middle, (rest - middle.astype(F32)).astype(LOW)


def exchange(block):
    return lax.all_to_all(block, ("dp", "col"), split_axis=0, concat_axis=0, tiled=True)


def attention_forward(state, gain, others, weight_in, weight_out, table, raw_others):
    tokens = state.shape[0]
    pslice = tokens - CLEN
    normed = norm_rows(state, gain).astype(LOW)
    if others is None:
        shared = lax.all_gather(normed[:pslice], "row", axis=0, tiled=True)
    else:
        shared = norm_rows(others.astype(F32), gain).astype(LOW)
    read = jnp.concatenate([shared, normed[pslice:]], 0)
    query = dot_low(normed, weight_in[:, :D]).astype(LOW)
    keys = dot_low(read, weight_in[:, D : 2 * D]).astype(LOW)
    values = dot_low(read, weight_in[:, 2 * D :]).astype(LOW)
    mixed, total = attend_forward(query, keys, values, table)
    return state + dot_low(mixed, weight_out), (state, normed, read, query, keys, values, mixed, total)


def attention_backward(grad_next, stash, gain, weight_in, weight_out, table, hot):
    state, normed, read, query, keys, values, mixed, total = stash
    pslice = state.shape[0] - CLEN
    branch = grad_next.astype(LOW)
    grad_out = dot_over(mixed, branch).astype(LOW)
    grad_mixed = dot_back(branch, weight_out).astype(LOW)
    grad_query, grad_keys, grad_values, grad_table = attend_backward(
        query, keys, values, table, total, grad_mixed
    )
    grad_in = jnp.concatenate(
        [dot_over(normed, grad_query), dot_over(read, grad_keys), dot_over(read, grad_values)], 1
    ).astype(LOW)
    grad_read = dot_back(grad_keys, weight_in[:, D : 2 * D]) + dot_back(
        grad_values, weight_in[:, 2 * D :]
    )
    own = lax.psum_scatter(
        grad_read[:PLEN].astype(LOW), "row", scatter_dimension=0, tiled=True
    ).astype(F32)
    grad_normed = dot_back(grad_query, weight_in[:, :D]) + jnp.concatenate(
        [own, grad_read[PLEN:]], 0
    )
    grad_state, grad_gain = norm_back(state, gain, grad_normed)
    grad_rel = jnp.dot(grad_table[:HEADS], hot.astype(F32), precision=HIGH).T
    return grad_next + grad_state, grad_in, grad_out, grad_rel, grad_gain


def general(
    inputs,
    cotangent,
    routes,
    buckets,
    norm_gains,
    attn_qkv,
    attn_out,
    rel_bias,
    mlp_in,
    mlp_out,
    router,
    expert_in,
    expert_out,
):
    grid = ("row", "col")
    places = lax.axis_size(grid)
    experts = lax.axis_size(("dp", "col"))
    tokens = inputs.shape[1]
    pslice = tokens - CLEN
    capacity = max(2, 3 * tokens // experts)

    small = [norm_gains.reshape(-1), rel_bias.reshape(-1), router.reshape(-1)]
    cuts = [part.shape[0] for part in small]
    packed = jnp.concatenate(small)
    packed = jnp.pad(packed, (0, -packed.shape[0] % 1024)).reshape(-1, 128)
    packed = lax.all_gather(packed, grid, axis=0, tiled=False).reshape(places, -1)
    gains = packed[:, : cuts[0]].reshape(places, 4, -1).transpose(1, 0, 2).reshape(4, 1, D).astype(F32)
    rel = packed[:, cuts[0] : cuts[0] + cuts[1]].reshape(places, 2, -1, HEADS)
    rel = rel.transpose(1, 0, 2, 3).reshape(2, BUCKETS, HEADS)
    route_w = packed[:, cuts[0] + cuts[1] : sum(cuts)].reshape(D, experts)

    qkv = [lax.all_gather(attn_qkv[i], grid, axis=0, tiled=True) for i in range(2)]
    out = [lax.all_gather(attn_out[i], grid, axis=0, tiled=True) for i in range(2)]
    dense_in = lax.all_gather(mlp_in, grid, axis=0, tiled=True)
    dense_out = lax.all_gather(mlp_out, grid, axis=0, tiled=True)
    first = lax.all_gather(expert_in[0], "row", axis=0, tiled=False)
    second = lax.all_gather(expert_out[0], "row", axis=0, tiled=False)

    hot, floor = bias_table(buckets, rel)
    tables = [
        jnp.pad(dot_low(rel[i].T, hot.T) + floor[None], ((0, 16 - HEADS), (0, 0))) for i in range(2)
    ]

    flat = routes[0].reshape(-1)
    levels = jnp.arange(experts, dtype=jnp.int32)
    choose = (routes[0][:, :, None] == levels[None, None, :]).astype(F32)
    hits = (flat[:, None] == levels[None, :]).astype(LOW)
    before = jnp.arange(2 * tokens)
    before = (before[:, None] > before[None, :]).astype(LOW)
    rank = jnp.sum(dot_low(before, hits) * hits.astype(F32), 1).astype(jnp.int32)
    place = (flat * capacity + rank).reshape(tokens, 2)
    slots = jnp.arange(experts * capacity, dtype=jnp.int32)
    picks = [(place[:, k][:, None] == slots[None, :]).astype(LOW) for k in range(2)]
    both = picks[0] + picks[1]
    sent_cotangent = dot_over(both, cotangent[0]).astype(LOW).reshape(experts, capacity, D)
    far_cotangent = exchange(sent_cotangent).reshape(experts * capacity, D)

    state0 = inputs[0].astype(F32)
    shared0 = lax.all_gather(inputs[0, :pslice], "row", axis=0, tiled=True)
    state1, stash1 = attention_forward(state0, gains[0], shared0, qkv[0], out[0], tables[0], None)
    state2, normed1 = mlp_forward(state1, gains[1], dense_in, dense_out)
    state3, stash3 = attention_forward(state2, gains[2], None, qkv[1], out[1], tables[1], None)

    normed3 = norm_rows(state3, gains[3]).astype(LOW)
    logits = dot_low(normed3, route_w)
    picked = jnp.sum(choose * logits[:, None, :], -1)
    raised = jnp.exp(picked - jnp.max(picked, -1, keepdims=True))
    gates = raised / jnp.sum(raised, -1, keepdims=True)
    parts = [split_low(gates[:, k]) for k in range(2)]
    spread = [
        dot_over(picks[k], jnp.pad(jnp.stack(parts[k], 1), ((0, 0), (0, 125)))) for k in range(2)
    ]
    sent = jnp.concatenate([dot_over(both, normed3), spread[0] + spread[1]], 1).astype(LOW)
    received = exchange(sent.reshape(experts, capacity, D + 128)).reshape(experts * capacity, D + 128)
    far_gate = jnp.sum(received[:, D : D + 3].astype(F32), 1, keepdims=True)
    far_gate = jnp.broadcast_to(far_gate, (experts * capacity, 128))
    result, grad_rows, grad_gate, grad_first, grad_second = expert_pass(
        received[:, :D], far_cotangent, far_gate, first, second
    )
    reach = jnp.pad(jnp.stack(split_low(grad_gate[:, 0]), 1), ((0, 0), (0, 125)))
    returned = exchange(
        jnp.concatenate([grad_rows, reach], 1).reshape(experts, capacity, D + 128)
    ).reshape(experts * capacity, D + 128)
    outcome = exchange(result.reshape(experts, capacity, D)).reshape(experts * capacity, D)
    output = state3 + sum(gates[:, k : k + 1] * dot_low(picks[k], outcome) for k in range(2))

    grad_gates = jnp.stack(
        [jnp.sum(dot_low(picks[k], returned[:, D:]), 1) for k in range(2)], 1
    )
    grad_picked = gates * (grad_gates - jnp.sum(gates * grad_gates, -1, keepdims=True))
    grad_logits = jnp.sum(choose * grad_picked[:, :, None], 1).astype(LOW)
    grad_route = dot_over(normed3, grad_logits)
    grad_normed3 = dot_low(both, returned[:, :D]) + dot_back(grad_logits, route_w)
    upstream = cotangent[0].astype(F32)
    grad_state3, gain_last = norm_back(state3, gains[3], grad_normed3)
    grad3 = upstream + grad_state3
    own_first = lax.psum_scatter(grad_first, "row", scatter_dimension=0, tiled=False)
    own_second = lax.psum_scatter(grad_second, "row", scatter_dimension=0, tiled=False)

    grad2, qkv_late, out_late, rel_late, gain_third = attention_backward(
        grad3, stash3, gains[2], qkv[1], out[1], tables[1], hot
    )
    grad1, gain_second, dense_grad_in, dense_grad_out = mlp_backward(
        grad2, state1, normed1, gains[1], dense_in, dense_out
    )
    grad0, qkv_early, out_early, rel_early, gain_first = attention_backward(
        grad1, stash1, gains[0], qkv[0], out[0], tables[0], hot
    )

    def share(block):
        block = lax.psum_scatter(block.astype(LOW), grid, scatter_dimension=0, tiled=True)
        return lax.psum(block, "dp").astype(F32)

    gain_grads = jnp.concatenate([gain_first, gain_second, gain_third, gain_last], 0)
    gain_grads = gain_grads.reshape(4, places, -1).transpose(1, 0, 2).reshape(places, -1)
    rel_grads = jnp.stack([rel_early, rel_late]).reshape(2, places, -1, HEADS)
    rel_grads = rel_grads.transpose(1, 0, 2, 3).reshape(places, -1)
    packed = jnp.concatenate([gain_grads, rel_grads, grad_route.reshape(places, -1)], 1)
    packed = jnp.pad(packed, ((0, 0), (0, -packed.shape[1] % 1024))).reshape(-1, 128)
    packed = share(packed).reshape(-1)
    gain_share = packed[: cuts[0]].reshape(4, -1)
    rel_share = packed[cuts[0] : cuts[0] + cuts[1]].reshape(2, -1, HEADS)
    route_share = packed[cuts[0] + cuts[1] : sum(cuts)].reshape(-1, experts)
    return (
        output[None],
        grad0[None],
        gain_share,
        jnp.stack([share(qkv_early), share(qkv_late)]),
        jnp.stack([share(out_early), share(out_late)]),
        rel_share,
        share(dense_grad_in),
        share(dense_grad_out),
        route_share,
        own_first.astype(F32)[None],
        own_second.astype(F32)[None],
    )


def once(shape):
    return pl.BlockSpec(shape, lambda *_: (0,) * len(shape), pipeline_mode=pl.Buffered(1))


def head_block(cols, piece, index):
    return pl.BlockSpec((4, cols, piece, 128), lambda i: (0, 0, 0, 6 * index + i))


def outer_block(cols, piece):
    return once((4, cols, piece, D))


def line_block(index, shape):
    return pl.BlockSpec(
        (None,) + shape, lambda i: (index,) + (0,) * len(shape), pipeline_mode=pl.Buffered(1)
    )


def up_kernel(
    raw_rows,
    pslice,
    state,
    own,
    shared,
    gain,
    table,
    wq,
    wk,
    wv,
    wo,
    result,
    normed,
    read,
    query,
    keys,
    values,
    mixed,
    total,
    strip,
    raw,
    weights,
    outer,
):
    pair = pl.program_id(0)
    lane = lax.broadcasted_iota(jnp.int32, (1, 128), 1)

    @pl.when(pair == 0)
    def _():
        weights[:pslice, PLEN:] = jnp.zeros((pslice, CLEN), LOW)
        outer[...] = wo[...].reshape(D, D)
        result[...] = state[...].astype(F32)
        if raw_rows:
            normed[...] = norm_rows(own[...].astype(F32), gain[...]).astype(LOW)
            for i in range(PLEN // pslice):
                rows = pl.ds(i * pslice, pslice)
                read[rows, :] = norm_rows(shared[i].astype(F32), gain[...]).astype(LOW)
        else:
            normed[...] = own[...]
            for i in range(PLEN // pslice):
                read[pl.ds(i * pslice, pslice), :] = shared[i]
        read[PLEN:, :] = normed[pslice:, :]

    query[...] = dot_low(normed[...], wq[...].reshape(D, 128)).astype(LOW)
    both = jnp.concatenate([wk[...].reshape(D, 128), wv[...].reshape(D, 128)], 1)
    both = dot_low(read[...], both).astype(LOW)
    keys[...] = both[:, :128]
    values[...] = both[:, 128:]

    for half in range(2):
        mine = (lane < HDIM) if half == 0 else (lane >= HDIM)
        fill_strip(strip, table, 2 * pair + half)
        part = jnp.where(mine, query[...], 0) * HDIM ** (-0.5)
        raw[...] = dot_back(part.astype(LOW), keys[...])
        for row, place, count in tiles_of(pslice):
            rows = pl.ds(row, 128)
            scores = raw[rows, :count] + strip[:, place]
            top = jnp.max(scores, -1, keepdims=True)
            raised = jnp.exp(scores - top)
            summed = jnp.sum(raised, -1, keepdims=True)
            weights[rows, :count] = (raised * (1.0 / summed)).astype(LOW)
            log_total = jnp.broadcast_to(top + jnp.log(summed), (128, 128))
            if half == 0:
                total[rows, :] = log_total
            else:
                total[rows, :] = jnp.where(mine, log_total, total[rows, :])
        part = dot_low(weights[...], values[...]).astype(LOW)
        if half == 0:
            mixed[...] = part
        else:
            mixed[...] = jnp.where(mine, part, mixed[...])
    result[...] += dot_low(mixed[...], outer[pl.ds(pl.multiple_of(pair * 128, 128), 128), :])


def attention_up(state, own, shared, layer_index, gains, tables, inner, output, moves, sources, name):
    tokens = own.shape[0]
    pslice = tokens - CLEN
    _, cols, piece, _ = inner.shape
    raw_rows = layer_index == 0
    block = lambda rows: pl.BlockSpec((rows, 128), lambda i: (0, i))
    low = lambda rows: jax.ShapeDtypeStruct((rows, D), LOW)
    result, normed, read, query, keys, values, mixed, total, *moved = carry(
        functools.partial(up_kernel, raw_rows, pslice),
        moves,
        grid=(HEADS // 2,),
        out_shape=(
            jax.ShapeDtypeStruct((tokens, D), F32),
            low(tokens),
            low(KEYS),
            low(tokens),
            low(KEYS),
            low(KEYS),
            low(tokens),
            jax.ShapeDtypeStruct((tokens, D), F32),
        ),
        in_specs=[
            once((tokens, D)),
            once((tokens, D)),
            once(shared.shape),
            line_block(2 * layer_index, (1, D)),
            line_block(layer_index, tables.shape[1:]),
            head_block(cols, piece, 0),
            head_block(cols, piece, 1),
            head_block(cols, piece, 2),
            outer_block(cols, piece),
        ],
        out_specs=(
            whole((tokens, D)),
            whole((tokens, D)),
            whole((KEYS, D)),
            block(tokens),
            block(KEYS),
            block(KEYS),
            block(tokens),
            block(tokens),
        ),
        scratch_shapes=[
            pltpu.VMEM((128, STRIP), F32),
            pltpu.VMEM((tokens, KEYS), F32),
            pltpu.VMEM((tokens, KEYS), LOW),
            pltpu.VMEM((D, D), LOW),
        ],
        mib=60,
        name=name,
    )(state, own, shared, gains, tables, inner, inner, inner, output, *sources)
    return result, (normed, read, query, keys, values, mixed, total, inner, output), moved


def slide_sum(grid):
    rows = grid.shape[0]
    while rows > 8:
        rows = rows // 2
        grid = grid[:rows] + pltpu.roll(grid[rows:], WRAP - rows, 1)
    for step in (4, 2, 1):
        grid = grid + pltpu.roll(pltpu.roll(grid, 8 - step, 0), WRAP - step, 1)
    return grid[:1]


def down_kernel(
    pslice,
    grad_next,
    state,
    gain,
    normed,
    read,
    query,
    keys,
    values,
    mixed,
    total,
    table,
    wq,
    wk,
    wv,
    wo,
    result,
    grad_gain,
    grads,
    grad_table,
    low,
    outer,
    grad_outer,
    sum_own,
    sum_read,
    spill,
    strip,
    raw,
    pulled,
    probs,
    slopes,
    folded,
    sum_keys,
    sum_values,
):
    pair = pl.program_id(0)
    lane = lax.broadcasted_iota(jnp.int32, (1, 128), 1)
    here = pl.ds(pl.multiple_of(pair * 128, 128), 128)

    @pl.when(pair == 0)
    def _():
        probs[:pslice, PLEN:] = jnp.zeros((pslice, CLEN), LOW)
        slopes[:pslice, PLEN:] = jnp.zeros((pslice, CLEN), LOW)
        low[...] = grad_next[...].astype(LOW)
        outer[...] = wo[...].reshape(D, D)
        sum_own[...] = jnp.zeros_like(sum_own)
        sum_read[...] = jnp.zeros_like(sum_read)

    grad_outer[here, :] = dot_over(mixed[...], low[...]).astype(LOW)
    grad_mixed = dot_back(low[...], outer[here, :]).astype(LOW)
    for half in range(2):
        mine = (lane < HDIM) if half == 0 else (lane >= HDIM)
        fill_strip(strip, table, 2 * pair + half)
        part = (jnp.where(mine, query[...], 0) * HDIM ** (-0.5)).astype(LOW)
        upstream = jnp.where(mine, grad_mixed, 0).astype(LOW)
        raw[...] = dot_back(part, keys[...])
        pulled[...] = dot_back(upstream, values[...])
        folded[...] = jnp.zeros_like(folded)
        for row, place, count in tiles_of(pslice):
            rows = pl.ds(row, 128)
            log_total = total[rows, half * HDIM : half * HDIM + 1]
            chance = jnp.exp(raw[rows, :count] + strip[:, place] - log_total)
            product = chance * pulled[rows, :count]
            centre = jnp.sum(product, -1, keepdims=True)
            slope = (product - chance * centre).astype(LOW)
            probs[rows, :count] = chance.astype(LOW)
            slopes[rows, :count] = slope
            folded[:, place] += slope.astype(F32)
        step = (dot_low(slopes[...], keys[...]) * HDIM ** (-0.5)).astype(LOW)
        if half == 0:
            grad_query = step
            sum_keys[...] = dot_over(part, slopes[...])
            sum_values[...] = dot_over(upstream, probs[...])
        else:
            grad_query = jnp.where(mine, step, grad_query)
            sum_keys[...] += dot_over(part, slopes[...])
            sum_values[...] += dot_over(upstream, probs[...])
        grad_table[pl.ds(2 * pair + half, 1), :] = slide_sum(folded[:, :WRAP])

    shape = grads.shape[:2] + grads.shape[3:4] + (128,)

    def keep(index, turned):
        grads[:, :, index, :, here] = turned.T.astype(LOW).reshape(shape)

    keep(0, dot_over(grad_query, normed[...]))
    keep(1, dot_low(sum_keys[...].astype(LOW), read[...]))
    keep(2, dot_low(sum_values[...].astype(LOW), read[...]))
    sum_own[...] += dot_back(grad_query, wq[...].reshape(D, 128))
    pairs = jnp.concatenate([sum_keys[...].T, sum_values[...].T], 1).astype(LOW)
    both = jnp.concatenate([wk[...].reshape(D, 128), wv[...].reshape(D, 128)], 1)
    sum_read[...] += dot_back(pairs, both)

    @pl.when(pair == pl.num_programs(0) - 1)
    def _():
        grads[:, :, 3] = grad_outer[...].reshape(shape[:3] + (D,))
        spill[...] = sum_read[:PLEN, :].astype(LOW).reshape(spill.shape)


def down_after(pslice, fill, own_in, own_out, extras, results):
    grad_next, state, gain = own_in[:3]
    result, grad_gain = own_out[:2]
    sum_own, sum_read = extras[3:5]
    shift = (pl.program_id(0) - (pl.num_programs(0) - 1)) * 8
    lines = 0.0
    for row, count in ((0, pslice), (pslice, CLEN)):
        rows = pl.ds(pl.multiple_of(row + shift, 8), count)
        if row == 0:
            more = results[0][...].reshape(pslice, D)
        else:
            more = sum_read[pl.ds(pl.multiple_of(PLEN + shift, 8), CLEN), :]
        grad_state, line = norm_back(state[rows, :].astype(F32), gain[...], sum_own[rows, :] + more)
        result[rows, :] = grad_next[rows, :] + grad_state
        lines = lines + line
    grad_gain[...] = lines
    if fill:
        first = lax.broadcasted_iota(jnp.int32, (16, 1), 0) == 0
        extras[-1][...] = jnp.where(first, lines, 0.0).astype(LOW)


def attention_down(
    grad_next, state, gains, layer_index, stash, tables, moves, sources, name, known=None
):
    normed, read, query, keys, values, mixed, total, inner, output = stash
    tokens = normed.shape[0]
    pslice = tokens - CLEN
    _, cols, piece, _ = inner.shape
    table = jax.ShapeDtypeStruct(tables.shape[1:], F32)
    block = lambda rows: pl.BlockSpec((rows, 128), lambda i: (0, i))
    rows = Reduce(
        (pslice // 16, 16, D), ("core", "x"), take=lambda outs, extras: extras[5], keep=True
    )
    share = (4, cols, 4, piece, D)
    body, shown, extra = down_kernel, [jax.ShapeDtypeStruct(share, LOW)], []
    more, more_specs = [], []
    last = known is not None
    if last:
        def body(pslice, *refs):
            refs = list(refs)
            known_lines, small = refs.pop(15), refs[-2]
            down_kernel(pslice, *refs[:17], refs[-3], refs[17], *refs[18:-3])

            @pl.when(pl.program_id(0) == pl.num_programs(0) - 1)
            def _():
                small[:16, :] = refs[17][...].astype(LOW)
                small[16:, :] = known_lines[...]

        shown = []
        extra = [
            pltpu.VMEM(share, LOW),
            pltpu.VMEM((16 + known.shape[0], WRAP), LOW),
            pltpu.VMEM((16, D), LOW),
        ]
        more, more_specs = [known], [once(known.shape)]
    return carry(
        functools.partial(body, pslice),
        [(rows, (LATE, LATE + 2, LATE + 4))] + moves,
        grid=(HEADS // 2,),
        out_shape=(
            jax.ShapeDtypeStruct((tokens, D), F32),
            jax.ShapeDtypeStruct((1, D), F32),
            *shown,
            jax.ShapeDtypeStruct(table.shape, F32),
        ),
        in_specs=[
            once((tokens, D)),
            once((tokens, D)),
            line_block(2 * layer_index, (1, D)),
            once((tokens, D)),
            once((KEYS, D)),
            block(tokens),
            block(KEYS),
            block(KEYS),
            block(tokens),
            block(tokens),
            line_block(layer_index, table.shape),
            head_block(cols, piece, 0),
            head_block(cols, piece, 1),
            head_block(cols, piece, 2),
            outer_block(cols, piece),
            *more_specs,
        ],
        out_specs=(
            once((tokens, D)),
            once((1, D)),
            *[once(share) for _ in shown],
            once(table.shape),
        ),
        scratch_shapes=[
            pltpu.VMEM((tokens, D), LOW),
            pltpu.VMEM((D, D), LOW),
            pltpu.VMEM((D, D), LOW),
            pltpu.VMEM((tokens, D), F32),
            pltpu.VMEM((KEYS, D), F32),
            pltpu.VMEM((4, 1, pslice // 16, 16, D), LOW),
            pltpu.VMEM((128, STRIP), F32),
            pltpu.VMEM((tokens, KEYS), F32),
            pltpu.VMEM((tokens, KEYS), F32),
            pltpu.VMEM((tokens, KEYS), LOW),
            pltpu.VMEM((tokens, KEYS), LOW),
            pltpu.VMEM((128, STRIP), F32),
            pltpu.VMEM((128, KEYS), F32),
            pltpu.VMEM((128, KEYS), F32),
            *extra,
        ],
        mib=62,
        name=name,
        after=(LATE + 4.5, functools.partial(down_after, pslice, last)),
    )(
        grad_next,
        state,
        gains,
        normed,
        read,
        query,
        keys,
        values,
        mixed,
        total,
        tables,
        inner,
        inner,
        inner,
        output,
        *more,
        *sources,
    )


def mlp_up_kernel(state, gain, gain_next, first, second, result, normed, normed_next):
    step = pl.program_id(0)

    @pl.when(step == 0)
    def _():
        normed[...] = norm_rows(state[...], gain[...]).astype(LOW)
        result[...] = state[...]

    active = gelu(dot_low(normed[...], first[...].reshape(D, D))).astype(LOW)
    result[...] += dot_low(active, second[...].reshape(D, D))

    @pl.when(step == pl.num_programs(0) - 1)
    def _():
        normed_next[...] = norm_rows(result[...], gain_next[...]).astype(LOW)


def mlp_blocks(cols, piece):
    return (
        pl.BlockSpec((4, cols, piece, D), lambda i: (0, 0, 0, i)),
        pl.BlockSpec((None, cols, 4 * piece, D), lambda i: (i, 0, 0, 0)),
    )


def mlp_up(state, gains, dense_in, dense_out, moves, sources, name):
    tokens = state.shape[0]
    pslice = tokens - CLEN
    _, cols, piece, _ = dense_in.shape
    rows = Rows((pslice, D), take=lambda outs, extras: outs[2].at[pl.ds(0, pslice)])
    return carry(
        mlp_up_kernel,
        [(rows, (LATE,) * 3)] + moves,
        grid=(4,),
        out_shape=(
            jax.ShapeDtypeStruct((tokens, D), F32),
            jax.ShapeDtypeStruct((tokens, D), LOW),
            jax.ShapeDtypeStruct((tokens, D), LOW),
        ),
        in_specs=[
            once((tokens, D)),
            line_block(1, (1, D)),
            line_block(2, (1, D)),
            *mlp_blocks(cols, piece),
        ],
        out_specs=(whole((tokens, D)),) * 3,
        scratch_shapes=[],
        mib=60,
        name=name,
    )(state, gains, gains, dense_in, dense_out, *sources)


def mlp_down_kernel(
    grad_next, state, normed, gain, first, second, result, grad_gain, low, total, grads
):
    step = pl.program_id(0)

    @pl.when(step == 0)
    def _():
        low[...] = grad_next[...].astype(LOW)
        total[...] = jnp.zeros_like(total)

    inner, outer = first[...].reshape(D, D), second[...].reshape(D, D)
    active, slope = gelu_parts(dot_low(normed[...], inner))
    grad_hidden = (slope * dot_back(low[...], outer)).astype(LOW)
    _, cols, _, piece, _ = grads.shape
    grad_second = dot_over(active.astype(LOW), low[...]).astype(LOW)
    grads[step, :, :4] = grad_second.reshape(cols, 4, piece, D)
    grads[:, :, 4 + step] = dot_over(normed[...], grad_hidden).astype(LOW).reshape(4, cols, piece, D)
    total[...] += dot_back(grad_hidden, inner)

    @pl.when(step == pl.num_programs(0) - 1)
    def _():
        grad_state, grad_line = norm_back(state[...], gain[...], total[...])
        result[...] = grad_next[...] + grad_state
        grad_gain[...] = grad_line


def mlp_down(grad_next, state, normed, gains, dense_in, dense_out, moves, sources, name):
    tokens = state.shape[0]
    _, cols, piece, _ = dense_in.shape
    pairs = CoreSum((piece, D), cols, lambda outs, extras: extras[2])
    return carry(
        mlp_down_kernel,
        [(pairs, (0, 1, 2, 3, LATE, LATE + 1))] + moves,
        grid=(4,),
        out_shape=(
            jax.ShapeDtypeStruct((tokens, D), F32),
            jax.ShapeDtypeStruct((1, D), F32),
        ),
        in_specs=[
            once((tokens, D)),
            once((tokens, D)),
            once((tokens, D)),
            line_block(1, (1, D)),
            *mlp_blocks(cols, piece),
        ],
        out_specs=(once((tokens, D)), once((1, D))),
        scratch_shapes=[
            pltpu.VMEM((tokens, D), LOW),
            pltpu.VMEM((tokens, D), F32),
            pltpu.VMEM((4, cols, 8, piece, D), LOW),
        ],
        mib=60,
        name=name,
    )(grad_next, state, normed, gains, dense_in, dense_out, *sources)


def routed_kernel(
    sent,
    sent_gates,
    sent_cotangent,
    first,
    second,
    outcome,
    returned,
    reach,
    grad_first,
    grad_second,
    rows,
    gates,
    cotangent,
    inner,
    outer,
    active_all,
    hidden_all,
    upstream,
    back,
    back_reach,
    turned,
    sum_up,
    sum_down,
    held,
    row_send,
    row_recv,
    gate_send,
    gate_recv,
    back_send,
    back_recv,
    reach_send,
    reach_recv,
    local,
    store,
):
    capacity = rows.shape[1]
    barrier = pltpu.get_barrier_semaphore()
    others = range(1, len(SLOTS))
    for slot in others:
        pl.semaphore_signal(barrier, inc=1, device_id=slot_device(slot), device_id_type=MESH)
    loads = [
        Within(sent.at[0], rows.at[0], local.at[0]),
        Within(sent_gates.at[0], gates.at[0], local.at[1]),
        Within(sent_cotangent, cotangent, local.at[2]),
        Within(first, inner, local.at[3]),
        Within(second, outer, local.at[4]),
    ]
    for load in loads:
        load.start()
    pl.semaphore_wait(barrier, len(others))

    def there(slot):
        device = slot_device(slot)
        return (
            remote(sent_gates.at[slot], gates.at[slot], gate_send, gate_recv, slot, **device),
            remote(sent.at[slot], rows.at[slot], row_send, row_recv, slot, **device),
        )

    def home(slot):
        device = slot_device(slot)
        return (
            remote(back_reach.at[slot], reach.at[slot], reach_send, reach_recv, slot, **device),
            remote(back.at[slot], returned.at[slot], back_send, back_recv, slot, **device),
        )

    own_home = [
        Within(back_reach.at[0], reach.at[0], local.at[5]),
        Within(back.at[0], returned.at[0], local.at[6]),
    ]
    for slot in (4, 5, 1, 6, 7, 2, 3):
        for copy in there(slot):
            copy.start()
    for load in loads:
        load.wait()
    ones = jnp.ones((8, D), F32)
    count = 2 * capacity
    for b in (0, 2, 1, 3):
        for a in range(2):
            slot = 2 * b + a
            if slot:
                for copy in there(slot):
                    copy.wait_recv()
            gate = gates[slot].T[:capacity, :1]
            at = pl.ds(slot * capacity, capacity)
            upstream[at, :] = (gate * cotangent[slot].astype(F32)).astype(LOW)
        both = pl.ds(2 * b * capacity, count)
        block = rows[2 * b : 2 * b + 2].reshape(count, D)
        sum_up[...] = jnp.zeros_like(sum_up)
        sum_down[...] = jnp.zeros_like(sum_down)

        def part(j):
            active, slope = gelu_parts(dot_low(block, inner[j]))
            active = active.astype(LOW)
            active_all[j, both, :] = active
            sum_up[...] += dot_low(active, outer[j])
            hidden = (slope * dot_back(upstream[both, :], outer[j])).astype(LOW)
            hidden_all[j, both, :] = hidden
            sum_down[...] += dot_back(hidden, inner[j])

        each(4, part)
        back[2 * b : 2 * b + 2] = sum_down[...].astype(LOW).reshape(2, capacity, D)
        outcome[2 * b : 2 * b + 2] = sum_up[...].astype(LOW).reshape(2, capacity, D)
        for a in range(2):
            slot = 2 * b + a
            met = cotangent[slot].astype(F32) * outcome[slot].astype(F32)
            line = lax.dot_general(
                ones, met, (((1,), (1,)), ((), ())), precision=HIGH, preferred_element_type=F32
            )
            back_reach[slot] = jnp.pad(line, ((0, 0), (0, back_reach.shape[2] - capacity)))
            if slot:
                for copy in home(slot):
                    copy.start()
            else:
                for copy in own_home:
                    copy.start()
    turned[...] = rows[...].reshape(len(SLOTS) * capacity, D).T

    def stored(j, side):
        return (
            Within(held.at[side, 0], grad_first.at[j], store.at[side, 0]),
            Within(held.at[side, 1], grad_second.at[j], store.at[side, 1]),
        )

    def weigh(j):
        side = lax.rem(j, 2)

        @pl.when(j >= 2)
        def _():
            for copy in stored(j - 2, side):
                copy.wait()

        held[side, 0] = dot_low(turned[...], hidden_all[j]).astype(LOW)
        held[side, 1] = dot_over(active_all[j], upstream[...]).astype(LOW)
        for copy in stored(j, side):
            copy.start()

    each(4, weigh)
    for j in (2, 3):
        for copy in stored(j, j % 2):
            copy.wait()
    for copy in own_home:
        copy.wait()
    for slot in (4, 5, 1, 6, 7, 2, 3):
        for copy in home(slot):
            copy.wait_recv()
    for slot in (4, 5, 1, 6, 7, 2, 3):
        for copy in there(slot) + home(slot):
            copy.wait_send()


def routed(sent, gates, cotangent, first, second, name):
    slots, capacity, _ = sent.shape
    hbm = pl.BlockSpec(memory_space=pl.ANY)
    count = slots * capacity
    low = jax.ShapeDtypeStruct(sent.shape, LOW)
    share = jax.ShapeDtypeStruct(first.shape, LOW)
    pairs = [pltpu.SemaphoreType.DMA((slots,)) for _ in range(8)]
    return pl.pallas_call(
        routed_kernel,
        out_shape=(low, low, jax.ShapeDtypeStruct(gates.shape, F32), share, share),
        in_specs=[hbm] * 5,
        out_specs=(pl.BlockSpec(memory_space=pltpu.VMEM), hbm, hbm, hbm, hbm),
        scratch_shapes=[
            pltpu.VMEM(sent.shape, LOW),
            pltpu.VMEM(gates.shape, F32),
            pltpu.VMEM(sent.shape, LOW),
            pltpu.VMEM(first.shape, LOW),
            pltpu.VMEM(second.shape, LOW),
            pltpu.VMEM((4, count, D), LOW),
            pltpu.VMEM((4, count, D), LOW),
            pltpu.VMEM((count, D), LOW),
            pltpu.VMEM(sent.shape, LOW),
            pltpu.VMEM(gates.shape, F32),
            pltpu.VMEM((D, count), LOW),
            pltpu.VMEM((2 * capacity, D), F32),
            pltpu.VMEM((2 * capacity, D), F32),
            pltpu.VMEM((2, 2, D, D), LOW),
            *pairs,
            pltpu.SemaphoreType.DMA((7,)),
            pltpu.SemaphoreType.DMA((2, 2)),
        ],
        compiler_params=pltpu.CompilerParams(
            vmem_limit_bytes=60 * MIB, collective_id=name, has_side_effects=True
        ),
    )(sent, gates, cotangent, first, second)


def finish_kernel(
    index,
    small,
    line,
    early_q,
    early_k,
    early_b,
    late_a,
    late_b,
    dense_b,
    gain_share,
    rel_share,
    route_share,
    qkv,
    out,
    dense_in,
):
    row, col = lax.axis_index("row"), lax.axis_index("col")
    place = row * 4 + col
    width = gain_share.shape[1]
    buckets = rel_share.shape[1]
    lines = jnp.concatenate([line[:8, :D], small[32:48, :D]], 0)
    lines = pltpu.roll(lines, lax.rem(D - place * width, D), 1)[:, :width]
    gain_share[...] = jnp.concatenate([lines[0:1], lines[10:11], lines[8:9], lines[9:10]], 0)
    route_share[...] = lines[11:19]
    wanted = place * buckets + lax.broadcasted_iota(jnp.int32, (8, 1), 0)
    hot = (index[...] == wanted).astype(F32)
    for i, block in enumerate((small[:16, :], small[16:32, :])):
        sums = lax.dot_general(
            hot, block, (((1,), (1,)), ((), ())), precision=HIGH, preferred_element_type=F32
        )
        rel_share[i] = sums[:buckets, :HEADS]
    for i, blocks in enumerate(
        ((early_q[0], early_k[0], early_b[0]), (late_a[0], late_a[1], late_b[0]))
    ):
        for k, block in enumerate(blocks):
            qkv[i, :, k * D : (k + 1) * D] = block
    out[0] = early_b[1]
    out[1] = late_b[1]
    for k in range(4):
        dense_in[:, k * D : (k + 1) * D] = dense_b[k]


def finish(index, *blocks):
    piece = blocks[2].shape[1]
    shapes = (
        (4, piece),
        (2, BUCKETS * piece // D, HEADS),
        (8, piece),
        (2, piece, 3 * D),
        (2, piece, D),
        (piece, FF),
    )
    return pl.pallas_call(
        finish_kernel,
        out_shape=tuple(jax.ShapeDtypeStruct(shape, F32) for shape in shapes),
        compiler_params=pltpu.CompilerParams(vmem_limit_bytes=32 * MIB),
    )(index, *blocks)


def tiled(
    inputs,
    cotangent,
    routes,
    buckets,
    norm_gains,
    attn_qkv,
    attn_out,
    rel_bias,
    mlp_in,
    mlp_out,
    router,
    expert_in,
    expert_out,
):
    grid = ("row", "col")
    places = lax.axis_size(grid)
    cols, planes = lax.axis_size("col"), lax.axis_size("dp")
    experts = planes * cols
    tokens = inputs.shape[1]
    pslice = tokens - CLEN
    capacity = 3 * tokens // experts
    piece = D // places

    small = [norm_gains.reshape(-1), rel_bias.reshape(-1), router.reshape(-1)]
    cuts = [part.shape[0] for part in small]
    packed = jnp.concatenate(small)
    packed = jnp.pad(packed, (0, -packed.shape[0] % 2048)).reshape(1, -1, 128)

    pair, cut = (2, piece, D), (piece, 3 * D)
    early = (0, LATE, LATE, LATE, LATE)
    inner_a = layer(Gather(cut, False, cols, span=(0, 2 * D)), 0)
    inner_b = layer(Gather(cut, True, cols, span=(2 * D, D), into=inner_a), 0)
    packed, inner0, output0, shared0 = carry(
        None,
        [
            (Gather(packed.shape, False, cols), early),
            (inner_a, early),
            (inner_b, early),
            (layer(Gather((piece, D), True, cols), 0), early),
            (Rows((pslice, D)), (0, LATE, LATE)),
        ],
        (1,),
        [],
        [],
        [],
        [],
        60,
        1,
    )(packed, attn_qkv, attn_qkv, attn_out, inputs[0, :pslice])
    packed = packed.reshape(places, -1)
    gains = packed[:, : cuts[0]].reshape(places, 4, -1).transpose(1, 0, 2).reshape(4, 1, D).astype(F32)
    rel = packed[:, cuts[0] : cuts[0] + cuts[1]].reshape(places, 2, -1, HEADS)
    rel = rel.transpose(1, 3, 0, 2).reshape(2, HEADS, BUCKETS)
    route_w = packed[:, cuts[0] + cuts[1] : sum(cuts)].reshape(D, experts)

    gap = jnp.full((WRAP - KEYS,), -1, jnp.int32)
    index = jnp.concatenate([jnp.flip(buckets[: PLEN + 1]), gap, jnp.flip(buckets[PLEN + 1 :])])
    hot = (jnp.arange(BUCKETS, dtype=jnp.int32)[:, None] == index[None, :]).astype(LOW)
    floor = jnp.where(index < 0, NEG, 0.0).astype(F32)
    tables = jnp.pad(rel, ((0, 0), (0, 16 - HEADS), (0, 0))).reshape(32, BUCKETS)
    tables = (dot_low(tables, hot) + floor[None]).reshape(2, 16, WRAP)

    flat = routes[0].reshape(-1)
    levels = jnp.arange(experts, dtype=jnp.int32)
    choose = (routes[0][:, :, None] == levels[None, None, :]).astype(F32)
    flipped_plane = (flat // cols) ^ lax.axis_index("dp")
    flipped_col = (flat % cols) ^ lax.axis_index("col")
    slot = 2 * flipped_col + flipped_plane
    hits = (slot[:, None] == levels[None, :]).astype(LOW)
    before = jnp.arange(2 * tokens)
    before = (before[:, None] > before[None, :]).astype(LOW)
    rank = jnp.sum(dot_low(before, hits) * hits.astype(F32), 1).astype(jnp.int32)
    place = (slot * capacity + rank).reshape(tokens, 2)
    spots = jnp.arange(experts * capacity, dtype=jnp.int32)
    picks = [(place[:, k][:, None] == spots[None, :]).astype(LOW) for k in range(2)]
    both = picks[0] + picks[1]
    sent_cotangent = dot_over(both, cotangent[0]).astype(LOW).reshape(experts, capacity, D)

    state1, stash1, (dense_in, dense_out, first) = attention_up(
        inputs[0],
        inputs[0],
        shared0,
        0,
        gains,
        tables,
        inner0,
        output0,
        [
            (Gather(mlp_in.shape, True, cols), (0, 2, 4, LATE, LATE)),
            (Gather(mlp_out.shape, True, cols), (0, 2, 4, LATE, LATE)),
            (Rows(expert_in.shape[1:]), (0, 4, LATE)),
        ],
        (mlp_in, mlp_out, expert_in[0]),
        2,
    )
    state2, normed1, normed2, shared2, inner1, output1, far_cotangent = mlp_up(
        state1,
        gains,
        dense_in,
        dense_out,
        [
            (layer(Gather(cut, True, cols), 1), (0, 2, LATE, LATE, LATE)),
            (layer(Gather((piece, D), True, cols), 1), (0, 2, LATE, LATE, LATE)),
            (Swap((capacity, D)), (0, LATE + 1)),
        ],
        (attn_qkv, attn_out, sent_cotangent),
        3,
    )
    state3, stash3, (second,) = attention_up(
        state2,
        normed2,
        shared2,
        1,
        gains,
        tables,
        inner1,
        output1,
        [(Rows(expert_out.shape[1:]), (0, 5, LATE))],
        (expert_out[0],),
        4,
    )

    normed3 = norm_rows(state3, gains[3]).astype(LOW)
    logits = dot_low(normed3, route_w)
    picked = jnp.sum(choose * logits[:, None, :], -1)
    raised = jnp.exp(picked - jnp.max(picked, -1, keepdims=True))
    gates = raised / jnp.sum(raised, -1, keepdims=True)
    line = sum(dot_over(jnp.stack(split_low(gates[:, k]), 1), picks[k]) for k in range(2))
    line = jnp.sum(line, 0).reshape(experts, 1, capacity)
    line = jnp.pad(line, ((0, 0), (0, 7), (0, -capacity % 128)))
    sent = dot_over(both, normed3).astype(LOW).reshape(experts, capacity, D)
    outcome, returned, reach, grad_first, grad_second = routed(
        sent, line, far_cotangent, first, second, 5
    )
    returned = returned.reshape(experts * capacity, D)
    reach = jnp.stack(split_low(reach[:, 0, :capacity].reshape(-1)), 1)
    grad_gates = jnp.stack([jnp.sum(dot_low(picks[k], reach), 1) for k in range(2)], 1)
    grad_picked = gates * (grad_gates - jnp.sum(gates * grad_gates, -1, keepdims=True))
    grad_logits = jnp.sum(choose * grad_picked[:, :, None], 1).astype(LOW)
    grad_route = dot_over(grad_logits, normed3)
    grad_normed3 = dot_low(both, returned) + dot_back(grad_logits, route_w)
    grad_state3, gain_last = norm_back(state3, gains[3], grad_normed3)
    grad3 = cotangent[0].astype(F32) + grad_state3

    laid = (4, 1, places, piece, D)
    octet = (places // 2, piece, D)
    grad_first, grad_second = grad_first.reshape(laid), grad_second.reshape(laid)
    grad2, gain_third, late, table_late, own_first, own_second, outcome = attention_down(
        grad3,
        state2,
        gains,
        1,
        stash3,
        tables,
        [
            (Reduce((places, piece, D), ("core", "x")), (0, 1, LATE)),
            (Reduce(octet, ("core", "x")), (0, 2, LATE + 3)),
            (Swap((capacity, D)), (0, LATE + 5)),
        ],
        (grad_first, grad_second, outcome),
        6,
    )
    outcome = outcome.reshape(experts * capacity, D)
    output = state3 + sum(gates[:, k : k + 1] * dot_low(picks[k], outcome) for k in range(2))
    grad1, gain_second, dense_pairs, own_rest, late_a, late_b = mlp_down(
        grad2,
        state1,
        normed1,
        gains,
        dense_in,
        dense_out,
        [
            (Reduce(octet, ("core", "x"), first=places // 2), (0, 2, LATE + 3)),
            (Reduce(pair, ("core", "x"), cols), (0, 1, LATE + 2)),
            (Reduce(pair, ("core", "y"), cols, first=2), (0, 1, LATE)),
        ],
        (grad_second, late, late),
        7,
    )
    lines = jnp.concatenate([gain_third, gain_last, gain_second, grad_route], 0)
    lines = jnp.pad(lines, ((0, 16 - lines.shape[0]), (0, WRAP - D)))
    known = jnp.concatenate([table_late, lines], 0).astype(LOW)
    quad = (4, piece, D)
    single = (1, piece, D)
    held = lambda outs, extras: extras[-3]
    (
        grad0,
        _,
        _,
        late_a,
        late_b,
        dense_a,
        dense_b,
        early_q,
        early_k,
        early_b,
        small,
        line,
    ) = attention_down(
        grad1,
        inputs[0],
        gains,
        0,
        stash1,
        tables,
        [
            (Reduce(pair, ("z", "sum"), cols), (0, 3, 5)),
            (Reduce(single, ("x", "z", "swap"), cols), (0, 2, 4, 5)),
            (Reduce(quad, ("x", "z", "sum"), cols), (0, 4, LATE + 3, LATE + 7)),
            (
                Reduce(quad, ("y", "x", "z", "swap"), cols, first=4),
                (0, 4, LATE + 1, LATE + 5, LATE + 7),
            ),
            (
                Reduce(single, ("core", "x", "z", "sum"), cols, take=held),
                (LATE, LATE + 2, LATE + 5, LATE + 8, LATE + 10),
            ),
            (
                Reduce(single, ("core", "x", "z", "sum"), cols, first=1, take=held),
                (LATE, LATE + 2, LATE + 6, LATE + 9, LATE + 10),
            ),
            (
                Reduce(pair, ("core", "y", "x", "z", "swap"), cols, first=2, take=held),
                (LATE, LATE + 2, LATE + 5, LATE + 7, LATE + 9, LATE + 10),
            ),
            (
                Total((16 + known.shape[0], WRAP), take=lambda outs, extras: extras[-2]),
                (LATE - 0.5, LATE + 0.5, LATE + 1.5, LATE + 2.5, LATE + 4.2),
            ),
            (
                Total((16, D), take=lambda outs, extras: extras[-1]),
                (LATE + 4.6, LATE + 5.5, LATE + 6.5, LATE + 7.5, LATE + 9.5),
            ),
        ],
        (late_a, late_b, dense_pairs, dense_pairs),
        8,
        known=known,
    )
    gain_share, rel_share, route_share, qkv_share, out_share, in_share = finish(
        index.reshape(1, -1), small, line, early_q, early_k, early_b, late_a, late_b, dense_b
    )
    return (
        output[None],
        grad0[None],
        gain_share,
        qkv_share,
        out_share,
        rel_share,
        in_share,
        dense_a.reshape(-1, D),
        route_share.T,
        own_first.reshape(1, D, D),
        jnp.concatenate([own_second, own_rest], 0).reshape(1, D, D),
    )


def solution(mesh):
    in_specs = (
        P(("dp", "col"), "row", None),
        P(("dp", "col"), "row", None),
        P(("dp", "col"), "row", None),
        P(),
        P(None, ("row", "col")),
        P(None, ("row", "col"), None),
        P(None, ("row", "col"), None),
        P(None, ("row", "col"), None),
        P(("row", "col"), None),
        P(("row", "col"), None),
        P(("row", "col"), None),
        P(("dp", "col"), None, "row"),
        P(("dp", "col"), "row", None),
    )
    out_specs = (
        P(("dp", "col"), "row", None),
        P(("dp", "col"), "row", None),
        P(None, ("row", "col")),
        P(None, ("row", "col"), None),
        P(None, ("row", "col"), None),
        P(None, ("row", "col"), None),
        P(("row", "col"), None),
        P(("row", "col"), None),
        P(("row", "col"), None),
        P(("dp", "col"), None, "row"),
        P(("dp", "col"), "row", None),
    )
    sizes = dict(mesh.shape)
    piece = D // (sizes["row"] * sizes["col"])
    capacity = 3 * (PLEN // sizes["row"] + CLEN) // (sizes["dp"] * sizes["col"])
    whole_tiles = (sizes["dp"], sizes["row"], sizes["col"]) == (2, 4, 4) and piece % 16 == 0 and capacity % 16 == 0
    return jax.shard_map(
        tiled if whole_tiles else general, mesh=mesh, in_specs=in_specs, out_specs=out_specs, check_vma=False
    )
```

```python
import functools

import jax
import jax.numpy as jnp
from jax import lax
from jax.experimental import pallas as pl
from jax.experimental.pallas import tpu as pltpu
from jax.sharding import PartitionSpec as P

D = 768
HEADS = 12
HDIM = 64
FF = 3072
BUCKETS = 32
PLEN = 1024
CLEN = 128
KEYS = PLEN + CLEN
WRAP = KEYS + 128
STRIP = 2 * PLEN
NEG = -1e30
EPS = 1e-06
CURVE = 0.7978845608028654
CUBE = 0.044715
HIGH = lax.Precision.HIGHEST
F32 = jnp.float32
LOW = jnp.bfloat16
MIB = 1 << 20


def dot_low(left, right):
    return jnp.dot(left, right, preferred_element_type=F32)


def dot_back(left, right):
    return lax.dot_general(left, right, (((1,), (1,)), ((), ())), preferred_element_type=F32)


def dot_over(left, right):
    return lax.dot_general(left, right, (((0,), (0,)), ((), ())), preferred_element_type=F32)


def normalise(values):
    center = values - jnp.mean(values, -1, keepdims=True)
    scale = lax.rsqrt(jnp.mean(center * center, -1, keepdims=True) + EPS)
    return center * scale, scale


def norm_rows(values, gain):
    return normalise(values)[0] * gain


def norm_back(values, gain, upstream):
    unit, scale = normalise(values)
    pulled = upstream * gain
    shift = jnp.mean(pulled, -1, keepdims=True)
    along = jnp.mean(pulled * unit, -1, keepdims=True)
    return (pulled - shift - unit * along) * scale, jnp.sum(upstream * unit, 0, keepdims=True)


def gelu_parts(values):
    square = values * values
    bend = jnp.tanh(CURVE * (values + CUBE * square * values))
    half = 0.5 * (1.0 + bend)
    slope = half + 0.5 * values * (1.0 - bend * bend) * (CURVE + 3.0 * CURVE * CUBE * square)
    return values * half, slope


def gelu(values):
    return 0.5 * values * (1.0 + jnp.tanh(CURVE * (values + CUBE * values * values * values)))


def params(mib, steps=1):
    return pltpu.CompilerParams(
        vmem_limit_bytes=mib * MIB, dimension_semantics=("arbitrary",) * steps
    )


def whole(shape):
    return pl.BlockSpec(shape, lambda *_: (0,) * len(shape))


MESH = pl.DeviceIdType.MESH


class Remote:
    def __init__(self, src, dst, send, recv, index, device):
        self.parts = (src, dst, send, recv, index, device)

    def described(self):
        src, dst, send, recv, index, device = self.parts
        return pltpu.make_async_remote_copy(
            src_ref=src,
            dst_ref=dst,
            send_sem=send.at[index],
            recv_sem=recv.at[index],
            device_id=device,
            device_id_type=MESH,
        )

    def start(self):
        self.described().start()

    def wait_recv(self):
        self.described().wait_recv()

    def wait_send(self):
        self.described().wait_send()


def remote(src, dst, send, recv, index, **device):
    return Remote(src, dst, send, recv, index, device)


def neighbours():
    row, dp = lax.axis_index("row"), lax.axis_index("dp")
    across = lax.rem(row + 2, 4)
    core = row + 1 - 2 * lax.rem(row, 2)
    return row, across, core, dp + 1 - 2 * lax.rem(dp, 2)


class Within:
    def __init__(self, src, dst, sem):
        self.parts = (src, dst, sem)

    def start(self):
        pltpu.make_async_copy(*self.parts).start()

    def wait(self):
        pltpu.make_async_copy(*self.parts).wait()


class Gather:
    phases = 5

    def __init__(self, shape, split, cols, span=None, into=None, take=None):
        self.shape, self.split, self.cols, self.take, self.into = shape, split, cols, take, into
        self.span = (0, shape[-1]) if span is None else span
        self.spec = pl.BlockSpec(memory_space=pl.ANY)
        self.result = jax.ShapeDtypeStruct((4, cols) + shape, LOW)
        count = 4 * cols - 1 + (4 * cols - 2 if split else 0)
        self.scratch = [
            pltpu.SemaphoreType.DMA((count + 2 * cols,)),
            pltpu.SemaphoreType.DMA((count + 2 * cols,)),
            pltpu.SemaphoreType.DMA((1,)),
        ]

    def copies(self, src, dst, send, recv, local):
        cols = self.cols
        row, across, core, plane = neighbours()
        col, dp = lax.axis_index("col"), lax.axis_index("dp")
        first, width = self.span
        half = width // 2
        lead = (slice(None),) * (len(self.shape) - 1)
        full = lead + (pl.ds(first, width),)
        mine = pl.multiple_of(first + dp * half, 128)
        others = pl.multiple_of(first + (1 - dp) * half, 128)
        part = lead + (pl.ds(mine, half),) if self.split else full
        rest = lead + (pl.ds(others, half),)
        number = [0]

        def make(source, target, **device):
            number[0] += 1
            return remote(source, target, send, recv, number[0] - 1, **device)

        def piece(where, step, which):
            return dst.at[where, lax.rem(col - step + cols, cols)].at[which]

        own = src.at[part]
        out = {}
        out["local"] = Within(src.at[full], piece(row, 0, full), local.at[0])
        out["z"] = [
            make(own, piece(row, 0, part), col=lax.rem(col + step, cols)) for step in range(1, cols)
        ]
        out["x"] = [make(own, piece(row, 0, part), row=across)]
        out["x"] += [
            make(piece(row, step, part), piece(row, step, part), row=across)
            for step in range(1, cols)
        ]
        out["core own"] = make(src.at[full], piece(row, 0, full), row=core)
        out["core z"] = [
            make(piece(row, step, part), piece(row, step, part), row=core) for step in range(1, cols)
        ]
        out["core x"] = [
            make(piece(across, step, part), piece(across, step, part), row=core)
            for step in range(cols)
        ]
        if self.split:
            out["y z"] = [
                make(piece(row, step, part), piece(row, step, part), dp=plane)
                for step in range(1, cols)
            ]
            out["y x"] = [
                make(piece(across, step, part), piece(across, step, part), dp=plane)
                for step in range(cols)
            ]
            out["core y z"] = [
                make(piece(row, step, rest), piece(row, step, rest), row=core)
                for step in range(1, cols)
            ]
            out["core y x"] = [
                make(piece(across, step, rest), piece(across, step, rest), row=core)
                for step in range(cols)
            ]
        return out

    def peers(self):
        cols, col = self.cols, lax.axis_index("col")
        row, across, core, plane = neighbours()
        found = {(0, step): dict(col=lax.rem(col + step, cols)) for step in range(1, cols)}
        found.update(across=dict(row=across), core=dict(row=core))
        if self.split:
            found[(1, 0)] = dict(dp=plane)
        return found

    def phase(self, number, *refs):
        out = self.copies(*refs)
        if number == 0:
            out["local"].start()
            for copy in out["z"]:
                copy.start()
            out["x"][0].start()
            out["core own"].start()
        elif number == 1:
            for step in self.order():
                out["z"][step - 1].wait_recv()
                out["x"][step].start()
                if self.split:
                    out["y z"][step - 1].start()
                out["core z"][step - 1].start()
        elif number == 2:
            for step in [0] + self.order():
                out["x"][step].wait_recv()
                if self.split:
                    out["y x"][step].start()
                out["core x"][step].start()
        elif number == 3 and self.split:
            for step in self.order():
                out["y z"][step - 1].wait_recv()
                out["core y z"][step - 1].start()
            for step in [0] + self.order():
                out["y x"][step].wait_recv()
                out["core y x"][step].start()
        elif number == 4:
            out["local"].wait()
            late = [out["core own"]] + out["core z"] + out["core x"]
            if self.split:
                late += out["core y z"] + out["core y x"]
            for copy in late:
                copy.wait_recv()
            early = out["z"] + out["x"] + late
            if self.split:
                early += out["y z"] + out["y x"]
            for copy in early:
                copy.wait_send()

    def order(self):
        steps = list(range(1, self.cols))
        return sorted(steps, key=lambda step: min(step, self.cols - step))


class Rows:
    phases = 3

    def __init__(self, shape, take=None):
        self.take = take
        self.result = jax.ShapeDtypeStruct((4,) + shape, LOW)
        self.spec = pl.BlockSpec(memory_space=pl.ANY)
        self.scratch = [
            pltpu.SemaphoreType.DMA((3,)),
            pltpu.SemaphoreType.DMA((3,)),
            pltpu.SemaphoreType.DMA((1,)),
        ]

    def peers(self):
        row, across, core, plane = neighbours()
        return dict(across=dict(row=across), core=dict(row=core))

    def phase(self, number, src, dst, send, recv, local):
        row, across, core, plane = neighbours()
        own = Within(src, dst.at[row], local.at[0])
        far = remote(src, dst.at[row], send, recv, 0, row=across)
        near = remote(src, dst.at[row], send, recv, 1, row=core)
        on = remote(dst.at[across], dst.at[across], send, recv, 2, row=core)
        if number == 0:
            own.start()
            far.start()
            near.start()
        elif number == 1:
            far.wait_recv()
            on.start()
        else:
            own.wait()
            near.wait_recv()
            on.wait_recv()
            for copy in (far, near, on):
                copy.wait_send()


SLOTS = [(a, b) for b in range(4) for a in range(2)]


def slot_device(slot):
    a, b = SLOTS[slot]
    dp, col = lax.axis_index("dp"), lax.axis_index("col")
    flipped = (col, col + 1 - 2 * lax.rem(col, 2), lax.rem(col + 2, 4), 3 - col)[b]
    device = {}
    if a:
        device["dp"] = 1 - dp
    if b:
        device["col"] = flipped
    return device


class Swap:
    phases = 2

    def __init__(self, shape, take=None):
        self.take = take
        self.result = jax.ShapeDtypeStruct((len(SLOTS),) + shape, LOW)
        self.spec = pl.BlockSpec(memory_space=pl.ANY)
        self.scratch = [
            pltpu.SemaphoreType.DMA((len(SLOTS),)),
            pltpu.SemaphoreType.DMA((len(SLOTS),)),
            pltpu.SemaphoreType.DMA((1,)),
        ]

    def peers(self):
        return {SLOTS[slot]: slot_device(slot) for slot in range(1, len(SLOTS))}

    def phase(self, number, src, dst, send, recv, local):
        own = Within(src.at[0], dst.at[0], local.at[0])
        copies = [
            remote(src.at[slot], dst.at[slot], send, recv, slot, **slot_device(slot))
            for slot in range(1, len(SLOTS))
        ]
        if number == 0:
            for copy in copies:
                copy.start()
            own.start()
        else:
            own.wait()
            for copy in copies:
                copy.wait_recv()
            for copy in copies:
                copy.wait_send()


def each(count, body):
    lax.fori_loop(0, count, lambda index, carried: (body(index), carried)[1], 0)


class Reduce:
    def __init__(self, shape, ops, cols=1, first=0, take=None, keep=False):
        self.ops, self.cols, self.first, self.take, self.keep = ops, cols, first, take, keep
        self.count, tail = shape[0], shape[1:]
        self.part = self.count // 2 if "y" in ops else self.count
        self.phases = len(ops) + 1
        self.lead = 1 if ops[0] == "z" else 2
        ends = {
            "y": ((2, cols, self.part), LOW),
            "x": ((cols, self.part), LOW) if cols > 1 else ((self.part,), F32),
            "sum": ((self.part,), F32),
            "swap": ((2 * self.part,), F32),
        }
        lead, kind = ends[ops[-1]]
        self.result = jax.ShapeDtypeStruct(lead + tail, kind)
        self.spec = once(self.result.shape)
        full = (self.lead, cols, self.count)
        buffers = {"total": [full]}
        if "core" in ops and take is None:
            buffers["near"] = [full]
        if "y" in ops:
            buffers["y"] = [(2, cols, self.part)]
        if "x" in ops:
            buffers["x"] = [(cols, self.part)]
        if "z" in ops:
            buffers["z"] = [(cols - 1, self.part), (self.part,)]
            buffers["end"] = [(self.part,)]
        self.names = list(buffers)
        self.lengths = [len(buffers[name]) for name in self.names]
        self.scratch = [pltpu.VMEM(lead + tail, LOW) for name in self.names for lead in buffers[name]]
        self.scratch += [
            pltpu.SemaphoreType.DMA((8,)),
            pltpu.SemaphoreType.DMA((8,)),
            pltpu.SemaphoreType.DMA((2,)),
        ]

    def peers(self):
        row, across, core, plane = neighbours()
        found = {}
        if "core" in self.ops:
            found["core"] = dict(row=core)
        if "x" in self.ops:
            found["across"] = dict(row=across)
        slots = (2, 4, 6) if "z" in self.ops else ()
        if {"y", "sum", "swap"} & set(self.ops):
            slots += (1,)
        for slot in slots:
            found[SLOTS[slot]] = slot_device(slot)
        return found

    def phase(self, number, src, out, *scratch):
        scratch = list(scratch)
        held = {
            name: [scratch.pop(0) for _ in range(length)]
            for name, length in zip(self.names, self.lengths)
        }
        send, recv, local = scratch
        row, across, core, plane = neighbours()
        x, c = row // 2, lax.rem(row, 2)
        if self.ops[0] == "z":
            x = 0
        dp, col = lax.axis_index("dp"), lax.axis_index("col")
        total = held["total"][0]
        span = pl.ds(self.first, self.count)
        start = dp * self.part if "y" in self.ops else 0
        part, rest = pl.ds(start, self.part), pl.ds((1 - dp) * self.part, self.part)
        if self.take is not None:
            loads = []
        elif self.ops[0] == "core":
            loads = [Within(src.at[2 * i + c, :, span], total.at[i], local.at[i]) for i in range(2)]
        elif self.ops[0] == "z":
            loads = [Within(src.at[:, span], total.at[0], local.at[0])]
        else:
            loads = [Within(src.at[:, :, span], total, local.at[0])]

        def copies(op):
            if op == "core":
                near = held["near"][0] if self.take is None else total
                return [
                    remote(src.at[2 * i + 1 - c, :, span], near.at[i], send, recv, i, row=core)
                    for i in range(2)
                ]
            begun = op == self.ops[0]
            if op == "y":
                view = total.at[:, :, rest]
                if begun:
                    view = src.at[:, :, pl.ds(self.first + (1 - dp) * self.part, self.part)]
                return [remote(view, held["y"][0], send, recv, 2, dp=plane)]
            if op == "x":
                view = src.at[1 - x, :, span] if begun else total.at[1 - x, :, part]
                return [remote(view, held["x"][0], send, recv, 3, row=across)]
            if op == "z":
                found = []
                for b in (2, 3, 1):
                    device = slot_device(2 * b)
                    view = total.at[x, device["col"], part]
                    if begun:
                        view = src.at[device["col"], span]
                    found.append(remote(view, held["z"][0].at[b - 1], send, recv, 3 + b, **device))
                return found
            return [remote(held["z"][1], held["end"][0], send, recv, 7, dp=plane)]

        wide = lambda value: value.astype(F32)
        count, cols, size = self.count, self.cols, self.part
        if number > 0:
            op = self.ops[number - 1]
            last = number == len(self.ops)
            if number == 1:
                for load in loads:
                    load.wait()
            for copy in copies(op):
                copy.wait_recv()
            if op == "core":

                def add(i):
                    at = (i // (cols * count), lax.rem(i // count, cols), lax.rem(i, count))
                    if self.take is None:
                        more = held["near"][0][at]
                    else:
                        more = src[2 * at[0] + c, at[1], self.first + at[2]]
                    total[at] = (wide(total[at]) + wide(more)).astype(LOW)

                each(2 * cols * count, add)
            elif op == "y":

                def add(i):
                    at = (i // (cols * size), lax.rem(i // size, cols))
                    k = lax.rem(i, size)
                    kept = at + (start + k,)
                    value = wide(total[kept]) + wide(held["y"][0][at + (k,)])
                    if last:
                        out[at + (k,)] = value.astype(LOW)
                    else:
                        total[kept] = value.astype(LOW)

                each(2 * cols * size, add)
            elif op == "x":

                def add(i):
                    z, k = i // size, lax.rem(i, size)
                    value = wide(total[x, z, start + k]) + wide(held["x"][0][z, k])
                    if last and cols == 1:
                        out[k] = value
                    elif last:
                        out[z, k] = value.astype(LOW)
                    else:
                        total[x, z, start + k] = value.astype(LOW)

                each(cols * size, add)
            elif op == "z":

                def add(k):
                    value = wide(total[x, col, start + k])
                    for b in range(cols - 1):
                        value = value + wide(held["z"][0][b, k])
                    held["z"][1][k] = value.astype(LOW)

                each(size, add)
            else:

                def add(k):
                    mine, other = wide(held["z"][1][k]), wide(held["end"][0][k])
                    if op == "sum":
                        out[k] = mine + other
                    else:
                        out[dp * size + k] = mine
                        out[(1 - dp) * size + k] = other

                each(size, add)
        if number < len(self.ops):
            op = self.ops[number]
            for copy in copies(op):
                copy.start()
            if number == 0:
                for load in loads:
                    load.start()
        else:
            for op in self.ops:
                for copy in copies(op):
                    copy.wait_send()


class CoreSum:
    phases = 6

    def __init__(self, shape, cols, take):
        self.take, self.cols = take, cols
        self.result = jax.ShapeDtypeStruct((2, cols, 8) + shape, LOW)
        self.spec = once(self.result.shape)
        self.scratch = [
            pltpu.VMEM(self.result.shape, LOW),
            pltpu.SemaphoreType.DMA((10,)),
            pltpu.SemaphoreType.DMA((10,)),
        ]

    def peers(self):
        row, across, core, plane = neighbours()
        return dict(core=dict(row=core))

    def phase(self, number, src, out, near, send, recv):
        row, across, core, plane = neighbours()
        c = lax.rem(row, 2)

        def inner(j, i):
            at = (slice(None), 4 + j)
            view = src.at[2 * i + 1 - c].at[at]
            return remote(view, near.at[i].at[at], send, recv, 2 * j + i, row=core)

        def outer(i):
            at = (slice(None), pl.ds(0, 4))
            view = src.at[2 * i + 1 - c].at[at]
            return remote(view, near.at[i].at[at], send, recv, 8 + i, row=core)

        def begin(j):
            for i in range(2):
                inner(j, i).start()
            if j % 2 == 1:
                outer(j // 2).start()

        def add(i, z, k):
            out[i, z, k] = (src[2 * i + c, z, k].astype(F32) + near[i, z, k].astype(F32)).astype(LOW)

        def end(j):
            for i in range(2):
                inner(j, i).wait_recv()
            each(2 * self.cols, lambda n: add(n // self.cols, lax.rem(n, self.cols), 4 + j))
            if j % 2 == 1:
                outer(j // 2).wait_recv()
                each(4 * self.cols, lambda n: add(j // 2, n // 4, lax.rem(n, 4)))

        if 1 <= number <= 4:
            begin(number - 1)
        if number in (3, 4):
            end(number - 3)
        if number == 5:
            end(2)
            end(3)
            for j in range(4):
                for i in range(2):
                    inner(j, i).wait_send()
            for i in range(2):
                outer(i).wait_send()


class Total:
    def __init__(self, shape, take=None, short=False):
        self.take, self.short = take, short
        self.phases = 3 if short else 5
        hops, arrivals = (2, 10) if short else (4, 6)
        self.result = jax.ShapeDtypeStruct(shape, F32)
        self.spec = once(shape)
        self.scratch = [
            pltpu.VMEM((hops,) + shape, LOW),
            pltpu.VMEM((arrivals,) + shape, LOW),
            pltpu.SemaphoreType.DMA((arrivals,)),
            pltpu.SemaphoreType.DMA((arrivals,)),
            pltpu.SemaphoreType.DMA((1,)),
        ]

    def hops(self):
        row, across, core, plane = neighbours()
        if self.short:
            first = [dict(row=across), dict(row=lax.rem(core + 2, 4)), dict(row=core)]
            return [first, [slot_device(slot) for slot in (4, 5, 6, 7, 2, 3, 1)]]
        found = [[dict(row=core)], [dict(row=across)], [dict(dp=plane)]]
        return found + [[slot_device(2 * b) for b in (1, 2, 3)]]

    def peers(self):
        row, across, core, plane = neighbours()
        found = dict(across=dict(row=across), core=dict(row=core))
        if self.short:
            found["far"] = dict(row=lax.rem(core + 2, 4))
        for slot in range(1, 8) if self.short else (1, 2, 4, 6):
            found[SLOTS[slot]] = slot_device(slot)
        return found

    def phase(self, number, src, out, mine, other, send, recv, local):
        hops = self.hops()
        starts = [sum(len(hop) for hop in hops[:i]) for i in range(len(hops))]

        def copies(hop):
            return [
                remote(mine.at[hop], other.at[starts[hop] + i], send, recv, starts[hop] + i, **device)
                for i, device in enumerate(hops[hop])
            ]

        if number == 0:
            load = Within(src, mine.at[0], local.at[0])
            load.start()
            load.wait()
        else:
            value = mine[number - 1].astype(F32)
            for i, copy in enumerate(copies(number - 1)):
                copy.wait_recv()
                value = value + other[starts[number - 1] + i].astype(F32)
            if number < len(hops):
                mine[number] = value.astype(LOW)
            else:
                out[...] = value
        if number < len(hops):
            for copy in copies(number):
                copy.start()
        else:
            for hop in range(len(hops)):
                for copy in copies(hop):
                    copy.wait_send()


def greet(flows):
    barrier = pltpu.get_barrier_semaphore()
    devices = {}
    for flow in flows:
        devices.update(flow.peers())
    for device in devices.values():
        pl.semaphore_signal(barrier, inc=1, device_id=device, device_id_type=MESH)
    pl.semaphore_wait(barrier, len(devices))


LATE = 99


def layer(flow, index):
    flow.view = lambda ref: ref.at[index]
    return flow


def carry(body, moves, grid, in_specs, out_specs, out_shape, scratch_shapes, mib, name, after=None):
    inputs, outputs, extras = len(in_specs), len(out_specs), len(scratch_shapes)
    steps = grid[0]
    hbm = pl.BlockSpec(memory_space=pl.ANY)
    flows = [flow for flow, _ in moves]
    given = [flow for flow in flows if flow.take is None]
    shared = [flow for flow in flows if getattr(flow, "into", None) is not None]
    kept = [flow for flow in flows if getattr(flow, "keep", False)]
    shown = [flow for flow in flows if flow not in shared and flow not in kept]

    def kernel(*refs):
        refs = list(refs)
        take = lambda count: [refs.pop(0) for _ in range(count)]
        own_in = take(inputs)
        sources = {flow: refs.pop(0) for flow in given}
        own_out = take(outputs)
        results = {flow: refs.pop(0) for flow in shown}
        own_extra = take(extras)
        packs = {}
        for flow in flows:
            if flow in kept:
                results[flow] = refs.pop(0)
            elif flow in shared:
                results[flow] = results[flow.into]
            if flow not in sources:
                sources[flow] = flow.take(own_out, own_extra)
            source_of = getattr(flow, "view", None)
            if source_of is not None:
                sources[flow] = source_of(sources[flow])
            packs[flow] = [sources[flow], results[flow]] + take(len(flow.scratch))
        step = pl.program_id(0)

        def run(low, high):
            plan = []
            for index, (flow, marks) in enumerate(moves):
                for number in range(flow.phases):
                    if low <= marks[number] < high:
                        call = functools.partial(flow.phase, number, *packs[flow])
                        plan.append((marks[number], number, index, call))
            if after is not None and low <= after[0] < high:
                call = functools.partial(
                    after[1], own_in, own_out, own_extra, [results[flow] for flow in flows]
                )
                plan.append((after[0], 0, len(moves), call))
            for entry in sorted(plan, key=lambda entry: entry[:3]):
                entry[3]()

        for mark in range(steps):
            if mark == 0 or any(mark <= at < mark + 1 for _, marks in moves for at in marks):

                @pl.when(step == mark)
                def _():
                    if mark == 0:
                        greet(flows)
                    run(mark, mark + 1)

        if body is not None:
            body(*own_in, *own_out, *own_extra)

        @pl.when(step == steps - 1)
        def _():
            run(LATE - 1, LATE + 100)

    scratch = list(scratch_shapes)
    for flow in flows:
        if flow in kept:
            scratch.append(pltpu.VMEM(flow.result.shape, flow.result.dtype))
        scratch += flow.scratch

    def call(*args):
        return pl.pallas_call(
            kernel,
            grid=grid,
            out_shape=tuple(out_shape) + tuple(flow.result for flow in shown),
            in_specs=list(in_specs) + [hbm] * len(given),
            out_specs=tuple(out_specs) + tuple(flow.spec for flow in shown),
            scratch_shapes=scratch,
            compiler_params=pltpu.CompilerParams(
                vmem_limit_bytes=mib * MIB,
                dimension_semantics=("arbitrary",),
                collective_id=name,
                has_side_effects=True,
            ),
        )(*args)

    return call


def bias_table(buckets, rel):
    place = jnp.arange(WRAP, dtype=jnp.int32)
    dist = jnp.where(place <= PLEN, PLEN - place, PLEN + WRAP - place)
    read = (place <= PLEN) | (place > KEYS)
    index = jnp.take(buckets, jnp.clip(dist, 0, KEYS - 1), axis=0)
    hot = ((index[:, None] == jnp.arange(BUCKETS)[None, :]) & read[:, None]).astype(LOW)
    floor = jnp.where(read, 0.0, NEG).astype(F32)
    return hot, floor


def fill_strip(strip, table, head):
    @pl.when(pl.program_id(0) == 0)
    def _():
        strip[:, KEYS:] = jnp.full((128, STRIP - KEYS), NEG, F32)

    line = jnp.broadcast_to(table[pl.ds(head, 1), :], (128, WRAP))
    strip[:, :KEYS] = pltpu.roll(line, 0, 1, stride=1, stride_axis=0)[:, :KEYS]


def tiles_of(pslice):
    places = []
    for tile in range(pslice // 128):
        start = PLEN - (lax.axis_index("row") * pslice + tile * 128)
        places.append((tile * 128, pl.ds(pl.multiple_of(start, 128), PLEN), PLEN))
    places.append((pslice, pl.ds(0, KEYS), KEYS))
    return places


def attend_kernel(pslice, query, keys, values, table, mixed, total, strip, raw, weights):
    pair = pl.program_id(0)
    lane = lax.broadcasted_iota(jnp.int32, (1, 128), 1)

    @pl.when(pair == 0)
    def _():
        weights[:pslice, PLEN:] = jnp.zeros((pslice, CLEN), LOW)

    for half in range(2):
        mine = (lane < HDIM) if half == 0 else (lane >= HDIM)
        fill_strip(strip, table, 2 * pair + half)
        part = jnp.where(mine, query[...], 0) * HDIM ** (-0.5)
        raw[...] = dot_back(part.astype(LOW), keys[...])
        for row, place, count in tiles_of(pslice):
            rows = pl.ds(row, 128)
            scores = raw[rows, :count] + strip[:, place]
            top = jnp.max(scores, -1, keepdims=True)
            raised = jnp.exp(scores - top)
            summed = jnp.sum(raised, -1, keepdims=True)
            weights[rows, :count] = (raised * (1.0 / summed)).astype(LOW)
            log_total = jnp.broadcast_to(top + jnp.log(summed), (128, 128))
            if half == 0:
                total[rows, :] = log_total
            else:
                total[rows, :] = jnp.where(mine, log_total, total[rows, :])
        result = dot_low(weights[...], values[...]).astype(LOW)
        if half == 0:
            mixed[...] = result
        else:
            mixed[...] = jnp.where(mine, result, mixed[...])


def attend_forward(query, keys, values, table):
    tokens = query.shape[0]
    pslice = tokens - CLEN
    block = lambda rows: pl.BlockSpec((rows, 128), lambda i: (0, i))
    return pl.pallas_call(
        functools.partial(attend_kernel, pslice),
        grid=(HEADS // 2,),
        out_shape=(
            jax.ShapeDtypeStruct((tokens, D), LOW),
            jax.ShapeDtypeStruct((tokens, D), F32),
        ),
        in_specs=[block(tokens), block(KEYS), block(KEYS), whole(table.shape)],
        out_specs=(block(tokens), block(tokens)),
        scratch_shapes=[
            pltpu.VMEM((128, STRIP), F32),
            pltpu.VMEM((tokens, KEYS), F32),
            pltpu.VMEM((tokens, KEYS), LOW),
        ],
        compiler_params=params(32),
    )(query, keys, values, table)


def attend_back_kernel(
    pslice,
    query,
    keys,
    values,
    table,
    total,
    grad_mixed,
    grad_query,
    grad_keys,
    grad_values,
    grad_table,
    strip,
    raw,
    pulled,
    probs,
    grads,
    folded,
    sum_keys,
    sum_values,
):
    pair = pl.program_id(0)
    lane = lax.broadcasted_iota(jnp.int32, (1, 128), 1)
    across = lax.broadcasted_iota(jnp.int32, (128, 128), 0)
    along = lax.broadcasted_iota(jnp.int32, (128, 128), 1)
    mirror = (across + along == 127).astype(LOW)

    @pl.when(pair == 0)
    def _():
        probs[:pslice, PLEN:] = jnp.zeros((pslice, CLEN), LOW)
        grads[:pslice, PLEN:] = jnp.zeros((pslice, CLEN), LOW)

    for half in range(2):
        mine = (lane < HDIM) if half == 0 else (lane >= HDIM)
        fill_strip(strip, table, 2 * pair + half)
        part = (jnp.where(mine, query[...], 0) * HDIM ** (-0.5)).astype(LOW)
        upstream = jnp.where(mine, grad_mixed[...], 0).astype(LOW)
        raw[...] = dot_back(part, keys[...])
        pulled[...] = dot_back(upstream, values[...])
        folded[...] = jnp.zeros_like(folded)
        for row, place, count in tiles_of(pslice):
            rows = pl.ds(row, 128)
            log_total = total[rows, half * HDIM : half * HDIM + 1]
            chance = jnp.exp(raw[rows, :count] + strip[:, place] - log_total)
            product = chance * pulled[rows, :count]
            centre = jnp.sum(product, -1, keepdims=True)
            slope = (product - chance * centre).astype(LOW)
            probs[rows, :count] = chance.astype(LOW)
            grads[rows, :count] = slope
            folded[:, place] += dot_low(mirror, slope)
        result = dot_low(grads[...], keys[...]) * HDIM ** (-0.5)
        if half == 0:
            grad_query[...] = result.astype(LOW)
            sum_keys[...] = dot_over(part, grads[...])
            sum_values[...] = dot_over(upstream, probs[...])
        else:
            grad_query[...] = jnp.where(mine, result.astype(LOW), grad_query[...])
            sum_keys[...] += dot_over(part, grads[...])
            sum_values[...] += dot_over(upstream, probs[...])
        turned = pltpu.roll(folded[:, :WRAP], WRAP - 127, 1, stride=1, stride_axis=0)
        grad_table[pl.ds(2 * pair + half, 1), :] = jnp.sum(turned, 0, keepdims=True)
    grad_keys[...] = sum_keys[...].T.astype(LOW)
    grad_values[...] = sum_values[...].T.astype(LOW)


def attend_backward(query, keys, values, table, total, grad_mixed):
    tokens = query.shape[0]
    pslice = tokens - CLEN
    block = lambda rows: pl.BlockSpec((rows, 128), lambda i: (0, i))
    return pl.pallas_call(
        functools.partial(attend_back_kernel, pslice),
        grid=(HEADS // 2,),
        out_shape=(
            jax.ShapeDtypeStruct((tokens, D), LOW),
            jax.ShapeDtypeStruct((KEYS, D), LOW),
            jax.ShapeDtypeStruct((KEYS, D), LOW),
            jax.ShapeDtypeStruct(table.shape, F32),
        ),
        in_specs=[
            block(tokens),
            block(KEYS),
            block(KEYS),
            whole(table.shape),
            block(tokens),
            block(tokens),
        ],
        out_specs=(block(tokens), block(KEYS), block(KEYS), whole(table.shape)),
        scratch_shapes=[
            pltpu.VMEM((128, STRIP), F32),
            pltpu.VMEM((tokens, KEYS), F32),
            pltpu.VMEM((tokens, KEYS), F32),
            pltpu.VMEM((tokens, KEYS), LOW),
            pltpu.VMEM((tokens, KEYS), LOW),
            pltpu.VMEM((128, STRIP), F32),
            pltpu.VMEM((128, KEYS), F32),
            pltpu.VMEM((128, KEYS), F32),
        ],
        compiler_params=params(32),
    )(query, keys, values, table, total, grad_mixed)


def mlp_forward_kernel(state, gain, first, second, result, normed):
    step = pl.program_id(0)

    @pl.when(step == 0)
    def _():
        normed[...] = norm_rows(state[...], gain[...]).astype(LOW)
        result[...] = state[...]

    active = gelu(dot_low(normed[...], first[...])).astype(LOW)
    result[...] += dot_low(active, second[...])


def mlp_forward(state, gain, first, second):
    tokens = state.shape[0]
    part = 768
    return pl.pallas_call(
        mlp_forward_kernel,
        grid=(FF // part,),
        out_shape=(
            jax.ShapeDtypeStruct((tokens, D), F32),
            jax.ShapeDtypeStruct((tokens, D), LOW),
        ),
        in_specs=[
            whole((tokens, D)),
            whole((1, D)),
            pl.BlockSpec((D, part), lambda i: (0, i)),
            pl.BlockSpec((part, D), lambda i: (i, 0)),
        ],
        out_specs=(whole((tokens, D)), whole((tokens, D))),
        compiler_params=params(32),
    )(state, gain, first, second)


def mlp_backward_kernel(
    grad_next, state, normed, gain, first, second, result, grad_gain, grad_first, grad_second, low, total
):
    step = pl.program_id(0)

    @pl.when(step == 0)
    def _():
        low[...] = grad_next[...].astype(LOW)
        total[...] = jnp.zeros_like(total)

    active, slope = gelu_parts(dot_low(normed[...], first[...]))
    grad_hidden = (slope * dot_back(low[...], second[...])).astype(LOW)
    grad_second[...] = dot_over(active.astype(LOW), low[...]).astype(LOW)
    grad_first[...] = dot_over(normed[...], grad_hidden).astype(LOW)
    total[...] += dot_back(grad_hidden, first[...])

    @pl.when(step == pl.num_programs(0) - 1)
    def _():
        grad_state, grad_line = norm_back(state[...], gain[...], total[...])
        result[...] = grad_next[...] + grad_state
        grad_gain[...] = grad_line


def mlp_backward(grad_next, state, normed, gain, first, second):
    tokens = state.shape[0]
    part = 768
    return pl.pallas_call(
        mlp_backward_kernel,
        grid=(FF // part,),
        out_shape=(
            jax.ShapeDtypeStruct((tokens, D), F32),
            jax.ShapeDtypeStruct((1, D), F32),
            jax.ShapeDtypeStruct((D, FF), LOW),
            jax.ShapeDtypeStruct((FF, D), LOW),
        ),
        in_specs=[
            whole((tokens, D)),
            whole((tokens, D)),
            whole((tokens, D)),
            whole((1, D)),
            pl.BlockSpec((D, part), lambda i: (0, i)),
            pl.BlockSpec((part, D), lambda i: (i, 0)),
        ],
        out_specs=(
            whole((tokens, D)),
            whole((1, D)),
            pl.BlockSpec((D, part), lambda i: (0, i)),
            pl.BlockSpec((part, D), lambda i: (i, 0)),
        ),
        scratch_shapes=[pltpu.VMEM((tokens, D), LOW), pltpu.VMEM((tokens, D), F32)],
        compiler_params=params(48),
    )(grad_next, state, normed, gain, first, second)


def expert_kernel(
    rows, cotangent, gate, first, second, result, grad_rows, grad_gate, grad_first, grad_second, upstream, total, back
):
    step = pl.program_id(0)

    @pl.when(step == 0)
    def _():
        upstream[...] = (gate[:, :1] * cotangent[...].astype(F32)).astype(LOW)
        total[...] = jnp.zeros_like(total)
        back[...] = jnp.zeros_like(back)

    active, slope = gelu_parts(dot_low(rows[...], first[...]))
    active = active.astype(LOW)
    total[...] += dot_low(active, second[...])
    grad_hidden = (slope * dot_back(upstream[...], second[...])).astype(LOW)
    grad_second[...] = dot_over(active, upstream[...]).astype(LOW)
    grad_first[...] = dot_over(rows[...], grad_hidden).astype(LOW)
    back[...] += dot_back(grad_hidden, first[...])

    @pl.when(step == pl.num_programs(0) - 1)
    def _():
        low = total[...].astype(LOW)
        result[...] = low
        grad_rows[...] = back[...].astype(LOW)
        reach = jnp.sum(cotangent[...].astype(F32) * low.astype(F32), -1, keepdims=True)
        grad_gate[...] = jnp.broadcast_to(reach, grad_gate.shape)


def expert_pass(rows, cotangent, gate, first, second):
    count = rows.shape[0]
    shards, _, width = first.shape
    part = 256
    split = width // part
    inner = pl.BlockSpec((None, D, part), lambda i: (i // split, 0, i % split))
    outer = pl.BlockSpec((None, part, D), lambda i: (i // split, i % split, 0))
    return pl.pallas_call(
        expert_kernel,
        grid=(shards * split,),
        out_shape=(
            jax.ShapeDtypeStruct((count, D), LOW),
            jax.ShapeDtypeStruct((count, D), LOW),
            jax.ShapeDtypeStruct((count, 128), F32),
            jax.ShapeDtypeStruct(first.shape, LOW),
            jax.ShapeDtypeStruct(second.shape, LOW),
        ),
        in_specs=[whole((count, D)), whole((count, D)), whole((count, 128)), inner, outer],
        out_specs=(whole((count, D)), whole((count, D)), whole((count, 128)), inner, outer),
        scratch_shapes=[
            pltpu.VMEM((count, D), LOW),
            pltpu.VMEM((count, D), F32),
            pltpu.VMEM((count, D), F32),
        ],
        compiler_params=params(56),
    )(rows, cotangent, gate, first, second)


def split_low(values):
    high = values.astype(LOW)
    rest = values - high.astype(F32)
    middle = rest.astype(LOW)
    return high, middle, (rest - middle.astype(F32)).astype(LOW)


def exchange(block):
    return lax.all_to_all(block, ("dp", "col"), split_axis=0, concat_axis=0, tiled=True)


def attention_forward(state, gain, others, weight_in, weight_out, table, raw_others):
    tokens = state.shape[0]
    pslice = tokens - CLEN
    normed = norm_rows(state, gain).astype(LOW)
    if others is None:
        shared = lax.all_gather(normed[:pslice], "row", axis=0, tiled=True)
    else:
        shared = norm_rows(others.astype(F32), gain).astype(LOW)
    read = jnp.concatenate([shared, normed[pslice:]], 0)
    query = dot_low(normed, weight_in[:, :D]).astype(LOW)
    keys = dot_low(read, weight_in[:, D : 2 * D]).astype(LOW)
    values = dot_low(read, weight_in[:, 2 * D :]).astype(LOW)
    mixed, total = attend_forward(query, keys, values, table)
    return state + dot_low(mixed, weight_out), (state, normed, read, query, keys, values, mixed, total)


def attention_backward(grad_next, stash, gain, weight_in, weight_out, table, hot):
    state, normed, read, query, keys, values, mixed, total = stash
    pslice = state.shape[0] - CLEN
    branch = grad_next.astype(LOW)
    grad_out = dot_over(mixed, branch).astype(LOW)
    grad_mixed = dot_back(branch, weight_out).astype(LOW)
    grad_query, grad_keys, grad_values, grad_table = attend_backward(
        query, keys, values, table, total, grad_mixed
    )
    grad_in = jnp.concatenate(
        [dot_over(normed, grad_query), dot_over(read, grad_keys), dot_over(read, grad_values)], 1
    ).astype(LOW)
    grad_read = dot_back(grad_keys, weight_in[:, D : 2 * D]) + dot_back(
        grad_values, weight_in[:, 2 * D :]
    )
    own = lax.psum_scatter(
        grad_read[:PLEN].astype(LOW), "row", scatter_dimension=0, tiled=True
    ).astype(F32)
    grad_normed = dot_back(grad_query, weight_in[:, :D]) + jnp.concatenate(
        [own, grad_read[PLEN:]], 0
    )
    grad_state, grad_gain = norm_back(state, gain, grad_normed)
    grad_rel = jnp.dot(grad_table[:HEADS], hot.astype(F32), precision=HIGH).T
    return grad_next + grad_state, grad_in, grad_out, grad_rel, grad_gain


def general(
    inputs,
    cotangent,
    routes,
    buckets,
    norm_gains,
    attn_qkv,
    attn_out,
    rel_bias,
    mlp_in,
    mlp_out,
    router,
    expert_in,
    expert_out,
):
    grid = ("row", "col")
    places = lax.axis_size(grid)
    experts = lax.axis_size(("dp", "col"))
    tokens = inputs.shape[1]
    pslice = tokens - CLEN
    capacity = max(2, 3 * tokens // experts)

    small = [norm_gains.reshape(-1), rel_bias.reshape(-1), router.reshape(-1)]
    cuts = [part.shape[0] for part in small]
    packed = jnp.concatenate(small)
    packed = jnp.pad(packed, (0, -packed.shape[0] % 1024)).reshape(-1, 128)
    packed = lax.all_gather(packed, grid, axis=0, tiled=False).reshape(places, -1)
    gains = packed[:, : cuts[0]].reshape(places, 4, -1).transpose(1, 0, 2).reshape(4, 1, D).astype(F32)
    rel = packed[:, cuts[0] : cuts[0] + cuts[1]].reshape(places, 2, -1, HEADS)
    rel = rel.transpose(1, 0, 2, 3).reshape(2, BUCKETS, HEADS)
    route_w = packed[:, cuts[0] + cuts[1] : sum(cuts)].reshape(D, experts)

    qkv = [lax.all_gather(attn_qkv[i], grid, axis=0, tiled=True) for i in range(2)]
    out = [lax.all_gather(attn_out[i], grid, axis=0, tiled=True) for i in range(2)]
    dense_in = lax.all_gather(mlp_in, grid, axis=0, tiled=True)
    dense_out = lax.all_gather(mlp_out, grid, axis=0, tiled=True)
    first = lax.all_gather(expert_in[0], "row", axis=0, tiled=False)
    second = lax.all_gather(expert_out[0], "row", axis=0, tiled=False)

    hot, floor = bias_table(buckets, rel)
    tables = [
        jnp.pad(dot_low(rel[i].T, hot.T) + floor[None], ((0, 16 - HEADS), (0, 0))) for i in range(2)
    ]

    flat = routes[0].reshape(-1)
    levels = jnp.arange(experts, dtype=jnp.int32)
    choose = (routes[0][:, :, None] == levels[None, None, :]).astype(F32)
    hits = (flat[:, None] == levels[None, :]).astype(LOW)
    before = jnp.arange(2 * tokens)
    before = (before[:, None] > before[None, :]).astype(LOW)
    rank = jnp.sum(dot_low(before, hits) * hits.astype(F32), 1).astype(jnp.int32)
    place = (flat * capacity + rank).reshape(tokens, 2)
    slots = jnp.arange(experts * capacity, dtype=jnp.int32)
    picks = [(place[:, k][:, None] == slots[None, :]).astype(LOW) for k in range(2)]
    both = picks[0] + picks[1]
    sent_cotangent = dot_over(both, cotangent[0]).astype(LOW).reshape(experts, capacity, D)
    far_cotangent = exchange(sent_cotangent).reshape(experts * capacity, D)

    state0 = inputs[0].astype(F32)
    shared0 = lax.all_gather(inputs[0, :pslice], "row", axis=0, tiled=True)
    state1, stash1 = attention_forward(state0, gains[0], shared0, qkv[0], out[0], tables[0], None)
    state2, normed1 = mlp_forward(state1, gains[1], dense_in, dense_out)
    state3, stash3 = attention_forward(state2, gains[2], None, qkv[1], out[1], tables[1], None)

    normed3 = norm_rows(state3, gains[3]).astype(LOW)
    logits = dot_low(normed3, route_w)
    picked = jnp.sum(choose * logits[:, None, :], -1)
    raised = jnp.exp(picked - jnp.max(picked, -1, keepdims=True))
    gates = raised / jnp.sum(raised, -1, keepdims=True)
    parts = [split_low(gates[:, k]) for k in range(2)]
    spread = [
        dot_over(picks[k], jnp.pad(jnp.stack(parts[k], 1), ((0, 0), (0, 125)))) for k in range(2)
    ]
    sent = jnp.concatenate([dot_over(both, normed3), spread[0] + spread[1]], 1).astype(LOW)
    received = exchange(sent.reshape(experts, capacity, D + 128)).reshape(experts * capacity, D + 128)
    far_gate = jnp.sum(received[:, D : D + 3].astype(F32), 1, keepdims=True)
    far_gate = jnp.broadcast_to(far_gate, (experts * capacity, 128))
    result, grad_rows, grad_gate, grad_first, grad_second = expert_pass(
        received[:, :D], far_cotangent, far_gate, first, second
    )
    reach = jnp.pad(jnp.stack(split_low(grad_gate[:, 0]), 1), ((0, 0), (0, 125)))
    returned = exchange(
        jnp.concatenate([grad_rows, reach], 1).reshape(experts, capacity, D + 128)
    ).reshape(experts * capacity, D + 128)
    outcome = exchange(result.reshape(experts, capacity, D)).reshape(experts * capacity, D)
    output = state3 + sum(gates[:, k : k + 1] * dot_low(picks[k], outcome) for k in range(2))

    grad_gates = jnp.stack(
        [jnp.sum(dot_low(picks[k], returned[:, D:]), 1) for k in range(2)], 1
    )
    grad_picked = gates * (grad_gates - jnp.sum(gates * grad_gates, -1, keepdims=True))
    grad_logits = jnp.sum(choose * grad_picked[:, :, None], 1).astype(LOW)
    grad_route = dot_over(normed3, grad_logits)
    grad_normed3 = dot_low(both, returned[:, :D]) + dot_back(grad_logits, route_w)
    upstream = cotangent[0].astype(F32)
    grad_state3, gain_last = norm_back(state3, gains[3], grad_normed3)
    grad3 = upstream + grad_state3
    own_first = lax.psum_scatter(grad_first, "row", scatter_dimension=0, tiled=False)
    own_second = lax.psum_scatter(grad_second, "row", scatter_dimension=0, tiled=False)

    grad2, qkv_late, out_late, rel_late, gain_third = attention_backward(
        grad3, stash3, gains[2], qkv[1], out[1], tables[1], hot
    )
    grad1, gain_second, dense_grad_in, dense_grad_out = mlp_backward(
        grad2, state1, normed1, gains[1], dense_in, dense_out
    )
    grad0, qkv_early, out_early, rel_early, gain_first = attention_backward(
        grad1, stash1, gains[0], qkv[0], out[0], tables[0], hot
    )

    def share(block):
        block = lax.psum_scatter(block.astype(LOW), grid, scatter_dimension=0, tiled=True)
        return lax.psum(block, "dp").astype(F32)

    gain_grads = jnp.concatenate([gain_first, gain_second, gain_third, gain_last], 0)
    gain_grads = gain_grads.reshape(4, places, -1).transpose(1, 0, 2).reshape(places, -1)
    rel_grads = jnp.stack([rel_early, rel_late]).reshape(2, places, -1, HEADS)
    rel_grads = rel_grads.transpose(1, 0, 2, 3).reshape(places, -1)
    packed = jnp.concatenate([gain_grads, rel_grads, grad_route.reshape(places, -1)], 1)
    packed = jnp.pad(packed, ((0, 0), (0, -packed.shape[1] % 1024))).reshape(-1, 128)
    packed = share(packed).reshape(-1)
    gain_share = packed[: cuts[0]].reshape(4, -1)
    rel_share = packed[cuts[0] : cuts[0] + cuts[1]].reshape(2, -1, HEADS)
    route_share = packed[cuts[0] + cuts[1] : sum(cuts)].reshape(-1, experts)
    return (
        output[None],
        grad0[None],
        gain_share,
        jnp.stack([share(qkv_early), share(qkv_late)]),
        jnp.stack([share(out_early), share(out_late)]),
        rel_share,
        share(dense_grad_in),
        share(dense_grad_out),
        route_share,
        own_first.astype(F32)[None],
        own_second.astype(F32)[None],
    )


def once(shape):
    return pl.BlockSpec(shape, lambda *_: (0,) * len(shape), pipeline_mode=pl.Buffered(1))


def head_block(cols, piece, index):
    return pl.BlockSpec((4, cols, piece, 128), lambda i: (0, 0, 0, 6 * index + i))


def outer_block(cols, piece):
    return once((4, cols, piece, D))


def strip_block():
    return pl.BlockSpec((2, 128, STRIP), lambda i: (i, 0, 0))


def line_block(index, shape):
    return pl.BlockSpec(
        (None,) + shape, lambda i: (index,) + (0,) * len(shape), pipeline_mode=pl.Buffered(1)
    )


def up_kernel(
    raw_rows,
    pslice,
    state,
    own,
    shared,
    gain,
    table,
    wq,
    wk,
    wv,
    wo,
    result,
    normed,
    read,
    query,
    keys,
    values,
    mixed,
    total,
    strips,
    raw,
    weights,
    outer,
):
    pair = pl.program_id(0)
    lane = lax.broadcasted_iota(jnp.int32, (1, 128), 1)

    @pl.when(pair == 0)
    def _():
        weights[:pslice, PLEN:] = jnp.zeros((pslice, CLEN), LOW)
        outer[...] = wo[...].reshape(D, D)
        result[...] = state[...].astype(F32)
        if raw_rows:
            normed[...] = norm_rows(own[...].astype(F32), gain[...]).astype(LOW)
            for i in range(PLEN // pslice):
                rows = pl.ds(i * pslice, pslice)
                read[rows, :] = norm_rows(shared[i].astype(F32), gain[...]).astype(LOW)
        else:
            normed[...] = own[...]
            for i in range(PLEN // pslice):
                read[pl.ds(i * pslice, pslice), :] = shared[i]
        read[PLEN:, :] = normed[pslice:, :]

    query[...] = dot_low(normed[...], wq[...].reshape(D, 128)).astype(LOW)
    both = jnp.concatenate([wk[...].reshape(D, 128), wv[...].reshape(D, 128)], 1)
    both = dot_low(read[...], both).astype(LOW)
    keys[...] = both[:, :128]
    values[...] = both[:, 128:]

    for half in range(2):
        mine = (lane < HDIM) if half == 0 else (lane >= HDIM)
        line = jnp.broadcast_to(table[pl.ds(2 * pair + half, 1), :], (128, WRAP))
        line = pltpu.roll(line, 0, 1, stride=1, stride_axis=0)[:, :KEYS]
        strips[half, :, :KEYS] = line.astype(LOW)
        strips[half, :, KEYS:] = jnp.full((128, STRIP - KEYS), NEG, LOW)
        part = jnp.where(mine, query[...], 0) * HDIM ** (-0.5)
        raw[...] = dot_back(part.astype(LOW), keys[...])
        for row, place, count in tiles_of(pslice):
            rows = pl.ds(row, 128)
            scores = raw[rows, :count] + strips[half, :, place].astype(F32)
            top = jnp.max(scores, -1, keepdims=True)
            raised = jnp.exp(scores - top)
            summed = jnp.sum(raised, -1, keepdims=True)
            weights[rows, :count] = (raised * (1.0 / summed)).astype(LOW)
            log_total = jnp.broadcast_to(top + jnp.log(summed), (128, 128))
            if half == 0:
                total[rows, :] = log_total
            else:
                total[rows, :] = jnp.where(mine, log_total, total[rows, :])
        part = dot_low(weights[...], values[...]).astype(LOW)
        if half == 0:
            mixed[...] = part
        else:
            mixed[...] = jnp.where(mine, part, mixed[...])
    result[...] += dot_low(mixed[...], outer[pl.ds(pl.multiple_of(pair * 128, 128), 128), :])


def route_rows(routes, cotangent, picks, sent):
    tokens = routes.shape[0]
    slots, capacity, _ = sent.shape
    dp, col = lax.axis_index("dp"), lax.axis_index("col")
    lanes = lax.broadcasted_iota(jnp.int32, (tokens, 128), 1)
    slot, hot = [], []
    for k in range(2):
        expert = routes[:, k : k + 1]
        slot.append(2 * ((expert & 3) ^ col) + ((expert >> 2) ^ dp))
        hot.append(jnp.where(slot[k] == lanes, 1.0, 0.0))
    up = lax.broadcasted_iota(jnp.int32, (tokens, tokens), 0)
    along = lax.broadcasted_iota(jnp.int32, (tokens, tokens), 1)
    before = dot_low(jnp.where(up > along, 1.0, 0.0).astype(LOW), (hot[0] + hot[1]).astype(LOW))
    spots = lax.broadcasted_iota(jnp.int32, (tokens, slots * capacity), 1).astype(F32)
    for k in range(2):
        rank = jnp.sum(before * hot[k], -1, keepdims=True)
        place = slot[k].astype(F32) * capacity + rank
        picks[k] = jnp.where(place == spots, 1.0, 0.0).astype(LOW)
    both = picks[0] + picks[1]
    sent[...] = dot_over(both, cotangent[...]).astype(LOW).reshape(sent.shape)


def laid_lanes(columns, tokens):
    lanes = lax.broadcasted_iota(jnp.int32, (tokens, 128), 1)
    laid = jnp.zeros((tokens, 128), F32)
    for i, column in enumerate(columns):
        laid = jnp.where(lanes == i, column, laid)
    return laid


def chosen(routes):
    lanes = lax.broadcasted_iota(jnp.int32, (routes.shape[0], 128), 1)
    return [jnp.where(routes[:, k : k + 1] == lanes, 1.0, 0.0) for k in range(2)]


def send_rows(state, gain, route_w, routes, picks, normed, gates, line, sent):
    tokens = routes.shape[0]
    slots, capacity, _ = sent.shape
    shift = pl.multiple_of((pl.program_id(0) - (pl.num_programs(0) - 1)) * 8, 8)
    normed[...] = norm_rows(state[pl.ds(shift, tokens), :], gain[...]).astype(LOW)
    logits = dot_low(normed[...], route_w[...])
    picked = [jnp.sum(hot * logits, -1, keepdims=True) for hot in chosen(routes)]
    top = jnp.maximum(picked[0], picked[1])
    raised = [jnp.exp(value - top) for value in picked]
    gate = [value / (raised[0] + raised[1]) for value in raised]
    gates[...] = laid_lanes(gate, tokens)
    total = 0.0
    for k in range(2):
        parts = laid_lanes([part.astype(F32) for part in split_low(gate[k])], tokens).astype(LOW)
        total = total + jnp.sum(dot_over(parts, picks[k]), 0, keepdims=True)
    for slot in range(slots):
        part = total[:, slot * capacity : (slot + 1) * capacity]
        part = jnp.pad(part, ((0, 0), (0, line.shape[2] - capacity)))
        line[slot] = jnp.broadcast_to(part, line.shape[1:])
    sent[...] = dot_over(picks[0] + picks[1], normed[...]).astype(LOW).reshape(sent.shape)


def take_rows(
    cotangent, returned, reach, picks, gates, normed, routes, route_w, state, gain, grad_gain, grad_route, result
):
    tokens = routes.shape[0]
    capacity = picks.shape[2] // reach.shape[0]
    line = jnp.concatenate([reach[slot, :1, :capacity] for slot in range(reach.shape[0])], 1)
    gate = [gates[:, k : k + 1] for k in range(2)]
    met = [jnp.sum(picks[k].astype(F32) * line, -1, keepdims=True) for k in range(2)]
    centre = gate[0] * met[0] + gate[1] * met[1]
    hots = chosen(routes)
    slopes = sum(hots[k] * (gate[k] * (met[k] - centre)) for k in range(2)).astype(LOW)
    grad_route[...] = dot_over(slopes, normed[...])[: grad_route.shape[0]]
    grad_normed = dot_low(picks[0] + picks[1], returned[...]) + dot_back(slopes, route_w[...])
    grad_state, grad_line = norm_back(state[...], gain[...], grad_normed)
    result[...] = cotangent[...].astype(F32) + grad_state
    grad_gain[...] = grad_line


def attention_up(
    state, own, shared, layer_index, gains, tables, inner, output, moves, sources, name, more=()
):
    tokens = own.shape[0]
    pslice = tokens - CLEN
    _, cols, piece, _ = inner.shape
    raw_rows = layer_index == 0
    slots = lax.axis_size(("dp", "col"))
    capacity = 3 * tokens // slots
    more_specs = [once(block.shape) for block in more]
    if not raw_rows:
        more_specs[0] = line_block(3, (1, D))
    if raw_rows:
        more_out = [
            jax.ShapeDtypeStruct((2, tokens, slots * capacity), LOW),
            jax.ShapeDtypeStruct((slots, capacity, D), LOW),
        ]
    else:
        more_out = [
            jax.ShapeDtypeStruct((tokens, D), LOW),
            jax.ShapeDtypeStruct((tokens, 128), F32),
            jax.ShapeDtypeStruct((slots, 8, capacity + -capacity % 128), F32),
            jax.ShapeDtypeStruct((slots, capacity, D), LOW),
        ]

    def body(*refs):
        refs = list(refs)
        given = [refs.pop(9) for _ in more]
        found = [refs.pop(18) for _ in more_out]
        up_kernel(raw_rows, pslice, *refs)

        @pl.when(pl.program_id(0) == (1 if raw_rows else pl.num_programs(0) - 1))
        def _():
            if raw_rows:
                route_rows(*given, *found)
            else:
                send_rows(refs[9], *given, *found)
    block = lambda rows: pl.BlockSpec((rows, 128), lambda i: (0, i))
    low = lambda rows: jax.ShapeDtypeStruct((rows, D), LOW)
    result, normed, read, query, keys, values, mixed, total, strips, *moved = carry(
        body,
        moves,
        grid=(HEADS // 2,),
        out_shape=(
            jax.ShapeDtypeStruct((tokens, D), F32),
            low(tokens),
            low(KEYS),
            low(tokens),
            low(KEYS),
            low(KEYS),
            low(tokens),
            jax.ShapeDtypeStruct((tokens, D), F32),
            jax.ShapeDtypeStruct((HEADS, 128, STRIP), LOW),
            *more_out,
        ),
        in_specs=[
            once((tokens, D)),
            once((tokens, D)),
            once(shared.shape),
            line_block(2 * layer_index, (1, D)),
            line_block(layer_index, tables.shape[1:]),
            head_block(cols, piece, 0),
            head_block(cols, piece, 1),
            head_block(cols, piece, 2),
            outer_block(cols, piece),
            *more_specs,
        ],
        out_specs=(
            whole((tokens, D)),
            whole((tokens, D)),
            whole((KEYS, D)),
            block(tokens),
            block(KEYS),
            block(KEYS),
            block(tokens),
            block(tokens),
            strip_block(),
            *[once(out.shape) for out in more_out],
        ),
        scratch_shapes=[
            pltpu.VMEM((tokens, KEYS), F32),
            pltpu.VMEM((tokens, KEYS), LOW),
            pltpu.VMEM((D, D), LOW),
        ],
        mib=60,
        name=name,
    )(state, own, shared, gains, tables, inner, inner, inner, output, *more, *sources)
    stash = (normed, read, query, keys, values, mixed, total, strips, inner, output)
    return result, stash, moved[: len(more_out)], moved[len(more_out) :]


def slide_sum(grid):
    rows = grid.shape[0]
    while rows > 8:
        rows = rows // 2
        grid = grid[:rows] + pltpu.roll(grid[rows:], WRAP - rows, 1)
    for step in (4, 2, 1):
        grid = grid + pltpu.roll(pltpu.roll(grid, 8 - step, 0), WRAP - step, 1)
    return grid[:1]


def down_kernel(
    pslice,
    grad_next,
    state,
    gain,
    normed,
    read,
    query,
    keys,
    values,
    mixed,
    total,
    strips,
    wq,
    wk,
    wv,
    wo,
    result,
    grad_gain,
    grads,
    grad_table,
    low,
    outer,
    grad_outer,
    sum_own,
    sum_read,
    spill,
    raw,
    pulled,
    probs,
    slopes,
    folded,
    sum_keys,
    sum_values,
):
    pair = pl.program_id(0)
    lane = lax.broadcasted_iota(jnp.int32, (1, 128), 1)
    here = pl.ds(pl.multiple_of(pair * 128, 128), 128)

    @pl.when(pair == 0)
    def _():
        probs[:pslice, PLEN:] = jnp.zeros((pslice, CLEN), LOW)
        slopes[:pslice, PLEN:] = jnp.zeros((pslice, CLEN), LOW)
        low[...] = grad_next[...].astype(LOW)
        outer[...] = wo[...].reshape(D, D)
        sum_own[...] = jnp.zeros_like(sum_own)
        sum_read[...] = jnp.zeros_like(sum_read)

    grad_outer[here, :] = dot_over(mixed[...], low[...]).astype(LOW)
    grad_mixed = dot_back(low[...], outer[here, :]).astype(LOW)
    for half in range(2):
        mine = (lane < HDIM) if half == 0 else (lane >= HDIM)
        part = (jnp.where(mine, query[...], 0) * HDIM ** (-0.5)).astype(LOW)
        upstream = jnp.where(mine, grad_mixed, 0).astype(LOW)
        raw[...] = dot_back(part, keys[...])
        pulled[...] = dot_back(upstream, values[...])
        folded[...] = jnp.zeros_like(folded)
        for row, place, count in tiles_of(pslice):
            rows = pl.ds(row, 128)
            log_total = total[rows, half * HDIM : half * HDIM + 1]
            scores = raw[rows, :count] + strips[half, :, place].astype(F32)
            chance = jnp.exp(scores - log_total)
            product = chance * pulled[rows, :count]
            centre = jnp.sum(product, -1, keepdims=True)
            slope = (product - chance * centre).astype(LOW)
            probs[rows, :count] = chance.astype(LOW)
            slopes[rows, :count] = slope
            folded[:, place] += slope.astype(F32)
        step = (dot_low(slopes[...], keys[...]) * HDIM ** (-0.5)).astype(LOW)
        if half == 0:
            grad_query = step
            sum_keys[...] = dot_over(part, slopes[...])
            sum_values[...] = dot_over(upstream, probs[...])
        else:
            grad_query = jnp.where(mine, step, grad_query)
            sum_keys[...] += dot_over(part, slopes[...])
            sum_values[...] += dot_over(upstream, probs[...])
        grad_table[pl.ds(2 * pair + half, 1), :] = slide_sum(folded[:, :WRAP])

    shape = grads.shape[:2] + grads.shape[3:4] + (128,)

    def keep(index, turned):
        grads[:, :, index, :, here] = turned.T.astype(LOW).reshape(shape)

    keep(0, dot_over(grad_query, normed[...]))
    keep(1, dot_low(sum_keys[...].astype(LOW), read[...]))
    keep(2, dot_low(sum_values[...].astype(LOW), read[...]))
    sum_own[...] += dot_back(grad_query, wq[...].reshape(D, 128))
    pairs = jnp.concatenate([sum_keys[...].T, sum_values[...].T], 1).astype(LOW)
    both = jnp.concatenate([wk[...].reshape(D, 128), wv[...].reshape(D, 128)], 1)
    sum_read[...] += dot_back(pairs, both)

    @pl.when(pair == pl.num_programs(0) - 1)
    def _():
        grads[:, :, 3] = grad_outer[...].reshape(shape[:3] + (D,))
        spill[...] = sum_read[:PLEN, :].astype(LOW).reshape(spill.shape)


def down_after(pslice, fill, own_in, own_out, extras, results):
    grad_next, state, gain = own_in[:3]
    if not fill:
        grad_next = extras[-1]
    result, grad_gain = own_out[:2]
    sum_own, sum_read = extras[3:5]
    shift = (pl.program_id(0) - (pl.num_programs(0) - 1)) * 8
    lines = 0.0
    for row, count in ((0, pslice), (pslice, CLEN)):
        rows = pl.ds(pl.multiple_of(row + shift, 8), count)
        if row == 0:
            more = results[0][...].reshape(pslice, D)
        else:
            more = sum_read[pl.ds(pl.multiple_of(PLEN + shift, 8), CLEN), :]
        grad_state, line = norm_back(state[rows, :].astype(F32), gain[...], sum_own[rows, :] + more)
        result[rows, :] = grad_next[rows, :] + grad_state
        lines = lines + line
    grad_gain[...] = lines
    if fill:
        first = lax.broadcasted_iota(jnp.int32, (16, 1), 0) == 0
        extras[-1][...] = jnp.where(first, lines, 0.0).astype(LOW)


def attention_down(
    grad_next, state, gains, layer_index, stash, moves, sources, name, known=None
):
    normed, read, query, keys, values, mixed, total, strips, inner, output = stash
    tokens = normed.shape[0]
    pslice = tokens - CLEN
    _, cols, piece, _ = inner.shape
    table = jax.ShapeDtypeStruct((16, WRAP), F32)
    block = lambda rows: pl.BlockSpec((rows, 128), lambda i: (0, i))
    rows = Reduce(
        (pslice // 16, 16, D), ("core", "x"), take=lambda outs, extras: extras[5], keep=True
    )
    share = (4, cols, 4, piece, D)
    body, shown, extra = down_kernel, [jax.ShapeDtypeStruct(share, LOW)], []
    more, more_specs = [], []
    last = known is not None
    ends = []
    if not last:
        (grad_next, *ends) = grad_next

        def body(pslice, *refs):
            refs = list(refs)
            given = [refs.pop(15) for _ in ends]
            found = [refs.pop(19) for _ in range(2)]
            formed = refs.pop()

            @pl.when(pl.program_id(0) == 0)
            def _():
                take_rows(refs[0], *given, *found, formed)

            down_kernel(pslice, formed, *refs[1:])

        shown = [jax.ShapeDtypeStruct(share, LOW)]
        extra = [pltpu.VMEM((tokens, D), F32)]
        more, more_specs = list(ends), [once(block.shape) for block in ends]
        more_specs[-1] = line_block(3, (1, D))
    if last:
        def body(pslice, *refs):
            refs = list(refs)
            known_lines, small = refs.pop(15), refs[-2]
            down_kernel(pslice, *refs[:17], refs[-3], refs[17], *refs[18:-3])

            @pl.when(pl.program_id(0) == pl.num_programs(0) - 1)
            def _():
                small[:16, :] = refs[17][...].astype(LOW)
                small[16:, :] = known_lines[...]

        shown = []
        extra = [
            pltpu.VMEM(share, LOW),
            pltpu.VMEM((16 + known.shape[0], WRAP), LOW),
            pltpu.VMEM((16, D), LOW),
        ]
        more, more_specs = [known], [once(known.shape)]
    return carry(
        functools.partial(body, pslice),
        [(rows, (LATE, LATE + 2, LATE + 4))] + moves,
        grid=(HEADS // 2,),
        out_shape=(
            jax.ShapeDtypeStruct((tokens, D), F32),
            jax.ShapeDtypeStruct((1, D), F32),
            *shown,
            jax.ShapeDtypeStruct(table.shape, F32),
            *([] if last else [jax.ShapeDtypeStruct((1, D), F32), jax.ShapeDtypeStruct((8, D), F32)]),
        ),
        in_specs=[
            once((tokens, D)),
            once((tokens, D)),
            line_block(2 * layer_index, (1, D)),
            once((tokens, D)),
            once((KEYS, D)),
            block(tokens),
            block(KEYS),
            block(KEYS),
            block(tokens),
            block(tokens),
            strip_block(),
            head_block(cols, piece, 0),
            head_block(cols, piece, 1),
            head_block(cols, piece, 2),
            outer_block(cols, piece),
            *more_specs,
        ],
        out_specs=(
            once((tokens, D)),
            once((1, D)),
            *[once(share) for _ in shown],
            once(table.shape),
            *([] if last else [once((1, D)), once((8, D))]),
        ),
        scratch_shapes=[
            pltpu.VMEM((tokens, D), LOW),
            pltpu.VMEM((D, D), LOW),
            pltpu.VMEM((D, D), LOW),
            pltpu.VMEM((tokens, D), F32),
            pltpu.VMEM((KEYS, D), F32),
            pltpu.VMEM((4, 1, pslice // 16, 16, D), LOW),
            pltpu.VMEM((tokens, KEYS), F32),
            pltpu.VMEM((tokens, KEYS), F32),
            pltpu.VMEM((tokens, KEYS), LOW),
            pltpu.VMEM((tokens, KEYS), LOW),
            pltpu.VMEM((128, STRIP), F32),
            pltpu.VMEM((128, KEYS), F32),
            pltpu.VMEM((128, KEYS), F32),
            *extra,
        ],
        mib=62,
        name=name,
        after=(LATE + 4.5, functools.partial(down_after, pslice, last)),
    )(
        grad_next,
        state,
        gains,
        normed,
        read,
        query,
        keys,
        values,
        mixed,
        total,
        strips,
        inner,
        inner,
        inner,
        output,
        *more,
        *sources,
    )


def mlp_up_kernel(state, gain, gain_next, first, second, result, normed, normed_next):
    step = pl.program_id(0)

    @pl.when(step == 0)
    def _():
        normed[...] = norm_rows(state[...], gain[...]).astype(LOW)
        result[...] = state[...]

    active = gelu(dot_low(normed[...], first[...].reshape(D, D))).astype(LOW)
    result[...] += dot_low(active, second[...].reshape(D, D))

    @pl.when(step == pl.num_programs(0) - 1)
    def _():
        normed_next[...] = norm_rows(result[...], gain_next[...]).astype(LOW)


def mlp_blocks(cols, piece):
    return (
        pl.BlockSpec((4, cols, piece, D), lambda i: (0, 0, 0, i)),
        pl.BlockSpec((None, cols, 4 * piece, D), lambda i: (i, 0, 0, 0)),
    )


def mlp_up(state, gains, dense_in, dense_out, moves, sources, name):
    tokens = state.shape[0]
    pslice = tokens - CLEN
    _, cols, piece, _ = dense_in.shape
    rows = Rows((pslice, D), take=lambda outs, extras: outs[2].at[pl.ds(0, pslice)])
    return carry(
        mlp_up_kernel,
        [(rows, (LATE,) * 3)] + moves,
        grid=(4,),
        out_shape=(
            jax.ShapeDtypeStruct((tokens, D), F32),
            jax.ShapeDtypeStruct((tokens, D), LOW),
            jax.ShapeDtypeStruct((tokens, D), LOW),
        ),
        in_specs=[
            once((tokens, D)),
            line_block(1, (1, D)),
            line_block(2, (1, D)),
            *mlp_blocks(cols, piece),
        ],
        out_specs=(whole((tokens, D)),) * 3,
        scratch_shapes=[],
        mib=60,
        name=name,
    )(state, gains, gains, dense_in, dense_out, *sources)


def mlp_down_kernel(
    grad_next,
    state,
    normed,
    gain,
    first,
    second,
    last_state,
    gates,
    picks,
    outcome,
    result,
    grad_gain,
    output,
    low,
    total,
    grads,
):
    step = pl.program_id(0)

    @pl.when(step == 0)
    def _():
        output[...] = last_state[...]

    @pl.when(step < 2)
    def _():
        gate = jnp.where(step == 0, gates[:, :1], gates[:, 1:2])
        output[...] += gate * dot_low(picks[step], outcome[...])

    @pl.when(step == 0)
    def _():
        low[...] = grad_next[...].astype(LOW)
        total[...] = jnp.zeros_like(total)

    inner, outer = first[...].reshape(D, D), second[...].reshape(D, D)
    active, slope = gelu_parts(dot_low(normed[...], inner))
    grad_hidden = (slope * dot_back(low[...], outer)).astype(LOW)
    _, cols, _, piece, _ = grads.shape
    grad_second = dot_over(active.astype(LOW), low[...]).astype(LOW)
    grads[step, :, :4] = grad_second.reshape(cols, 4, piece, D)
    grads[:, :, 4 + step] = dot_over(normed[...], grad_hidden).astype(LOW).reshape(4, cols, piece, D)
    total[...] += dot_back(grad_hidden, inner)

    @pl.when(step == pl.num_programs(0) - 1)
    def _():
        grad_state, grad_line = norm_back(state[...], gain[...], total[...])
        result[...] = grad_next[...] + grad_state
        grad_gain[...] = grad_line


def mlp_down(grad_next, state, normed, gains, dense_in, dense_out, ends, moves, sources, name):
    tokens = state.shape[0]
    _, cols, piece, _ = dense_in.shape
    pairs = CoreSum((piece, D), cols, lambda outs, extras: extras[2])
    return carry(
        mlp_down_kernel,
        [(pairs, (0, 1, 2, 3, LATE, LATE + 1))] + moves,
        grid=(4,),
        out_shape=(
            jax.ShapeDtypeStruct((tokens, D), F32),
            jax.ShapeDtypeStruct((1, D), F32),
            jax.ShapeDtypeStruct((tokens, D), F32),
        ),
        in_specs=[
            once((tokens, D)),
            once((tokens, D)),
            once((tokens, D)),
            line_block(1, (1, D)),
            *mlp_blocks(cols, piece),
            *[once(block.shape) for block in ends],
        ],
        out_specs=(once((tokens, D)), once((1, D)), once((tokens, D))),
        scratch_shapes=[
            pltpu.VMEM((tokens, D), LOW),
            pltpu.VMEM((tokens, D), F32),
            pltpu.VMEM((4, cols, 8, piece, D), LOW),
        ],
        mib=60,
        name=name,
    )(grad_next, state, normed, gains, dense_in, dense_out, *ends, *sources)


def routed_kernel(
    sent,
    sent_gates,
    sent_cotangent,
    first,
    second,
    outcome,
    returned,
    reach,
    grad_first,
    grad_second,
    rows,
    gates,
    cotangent,
    inner,
    outer,
    active_all,
    hidden_all,
    upstream,
    back,
    back_reach,
    turned,
    sum_up,
    sum_down,
    held,
    near,
    row_send,
    row_recv,
    gate_send,
    gate_recv,
    back_send,
    back_recv,
    reach_send,
    reach_recv,
    core_send,
    core_recv,
    local,
    store,
):
    capacity = rows.shape[1]
    barrier = pltpu.get_barrier_semaphore()
    others = range(1, len(SLOTS))
    row, across, core, plane = neighbours()
    c = lax.rem(row, 2)
    for slot in others:
        pl.semaphore_signal(barrier, inc=1, device_id=slot_device(slot), device_id_type=MESH)
    pl.semaphore_signal(barrier, inc=1, device_id=dict(row=core), device_id_type=MESH)
    loads = [
        Within(sent.at[0], rows.at[0], local.at[0]),
        Within(sent_gates.at[0], gates.at[0], local.at[1]),
        Within(sent_cotangent, cotangent, local.at[2]),
        Within(first, inner, local.at[3]),
        Within(second, outer, local.at[4]),
    ]
    for load in loads:
        load.start()
    pl.semaphore_wait(barrier, len(others) + 1)

    def there(slot):
        device = slot_device(slot)
        return (
            remote(sent_gates.at[slot], gates.at[slot], gate_send, gate_recv, slot, **device),
            remote(sent.at[slot], rows.at[slot], row_send, row_recv, slot, **device),
        )

    def home(slot):
        device = slot_device(slot)
        return (
            remote(back_reach.at[slot], reach.at[slot], reach_send, reach_recv, slot, **device),
            remote(back.at[slot], returned.at[slot], back_send, back_recv, slot, **device),
        )

    own_home = [
        Within(back_reach.at[0], reach.at[0], local.at[5]),
        Within(back.at[0], returned.at[0], local.at[6]),
    ]
    for slot in (4, 5, 1, 6, 7, 2, 3):
        for copy in there(slot):
            copy.start()
    for load in loads:
        load.wait()
    ones = jnp.ones((8, D), F32)
    count = 2 * capacity
    for b in (0, 2, 1, 3):
        for a in range(2):
            slot = 2 * b + a
            if slot:
                for copy in there(slot):
                    copy.wait_recv()
            gate = gates[slot].T[:capacity, :1]
            at = pl.ds(slot * capacity, capacity)
            upstream[at, :] = (gate * cotangent[slot].astype(F32)).astype(LOW)
        both = pl.ds(2 * b * capacity, count)
        block = rows[2 * b : 2 * b + 2].reshape(count, D)
        sum_up[...] = jnp.zeros_like(sum_up)
        sum_down[...] = jnp.zeros_like(sum_down)

        def part(j):
            active, slope = gelu_parts(dot_low(block, inner[j]))
            active = active.astype(LOW)
            active_all[j, both, :] = active
            sum_up[...] += dot_low(active, outer[j])
            hidden = (slope * dot_back(upstream[both, :], outer[j])).astype(LOW)
            hidden_all[j, both, :] = hidden
            sum_down[...] += dot_back(hidden, inner[j])

        each(4, part)
        back[2 * b : 2 * b + 2] = sum_down[...].astype(LOW).reshape(2, capacity, D)
        outcome[2 * b : 2 * b + 2] = sum_up[...].astype(LOW).reshape(2, capacity, D)
        for a in range(2):
            slot = 2 * b + a
            met = cotangent[slot].astype(F32) * outcome[slot].astype(F32)
            line = lax.dot_general(
                ones, met, (((1,), (1,)), ((), ())), precision=HIGH, preferred_element_type=F32
            )
            back_reach[slot] = jnp.pad(line, ((0, 0), (0, back_reach.shape[2] - capacity)))
            if slot:
                for copy in home(slot):
                    copy.start()
            else:
                for copy in own_home:
                    copy.start()
    turned[...] = rows[...].reshape(len(SLOTS) * capacity, D).T

    def formed(j):
        return dot_low(turned[...], hidden_all[j]), dot_over(active_all[j], upstream[...])

    def passed(i, k):
        return remote(held.at[i, k], near.at[i, k], core_send, core_recv, 2 * i + k, row=core)

    def stored(i, k):
        return Within(near.at[i, k], (grad_first, grad_second)[k].at[i], store.at[i, k])

    def give(i):
        for k, value in enumerate(formed(2 * i + 1 - c)):
            held[i, k] = value.astype(LOW)
            passed(i, k).start()

    def meet(i):
        for k, value in enumerate(formed(2 * i + c)):
            passed(i, k).wait_recv()
            near[i, k] = (value + near[i, k].astype(F32)).astype(LOW)
            stored(i, k).start()

    each(2, give)
    each(2, meet)
    for i in range(2):
        for k in range(2):
            stored(i, k).wait()
            passed(i, k).wait_send()
    for copy in own_home:
        copy.wait()
    for slot in (4, 5, 1, 6, 7, 2, 3):
        for copy in home(slot):
            copy.wait_recv()
    for slot in (4, 5, 1, 6, 7, 2, 3):
        for copy in there(slot) + home(slot):
            copy.wait_send()


def routed(sent, gates, cotangent, first, second, name):
    slots, capacity, _ = sent.shape
    hbm = pl.BlockSpec(memory_space=pl.ANY)
    count = slots * capacity
    low = jax.ShapeDtypeStruct(sent.shape, LOW)
    share = jax.ShapeDtypeStruct((2,) + first.shape[1:], LOW)
    pairs = [pltpu.SemaphoreType.DMA((slots,)) for _ in range(8)]
    return pl.pallas_call(
        routed_kernel,
        out_shape=(low, low, jax.ShapeDtypeStruct(gates.shape, F32), share, share),
        in_specs=[hbm] * 5,
        out_specs=(pl.BlockSpec(memory_space=pltpu.VMEM), hbm, hbm, hbm, hbm),
        scratch_shapes=[
            pltpu.VMEM(sent.shape, LOW),
            pltpu.VMEM(gates.shape, F32),
            pltpu.VMEM(sent.shape, LOW),
            pltpu.VMEM(first.shape, LOW),
            pltpu.VMEM(second.shape, LOW),
            pltpu.VMEM((4, count, D), LOW),
            pltpu.VMEM((4, count, D), LOW),
            pltpu.VMEM((count, D), LOW),
            pltpu.VMEM(sent.shape, LOW),
            pltpu.VMEM(gates.shape, F32),
            pltpu.VMEM((D, count), LOW),
            pltpu.VMEM((2 * capacity, D), F32),
            pltpu.VMEM((2 * capacity, D), F32),
            pltpu.VMEM((2, 2, D, D), LOW),
            pltpu.VMEM((2, 2, D, D), LOW),
            *pairs,
            pltpu.SemaphoreType.DMA((4,)),
            pltpu.SemaphoreType.DMA((4,)),
            pltpu.SemaphoreType.DMA((7,)),
            pltpu.SemaphoreType.DMA((2, 2)),
        ],
        compiler_params=pltpu.CompilerParams(
            vmem_limit_bytes=62 * MIB, collective_id=name, has_side_effects=True
        ),
    )(sent, gates, cotangent, first, second)


def finish_kernel(
    index,
    small,
    line,
    early_q,
    early_k,
    early_b,
    late_a,
    late_b,
    dense_b,
    dense_a,
    dense_rest,
    gain_share,
    rel_share,
    route_share,
    qkv,
    out,
    dense_in,
    dense_out,
):
    row, col = lax.axis_index("row"), lax.axis_index("col")
    place = row * 4 + col
    width = gain_share.shape[1]
    buckets = rel_share.shape[1]
    lines = jnp.concatenate([line[:8, :D], small[32:48, :D]], 0)
    lines = pltpu.roll(lines, lax.rem(D - place * width, D), 1)[:, :width]
    gain_share[...] = jnp.concatenate([lines[0:1], lines[10:11], lines[8:9], lines[9:10]], 0)
    route_share[...] = lines[11:19]
    wanted = place * buckets + lax.broadcasted_iota(jnp.int32, (8, 1), 0)
    hot = (index[...] == wanted).astype(F32)
    for i, block in enumerate((small[:16, :], small[16:32, :])):
        sums = lax.dot_general(
            hot, block, (((1,), (1,)), ((), ())), precision=HIGH, preferred_element_type=F32
        )
        rel_share[i] = sums[:buckets, :HEADS]
    for i, blocks in enumerate(
        ((early_q[0], early_k[0], early_b[0]), (late_a[0], late_a[1], late_b[0]))
    ):
        for k, block in enumerate(blocks):
            qkv[i, :, k * D : (k + 1) * D] = block
    out[0] = early_b[1]
    out[1] = late_b[1]
    for k in range(4):
        dense_in[:, k * D : (k + 1) * D] = dense_b[k]
    for k in range(2):
        dense_out[k] = dense_a[k]
        dense_out[2 + k] = dense_rest[k]


def finish(index, *blocks):
    piece = blocks[2].shape[1]
    shapes = (
        (4, piece),
        (2, BUCKETS * piece // D, HEADS),
        (8, piece),
        (2, piece, 3 * D),
        (2, piece, D),
        (piece, FF),
        (4, piece, D),
    )
    return pl.pallas_call(
        finish_kernel,
        out_shape=tuple(jax.ShapeDtypeStruct(shape, F32) for shape in shapes),
        compiler_params=pltpu.CompilerParams(vmem_limit_bytes=32 * MIB),
    )(index, *blocks)


def tiled(
    inputs,
    cotangent,
    routes,
    buckets,
    norm_gains,
    attn_qkv,
    attn_out,
    rel_bias,
    mlp_in,
    mlp_out,
    router,
    expert_in,
    expert_out,
):
    grid = ("row", "col")
    places = lax.axis_size(grid)
    cols, planes = lax.axis_size("col"), lax.axis_size("dp")
    experts = planes * cols
    tokens = inputs.shape[1]
    pslice = tokens - CLEN
    capacity = 3 * tokens // experts
    piece = D // places

    small = [norm_gains.reshape(-1), rel_bias.reshape(-1), router.reshape(-1)]
    cuts = [part.shape[0] for part in small]
    packed = jnp.concatenate(small)
    packed = jnp.pad(packed, (0, -packed.shape[0] % 2048)).reshape(1, -1, 128)

    pair, cut = (2, piece, D), (piece, 3 * D)
    early = (0, LATE, LATE, LATE, LATE)
    inner_a = layer(Gather(cut, False, cols, span=(0, 2 * D)), 0)
    inner_b = layer(Gather(cut, True, cols, span=(2 * D, D), into=inner_a), 0)
    packed, inner0, output0, shared0 = carry(
        None,
        [
            (Gather(packed.shape, False, cols), early),
            (inner_a, early),
            (inner_b, early),
            (layer(Gather((piece, D), True, cols), 0), early),
            (Rows((pslice, D)), (0, LATE, LATE)),
        ],
        (1,),
        [],
        [],
        [],
        [],
        60,
        1,
    )(packed, attn_qkv, attn_qkv, attn_out, inputs[0, :pslice])
    packed = packed.reshape(places, -1)
    gains = packed[:, : cuts[0]].reshape(places, 4, -1).transpose(1, 0, 2).reshape(4, 1, D).astype(F32)
    rel = packed[:, cuts[0] : cuts[0] + cuts[1]].reshape(places, 2, -1, HEADS)
    rel = rel.transpose(1, 3, 0, 2).reshape(2, HEADS, BUCKETS)
    route_w = packed[:, cuts[0] + cuts[1] : sum(cuts)].reshape(D, experts)

    gap = jnp.full((WRAP - KEYS,), -1, jnp.int32)
    index = jnp.concatenate([jnp.flip(buckets[: PLEN + 1]), gap, jnp.flip(buckets[PLEN + 1 :])])
    hot = (jnp.arange(BUCKETS, dtype=jnp.int32)[:, None] == index[None, :]).astype(LOW)
    floor = jnp.where(index < 0, NEG, 0.0).astype(F32)
    tables = jnp.pad(rel, ((0, 0), (0, 16 - HEADS), (0, 0))).reshape(32, BUCKETS)
    tables = (dot_low(tables, hot) + floor[None]).reshape(2, 16, WRAP)

    state1, stash1, (picks, sent_cotangent), (dense_in, dense_out, first) = attention_up(
        inputs[0],
        inputs[0],
        shared0,
        0,
        gains,
        tables,
        inner0,
        output0,
        [
            (Gather(mlp_in.shape, True, cols), (0, 2, 4, LATE, LATE)),
            (Gather(mlp_out.shape, True, cols), (0, 2, 4, LATE, LATE)),
            (Rows(expert_in.shape[1:]), (0, 4, LATE)),
        ],
        (mlp_in, mlp_out, expert_in[0]),
        2,
        more=(routes[0], cotangent[0]),
    )
    state2, normed1, normed2, shared2, inner1, output1, far_cotangent = mlp_up(
        state1,
        gains,
        dense_in,
        dense_out,
        [
            (layer(Gather(cut, True, cols), 1), (0, 2, LATE, LATE, LATE)),
            (layer(Gather((piece, D), True, cols), 1), (0, 2, LATE, LATE, LATE)),
            (Swap((capacity, D)), (0, LATE + 1)),
        ],
        (attn_qkv, attn_out, sent_cotangent),
        3,
    )
    route_w = jnp.pad(route_w, ((0, 0), (0, 128 - experts)))
    state3, stash3, (normed3, gates, line, sent), (second,) = attention_up(
        state2,
        normed2,
        shared2,
        1,
        gains,
        tables,
        inner1,
        output1,
        [(Rows(expert_out.shape[1:]), (0, 5, LATE))],
        (expert_out[0],),
        4,
        more=(gains, route_w, routes[0], picks),
    )

    outcome, returned, reach, grad_first, grad_second = routed(
        sent, line, far_cotangent, first, second, 5
    )
    returned = returned.reshape(experts * capacity, D)
    laid = (2, 1, places, piece, D)
    octet = (places // 2, piece, D)
    grad_first, grad_second = grad_first.reshape(laid), grad_second.reshape(laid)
    grad2, gain_third, late, table_late, gain_last, grad_route, own_first, own_second, outcome = (
        attention_down(
        (cotangent[0], returned, reach, picks, gates, normed3, routes[0], route_w, state3, gains),
        state2,
        gains,
        1,
        stash3,
        [
            (Reduce((places, piece, D), ("x",)), (0, 5)),
            (Reduce(octet, ("x",)), (1, LATE + 3)),
            (Swap((capacity, D)), (0, LATE + 5)),
        ],
        (grad_first, grad_second, outcome),
        6,
    ))
    outcome = outcome.reshape(experts * capacity, D)
    grad1, gain_second, output, dense_pairs, own_rest, late_a, late_b = mlp_down(
        grad2,
        state1,
        normed1,
        gains,
        dense_in,
        dense_out,
        (state3, gates, picks, outcome),
        [
            (Reduce(octet, ("x",), first=places // 2), (0, LATE)),
            (Reduce(pair, ("core", "x"), cols), (0, 1, LATE + 2)),
            (Reduce(pair, ("core", "y"), cols, first=2), (0, 1, LATE)),
        ],
        (grad_second, late, late),
        7,
    )
    lines = jnp.concatenate([gain_third, gain_last, gain_second, grad_route], 0)
    lines = jnp.pad(lines, ((0, 16 - lines.shape[0]), (0, WRAP - D)))
    known = jnp.concatenate([table_late, lines], 0).astype(LOW)
    quad = (4, piece, D)
    single = (1, piece, D)
    held = lambda outs, extras: extras[-3]
    (
        grad0,
        _,
        _,
        late_a,
        late_b,
        dense_a,
        dense_a_rest,
        dense_b,
        early_q,
        early_k,
        early_b,
        small,
        line,
    ) = attention_down(
        grad1,
        inputs[0],
        gains,
        0,
        stash1,
        [
            (Reduce(pair, ("z", "sum"), cols), (0, 2, 4)),
            (Reduce(single, ("x", "z", "swap"), cols), (0, 1, 3, 5)),
            (Reduce(pair, ("x", "z", "sum"), cols), (0, 2, 5, LATE + 3)),
            (Reduce(pair, ("x", "z", "sum"), cols, first=2), (2, 4, LATE + 1, LATE + 4)),
            (
                Reduce(quad, ("y", "x", "z", "swap"), cols, first=4),
                (0, 4, LATE + 0.2, LATE + 5, LATE + 7),
            ),
            (
                Reduce(single, ("core", "x", "z", "sum"), cols, take=held),
                (LATE, LATE + 2, LATE + 5, LATE + 8, LATE + 10),
            ),
            (
                Reduce(single, ("core", "x", "z", "sum"), cols, first=1, take=held),
                (LATE, LATE + 2, LATE + 6, LATE + 9, LATE + 10),
            ),
            (
                Reduce(pair, ("core", "y", "x", "z", "swap"), cols, first=2, take=held),
                (LATE, LATE + 2, LATE + 5, LATE + 7, LATE + 9, LATE + 10),
            ),
            (
                Total((16 + known.shape[0], WRAP), take=lambda outs, extras: extras[-2]),
                (LATE - 0.5, LATE + 0.5, LATE + 1.5, LATE + 2.5, LATE + 4.2),
            ),
            (
                Total((16, D), take=lambda outs, extras: extras[-1], short=True),
                (LATE + 4.6, LATE + 6.5, LATE + 9.5),
            ),
        ],
        (late_a, late_b, dense_pairs, dense_pairs, dense_pairs),
        8,
        known=known,
    )
    gain_share, rel_share, route_share, qkv_share, out_share, in_share, up_share = finish(
        index.reshape(1, -1),
        small,
        line,
        early_q,
        early_k,
        early_b,
        late_a,
        late_b,
        dense_b,
        dense_a,
        dense_a_rest,
    )
    return (
        output[None],
        grad0[None],
        gain_share,
        qkv_share,
        out_share,
        rel_share,
        in_share,
        up_share.reshape(-1, D),
        route_share.T,
        own_first.reshape(1, D, D),
        jnp.concatenate([own_second, own_rest], 0).reshape(1, D, D),
    )


def solution(mesh):
    in_specs = (
        P(("dp", "col"), "row", None),
        P(("dp", "col"), "row", None),
        P(("dp", "col"), "row", None),
        P(),
        P(None, ("row", "col")),
        P(None, ("row", "col"), None),
        P(None, ("row", "col"), None),
        P(None, ("row", "col"), None),
        P(("row", "col"), None),
        P(("row", "col"), None),
        P(("row", "col"), None),
        P(("dp", "col"), None, "row"),
        P(("dp", "col"), "row", None),
    )
    out_specs = (
        P(("dp", "col"), "row", None),
        P(("dp", "col"), "row", None),
        P(None, ("row", "col")),
        P(None, ("row", "col"), None),
        P(None, ("row", "col"), None),
        P(None, ("row", "col"), None),
        P(("row", "col"), None),
        P(("row", "col"), None),
        P(("row", "col"), None),
        P(("dp", "col"), None, "row"),
        P(("dp", "col"), "row", None),
    )
    sizes = dict(mesh.shape)
    piece = D // (sizes["row"] * sizes["col"])
    capacity = 3 * (PLEN // sizes["row"] + CLEN) // (sizes["dp"] * sizes["col"])
    whole_tiles = (sizes["dp"], sizes["row"], sizes["col"]) == (2, 4, 4) and piece % 16 == 0 and capacity % 16 == 0
    return jax.shard_map(
        tiled if whole_tiles else general, mesh=mesh, in_specs=in_specs, out_specs=out_specs, check_vma=False
    )
```

```python
import functools

import jax
import jax.numpy as jnp
from jax import lax
from jax.experimental import pallas as pl
from jax.experimental.pallas import tpu as pltpu
from jax.sharding import PartitionSpec as P

D = 768
HEADS = 12
HDIM = 64
FF = 3072
BUCKETS = 32
PLEN = 1024
CLEN = 128
KEYS = PLEN + CLEN
WRAP = KEYS + 128
STRIP = 2 * PLEN
NEG = -1e30
EPS = 1e-06
CURVE = 0.7978845608028654
CUBE = 0.044715
HIGH = lax.Precision.HIGHEST
F32 = jnp.float32
LOW = jnp.bfloat16
MIB = 1 << 20


def dot_low(left, right):
    return jnp.dot(left, right, preferred_element_type=F32)


def dot_back(left, right):
    return lax.dot_general(left, right, (((1,), (1,)), ((), ())), preferred_element_type=F32)


def dot_over(left, right):
    return lax.dot_general(left, right, (((0,), (0,)), ((), ())), preferred_element_type=F32)


def normalise(values):
    center = values - jnp.mean(values, -1, keepdims=True)
    scale = lax.rsqrt(jnp.mean(center * center, -1, keepdims=True) + EPS)
    return center * scale, scale


def norm_rows(values, gain):
    return normalise(values)[0] * gain


def norm_back(values, gain, upstream):
    unit, scale = normalise(values)
    pulled = upstream * gain
    shift = jnp.mean(pulled, -1, keepdims=True)
    along = jnp.mean(pulled * unit, -1, keepdims=True)
    return (pulled - shift - unit * along) * scale, jnp.sum(upstream * unit, 0, keepdims=True)


def gelu_parts(values):
    square = values * values
    bend = jnp.tanh(CURVE * (values + CUBE * square * values))
    half = 0.5 * (1.0 + bend)
    slope = half + 0.5 * values * (1.0 - bend * bend) * (CURVE + 3.0 * CURVE * CUBE * square)
    return values * half, slope


def gelu(values):
    return 0.5 * values * (1.0 + jnp.tanh(CURVE * (values + CUBE * values * values * values)))


def params(mib, steps=1):
    return pltpu.CompilerParams(
        vmem_limit_bytes=mib * MIB, dimension_semantics=("arbitrary",) * steps
    )


def whole(shape):
    return pl.BlockSpec(shape, lambda *_: (0,) * len(shape))


MESH = pl.DeviceIdType.MESH


class Remote:
    def __init__(self, src, dst, send, recv, index, device):
        self.parts = (src, dst, send, recv, index, device)

    def described(self):
        src, dst, send, recv, index, device = self.parts
        return pltpu.make_async_remote_copy(
            src_ref=src,
            dst_ref=dst,
            send_sem=send.at[index],
            recv_sem=recv.at[index],
            device_id=device,
            device_id_type=MESH,
        )

    def start(self):
        self.described().start()

    def wait_recv(self):
        self.described().wait_recv()

    def wait_send(self):
        self.described().wait_send()


def remote(src, dst, send, recv, index, **device):
    return Remote(src, dst, send, recv, index, device)


def neighbours():
    row, dp = lax.axis_index("row"), lax.axis_index("dp")
    across = lax.rem(row + 2, 4)
    core = row + 1 - 2 * lax.rem(row, 2)
    return row, across, core, dp + 1 - 2 * lax.rem(dp, 2)


class Within:
    def __init__(self, src, dst, sem):
        self.parts = (src, dst, sem)

    def start(self):
        pltpu.make_async_copy(*self.parts).start()

    def wait(self):
        pltpu.make_async_copy(*self.parts).wait()


class Gather:
    phases = 5

    def __init__(self, shape, split, cols, span=None, into=None, take=None):
        self.shape, self.split, self.cols, self.take, self.into = shape, split, cols, take, into
        self.span = (0, shape[-1]) if span is None else span
        self.spec = pl.BlockSpec(memory_space=pl.ANY)
        self.result = jax.ShapeDtypeStruct((4, cols) + shape, LOW)
        count = 4 * cols - 1 + (4 * cols - 2 if split else 0)
        self.scratch = [
            pltpu.SemaphoreType.DMA((count + 2 * cols,)),
            pltpu.SemaphoreType.DMA((count + 2 * cols,)),
            pltpu.SemaphoreType.DMA((1,)),
        ]

    def copies(self, src, dst, send, recv, local):
        cols = self.cols
        row, across, core, plane = neighbours()
        col, dp = lax.axis_index("col"), lax.axis_index("dp")
        first, width = self.span
        half = width // 2
        lead = (slice(None),) * (len(self.shape) - 1)
        full = lead + (pl.ds(first, width),)
        mine = pl.multiple_of(first + dp * half, 128)
        others = pl.multiple_of(first + (1 - dp) * half, 128)
        part = lead + (pl.ds(mine, half),) if self.split else full
        rest = lead + (pl.ds(others, half),)
        number = [0]

        def make(source, target, **device):
            number[0] += 1
            return remote(source, target, send, recv, number[0] - 1, **device)

        def piece(where, step, which):
            return dst.at[where, lax.rem(col - step + cols, cols)].at[which]

        own = src.at[part]
        out = {}
        out["local"] = Within(src.at[full], piece(row, 0, full), local.at[0])
        out["z"] = [
            make(own, piece(row, 0, part), col=lax.rem(col + step, cols)) for step in range(1, cols)
        ]
        out["x"] = [make(own, piece(row, 0, part), row=across)]
        out["x"] += [
            make(piece(row, step, part), piece(row, step, part), row=across)
            for step in range(1, cols)
        ]
        out["core own"] = make(src.at[full], piece(row, 0, full), row=core)
        out["core z"] = [
            make(piece(row, step, part), piece(row, step, part), row=core) for step in range(1, cols)
        ]
        out["core x"] = [
            make(piece(across, step, part), piece(across, step, part), row=core)
            for step in range(cols)
        ]
        if self.split:
            out["y z"] = [
                make(piece(row, step, part), piece(row, step, part), dp=plane)
                for step in range(1, cols)
            ]
            out["y x"] = [
                make(piece(across, step, part), piece(across, step, part), dp=plane)
                for step in range(cols)
            ]
            out["core y z"] = [
                make(piece(row, step, rest), piece(row, step, rest), row=core)
                for step in range(1, cols)
            ]
            out["core y x"] = [
                make(piece(across, step, rest), piece(across, step, rest), row=core)
                for step in range(cols)
            ]
        return out

    def peers(self):
        cols, col = self.cols, lax.axis_index("col")
        row, across, core, plane = neighbours()
        found = {(0, step): dict(col=lax.rem(col + step, cols)) for step in range(1, cols)}
        found.update(across=dict(row=across), core=dict(row=core))
        if self.split:
            found[(1, 0)] = dict(dp=plane)
        return found

    def phase(self, number, *refs):
        out = self.copies(*refs)
        if number == 0:
            out["local"].start()
            for copy in out["z"]:
                copy.start()
            out["x"][0].start()
            out["core own"].start()
        elif number == 1:
            for step in self.order():
                out["z"][step - 1].wait_recv()
                out["x"][step].start()
                if self.split:
                    out["y z"][step - 1].start()
                out["core z"][step - 1].start()
        elif number == 2:
            for step in [0] + self.order():
                out["x"][step].wait_recv()
                if self.split:
                    out["y x"][step].start()
                out["core x"][step].start()
        elif number == 3 and self.split:
            for step in self.order():
                out["y z"][step - 1].wait_recv()
                out["core y z"][step - 1].start()
            for step in [0] + self.order():
                out["y x"][step].wait_recv()
                out["core y x"][step].start()
        elif number == 4:
            out["local"].wait()
            late = [out["core own"]] + out["core z"] + out["core x"]
            if self.split:
                late += out["core y z"] + out["core y x"]
            for copy in late:
                copy.wait_recv()
            early = out["z"] + out["x"] + late
            if self.split:
                early += out["y z"] + out["y x"]
            for copy in early:
                copy.wait_send()

    def order(self):
        steps = list(range(1, self.cols))
        return sorted(steps, key=lambda step: min(step, self.cols - step))


class Rows:
    phases = 3

    def __init__(self, shape, take=None):
        self.take = take
        self.result = jax.ShapeDtypeStruct((4,) + shape, LOW)
        self.spec = pl.BlockSpec(memory_space=pl.ANY)
        self.scratch = [
            pltpu.SemaphoreType.DMA((3,)),
            pltpu.SemaphoreType.DMA((3,)),
            pltpu.SemaphoreType.DMA((1,)),
        ]

    def peers(self):
        row, across, core, plane = neighbours()
        return dict(across=dict(row=across), core=dict(row=core))

    def phase(self, number, src, dst, send, recv, local):
        row, across, core, plane = neighbours()
        own = Within(src, dst.at[row], local.at[0])
        far = remote(src, dst.at[row], send, recv, 0, row=across)
        near = remote(src, dst.at[row], send, recv, 1, row=core)
        on = remote(dst.at[across], dst.at[across], send, recv, 2, row=core)
        if number == 0:
            own.start()
            far.start()
            near.start()
        elif number == 1:
            far.wait_recv()
            on.start()
        else:
            own.wait()
            near.wait_recv()
            on.wait_recv()
            for copy in (far, near, on):
                copy.wait_send()


SLOTS = [(a, b) for b in range(4) for a in range(2)]


def slot_device(slot):
    a, b = SLOTS[slot]
    dp, col = lax.axis_index("dp"), lax.axis_index("col")
    flipped = (col, col + 1 - 2 * lax.rem(col, 2), lax.rem(col + 2, 4), 3 - col)[b]
    device = {}
    if a:
        device["dp"] = 1 - dp
    if b:
        device["col"] = flipped
    return device


class Swap:
    phases = 2

    def __init__(self, shape, take=None):
        self.take = take
        self.result = jax.ShapeDtypeStruct((len(SLOTS),) + shape, LOW)
        self.spec = pl.BlockSpec(memory_space=pl.ANY)
        self.scratch = [
            pltpu.SemaphoreType.DMA((len(SLOTS),)),
            pltpu.SemaphoreType.DMA((len(SLOTS),)),
            pltpu.SemaphoreType.DMA((1,)),
        ]

    def peers(self):
        return {SLOTS[slot]: slot_device(slot) for slot in range(1, len(SLOTS))}

    def phase(self, number, src, dst, send, recv, local):
        own = Within(src.at[0], dst.at[0], local.at[0])
        copies = [
            remote(src.at[slot], dst.at[slot], send, recv, slot, **slot_device(slot))
            for slot in range(1, len(SLOTS))
        ]
        if number == 0:
            for copy in copies:
                copy.start()
            own.start()
        else:
            own.wait()
            for copy in copies:
                copy.wait_recv()
            for copy in copies:
                copy.wait_send()


def each(count, body):
    lax.fori_loop(0, count, lambda index, carried: (body(index), carried)[1], 0)


class Reduce:
    def __init__(self, shape, ops, cols=1, first=0, take=None, keep=False):
        self.ops, self.cols, self.first, self.take, self.keep = ops, cols, first, take, keep
        self.count, tail = shape[0], shape[1:]
        self.part = self.count // 2 if "y" in ops else self.count
        self.phases = len(ops) + 1
        self.lead = 1 if ops[0] == "z" else 2
        ends = {
            "y": ((2, cols, self.part), LOW),
            "x": ((cols, self.part), LOW) if cols > 1 else ((self.part,), F32),
            "sum": ((self.part,), F32),
            "swap": ((2 * self.part,), F32),
        }
        lead, kind = ends[ops[-1]]
        self.result = jax.ShapeDtypeStruct(lead + tail, kind)
        self.spec = once(self.result.shape)
        full = (self.lead, cols, self.count)
        buffers = {"total": [full]}
        if "core" in ops and take is None:
            buffers["near"] = [full]
        if "y" in ops:
            buffers["y"] = [(2, cols, self.part)]
        if "x" in ops:
            buffers["x"] = [(cols, self.part)]
        if "z" in ops:
            buffers["z"] = [(cols - 1, self.part), (self.part,)]
            buffers["end"] = [(self.part,)]
        self.names = list(buffers)
        self.lengths = [len(buffers[name]) for name in self.names]
        self.scratch = [pltpu.VMEM(lead + tail, LOW) for name in self.names for lead in buffers[name]]
        self.scratch += [
            pltpu.SemaphoreType.DMA((8,)),
            pltpu.SemaphoreType.DMA((8,)),
            pltpu.SemaphoreType.DMA((2,)),
        ]

    def peers(self):
        row, across, core, plane = neighbours()
        found = {}
        if "core" in self.ops:
            found["core"] = dict(row=core)
        if "x" in self.ops:
            found["across"] = dict(row=across)
        slots = (2, 4, 6) if "z" in self.ops else ()
        if {"y", "sum", "swap"} & set(self.ops):
            slots += (1,)
        for slot in slots:
            found[SLOTS[slot]] = slot_device(slot)
        return found

    def phase(self, number, src, out, *scratch):
        scratch = list(scratch)
        held = {
            name: [scratch.pop(0) for _ in range(length)]
            for name, length in zip(self.names, self.lengths)
        }
        send, recv, local = scratch
        row, across, core, plane = neighbours()
        x, c = row // 2, lax.rem(row, 2)
        if self.ops[0] == "z":
            x = 0
        dp, col = lax.axis_index("dp"), lax.axis_index("col")
        total = held["total"][0]
        span = pl.ds(self.first, self.count)
        start = dp * self.part if "y" in self.ops else 0
        part, rest = pl.ds(start, self.part), pl.ds((1 - dp) * self.part, self.part)
        if self.take is not None:
            loads = []
        elif self.ops[0] == "core":
            loads = [Within(src.at[2 * i + c, :, span], total.at[i], local.at[i]) for i in range(2)]
        elif self.ops[0] == "z":
            loads = [Within(src.at[:, span], total.at[0], local.at[0])]
        else:
            loads = [Within(src.at[:, :, span], total, local.at[0])]

        def copies(op):
            if op == "core":
                near = held["near"][0] if self.take is None else total
                return [
                    remote(src.at[2 * i + 1 - c, :, span], near.at[i], send, recv, i, row=core)
                    for i in range(2)
                ]
            begun = op == self.ops[0]
            if op == "y":
                view = total.at[:, :, rest]
                if begun:
                    view = src.at[:, :, pl.ds(self.first + (1 - dp) * self.part, self.part)]
                return [remote(view, held["y"][0], send, recv, 2, dp=plane)]
            if op == "x":
                view = src.at[1 - x, :, span] if begun else total.at[1 - x, :, part]
                return [remote(view, held["x"][0], send, recv, 3, row=across)]
            if op == "z":
                found = []
                for b in (2, 3, 1):
                    device = slot_device(2 * b)
                    view = total.at[x, device["col"], part]
                    if begun:
                        view = src.at[device["col"], span]
                    found.append(remote(view, held["z"][0].at[b - 1], send, recv, 3 + b, **device))
                return found
            return [remote(held["z"][1], held["end"][0], send, recv, 7, dp=plane)]

        wide = lambda value: value.astype(F32)
        count, cols, size = self.count, self.cols, self.part
        if number > 0:
            op = self.ops[number - 1]
            last = number == len(self.ops)
            if number == 1:
                for load in loads:
                    load.wait()
            for copy in copies(op):
                copy.wait_recv()
            if op == "core":

                def add(i):
                    at = (i // (cols * count), lax.rem(i // count, cols), lax.rem(i, count))
                    if self.take is None:
                        more = held["near"][0][at]
                    else:
                        more = src[2 * at[0] + c, at[1], self.first + at[2]]
                    total[at] = (wide(total[at]) + wide(more)).astype(LOW)

                each(2 * cols * count, add)
            elif op == "y":

                def add(i):
                    at = (i // (cols * size), lax.rem(i // size, cols))
                    k = lax.rem(i, size)
                    kept = at + (start + k,)
                    value = wide(total[kept]) + wide(held["y"][0][at + (k,)])
                    if last:
                        out[at + (k,)] = value.astype(LOW)
                    else:
                        total[kept] = value.astype(LOW)

                each(2 * cols * size, add)
            elif op == "x":

                def add(i):
                    z, k = i // size, lax.rem(i, size)
                    value = wide(total[x, z, start + k]) + wide(held["x"][0][z, k])
                    if last and cols == 1:
                        out[k] = value
                    elif last:
                        out[z, k] = value.astype(LOW)
                    else:
                        total[x, z, start + k] = value.astype(LOW)

                each(cols * size, add)
            elif op == "z":

                def add(k):
                    value = wide(total[x, col, start + k])
                    for b in range(cols - 1):
                        value = value + wide(held["z"][0][b, k])
                    held["z"][1][k] = value.astype(LOW)

                each(size, add)
            else:

                def add(k):
                    mine, other = wide(held["z"][1][k]), wide(held["end"][0][k])
                    if op == "sum":
                        out[k] = mine + other
                    else:
                        out[dp * size + k] = mine
                        out[(1 - dp) * size + k] = other

                each(size, add)
        if number < len(self.ops):
            op = self.ops[number]
            for copy in copies(op):
                copy.start()
            if number == 0:
                for load in loads:
                    load.start()
        else:
            for op in self.ops:
                for copy in copies(op):
                    copy.wait_send()


class CoreSum:
    phases = 6

    def __init__(self, shape, cols, take):
        self.take, self.cols = take, cols
        self.result = jax.ShapeDtypeStruct((2, cols, 8) + shape, LOW)
        self.spec = once(self.result.shape)
        self.scratch = [
            pltpu.VMEM(self.result.shape, LOW),
            pltpu.SemaphoreType.DMA((10,)),
            pltpu.SemaphoreType.DMA((10,)),
        ]

    def peers(self):
        row, across, core, plane = neighbours()
        return dict(core=dict(row=core))

    def phase(self, number, src, out, near, send, recv):
        row, across, core, plane = neighbours()
        c = lax.rem(row, 2)

        def inner(j, i):
            at = (slice(None), 4 + j)
            view = src.at[2 * i + 1 - c].at[at]
            return remote(view, near.at[i].at[at], send, recv, 2 * j + i, row=core)

        def outer(i):
            at = (slice(None), pl.ds(0, 4))
            view = src.at[2 * i + 1 - c].at[at]
            return remote(view, near.at[i].at[at], send, recv, 8 + i, row=core)

        def begin(j):
            for i in range(2):
                inner(j, i).start()
            if j % 2 == 1:
                outer(j // 2).start()

        def add(i, z, k):
            out[i, z, k] = (src[2 * i + c, z, k].astype(F32) + near[i, z, k].astype(F32)).astype(LOW)

        def end(j):
            for i in range(2):
                inner(j, i).wait_recv()
            each(2 * self.cols, lambda n: add(n // self.cols, lax.rem(n, self.cols), 4 + j))
            if j % 2 == 1:
                outer(j // 2).wait_recv()
                each(4 * self.cols, lambda n: add(j // 2, n // 4, lax.rem(n, 4)))

        if 1 <= number <= 4:
            begin(number - 1)
        if number in (3, 4):
            end(number - 3)
        if number == 5:
            end(2)
            end(3)
            for j in range(4):
                for i in range(2):
                    inner(j, i).wait_send()
            for i in range(2):
                outer(i).wait_send()


class Total:
    def __init__(self, shape, take=None, short=False):
        self.take, self.short = take, short
        self.phases = 3 if short else 5
        hops, arrivals = (2, 10) if short else (4, 6)
        self.result = jax.ShapeDtypeStruct(shape, F32)
        self.spec = once(shape)
        self.scratch = [
            pltpu.VMEM((hops,) + shape, LOW),
            pltpu.VMEM((arrivals,) + shape, LOW),
            pltpu.SemaphoreType.DMA((arrivals,)),
            pltpu.SemaphoreType.DMA((arrivals,)),
            pltpu.SemaphoreType.DMA((1,)),
        ]

    def hops(self):
        row, across, core, plane = neighbours()
        if self.short:
            first = [dict(row=across), dict(row=lax.rem(core + 2, 4)), dict(row=core)]
            return [first, [slot_device(slot) for slot in (4, 5, 6, 7, 2, 3, 1)]]
        found = [[dict(row=core)], [dict(row=across)], [dict(dp=plane)]]
        return found + [[slot_device(2 * b) for b in (1, 2, 3)]]

    def peers(self):
        row, across, core, plane = neighbours()
        found = dict(across=dict(row=across), core=dict(row=core))
        if self.short:
            found["far"] = dict(row=lax.rem(core + 2, 4))
        for slot in range(1, 8) if self.short else (1, 2, 4, 6):
            found[SLOTS[slot]] = slot_device(slot)
        return found

    def phase(self, number, src, out, mine, other, send, recv, local):
        hops = self.hops()
        starts = [sum(len(hop) for hop in hops[:i]) for i in range(len(hops))]

        def copies(hop):
            return [
                remote(mine.at[hop], other.at[starts[hop] + i], send, recv, starts[hop] + i, **device)
                for i, device in enumerate(hops[hop])
            ]

        if number == 0:
            load = Within(src, mine.at[0], local.at[0])
            load.start()
            load.wait()
        else:
            value = mine[number - 1].astype(F32)
            for i, copy in enumerate(copies(number - 1)):
                copy.wait_recv()
                value = value + other[starts[number - 1] + i].astype(F32)
            if number < len(hops):
                mine[number] = value.astype(LOW)
            else:
                out[...] = value
        if number < len(hops):
            for copy in copies(number):
                copy.start()
        else:
            for hop in range(len(hops)):
                for copy in copies(hop):
                    copy.wait_send()


def greet(flows):
    barrier = pltpu.get_barrier_semaphore()
    devices = {}
    for flow in flows:
        devices.update(flow.peers())
    for device in devices.values():
        pl.semaphore_signal(barrier, inc=1, device_id=device, device_id_type=MESH)
    pl.semaphore_wait(barrier, len(devices))


LATE = 99


def layer(flow, index):
    flow.view = lambda ref: ref.at[index]
    return flow


def carry(body, moves, grid, in_specs, out_specs, out_shape, scratch_shapes, mib, name, after=()):
    inputs, outputs, extras = len(in_specs), len(out_specs), len(scratch_shapes)
    steps = grid[0]
    hbm = pl.BlockSpec(memory_space=pl.ANY)
    flows = [flow for flow, _ in moves]
    used = [at for _, marks in moves for at in marks] + [at for at, _ in after]
    given = [flow for flow in flows if flow.take is None]
    shared = [flow for flow in flows if getattr(flow, "into", None) is not None]
    kept = [flow for flow in flows if getattr(flow, "keep", False)]
    shown = [flow for flow in flows if flow not in shared and flow not in kept]

    def kernel(*refs):
        refs = list(refs)
        take = lambda count: [refs.pop(0) for _ in range(count)]
        own_in = take(inputs)
        sources = {flow: refs.pop(0) for flow in given}
        own_out = take(outputs)
        results = {flow: refs.pop(0) for flow in shown}
        own_extra = take(extras)
        packs = {}
        for flow in flows:
            if flow in kept:
                results[flow] = refs.pop(0)
            elif flow in shared:
                results[flow] = results[flow.into]
            if flow not in sources:
                sources[flow] = flow.take(own_out, own_extra)
            source_of = getattr(flow, "view", None)
            if source_of is not None:
                sources[flow] = source_of(sources[flow])
            packs[flow] = [sources[flow], results[flow]] + take(len(flow.scratch))
        step = pl.program_id(0)

        def run(low, high):
            plan = []
            for index, (flow, marks) in enumerate(moves):
                for number in range(flow.phases):
                    if low <= marks[number] < high:
                        call = functools.partial(flow.phase, number, *packs[flow])
                        plan.append((marks[number], number, index, call))
            for mark, function in after:
                if low <= mark < high:
                    call = functools.partial(
                        function, own_in, own_out, own_extra, [results[flow] for flow in flows]
                    )
                    plan.append((mark, 0, len(moves), call))
            for entry in sorted(plan, key=lambda entry: entry[:3]):
                entry[3]()

        for mark in range(steps):
            if mark == 0 or any(mark <= at < mark + 1 for at in used):

                @pl.when(step == mark)
                def _():
                    if mark == 0:
                        greet(flows)
                    run(mark, mark + 1)

        if body is not None:
            body(*own_in, *own_out, *own_extra)

        @pl.when(step == steps - 1)
        def _():
            run(LATE - 1, LATE + 100)

    scratch = list(scratch_shapes)
    for flow in flows:
        if flow in kept:
            scratch.append(pltpu.VMEM(flow.result.shape, flow.result.dtype))
        scratch += flow.scratch

    def call(*args):
        return pl.pallas_call(
            kernel,
            grid=grid,
            out_shape=tuple(out_shape) + tuple(flow.result for flow in shown),
            in_specs=list(in_specs) + [hbm] * len(given),
            out_specs=tuple(out_specs) + tuple(flow.spec for flow in shown),
            scratch_shapes=scratch,
            compiler_params=pltpu.CompilerParams(
                vmem_limit_bytes=mib * MIB,
                dimension_semantics=("arbitrary",),
                collective_id=name,
                has_side_effects=True,
            ),
        )(*args)

    return call


def bias_table(buckets, rel):
    place = jnp.arange(WRAP, dtype=jnp.int32)
    dist = jnp.where(place <= PLEN, PLEN - place, PLEN + WRAP - place)
    read = (place <= PLEN) | (place > KEYS)
    index = jnp.take(buckets, jnp.clip(dist, 0, KEYS - 1), axis=0)
    hot = ((index[:, None] == jnp.arange(BUCKETS)[None, :]) & read[:, None]).astype(LOW)
    floor = jnp.where(read, 0.0, NEG).astype(F32)
    return hot, floor


def fill_strip(strip, table, head):
    @pl.when(pl.program_id(0) == 0)
    def _():
        strip[:, KEYS:] = jnp.full((128, STRIP - KEYS), NEG, F32)

    line = jnp.broadcast_to(table[pl.ds(head, 1), :], (128, WRAP))
    strip[:, :KEYS] = pltpu.roll(line, 0, 1, stride=1, stride_axis=0)[:, :KEYS]


def tiles_of(pslice):
    places = []
    for tile in range(pslice // 128):
        start = PLEN - (lax.axis_index("row") * pslice + tile * 128)
        places.append((tile * 128, pl.ds(pl.multiple_of(start, 128), PLEN), PLEN))
    places.append((pslice, pl.ds(0, KEYS), KEYS))
    return places


def attend_kernel(pslice, query, keys, values, table, mixed, total, strip, raw, weights):
    pair = pl.program_id(0)
    lane = lax.broadcasted_iota(jnp.int32, (1, 128), 1)

    @pl.when(pair == 0)
    def _():
        weights[:pslice, PLEN:] = jnp.zeros((pslice, CLEN), LOW)

    for half in range(2):
        mine = (lane < HDIM) if half == 0 else (lane >= HDIM)
        fill_strip(strip, table, 2 * pair + half)
        part = jnp.where(mine, query[...], 0) * HDIM ** (-0.5)
        raw[...] = dot_back(part.astype(LOW), keys[...])
        for row, place, count in tiles_of(pslice):
            rows = pl.ds(row, 128)
            scores = raw[rows, :count] + strip[:, place]
            top = jnp.max(scores, -1, keepdims=True)
            raised = jnp.exp(scores - top)
            summed = jnp.sum(raised, -1, keepdims=True)
            weights[rows, :count] = (raised * (1.0 / summed)).astype(LOW)
            log_total = jnp.broadcast_to(top + jnp.log(summed), (128, 128))
            if half == 0:
                total[rows, :] = log_total
            else:
                total[rows, :] = jnp.where(mine, log_total, total[rows, :])
        result = dot_low(weights[...], values[...]).astype(LOW)
        if half == 0:
            mixed[...] = result
        else:
            mixed[...] = jnp.where(mine, result, mixed[...])


def attend_forward(query, keys, values, table):
    tokens = query.shape[0]
    pslice = tokens - CLEN
    block = lambda rows: pl.BlockSpec((rows, 128), lambda i: (0, i))
    return pl.pallas_call(
        functools.partial(attend_kernel, pslice),
        grid=(HEADS // 2,),
        out_shape=(
            jax.ShapeDtypeStruct((tokens, D), LOW),
            jax.ShapeDtypeStruct((tokens, D), F32),
        ),
        in_specs=[block(tokens), block(KEYS), block(KEYS), whole(table.shape)],
        out_specs=(block(tokens), block(tokens)),
        scratch_shapes=[
            pltpu.VMEM((128, STRIP), F32),
            pltpu.VMEM((tokens, KEYS), F32),
            pltpu.VMEM((tokens, KEYS), LOW),
        ],
        compiler_params=params(32),
    )(query, keys, values, table)


def attend_back_kernel(
    pslice,
    query,
    keys,
    values,
    table,
    total,
    grad_mixed,
    grad_query,
    grad_keys,
    grad_values,
    grad_table,
    strip,
    raw,
    pulled,
    probs,
    grads,
    folded,
    sum_keys,
    sum_values,
):
    pair = pl.program_id(0)
    lane = lax.broadcasted_iota(jnp.int32, (1, 128), 1)
    across = lax.broadcasted_iota(jnp.int32, (128, 128), 0)
    along = lax.broadcasted_iota(jnp.int32, (128, 128), 1)
    mirror = (across + along == 127).astype(LOW)

    @pl.when(pair == 0)
    def _():
        probs[:pslice, PLEN:] = jnp.zeros((pslice, CLEN), LOW)
        grads[:pslice, PLEN:] = jnp.zeros((pslice, CLEN), LOW)

    for half in range(2):
        mine = (lane < HDIM) if half == 0 else (lane >= HDIM)
        fill_strip(strip, table, 2 * pair + half)
        part = (jnp.where(mine, query[...], 0) * HDIM ** (-0.5)).astype(LOW)
        upstream = jnp.where(mine, grad_mixed[...], 0).astype(LOW)
        raw[...] = dot_back(part, keys[...])
        pulled[...] = dot_back(upstream, values[...])
        folded[...] = jnp.zeros_like(folded)
        for row, place, count in tiles_of(pslice):
            rows = pl.ds(row, 128)
            log_total = total[rows, half * HDIM : half * HDIM + 1]
            chance = jnp.exp(raw[rows, :count] + strip[:, place] - log_total)
            product = chance * pulled[rows, :count]
            centre = jnp.sum(product, -1, keepdims=True)
            slope = (product - chance * centre).astype(LOW)
            probs[rows, :count] = chance.astype(LOW)
            grads[rows, :count] = slope
            folded[:, place] += dot_low(mirror, slope)
        result = dot_low(grads[...], keys[...]) * HDIM ** (-0.5)
        if half == 0:
            grad_query[...] = result.astype(LOW)
            sum_keys[...] = dot_over(part, grads[...])
            sum_values[...] = dot_over(upstream, probs[...])
        else:
            grad_query[...] = jnp.where(mine, result.astype(LOW), grad_query[...])
            sum_keys[...] += dot_over(part, grads[...])
            sum_values[...] += dot_over(upstream, probs[...])
        turned = pltpu.roll(folded[:, :WRAP], WRAP - 127, 1, stride=1, stride_axis=0)
        grad_table[pl.ds(2 * pair + half, 1), :] = jnp.sum(turned, 0, keepdims=True)
    grad_keys[...] = sum_keys[...].T.astype(LOW)
    grad_values[...] = sum_values[...].T.astype(LOW)


def attend_backward(query, keys, values, table, total, grad_mixed):
    tokens = query.shape[0]
    pslice = tokens - CLEN
    block = lambda rows: pl.BlockSpec((rows, 128), lambda i: (0, i))
    return pl.pallas_call(
        functools.partial(attend_back_kernel, pslice),
        grid=(HEADS // 2,),
        out_shape=(
            jax.ShapeDtypeStruct((tokens, D), LOW),
            jax.ShapeDtypeStruct((KEYS, D), LOW),
            jax.ShapeDtypeStruct((KEYS, D), LOW),
            jax.ShapeDtypeStruct(table.shape, F32),
        ),
        in_specs=[
            block(tokens),
            block(KEYS),
            block(KEYS),
            whole(table.shape),
            block(tokens),
            block(tokens),
        ],
        out_specs=(block(tokens), block(KEYS), block(KEYS), whole(table.shape)),
        scratch_shapes=[
            pltpu.VMEM((128, STRIP), F32),
            pltpu.VMEM((tokens, KEYS), F32),
            pltpu.VMEM((tokens, KEYS), F32),
            pltpu.VMEM((tokens, KEYS), LOW),
            pltpu.VMEM((tokens, KEYS), LOW),
            pltpu.VMEM((128, STRIP), F32),
            pltpu.VMEM((128, KEYS), F32),
            pltpu.VMEM((128, KEYS), F32),
        ],
        compiler_params=params(32),
    )(query, keys, values, table, total, grad_mixed)


def mlp_forward_kernel(state, gain, first, second, result, normed):
    step = pl.program_id(0)

    @pl.when(step == 0)
    def _():
        normed[...] = norm_rows(state[...], gain[...]).astype(LOW)
        result[...] = state[...]

    active = gelu(dot_low(normed[...], first[...])).astype(LOW)
    result[...] += dot_low(active, second[...])


def mlp_forward(state, gain, first, second):
    tokens = state.shape[0]
    part = 768
    return pl.pallas_call(
        mlp_forward_kernel,
        grid=(FF // part,),
        out_shape=(
            jax.ShapeDtypeStruct((tokens, D), F32),
            jax.ShapeDtypeStruct((tokens, D), LOW),
        ),
        in_specs=[
            whole((tokens, D)),
            whole((1, D)),
            pl.BlockSpec((D, part), lambda i: (0, i)),
            pl.BlockSpec((part, D), lambda i: (i, 0)),
        ],
        out_specs=(whole((tokens, D)), whole((tokens, D))),
        compiler_params=params(32),
    )(state, gain, first, second)


def mlp_backward_kernel(
    grad_next, state, normed, gain, first, second, result, grad_gain, grad_first, grad_second, low, total
):
    step = pl.program_id(0)

    @pl.when(step == 0)
    def _():
        low[...] = grad_next[...].astype(LOW)
        total[...] = jnp.zeros_like(total)

    active, slope = gelu_parts(dot_low(normed[...], first[...]))
    grad_hidden = (slope * dot_back(low[...], second[...])).astype(LOW)
    grad_second[...] = dot_over(active.astype(LOW), low[...]).astype(LOW)
    grad_first[...] = dot_over(normed[...], grad_hidden).astype(LOW)
    total[...] += dot_back(grad_hidden, first[...])

    @pl.when(step == pl.num_programs(0) - 1)
    def _():
        grad_state, grad_line = norm_back(state[...], gain[...], total[...])
        result[...] = grad_next[...] + grad_state
        grad_gain[...] = grad_line


def mlp_backward(grad_next, state, normed, gain, first, second):
    tokens = state.shape[0]
    part = 768
    return pl.pallas_call(
        mlp_backward_kernel,
        grid=(FF // part,),
        out_shape=(
            jax.ShapeDtypeStruct((tokens, D), F32),
            jax.ShapeDtypeStruct((1, D), F32),
            jax.ShapeDtypeStruct((D, FF), LOW),
            jax.ShapeDtypeStruct((FF, D), LOW),
        ),
        in_specs=[
            whole((tokens, D)),
            whole((tokens, D)),
            whole((tokens, D)),
            whole((1, D)),
            pl.BlockSpec((D, part), lambda i: (0, i)),
            pl.BlockSpec((part, D), lambda i: (i, 0)),
        ],
        out_specs=(
            whole((tokens, D)),
            whole((1, D)),
            pl.BlockSpec((D, part), lambda i: (0, i)),
            pl.BlockSpec((part, D), lambda i: (i, 0)),
        ),
        scratch_shapes=[pltpu.VMEM((tokens, D), LOW), pltpu.VMEM((tokens, D), F32)],
        compiler_params=params(48),
    )(grad_next, state, normed, gain, first, second)


def expert_kernel(
    rows, cotangent, gate, first, second, result, grad_rows, grad_gate, grad_first, grad_second, upstream, total, back
):
    step = pl.program_id(0)

    @pl.when(step == 0)
    def _():
        upstream[...] = (gate[:, :1] * cotangent[...].astype(F32)).astype(LOW)
        total[...] = jnp.zeros_like(total)
        back[...] = jnp.zeros_like(back)

    active, slope = gelu_parts(dot_low(rows[...], first[...]))
    active = active.astype(LOW)
    total[...] += dot_low(active, second[...])
    grad_hidden = (slope * dot_back(upstream[...], second[...])).astype(LOW)
    grad_second[...] = dot_over(active, upstream[...]).astype(LOW)
    grad_first[...] = dot_over(rows[...], grad_hidden).astype(LOW)
    back[...] += dot_back(grad_hidden, first[...])

    @pl.when(step == pl.num_programs(0) - 1)
    def _():
        low = total[...].astype(LOW)
        result[...] = low
        grad_rows[...] = back[...].astype(LOW)
        reach = jnp.sum(cotangent[...].astype(F32) * low.astype(F32), -1, keepdims=True)
        grad_gate[...] = jnp.broadcast_to(reach, grad_gate.shape)


def expert_pass(rows, cotangent, gate, first, second):
    count = rows.shape[0]
    shards, _, width = first.shape
    part = 256
    split = width // part
    inner = pl.BlockSpec((None, D, part), lambda i: (i // split, 0, i % split))
    outer = pl.BlockSpec((None, part, D), lambda i: (i // split, i % split, 0))
    return pl.pallas_call(
        expert_kernel,
        grid=(shards * split,),
        out_shape=(
            jax.ShapeDtypeStruct((count, D), LOW),
            jax.ShapeDtypeStruct((count, D), LOW),
            jax.ShapeDtypeStruct((count, 128), F32),
            jax.ShapeDtypeStruct(first.shape, LOW),
            jax.ShapeDtypeStruct(second.shape, LOW),
        ),
        in_specs=[whole((count, D)), whole((count, D)), whole((count, 128)), inner, outer],
        out_specs=(whole((count, D)), whole((count, D)), whole((count, 128)), inner, outer),
        scratch_shapes=[
            pltpu.VMEM((count, D), LOW),
            pltpu.VMEM((count, D), F32),
            pltpu.VMEM((count, D), F32),
        ],
        compiler_params=params(56),
    )(rows, cotangent, gate, first, second)


def split_low(values):
    high = values.astype(LOW)
    rest = values - high.astype(F32)
    middle = rest.astype(LOW)
    return high, middle, (rest - middle.astype(F32)).astype(LOW)


def exchange(block):
    return lax.all_to_all(block, ("dp", "col"), split_axis=0, concat_axis=0, tiled=True)


def attention_forward(state, gain, others, weight_in, weight_out, table, raw_others):
    tokens = state.shape[0]
    pslice = tokens - CLEN
    normed = norm_rows(state, gain).astype(LOW)
    if others is None:
        shared = lax.all_gather(normed[:pslice], "row", axis=0, tiled=True)
    else:
        shared = norm_rows(others.astype(F32), gain).astype(LOW)
    read = jnp.concatenate([shared, normed[pslice:]], 0)
    query = dot_low(normed, weight_in[:, :D]).astype(LOW)
    keys = dot_low(read, weight_in[:, D : 2 * D]).astype(LOW)
    values = dot_low(read, weight_in[:, 2 * D :]).astype(LOW)
    mixed, total = attend_forward(query, keys, values, table)
    return state + dot_low(mixed, weight_out), (state, normed, read, query, keys, values, mixed, total)


def attention_backward(grad_next, stash, gain, weight_in, weight_out, table, hot):
    state, normed, read, query, keys, values, mixed, total = stash
    pslice = state.shape[0] - CLEN
    branch = grad_next.astype(LOW)
    grad_out = dot_over(mixed, branch).astype(LOW)
    grad_mixed = dot_back(branch, weight_out).astype(LOW)
    grad_query, grad_keys, grad_values, grad_table = attend_backward(
        query, keys, values, table, total, grad_mixed
    )
    grad_in = jnp.concatenate(
        [dot_over(normed, grad_query), dot_over(read, grad_keys), dot_over(read, grad_values)], 1
    ).astype(LOW)
    grad_read = dot_back(grad_keys, weight_in[:, D : 2 * D]) + dot_back(
        grad_values, weight_in[:, 2 * D :]
    )
    own = lax.psum_scatter(
        grad_read[:PLEN].astype(LOW), "row", scatter_dimension=0, tiled=True
    ).astype(F32)
    grad_normed = dot_back(grad_query, weight_in[:, :D]) + jnp.concatenate(
        [own, grad_read[PLEN:]], 0
    )
    grad_state, grad_gain = norm_back(state, gain, grad_normed)
    grad_rel = jnp.dot(grad_table[:HEADS], hot.astype(F32), precision=HIGH).T
    return grad_next + grad_state, grad_in, grad_out, grad_rel, grad_gain


def general(
    inputs,
    cotangent,
    routes,
    buckets,
    norm_gains,
    attn_qkv,
    attn_out,
    rel_bias,
    mlp_in,
    mlp_out,
    router,
    expert_in,
    expert_out,
):
    grid = ("row", "col")
    places = lax.axis_size(grid)
    experts = lax.axis_size(("dp", "col"))
    tokens = inputs.shape[1]
    pslice = tokens - CLEN
    capacity = max(2, 3 * tokens // experts)

    small = [norm_gains.reshape(-1), rel_bias.reshape(-1), router.reshape(-1)]
    cuts = [part.shape[0] for part in small]
    packed = jnp.concatenate(small)
    packed = jnp.pad(packed, (0, -packed.shape[0] % 1024)).reshape(-1, 128)
    packed = lax.all_gather(packed, grid, axis=0, tiled=False).reshape(places, -1)
    gains = packed[:, : cuts[0]].reshape(places, 4, -1).transpose(1, 0, 2).reshape(4, 1, D).astype(F32)
    rel = packed[:, cuts[0] : cuts[0] + cuts[1]].reshape(places, 2, -1, HEADS)
    rel = rel.transpose(1, 0, 2, 3).reshape(2, BUCKETS, HEADS)
    route_w = packed[:, cuts[0] + cuts[1] : sum(cuts)].reshape(D, experts)

    qkv = [lax.all_gather(attn_qkv[i], grid, axis=0, tiled=True) for i in range(2)]
    out = [lax.all_gather(attn_out[i], grid, axis=0, tiled=True) for i in range(2)]
    dense_in = lax.all_gather(mlp_in, grid, axis=0, tiled=True)
    dense_out = lax.all_gather(mlp_out, grid, axis=0, tiled=True)
    first = lax.all_gather(expert_in[0], "row", axis=0, tiled=False)
    second = lax.all_gather(expert_out[0], "row", axis=0, tiled=False)

    hot, floor = bias_table(buckets, rel)
    tables = [
        jnp.pad(dot_low(rel[i].T, hot.T) + floor[None], ((0, 16 - HEADS), (0, 0))) for i in range(2)
    ]

    flat = routes[0].reshape(-1)
    levels = jnp.arange(experts, dtype=jnp.int32)
    choose = (routes[0][:, :, None] == levels[None, None, :]).astype(F32)
    hits = (flat[:, None] == levels[None, :]).astype(LOW)
    before = jnp.arange(2 * tokens)
    before = (before[:, None] > before[None, :]).astype(LOW)
    rank = jnp.sum(dot_low(before, hits) * hits.astype(F32), 1).astype(jnp.int32)
    place = (flat * capacity + rank).reshape(tokens, 2)
    slots = jnp.arange(experts * capacity, dtype=jnp.int32)
    picks = [(place[:, k][:, None] == slots[None, :]).astype(LOW) for k in range(2)]
    both = picks[0] + picks[1]
    sent_cotangent = dot_over(both, cotangent[0]).astype(LOW).reshape(experts, capacity, D)
    far_cotangent = exchange(sent_cotangent).reshape(experts * capacity, D)

    state0 = inputs[0].astype(F32)
    shared0 = lax.all_gather(inputs[0, :pslice], "row", axis=0, tiled=True)
    state1, stash1 = attention_forward(state0, gains[0], shared0, qkv[0], out[0], tables[0], None)
    state2, normed1 = mlp_forward(state1, gains[1], dense_in, dense_out)
    state3, stash3 = attention_forward(state2, gains[2], None, qkv[1], out[1], tables[1], None)

    normed3 = norm_rows(state3, gains[3]).astype(LOW)
    logits = dot_low(normed3, route_w)
    picked = jnp.sum(choose * logits[:, None, :], -1)
    raised = jnp.exp(picked - jnp.max(picked, -1, keepdims=True))
    gates = raised / jnp.sum(raised, -1, keepdims=True)
    parts = [split_low(gates[:, k]) for k in range(2)]
    spread = [
        dot_over(picks[k], jnp.pad(jnp.stack(parts[k], 1), ((0, 0), (0, 125)))) for k in range(2)
    ]
    sent = jnp.concatenate([dot_over(both, normed3), spread[0] + spread[1]], 1).astype(LOW)
    received = exchange(sent.reshape(experts, capacity, D + 128)).reshape(experts * capacity, D + 128)
    far_gate = jnp.sum(received[:, D : D + 3].astype(F32), 1, keepdims=True)
    far_gate = jnp.broadcast_to(far_gate, (experts * capacity, 128))
    result, grad_rows, grad_gate, grad_first, grad_second = expert_pass(
        received[:, :D], far_cotangent, far_gate, first, second
    )
    reach = jnp.pad(jnp.stack(split_low(grad_gate[:, 0]), 1), ((0, 0), (0, 125)))
    returned = exchange(
        jnp.concatenate([grad_rows, reach], 1).reshape(experts, capacity, D + 128)
    ).reshape(experts * capacity, D + 128)
    outcome = exchange(result.reshape(experts, capacity, D)).reshape(experts * capacity, D)
    output = state3 + sum(gates[:, k : k + 1] * dot_low(picks[k], outcome) for k in range(2))

    grad_gates = jnp.stack(
        [jnp.sum(dot_low(picks[k], returned[:, D:]), 1) for k in range(2)], 1
    )
    grad_picked = gates * (grad_gates - jnp.sum(gates * grad_gates, -1, keepdims=True))
    grad_logits = jnp.sum(choose * grad_picked[:, :, None], 1).astype(LOW)
    grad_route = dot_over(normed3, grad_logits)
    grad_normed3 = dot_low(both, returned[:, :D]) + dot_back(grad_logits, route_w)
    upstream = cotangent[0].astype(F32)
    grad_state3, gain_last = norm_back(state3, gains[3], grad_normed3)
    grad3 = upstream + grad_state3
    own_first = lax.psum_scatter(grad_first, "row", scatter_dimension=0, tiled=False)
    own_second = lax.psum_scatter(grad_second, "row", scatter_dimension=0, tiled=False)

    grad2, qkv_late, out_late, rel_late, gain_third = attention_backward(
        grad3, stash3, gains[2], qkv[1], out[1], tables[1], hot
    )
    grad1, gain_second, dense_grad_in, dense_grad_out = mlp_backward(
        grad2, state1, normed1, gains[1], dense_in, dense_out
    )
    grad0, qkv_early, out_early, rel_early, gain_first = attention_backward(
        grad1, stash1, gains[0], qkv[0], out[0], tables[0], hot
    )

    def share(block):
        block = lax.psum_scatter(block.astype(LOW), grid, scatter_dimension=0, tiled=True)
        return lax.psum(block, "dp").astype(F32)

    gain_grads = jnp.concatenate([gain_first, gain_second, gain_third, gain_last], 0)
    gain_grads = gain_grads.reshape(4, places, -1).transpose(1, 0, 2).reshape(places, -1)
    rel_grads = jnp.stack([rel_early, rel_late]).reshape(2, places, -1, HEADS)
    rel_grads = rel_grads.transpose(1, 0, 2, 3).reshape(places, -1)
    packed = jnp.concatenate([gain_grads, rel_grads, grad_route.reshape(places, -1)], 1)
    packed = jnp.pad(packed, ((0, 0), (0, -packed.shape[1] % 1024))).reshape(-1, 128)
    packed = share(packed).reshape(-1)
    gain_share = packed[: cuts[0]].reshape(4, -1)
    rel_share = packed[cuts[0] : cuts[0] + cuts[1]].reshape(2, -1, HEADS)
    route_share = packed[cuts[0] + cuts[1] : sum(cuts)].reshape(-1, experts)
    return (
        output[None],
        grad0[None],
        gain_share,
        jnp.stack([share(qkv_early), share(qkv_late)]),
        jnp.stack([share(out_early), share(out_late)]),
        rel_share,
        share(dense_grad_in),
        share(dense_grad_out),
        route_share,
        own_first.astype(F32)[None],
        own_second.astype(F32)[None],
    )


def once(shape):
    return pl.BlockSpec(shape, lambda *_: (0,) * len(shape), pipeline_mode=pl.Buffered(1))


def head_block(cols, piece, index):
    pair = lambda i: jnp.minimum(i, HEADS // 2 - 1)
    return pl.BlockSpec((4, cols, piece, 128), lambda i: (0, 0, 0, 6 * index + pair(i)))


def outer_block(cols, piece):
    return once((4, cols, piece, D))


def strip_block():
    return pl.BlockSpec((2, 128, STRIP), lambda i: (jnp.minimum(i, HEADS // 2 - 1), 0, 0))


def line_block(index, shape):
    return pl.BlockSpec(
        (None,) + shape, lambda i: (index,) + (0,) * len(shape), pipeline_mode=pl.Buffered(1)
    )


def up_kernel(
    raw_rows,
    pslice,
    state,
    own,
    shared,
    gain,
    table,
    wq,
    wk,
    wv,
    wo,
    result,
    normed,
    read,
    query,
    keys,
    values,
    mixed,
    total,
    strips,
    raw,
    weights,
    outer,
):
    pair = pl.program_id(0)
    lane = lax.broadcasted_iota(jnp.int32, (1, 128), 1)

    @pl.when(pair == 0)
    def _():
        weights[:pslice, PLEN:] = jnp.zeros((pslice, CLEN), LOW)
        outer[...] = wo[...].reshape(D, D)
        result[...] = state[...].astype(F32)
        if raw_rows:
            normed[...] = norm_rows(own[...].astype(F32), gain[...]).astype(LOW)
            for i in range(PLEN // pslice):
                rows = pl.ds(i * pslice, pslice)
                read[rows, :] = norm_rows(shared[i].astype(F32), gain[...]).astype(LOW)
        else:
            normed[...] = own[...]
            for i in range(PLEN // pslice):
                read[pl.ds(i * pslice, pslice), :] = shared[i]
        read[PLEN:, :] = normed[pslice:, :]

    query[...] = dot_low(normed[...], wq[...].reshape(D, 128)).astype(LOW)
    both = jnp.concatenate([wk[...].reshape(D, 128), wv[...].reshape(D, 128)], 1)
    both = dot_low(read[...], both).astype(LOW)
    keys[...] = both[:, :128]
    values[...] = both[:, 128:]

    for half in range(2):
        mine = (lane < HDIM) if half == 0 else (lane >= HDIM)
        line = jnp.broadcast_to(table[pl.ds(2 * pair + half, 1), :], (128, WRAP))
        line = pltpu.roll(line, 0, 1, stride=1, stride_axis=0)[:, :KEYS]
        strips[half, :, :KEYS] = line.astype(LOW)
        strips[half, :, KEYS:] = jnp.full((128, STRIP - KEYS), NEG, LOW)
        part = jnp.where(mine, query[...], 0) * HDIM ** (-0.5)
        raw[...] = dot_back(part.astype(LOW), keys[...])
        for row, place, count in tiles_of(pslice):
            rows = pl.ds(row, 128)
            scores = raw[rows, :count] + strips[half, :, place].astype(F32)
            top = jnp.max(scores, -1, keepdims=True)
            raised = jnp.exp(scores - top)
            summed = jnp.sum(raised, -1, keepdims=True)
            weights[rows, :count] = (raised * (1.0 / summed)).astype(LOW)
            log_total = jnp.broadcast_to(top + jnp.log(summed), (128, 128))
            if half == 0:
                total[rows, :] = log_total
            else:
                total[rows, :] = jnp.where(mine, log_total, total[rows, :])
        part = dot_low(weights[...], values[...]).astype(LOW)
        if half == 0:
            mixed[...] = part
        else:
            mixed[...] = jnp.where(mine, part, mixed[...])
    result[...] += dot_low(mixed[...], outer[pl.ds(pl.multiple_of(pair * 128, 128), 128), :])


def route_rows(routes, cotangent, picks, sent):
    tokens = routes.shape[0]
    slots, capacity, _ = sent.shape
    dp, col = lax.axis_index("dp"), lax.axis_index("col")
    lanes = lax.broadcasted_iota(jnp.int32, (tokens, 128), 1)
    slot, hot = [], []
    for k in range(2):
        expert = routes[:, k : k + 1]
        slot.append(2 * ((expert & 3) ^ col) + ((expert >> 2) ^ dp))
        hot.append(jnp.where(slot[k] == lanes, 1.0, 0.0))
    up = lax.broadcasted_iota(jnp.int32, (tokens, tokens), 0)
    along = lax.broadcasted_iota(jnp.int32, (tokens, tokens), 1)
    before = dot_low(jnp.where(up > along, 1.0, 0.0).astype(LOW), (hot[0] + hot[1]).astype(LOW))
    spots = lax.broadcasted_iota(jnp.int32, (tokens, slots * capacity), 1).astype(F32)
    for k in range(2):
        rank = jnp.sum(before * hot[k], -1, keepdims=True)
        place = slot[k].astype(F32) * capacity + rank
        picks[k] = jnp.where(place == spots, 1.0, 0.0).astype(LOW)
    both = picks[0] + picks[1]
    sent[...] = dot_over(both, cotangent[...]).astype(LOW).reshape(sent.shape)


def laid_lanes(columns, tokens):
    lanes = lax.broadcasted_iota(jnp.int32, (tokens, 128), 1)
    laid = jnp.zeros((tokens, 128), F32)
    for i, column in enumerate(columns):
        laid = jnp.where(lanes == i, column, laid)
    return laid


def chosen(routes):
    lanes = lax.broadcasted_iota(jnp.int32, (routes.shape[0], 128), 1)
    return [jnp.where(routes[:, k : k + 1] == lanes, 1.0, 0.0) for k in range(2)]


def send_rows(state, gain, route_w, routes, picks, normed, gates, line, sent):
    tokens = routes.shape[0]
    slots, capacity, _ = sent.shape
    shift = pl.multiple_of((pl.program_id(0) - (pl.num_programs(0) - 1)) * 8, 8)
    normed[...] = norm_rows(state[pl.ds(shift, tokens), :], gain[...]).astype(LOW)
    logits = dot_low(normed[...], route_w[...])
    picked = [jnp.sum(hot * logits, -1, keepdims=True) for hot in chosen(routes)]
    top = jnp.maximum(picked[0], picked[1])
    raised = [jnp.exp(value - top) for value in picked]
    gate = [value / (raised[0] + raised[1]) for value in raised]
    gates[...] = laid_lanes(gate, tokens)
    total = 0.0
    for k in range(2):
        parts = laid_lanes([part.astype(F32) for part in split_low(gate[k])], tokens).astype(LOW)
        total = total + jnp.sum(dot_over(parts, picks[k]), 0, keepdims=True)
    for slot in range(slots):
        part = total[:, slot * capacity : (slot + 1) * capacity]
        part = jnp.pad(part, ((0, 0), (0, line.shape[2] - capacity)))
        line[slot] = jnp.broadcast_to(part, line.shape[1:])
    sent[...] = dot_over(picks[0] + picks[1], normed[...]).astype(LOW).reshape(sent.shape)


def take_rows(
    cotangent, returned, reach, picks, gates, normed, routes, route_w, state, gain, grad_gain, grad_route, result
):
    tokens = routes.shape[0]
    capacity = picks.shape[2] // reach.shape[0]
    line = jnp.concatenate([reach[slot, :1, :capacity] for slot in range(reach.shape[0])], 1)
    gate = [gates[:, k : k + 1] for k in range(2)]
    met = [jnp.sum(picks[k].astype(F32) * line, -1, keepdims=True) for k in range(2)]
    centre = gate[0] * met[0] + gate[1] * met[1]
    hots = chosen(routes)
    slopes = sum(hots[k] * (gate[k] * (met[k] - centre)) for k in range(2)).astype(LOW)
    grad_route[...] = dot_over(slopes, normed[...])[: grad_route.shape[0]]
    grad_normed = dot_low(picks[0] + picks[1], returned[...]) + dot_back(slopes, route_w[...])
    grad_state, grad_line = norm_back(state[...], gain[...], grad_normed)
    result[...] = cotangent[...].astype(F32) + grad_state
    grad_gain[...] = grad_line


def attention_up(
    state,
    own,
    shared,
    layer_index,
    gains,
    tables,
    inner,
    output,
    moves,
    sources,
    name,
    more=(),
    extra=(),
    after=(),
):
    tokens = own.shape[0]
    pslice = tokens - CLEN
    _, cols, piece, _ = inner.shape
    raw_rows = layer_index == 0
    slots = lax.axis_size(("dp", "col"))
    capacity = 3 * tokens // slots
    more_specs = [once(block.shape) for block in more]
    if not raw_rows:
        more_specs[0] = line_block(3, (1, D))
    if raw_rows:
        more_out = [
            jax.ShapeDtypeStruct((2, tokens, slots * capacity), LOW),
            jax.ShapeDtypeStruct((tokens, D), LOW),
            jax.ShapeDtypeStruct((tokens, D), F32),
            jax.ShapeDtypeStruct((tokens, D), LOW),
            jax.ShapeDtypeStruct((slots, capacity, D), LOW),
        ]
        more_specs[2:] = [line_block(1, (1, D)), line_block(2, (1, D))]
    else:
        more_out = [
            jax.ShapeDtypeStruct((tokens, D), LOW),
            jax.ShapeDtypeStruct((tokens, 128), F32),
            jax.ShapeDtypeStruct((slots, 8, capacity + -capacity % 128), F32),
            jax.ShapeDtypeStruct((slots, capacity, D), LOW),
        ]

    def body(*refs):
        refs = list(refs)
        given = [refs.pop(9) for _ in more]
        found = [refs.pop(18) for _ in more_out]
        step = pl.program_id(0)
        for _ in extra:
            refs.pop()

        @pl.when(step < HEADS // 2)
        def _():
            up_kernel(raw_rows, pslice, *refs)

        @pl.when(step == (1 if raw_rows else HEADS // 2 - 1))
        def _():
            if raw_rows:
                route_rows(given[0], given[1], found[0], found[-1])
            else:
                send_rows(refs[9], *given, *found)
    block = lambda rows: pl.BlockSpec((rows, 128), lambda i: (0, jnp.minimum(i, HEADS // 2 - 1)))
    low = lambda rows: jax.ShapeDtypeStruct((rows, D), LOW)
    result, normed, read, query, keys, values, mixed, total, strips, *moved = carry(
        body,
        moves,
        grid=(HEADS // 2 + (4 if raw_rows else 0),),
        out_shape=(
            jax.ShapeDtypeStruct((tokens, D), F32),
            low(tokens),
            low(KEYS),
            low(tokens),
            low(KEYS),
            low(KEYS),
            low(tokens),
            jax.ShapeDtypeStruct((tokens, D), F32),
            jax.ShapeDtypeStruct((HEADS, 128, STRIP), LOW),
            *more_out,
        ),
        in_specs=[
            once((tokens, D)),
            once((tokens, D)),
            once(shared.shape),
            line_block(2 * layer_index, (1, D)),
            line_block(layer_index, tables.shape[1:]),
            head_block(cols, piece, 0),
            head_block(cols, piece, 1),
            head_block(cols, piece, 2),
            outer_block(cols, piece),
            *more_specs,
        ],
        out_specs=(
            whole((tokens, D)),
            whole((tokens, D)),
            whole((KEYS, D)),
            block(tokens),
            block(KEYS),
            block(KEYS),
            block(tokens),
            block(tokens),
            strip_block(),
            *[once(out.shape) for out in more_out],
        ),
        scratch_shapes=[
            pltpu.VMEM((tokens, KEYS), F32),
            pltpu.VMEM((tokens, KEYS), LOW),
            pltpu.VMEM((D, D), LOW),
            *extra,
        ],
        mib=60,
        name=name,
        after=after,
    )(state, own, shared, gains, tables, inner, inner, inner, output, *more, *sources)
    stash = (normed, read, query, keys, values, mixed, total, strips, inner, output)
    return result, stash, moved[: len(more_out)], moved[len(more_out) :]


def slide_sum(grid):
    rows = grid.shape[0]
    while rows > 8:
        rows = rows // 2
        grid = grid[:rows] + pltpu.roll(grid[rows:], WRAP - rows, 1)
    for step in (4, 2, 1):
        grid = grid + pltpu.roll(pltpu.roll(grid, 8 - step, 0), WRAP - step, 1)
    return grid[:1]


def down_kernel(
    pslice,
    grad_next,
    state,
    gain,
    normed,
    read,
    query,
    keys,
    values,
    mixed,
    total,
    strips,
    wq,
    wk,
    wv,
    wo,
    result,
    grad_gain,
    grads,
    grad_table,
    low,
    outer,
    grad_outer,
    sum_own,
    sum_read,
    spill,
    raw,
    pulled,
    probs,
    slopes,
    folded,
    sum_keys,
    sum_values,
):
    pair = pl.program_id(0)
    lane = lax.broadcasted_iota(jnp.int32, (1, 128), 1)
    here = pl.ds(pl.multiple_of(pair * 128, 128), 128)

    @pl.when(pair == 0)
    def _():
        probs[:pslice, PLEN:] = jnp.zeros((pslice, CLEN), LOW)
        slopes[:pslice, PLEN:] = jnp.zeros((pslice, CLEN), LOW)
        low[...] = grad_next[...].astype(LOW)
        outer[...] = wo[...].reshape(D, D)
        sum_own[...] = jnp.zeros_like(sum_own)
        sum_read[...] = jnp.zeros_like(sum_read)

    grad_outer[here, :] = dot_over(mixed[...], low[...]).astype(LOW)
    grad_mixed = dot_back(low[...], outer[here, :]).astype(LOW)
    for half in range(2):
        mine = (lane < HDIM) if half == 0 else (lane >= HDIM)
        part = (jnp.where(mine, query[...], 0) * HDIM ** (-0.5)).astype(LOW)
        upstream = jnp.where(mine, grad_mixed, 0).astype(LOW)
        raw[...] = dot_back(part, keys[...])
        pulled[...] = dot_back(upstream, values[...])
        folded[...] = jnp.zeros_like(folded)
        for row, place, count in tiles_of(pslice):
            rows = pl.ds(row, 128)
            log_total = total[rows, half * HDIM : half * HDIM + 1]
            scores = raw[rows, :count] + strips[half, :, place].astype(F32)
            chance = jnp.exp(scores - log_total)
            product = chance * pulled[rows, :count]
            centre = jnp.sum(product, -1, keepdims=True)
            slope = (product - chance * centre).astype(LOW)
            probs[rows, :count] = chance.astype(LOW)
            slopes[rows, :count] = slope
            folded[:, place] += slope.astype(F32)
        step = (dot_low(slopes[...], keys[...]) * HDIM ** (-0.5)).astype(LOW)
        if half == 0:
            grad_query = step
            sum_keys[...] = dot_over(part, slopes[...])
            sum_values[...] = dot_over(upstream, probs[...])
        else:
            grad_query = jnp.where(mine, step, grad_query)
            sum_keys[...] += dot_over(part, slopes[...])
            sum_values[...] += dot_over(upstream, probs[...])
        grad_table[pl.ds(2 * pair + half, 1), :] = slide_sum(folded[:, :WRAP])

    shape = grads.shape[:2] + grads.shape[3:4] + (128,)

    def keep(index, turned):
        grads[:, :, index, :, here] = turned.T.astype(LOW).reshape(shape)

    keep(0, dot_over(grad_query, normed[...]))
    keep(1, dot_low(sum_keys[...].astype(LOW), read[...]))
    keep(2, dot_low(sum_values[...].astype(LOW), read[...]))
    sum_own[...] += dot_back(grad_query, wq[...].reshape(D, 128))
    pairs = jnp.concatenate([sum_keys[...].T, sum_values[...].T], 1).astype(LOW)
    both = jnp.concatenate([wk[...].reshape(D, 128), wv[...].reshape(D, 128)], 1)
    sum_read[...] += dot_back(pairs, both)

    @pl.when(pair == pl.num_programs(0) - 1)
    def _():
        grads[:, :, 3] = grad_outer[...].reshape(shape[:3] + (D,))
        spill[...] = sum_read[:PLEN, :].astype(LOW).reshape(spill.shape)


def down_after(pslice, fill, own_in, own_out, extras, results):
    grad_next, state, gain = own_in[:3]
    if not fill:
        grad_next = extras[-1]
    result, grad_gain = own_out[:2]
    sum_own, sum_read = extras[3:5]
    shift = (pl.program_id(0) - (pl.num_programs(0) - 1)) * 8
    lines = 0.0
    for row, count in ((0, pslice), (pslice, CLEN)):
        rows = pl.ds(pl.multiple_of(row + shift, 8), count)
        if row == 0:
            more = results[0][...].reshape(pslice, D)
        else:
            more = sum_read[pl.ds(pl.multiple_of(PLEN + shift, 8), CLEN), :]
        grad_state, line = norm_back(state[rows, :].astype(F32), gain[...], sum_own[rows, :] + more)
        result[rows, :] = grad_next[rows, :] + grad_state
        lines = lines + line
    grad_gain[...] = lines
    if fill:
        first = lax.broadcasted_iota(jnp.int32, (16, 1), 0) == 0
        extras[-1][...] = jnp.where(first, lines, 0.0).astype(LOW)


def attention_down(
    grad_next, state, gains, layer_index, stash, moves, sources, name, known=None
):
    normed, read, query, keys, values, mixed, total, strips, inner, output = stash
    tokens = normed.shape[0]
    pslice = tokens - CLEN
    _, cols, piece, _ = inner.shape
    table = jax.ShapeDtypeStruct((16, WRAP), F32)
    block = lambda rows: pl.BlockSpec((rows, 128), lambda i: (0, i))
    rows = Reduce(
        (pslice // 16, 16, D), ("core", "x"), take=lambda outs, extras: extras[5], keep=True
    )
    share = (4, cols, 4, piece, D)
    body, shown, extra = down_kernel, [jax.ShapeDtypeStruct(share, LOW)], []
    more, more_specs = [], []
    last = known is not None
    ends = []
    if not last:
        (grad_next, *ends) = grad_next

        def body(pslice, *refs):
            refs = list(refs)
            given = [refs.pop(15) for _ in ends]
            found = [refs.pop(19) for _ in range(2)]
            formed = refs.pop()

            @pl.when(pl.program_id(0) == 0)
            def _():
                take_rows(refs[0], *given, *found, formed)

            down_kernel(pslice, formed, *refs[1:])

        shown = [jax.ShapeDtypeStruct(share, LOW)]
        extra = [pltpu.VMEM((tokens, D), F32)]
        more, more_specs = list(ends), [once(block.shape) for block in ends]
        more_specs[-1] = line_block(3, (1, D))
    if last:
        def body(pslice, *refs):
            refs = list(refs)
            known_lines, small = refs.pop(15), refs[-2]
            down_kernel(pslice, *refs[:17], refs[-3], refs[17], *refs[18:-3])

            @pl.when(pl.program_id(0) == pl.num_programs(0) - 1)
            def _():
                small[:16, :] = refs[17][...].astype(LOW)
                small[16:, :] = known_lines[...]

        shown = []
        extra = [
            pltpu.VMEM(share, LOW),
            pltpu.VMEM((16 + known.shape[0], WRAP), LOW),
            pltpu.VMEM((16, D), LOW),
        ]
        more, more_specs = [known], [once(known.shape)]
    return carry(
        functools.partial(body, pslice),
        [(rows, (LATE, LATE + 2, LATE + 4))] + moves,
        grid=(HEADS // 2,),
        out_shape=(
            jax.ShapeDtypeStruct((tokens, D), F32),
            jax.ShapeDtypeStruct((1, D), F32),
            *shown,
            jax.ShapeDtypeStruct(table.shape, F32),
            *([] if last else [jax.ShapeDtypeStruct((1, D), F32), jax.ShapeDtypeStruct((8, D), F32)]),
        ),
        in_specs=[
            once((tokens, D)),
            once((tokens, D)),
            line_block(2 * layer_index, (1, D)),
            once((tokens, D)),
            once((KEYS, D)),
            block(tokens),
            block(KEYS),
            block(KEYS),
            block(tokens),
            block(tokens),
            strip_block(),
            head_block(cols, piece, 0),
            head_block(cols, piece, 1),
            head_block(cols, piece, 2),
            outer_block(cols, piece),
            *more_specs,
        ],
        out_specs=(
            once((tokens, D)),
            once((1, D)),
            *[once(share) for _ in shown],
            once(table.shape),
            *([] if last else [once((1, D)), once((8, D))]),
        ),
        scratch_shapes=[
            pltpu.VMEM((tokens, D), LOW),
            pltpu.VMEM((D, D), LOW),
            pltpu.VMEM((D, D), LOW),
            pltpu.VMEM((tokens, D), F32),
            pltpu.VMEM((KEYS, D), F32),
            pltpu.VMEM((4, 1, pslice // 16, 16, D), LOW),
            pltpu.VMEM((tokens, KEYS), F32),
            pltpu.VMEM((tokens, KEYS), F32),
            pltpu.VMEM((tokens, KEYS), LOW),
            pltpu.VMEM((tokens, KEYS), LOW),
            pltpu.VMEM((128, STRIP), F32),
            pltpu.VMEM((128, KEYS), F32),
            pltpu.VMEM((128, KEYS), F32),
            *extra,
        ],
        mib=62,
        name=name,
        after=[(LATE + 4.5, functools.partial(down_after, pslice, last))],
    )(
        grad_next,
        state,
        gains,
        normed,
        read,
        query,
        keys,
        values,
        mixed,
        total,
        strips,
        inner,
        inner,
        inner,
        output,
        *more,
        *sources,
    )


def mlp_blocks(cols, piece):
    return (
        pl.BlockSpec((4, cols, piece, D), lambda i: (0, 0, 0, i)),
        pl.BlockSpec((None, cols, 4 * piece, D), lambda i: (i, 0, 0, 0)),
    )


MLP_STEP = HEADS // 2


def mlp_load(extras, results):
    dense_in, dense_out = results[:2]
    inner, outer, arrived = extras[-3:]
    copies = []
    for j in range(4):
        source = dense_in.at[:, :, :, pl.ds(j * D, D)]
        copies.append((Within(source, inner.at[j], arrived.at[0, j]),))
        copies[j] += (Within(dense_out.at[j], outer.at[j], arrived.at[1, j]),)
    return copies


def mlp_part(j, own_in, own_out, extras, results):
    state, gain = own_out[0], own_in[-2]
    normed, result = own_out[10:12]
    inner, outer = extras[-3:-1]
    copies = mlp_load(extras, results)
    if j == 0:
        for pair in copies:
            for copy in pair:
                copy.start()
        normed[...] = norm_rows(state[...], gain[...]).astype(LOW)
        result[...] = state[...]
    for copy in copies[j]:
        copy.wait()
    active = gelu(dot_low(normed[...], inner[j].reshape(D, D))).astype(LOW)
    result[...] += dot_low(active, outer[j].reshape(D, D))


def mlp_end(own_in, own_out, extras, results):
    gain, result, normed = own_in[-1], own_out[11], own_out[12]
    shift = pl.multiple_of((pl.program_id(0) - (pl.num_programs(0) - 1)) * 8, 8)
    normed[...] = norm_rows(result[pl.ds(shift, normed.shape[0]), :], gain[...]).astype(LOW)


def mlp_down_kernel(
    grad_next,
    state,
    normed,
    gain,
    first,
    second,
    last_state,
    gates,
    picks,
    outcome,
    result,
    grad_gain,
    output,
    low,
    total,
    grads,
):
    step = pl.program_id(0)

    @pl.when(step == 0)
    def _():
        output[...] = last_state[...]

    @pl.when(step < 2)
    def _():
        gate = jnp.where(step == 0, gates[:, :1], gates[:, 1:2])
        output[...] += gate * dot_low(picks[step], outcome[...])

    @pl.when(step == 0)
    def _():
        low[...] = grad_next[...].astype(LOW)
        total[...] = jnp.zeros_like(total)

    inner, outer = first[...].reshape(D, D), second[...].reshape(D, D)
    active, slope = gelu_parts(dot_low(normed[...], inner))
    grad_hidden = (slope * dot_back(low[...], outer)).astype(LOW)
    _, cols, _, piece, _ = grads.shape
    grad_second = dot_over(active.astype(LOW), low[...]).astype(LOW)
    grads[step, :, :4] = grad_second.reshape(cols, 4, piece, D)
    grads[:, :, 4 + step] = dot_over(normed[...], grad_hidden).astype(LOW).reshape(4, cols, piece, D)
    total[...] += dot_back(grad_hidden, inner)

    @pl.when(step == pl.num_programs(0) - 1)
    def _():
        grad_state, grad_line = norm_back(state[...], gain[...], total[...])
        result[...] = grad_next[...] + grad_state
        grad_gain[...] = grad_line


def mlp_down(grad_next, state, normed, gains, dense_in, dense_out, ends, moves, sources, name):
    tokens = state.shape[0]
    _, cols, piece, _ = dense_in.shape
    pairs = CoreSum((piece, D), cols, lambda outs, extras: extras[2])
    return carry(
        mlp_down_kernel,
        [(pairs, (0, 1, 2, 3, LATE, LATE + 1))] + moves,
        grid=(4,),
        out_shape=(
            jax.ShapeDtypeStruct((tokens, D), F32),
            jax.ShapeDtypeStruct((1, D), F32),
            jax.ShapeDtypeStruct((tokens, D), F32),
        ),
        in_specs=[
            once((tokens, D)),
            once((tokens, D)),
            once((tokens, D)),
            line_block(1, (1, D)),
            *mlp_blocks(cols, piece),
            *[once(block.shape) for block in ends],
        ],
        out_specs=(once((tokens, D)), once((1, D)), once((tokens, D))),
        scratch_shapes=[
            pltpu.VMEM((tokens, D), LOW),
            pltpu.VMEM((tokens, D), F32),
            pltpu.VMEM((4, cols, 8, piece, D), LOW),
        ],
        mib=60,
        name=name,
    )(grad_next, state, normed, gains, dense_in, dense_out, *ends, *sources)


def routed_kernel(
    sent,
    sent_gates,
    sent_cotangent,
    first,
    second,
    outcome,
    returned,
    reach,
    grad_first,
    grad_second,
    rows,
    gates,
    cotangent,
    inner,
    outer,
    active_all,
    hidden_all,
    upstream,
    back,
    back_reach,
    turned,
    sum_up,
    sum_down,
    held,
    near,
    row_send,
    row_recv,
    gate_send,
    gate_recv,
    back_send,
    back_recv,
    reach_send,
    reach_recv,
    core_send,
    core_recv,
    local,
    store,
):
    capacity = rows.shape[1]
    barrier = pltpu.get_barrier_semaphore()
    others = range(1, len(SLOTS))
    row, across, core, plane = neighbours()
    c = lax.rem(row, 2)
    for slot in others:
        pl.semaphore_signal(barrier, inc=1, device_id=slot_device(slot), device_id_type=MESH)
    pl.semaphore_signal(barrier, inc=1, device_id=dict(row=core), device_id_type=MESH)
    loads = [
        Within(sent.at[0], rows.at[0], local.at[0]),
        Within(sent_gates.at[0], gates.at[0], local.at[1]),
        Within(sent_cotangent, cotangent, local.at[2]),
        Within(first, inner, local.at[3]),
        Within(second, outer, local.at[4]),
    ]
    for load in loads:
        load.start()
    pl.semaphore_wait(barrier, len(others) + 1)

    def there(slot):
        device = slot_device(slot)
        return (
            remote(sent_gates.at[slot], gates.at[slot], gate_send, gate_recv, slot, **device),
            remote(sent.at[slot], rows.at[slot], row_send, row_recv, slot, **device),
        )

    def home(slot):
        device = slot_device(slot)
        return (
            remote(back_reach.at[slot], reach.at[slot], reach_send, reach_recv, slot, **device),
            remote(back.at[slot], returned.at[slot], back_send, back_recv, slot, **device),
        )

    own_home = [
        Within(back_reach.at[0], reach.at[0], local.at[5]),
        Within(back.at[0], returned.at[0], local.at[6]),
    ]
    for slot in (4, 5, 1, 6, 7, 2, 3):
        for copy in there(slot):
            copy.start()
    for load in loads:
        load.wait()
    ones = jnp.ones((8, D), F32)
    count = 2 * capacity
    for b in (0, 2, 1, 3):
        for a in range(2):
            slot = 2 * b + a
            if slot:
                for copy in there(slot):
                    copy.wait_recv()
            gate = gates[slot].T[:capacity, :1]
            at = pl.ds(slot * capacity, capacity)
            upstream[at, :] = (gate * cotangent[slot].astype(F32)).astype(LOW)
        both = pl.ds(2 * b * capacity, count)
        block = rows[2 * b : 2 * b + 2].reshape(count, D)
        sum_up[...] = jnp.zeros_like(sum_up)
        sum_down[...] = jnp.zeros_like(sum_down)

        def part(j):
            active, slope = gelu_parts(dot_low(block, inner[j]))
            active = active.astype(LOW)
            active_all[j, both, :] = active
            sum_up[...] += dot_low(active, outer[j])
            hidden = (slope * dot_back(upstream[both, :], outer[j])).astype(LOW)
            hidden_all[j, both, :] = hidden
            sum_down[...] += dot_back(hidden, inner[j])

        each(4, part)
        back[2 * b : 2 * b + 2] = sum_down[...].astype(LOW).reshape(2, capacity, D)
        outcome[2 * b : 2 * b + 2] = sum_up[...].astype(LOW).reshape(2, capacity, D)
        for a in range(2):
            slot = 2 * b + a
            met = cotangent[slot].astype(F32) * outcome[slot].astype(F32)
            line = lax.dot_general(
                ones, met, (((1,), (1,)), ((), ())), precision=HIGH, preferred_element_type=F32
            )
            back_reach[slot] = jnp.pad(line, ((0, 0), (0, back_reach.shape[2] - capacity)))
            if slot:
                for copy in home(slot):
                    copy.start()
            else:
                for copy in own_home:
                    copy.start()
    turned[...] = rows[...].reshape(len(SLOTS) * capacity, D).T

    def formed(j):
        return dot_low(turned[...], hidden_all[j]), dot_over(active_all[j], upstream[...])

    def passed(i, k):
        return remote(held.at[i, k], near.at[i, k], core_send, core_recv, 2 * i + k, row=core)

    def stored(i, k):
        return Within(near.at[i, k], (grad_first, grad_second)[k].at[i], store.at[i, k])

    def give(i):
        for k, value in enumerate(formed(2 * i + 1 - c)):
            held[i, k] = value.astype(LOW)
            passed(i, k).start()

    def meet(i):
        for k, value in enumerate(formed(2 * i + c)):
            passed(i, k).wait_recv()
            near[i, k] = (value + near[i, k].astype(F32)).astype(LOW)
            stored(i, k).start()

    each(2, give)
    each(2, meet)
    for i in range(2):
        for k in range(2):
            stored(i, k).wait()
            passed(i, k).wait_send()
    for copy in own_home:
        copy.wait()
    for slot in (4, 5, 1, 6, 7, 2, 3):
        for copy in home(slot):
            copy.wait_recv()
    for slot in (4, 5, 1, 6, 7, 2, 3):
        for copy in there(slot) + home(slot):
            copy.wait_send()


def routed(sent, gates, cotangent, first, second, name):
    slots, capacity, _ = sent.shape
    hbm = pl.BlockSpec(memory_space=pl.ANY)
    count = slots * capacity
    low = jax.ShapeDtypeStruct(sent.shape, LOW)
    share = jax.ShapeDtypeStruct((2,) + first.shape[1:], LOW)
    pairs = [pltpu.SemaphoreType.DMA((slots,)) for _ in range(8)]
    return pl.pallas_call(
        routed_kernel,
        out_shape=(low, low, jax.ShapeDtypeStruct(gates.shape, F32), share, share),
        in_specs=[hbm] * 5,
        out_specs=(pl.BlockSpec(memory_space=pltpu.VMEM), hbm, hbm, hbm, hbm),
        scratch_shapes=[
            pltpu.VMEM(sent.shape, LOW),
            pltpu.VMEM(gates.shape, F32),
            pltpu.VMEM(sent.shape, LOW),
            pltpu.VMEM(first.shape, LOW),
            pltpu.VMEM(second.shape, LOW),
            pltpu.VMEM((4, count, D), LOW),
            pltpu.VMEM((4, count, D), LOW),
            pltpu.VMEM((count, D), LOW),
            pltpu.VMEM(sent.shape, LOW),
            pltpu.VMEM(gates.shape, F32),
            pltpu.VMEM((D, count), LOW),
            pltpu.VMEM((2 * capacity, D), F32),
            pltpu.VMEM((2 * capacity, D), F32),
            pltpu.VMEM((2, 2, D, D), LOW),
            pltpu.VMEM((2, 2, D, D), LOW),
            *pairs,
            pltpu.SemaphoreType.DMA((4,)),
            pltpu.SemaphoreType.DMA((4,)),
            pltpu.SemaphoreType.DMA((7,)),
            pltpu.SemaphoreType.DMA((2, 2)),
        ],
        compiler_params=pltpu.CompilerParams(
            vmem_limit_bytes=62 * MIB, collective_id=name, has_side_effects=True
        ),
    )(sent, gates, cotangent, first, second)


def finish_kernel(
    index,
    small,
    line,
    early_q,
    early_k,
    early_b,
    late_a,
    late_b,
    dense_b,
    dense_a,
    dense_rest,
    gain_share,
    rel_share,
    route_share,
    qkv,
    out,
    dense_in,
    dense_out,
):
    row, col = lax.axis_index("row"), lax.axis_index("col")
    place = row * 4 + col
    width = gain_share.shape[1]
    buckets = rel_share.shape[1]
    lines = jnp.concatenate([line[:8, :D], small[32:48, :D]], 0)
    lines = pltpu.roll(lines, lax.rem(D - place * width, D), 1)[:, :width]
    gain_share[...] = jnp.concatenate([lines[0:1], lines[10:11], lines[8:9], lines[9:10]], 0)
    route_share[...] = lines[11:19]
    wanted = place * buckets + lax.broadcasted_iota(jnp.int32, (8, 1), 0)
    hot = (index[...] == wanted).astype(F32)
    for i, block in enumerate((small[:16, :], small[16:32, :])):
        sums = lax.dot_general(
            hot, block, (((1,), (1,)), ((), ())), precision=HIGH, preferred_element_type=F32
        )
        rel_share[i] = sums[:buckets, :HEADS]
    for i, blocks in enumerate(
        ((early_q[0], early_k[0], early_b[0]), (late_a[0], late_a[1], late_b[0]))
    ):
        for k, block in enumerate(blocks):
            qkv[i, :, k * D : (k + 1) * D] = block
    out[0] = early_b[1]
    out[1] = late_b[1]
    for k in range(4):
        dense_in[:, k * D : (k + 1) * D] = dense_b[k]
    for k in range(2):
        dense_out[k] = dense_a[k]
        dense_out[2 + k] = dense_rest[k]


def finish(index, *blocks):
    piece = blocks[2].shape[1]
    shapes = (
        (4, piece),
        (2, BUCKETS * piece // D, HEADS),
        (8, piece),
        (2, piece, 3 * D),
        (2, piece, D),
        (piece, FF),
        (4, piece, D),
    )
    return pl.pallas_call(
        finish_kernel,
        out_shape=tuple(jax.ShapeDtypeStruct(shape, F32) for shape in shapes),
        compiler_params=pltpu.CompilerParams(vmem_limit_bytes=32 * MIB),
    )(index, *blocks)


def tiled(
    inputs,
    cotangent,
    routes,
    buckets,
    norm_gains,
    attn_qkv,
    attn_out,
    rel_bias,
    mlp_in,
    mlp_out,
    router,
    expert_in,
    expert_out,
):
    grid = ("row", "col")
    places = lax.axis_size(grid)
    cols, planes = lax.axis_size("col"), lax.axis_size("dp")
    experts = planes * cols
    tokens = inputs.shape[1]
    pslice = tokens - CLEN
    capacity = 3 * tokens // experts
    piece = D // places

    small = [norm_gains.reshape(-1), rel_bias.reshape(-1), router.reshape(-1)]
    cuts = [part.shape[0] for part in small]
    packed = jnp.concatenate(small)
    packed = jnp.pad(packed, (0, -packed.shape[0] % 2048)).reshape(1, -1, 128)

    pair, cut = (2, piece, D), (piece, 3 * D)
    early = (0, LATE, LATE, LATE, LATE)
    inner_a = layer(Gather(cut, False, cols, span=(0, 2 * D)), 0)
    inner_b = layer(Gather(cut, True, cols, span=(2 * D, D), into=inner_a), 0)
    packed, inner0, output0, shared0 = carry(
        None,
        [
            (Gather(packed.shape, False, cols), early),
            (inner_a, early),
            (inner_b, early),
            (layer(Gather((piece, D), True, cols), 0), early),
            (Rows((pslice, D)), (0, LATE, LATE)),
        ],
        (1,),
        [],
        [],
        [],
        [],
        60,
        1,
    )(packed, attn_qkv, attn_qkv, attn_out, inputs[0, :pslice])
    packed = packed.reshape(places, -1)
    gains = packed[:, : cuts[0]].reshape(places, 4, -1).transpose(1, 0, 2).reshape(4, 1, D).astype(F32)
    rel = packed[:, cuts[0] : cuts[0] + cuts[1]].reshape(places, 2, -1, HEADS)
    rel = rel.transpose(1, 3, 0, 2).reshape(2, HEADS, BUCKETS)
    route_w = packed[:, cuts[0] + cuts[1] : sum(cuts)].reshape(D, experts)

    gap = jnp.full((WRAP - KEYS,), -1, jnp.int32)
    index = jnp.concatenate([jnp.flip(buckets[: PLEN + 1]), gap, jnp.flip(buckets[PLEN + 1 :])])
    hot = (jnp.arange(BUCKETS, dtype=jnp.int32)[:, None] == index[None, :]).astype(LOW)
    floor = jnp.where(index < 0, NEG, 0.0).astype(F32)
    tables = jnp.pad(rel, ((0, 0), (0, 16 - HEADS), (0, 0))).reshape(32, BUCKETS)
    tables = (dot_low(tables, hot) + floor[None]).reshape(2, 16, WRAP)

    rows = Rows((pslice, D), take=lambda outs, extras: outs[12].at[pl.ds(0, pslice)])
    state1, stash1, (picks, normed1, state2, normed2, sent_cotangent), moved = attention_up(
        inputs[0],
        inputs[0],
        shared0,
        0,
        gains,
        tables,
        inner0,
        output0,
        [
            (Gather(mlp_in.shape, True, cols), (0, 2, 4, MLP_STEP, MLP_STEP + 0.1)),
            (Gather(mlp_out.shape, True, cols), (0, 2, 4, MLP_STEP, MLP_STEP + 0.1)),
            (Rows(expert_in.shape[1:]), (0, 4, LATE + 0.5)),
            (layer(Gather(cut, True, cols), 1), (3, 5, 7, LATE + 0.4, LATE + 0.5)),
            (layer(Gather((piece, D), True, cols), 1), (3, 5, 7, LATE + 0.4, LATE + 0.5)),
            (rows, (LATE + 0.1, LATE + 0.3, LATE + 0.5)),
        ],
        (mlp_in, mlp_out, expert_in[0], attn_qkv, attn_out),
        2,
        more=(routes[0], cotangent[0], gains, gains),
        extra=(
            pltpu.VMEM((4, 4, cols, piece, D), LOW),
            pltpu.VMEM((4, cols, 4 * piece, D), LOW),
            pltpu.SemaphoreType.DMA((2, 4)),
        ),
        after=[(MLP_STEP + j + 0.5, functools.partial(mlp_part, j)) for j in range(4)]
        + [(LATE, mlp_end)],
    )
    dense_in, dense_out, first, inner1, output1, shared2 = moved
    route_w = jnp.pad(route_w, ((0, 0), (0, 128 - experts)))
    state3, stash3, (normed3, gates, line, sent), (second, far_cotangent) = attention_up(
        state2,
        normed2,
        shared2,
        1,
        gains,
        tables,
        inner1,
        output1,
        [(Rows(expert_out.shape[1:]), (0, 5, LATE)), (Swap((capacity, D)), (0, LATE))],
        (expert_out[0], sent_cotangent),
        4,
        more=(gains, route_w, routes[0], picks),
    )

    outcome, returned, reach, grad_first, grad_second = routed(
        sent, line, far_cotangent, first, second, 5
    )
    returned = returned.reshape(experts * capacity, D)
    laid = (2, 1, places, piece, D)
    octet = (places // 2, piece, D)
    grad_first, grad_second = grad_first.reshape(laid), grad_second.reshape(laid)
    grad2, gain_third, late, table_late, gain_last, grad_route, own_first, own_second, outcome = (
        attention_down(
        (cotangent[0], returned, reach, picks, gates, normed3, routes[0], route_w, state3, gains),
        state2,
        gains,
        1,
        stash3,
        [
            (Reduce((places, piece, D), ("x",)), (0, 5)),
            (Reduce(octet, ("x",)), (1, LATE + 3)),
            (Swap((capacity, D)), (0, LATE + 5)),
        ],
        (grad_first, grad_second, outcome),
        6,
    ))
    outcome = outcome.reshape(experts * capacity, D)
    grad1, gain_second, output, dense_pairs, own_rest, late_a, late_b = mlp_down(
        grad2,
        state1,
        normed1,
        gains,
        dense_in,
        dense_out,
        (state3, gates, picks, outcome),
        [
            (Reduce(octet, ("x",), first=places // 2), (0, LATE)),
            (Reduce(pair, ("core", "x"), cols), (0, 1, LATE + 2)),
            (Reduce(pair, ("core", "y"), cols, first=2), (0, 1, LATE)),
        ],
        (grad_second, late, late),
        7,
    )
    lines = jnp.concatenate([gain_third, gain_last, gain_second, grad_route], 0)
    lines = jnp.pad(lines, ((0, 16 - lines.shape[0]), (0, WRAP - D)))
    known = jnp.concatenate([table_late, lines], 0).astype(LOW)
    quad = (4, piece, D)
    single = (1, piece, D)
    held = lambda outs, extras: extras[-3]
    (
        grad0,
        _,
        _,
        late_a,
        late_b,
        dense_a,
        dense_a_rest,
        dense_b,
        early_q,
        early_k,
        early_b,
        small,
        line,
    ) = attention_down(
        grad1,
        inputs[0],
        gains,
        0,
        stash1,
        [
            (Reduce(pair, ("z", "sum"), cols), (0, 2, 4)),
            (Reduce(single, ("x", "z", "swap"), cols), (0, 1, 3, 5)),
            (Reduce(pair, ("x", "z", "sum"), cols), (0, 2, 5, LATE + 3)),
            (Reduce(pair, ("x", "z", "sum"), cols, first=2), (2, 4, LATE + 1, LATE + 4)),
            (
                Reduce(quad, ("y", "x", "z", "swap"), cols, first=4),
                (0, 4, LATE + 0.2, LATE + 5, LATE + 7),
            ),
            (
                Reduce(single, ("core", "x", "z", "sum"), cols, take=held),
                (LATE, LATE + 2, LATE + 5, LATE + 8, LATE + 10),
            ),
            (
                Reduce(single, ("core", "x", "z", "sum"), cols, first=1, take=held),
                (LATE, LATE + 2, LATE + 6, LATE + 9, LATE + 10),
            ),
            (
                Reduce(pair, ("core", "y", "x", "z", "swap"), cols, first=2, take=held),
                (LATE, LATE + 2, LATE + 5, LATE + 7, LATE + 9, LATE + 10),
            ),
            (
                Total((16 + known.shape[0], WRAP), take=lambda outs, extras: extras[-2]),
                (LATE - 0.5, LATE + 0.5, LATE + 1.5, LATE + 2.5, LATE + 4.2),
            ),
            (
                Total((16, D), take=lambda outs, extras: extras[-1], short=True),
                (LATE + 4.6, LATE + 6.5, LATE + 9.5),
            ),
        ],
        (late_a, late_b, dense_pairs, dense_pairs, dense_pairs),
        8,
        known=known,
    )
    gain_share, rel_share, route_share, qkv_share, out_share, in_share, up_share = finish(
        index.reshape(1, -1),
        small,
        line,
        early_q,
        early_k,
        early_b,
        late_a,
        late_b,
        dense_b,
        dense_a,
        dense_a_rest,
    )
    return (
        output[None],
        grad0[None],
        gain_share,
        qkv_share,
        out_share,
        rel_share,
        in_share,
        up_share.reshape(-1, D),
        route_share.T,
        own_first.reshape(1, D, D),
        jnp.concatenate([own_second, own_rest], 0).reshape(1, D, D),
    )


def solution(mesh):
    in_specs = (
        P(("dp", "col"), "row", None),
        P(("dp", "col"), "row", None),
        P(("dp", "col"), "row", None),
        P(),
        P(None, ("row", "col")),
        P(None, ("row", "col"), None),
        P(None, ("row", "col"), None),
        P(None, ("row", "col"), None),
        P(("row", "col"), None),
        P(("row", "col"), None),
        P(("row", "col"), None),
        P(("dp", "col"), None, "row"),
        P(("dp", "col"), "row", None),
    )
    out_specs = (
        P(("dp", "col"), "row", None),
        P(("dp", "col"), "row", None),
        P(None, ("row", "col")),
        P(None, ("row", "col"), None),
        P(None, ("row", "col"), None),
        P(None, ("row", "col"), None),
        P(("row", "col"), None),
        P(("row", "col"), None),
        P(("row", "col"), None),
        P(("dp", "col"), None, "row"),
        P(("dp", "col"), "row", None),
    )
    sizes = dict(mesh.shape)
    piece = D // (sizes["row"] * sizes["col"])
    capacity = 3 * (PLEN // sizes["row"] + CLEN) // (sizes["dp"] * sizes["col"])
    whole_tiles = (sizes["dp"], sizes["row"], sizes["col"]) == (2, 4, 4) and piece % 16 == 0 and capacity % 16 == 0
    return jax.shard_map(
        tiled if whole_tiles else general, mesh=mesh, in_specs=in_specs, out_specs=out_specs, check_vma=False
    )
```

```python
import functools

import jax
import jax.numpy as jnp
from jax import lax
from jax.experimental import pallas as pl
from jax.experimental.pallas import tpu as pltpu
from jax.sharding import PartitionSpec as P

D = 768
HEADS = 12
HDIM = 64
FF = 3072
BUCKETS = 32
PLEN = 1024
CLEN = 128
KEYS = PLEN + CLEN
WRAP = KEYS + 128
STRIP = 2 * PLEN
NEG = -1e30
EPS = 1e-06
CURVE = 0.7978845608028654
CUBE = 0.044715
HIGH = lax.Precision.HIGHEST
F32 = jnp.float32
LOW = jnp.bfloat16
MIB = 1 << 20


def dot_low(left, right):
    return jnp.dot(left, right, preferred_element_type=F32)


def dot_back(left, right):
    return lax.dot_general(left, right, (((1,), (1,)), ((), ())), preferred_element_type=F32)


def dot_over(left, right):
    return lax.dot_general(left, right, (((0,), (0,)), ((), ())), preferred_element_type=F32)


def normalise(values):
    center = values - jnp.mean(values, -1, keepdims=True)
    scale = lax.rsqrt(jnp.mean(center * center, -1, keepdims=True) + EPS)
    return center * scale, scale


def norm_rows(values, gain):
    return normalise(values)[0] * gain


def norm_back(values, gain, upstream):
    unit, scale = normalise(values)
    pulled = upstream * gain
    shift = jnp.mean(pulled, -1, keepdims=True)
    along = jnp.mean(pulled * unit, -1, keepdims=True)
    return (pulled - shift - unit * along) * scale, jnp.sum(upstream * unit, 0, keepdims=True)


def gelu_parts(values):
    square = values * values
    bend = jnp.tanh(CURVE * (values + CUBE * square * values))
    half = 0.5 * (1.0 + bend)
    slope = half + 0.5 * values * (1.0 - bend * bend) * (CURVE + 3.0 * CURVE * CUBE * square)
    return values * half, slope


def gelu(values):
    return 0.5 * values * (1.0 + jnp.tanh(CURVE * (values + CUBE * values * values * values)))


def params(mib, steps=1):
    return pltpu.CompilerParams(
        vmem_limit_bytes=mib * MIB, dimension_semantics=("arbitrary",) * steps
    )


def whole(shape):
    return pl.BlockSpec(shape, lambda *_: (0,) * len(shape))


MESH = pl.DeviceIdType.MESH


class Remote:
    def __init__(self, src, dst, send, recv, index, device):
        self.parts = (src, dst, send, recv, index, device)

    def described(self):
        src, dst, send, recv, index, device = self.parts
        return pltpu.make_async_remote_copy(
            src_ref=src,
            dst_ref=dst,
            send_sem=send.at[index],
            recv_sem=recv.at[index],
            device_id=device,
            device_id_type=MESH,
        )

    def start(self):
        self.described().start()

    def wait_recv(self):
        self.described().wait_recv()

    def wait_send(self):
        self.described().wait_send()


def remote(src, dst, send, recv, index, **device):
    return Remote(src, dst, send, recv, index, device)


def neighbours():
    row, dp = lax.axis_index("row"), lax.axis_index("dp")
    across = lax.rem(row + 2, 4)
    core = row + 1 - 2 * lax.rem(row, 2)
    return row, across, core, dp + 1 - 2 * lax.rem(dp, 2)


class Within:
    def __init__(self, src, dst, sem):
        self.parts = (src, dst, sem)

    def start(self):
        pltpu.make_async_copy(*self.parts).start()

    def wait(self):
        pltpu.make_async_copy(*self.parts).wait()


class Gather:
    phases = 5

    def __init__(self, shape, split, cols, span=None, into=None, take=None):
        self.shape, self.split, self.cols, self.take, self.into = shape, split, cols, take, into
        self.span = (0, shape[-1]) if span is None else span
        self.spec = pl.BlockSpec(memory_space=pl.ANY)
        self.result = jax.ShapeDtypeStruct((4, cols) + shape, LOW)
        count = 4 * cols - 1 + (4 * cols - 2 if split else 0)
        self.scratch = [
            pltpu.SemaphoreType.DMA((count + 2 * cols,)),
            pltpu.SemaphoreType.DMA((count + 2 * cols,)),
            pltpu.SemaphoreType.DMA((1,)),
        ]

    def copies(self, src, dst, send, recv, local):
        cols = self.cols
        row, across, core, plane = neighbours()
        col, dp = lax.axis_index("col"), lax.axis_index("dp")
        first, width = self.span
        half = width // 2
        lead = (slice(None),) * (len(self.shape) - 1)
        full = lead + (pl.ds(first, width),)
        mine = pl.multiple_of(first + dp * half, 128)
        others = pl.multiple_of(first + (1 - dp) * half, 128)
        part = lead + (pl.ds(mine, half),) if self.split else full
        rest = lead + (pl.ds(others, half),)
        number = [0]

        def make(source, target, **device):
            number[0] += 1
            return remote(source, target, send, recv, number[0] - 1, **device)

        def piece(where, step, which):
            return dst.at[where, lax.rem(col - step + cols, cols)].at[which]

        own = src.at[part]
        out = {}
        out["local"] = Within(src.at[full], piece(row, 0, full), local.at[0])
        out["z"] = [
            make(own, piece(row, 0, part), col=lax.rem(col + step, cols)) for step in range(1, cols)
        ]
        out["x"] = [make(own, piece(row, 0, part), row=across)]
        out["x"] += [
            make(piece(row, step, part), piece(row, step, part), row=across)
            for step in range(1, cols)
        ]
        out["core own"] = make(src.at[full], piece(row, 0, full), row=core)
        out["core z"] = [
            make(piece(row, step, part), piece(row, step, part), row=core) for step in range(1, cols)
        ]
        out["core x"] = [
            make(piece(across, step, part), piece(across, step, part), row=core)
            for step in range(cols)
        ]
        if self.split:
            out["y z"] = [
                make(piece(row, step, part), piece(row, step, part), dp=plane)
                for step in range(1, cols)
            ]
            out["y x"] = [
                make(piece(across, step, part), piece(across, step, part), dp=plane)
                for step in range(cols)
            ]
            out["core y z"] = [
                make(piece(row, step, rest), piece(row, step, rest), row=core)
                for step in range(1, cols)
            ]
            out["core y x"] = [
                make(piece(across, step, rest), piece(across, step, rest), row=core)
                for step in range(cols)
            ]
        return out

    def peers(self):
        cols, col = self.cols, lax.axis_index("col")
        row, across, core, plane = neighbours()
        found = {(0, step): dict(col=lax.rem(col + step, cols)) for step in range(1, cols)}
        found.update(across=dict(row=across), core=dict(row=core))
        if self.split:
            found[(1, 0)] = dict(dp=plane)
        return found

    def phase(self, number, *refs):
        out = self.copies(*refs)
        if number == 0:
            out["local"].start()
            for copy in out["z"]:
                copy.start()
            out["x"][0].start()
            out["core own"].start()
        elif number == 1:
            for step in self.order():
                out["z"][step - 1].wait_recv()
                out["x"][step].start()
                if self.split:
                    out["y z"][step - 1].start()
                out["core z"][step - 1].start()
        elif number == 2:
            for step in [0] + self.order():
                out["x"][step].wait_recv()
                if self.split:
                    out["y x"][step].start()
                out["core x"][step].start()
        elif number == 3 and self.split:
            for step in self.order():
                out["y z"][step - 1].wait_recv()
                out["core y z"][step - 1].start()
            for step in [0] + self.order():
                out["y x"][step].wait_recv()
                out["core y x"][step].start()
        elif number == 4:
            out["local"].wait()
            late = [out["core own"]] + out["core z"] + out["core x"]
            if self.split:
                late += out["core y z"] + out["core y x"]
            for copy in late:
                copy.wait_recv()
            early = out["z"] + out["x"] + late
            if self.split:
                early += out["y z"] + out["y x"]
            for copy in early:
                copy.wait_send()

    def order(self):
        steps = list(range(1, self.cols))
        return sorted(steps, key=lambda step: min(step, self.cols - step))


class Rows:
    phases = 3

    def __init__(self, shape, take=None):
        self.take = take
        self.result = jax.ShapeDtypeStruct((4,) + shape, LOW)
        self.spec = pl.BlockSpec(memory_space=pl.ANY)
        self.scratch = [
            pltpu.VMEM(shape, LOW),
            pltpu.SemaphoreType.DMA((3,)),
            pltpu.SemaphoreType.DMA((3,)),
            pltpu.SemaphoreType.DMA((2,)),
        ]

    def peers(self):
        row, across, core, plane = neighbours()
        return dict(across=dict(row=across), core=dict(row=core))

    def phase(self, number, src, dst, held, send, recv, local):
        row, across, core, plane = neighbours()
        load = Within(src, held, local.at[0])
        own = Within(held, dst.at[row], local.at[1])
        far = remote(src, dst.at[row], send, recv, 0, row=across)
        near = remote(src, dst.at[row], send, recv, 1, row=core)
        on = remote(dst.at[across], dst.at[across], send, recv, 2, row=core)
        if number == 0:
            far.start()
            near.start()
            load.start()
        elif number == 1:
            load.wait()
            own.start()
            far.wait_recv()
            on.start()
        else:
            own.wait()
            near.wait_recv()
            on.wait_recv()
            for copy in (far, near, on):
                copy.wait_send()


SLOTS = [(a, b) for b in range(4) for a in range(2)]


def slot_device(slot):
    a, b = SLOTS[slot]
    dp, col = lax.axis_index("dp"), lax.axis_index("col")
    flipped = (col, col + 1 - 2 * lax.rem(col, 2), lax.rem(col + 2, 4), 3 - col)[b]
    device = {}
    if a:
        device["dp"] = 1 - dp
    if b:
        device["col"] = flipped
    return device


class Swap:
    phases = 2

    def __init__(self, shape, take=None):
        self.take = take
        self.result = jax.ShapeDtypeStruct((len(SLOTS),) + shape, LOW)
        self.spec = pl.BlockSpec(memory_space=pl.ANY)
        self.scratch = [
            pltpu.SemaphoreType.DMA((len(SLOTS),)),
            pltpu.SemaphoreType.DMA((len(SLOTS),)),
            pltpu.SemaphoreType.DMA((1,)),
        ]

    def peers(self):
        return {SLOTS[slot]: slot_device(slot) for slot in range(1, len(SLOTS))}

    def phase(self, number, src, dst, send, recv, local):
        own = Within(src.at[0], dst.at[0], local.at[0])
        copies = [
            remote(src.at[slot], dst.at[slot], send, recv, slot, **slot_device(slot))
            for slot in range(1, len(SLOTS))
        ]
        if number == 0:
            for copy in copies:
                copy.start()
            own.start()
        else:
            own.wait()
            for copy in copies:
                copy.wait_recv()
            for copy in copies:
                copy.wait_send()


def each(count, body):
    lax.fori_loop(0, count, lambda index, carried: (body(index), carried)[1], 0)


class Reduce:
    def __init__(self, shape, ops, cols=1, first=0, take=None, keep=False):
        self.ops, self.cols, self.first, self.take, self.keep = ops, cols, first, take, keep
        self.count, tail = shape[0], shape[1:]
        self.part = self.count // 2 if "y" in ops else self.count
        self.phases = len(ops) + 1
        self.lead = 1 if ops[0] == "z" else 2
        ends = {
            "y": ((2, cols, self.part), LOW),
            "x": ((cols, self.part), LOW) if cols > 1 else ((self.part,), F32),
            "sum": ((self.part,), F32),
            "swap": ((2 * self.part,), F32),
        }
        lead, kind = ends[ops[-1]]
        self.result = jax.ShapeDtypeStruct(lead + tail, kind)
        self.spec = once(self.result.shape)
        full = (self.lead, cols, self.count)
        buffers = {"total": [full]}
        if "core" in ops and take is None:
            buffers["near"] = [full]
        if "y" in ops:
            buffers["y"] = [(2, cols, self.part)]
        if "x" in ops:
            buffers["x"] = [(cols, self.part)]
        if "z" in ops:
            buffers["z"] = [(cols - 1, self.part), (self.part,)]
            buffers["end"] = [(self.part,)]
        self.names = list(buffers)
        self.lengths = [len(buffers[name]) for name in self.names]
        self.scratch = [pltpu.VMEM(lead + tail, LOW) for name in self.names for lead in buffers[name]]
        self.scratch += [
            pltpu.SemaphoreType.DMA((8,)),
            pltpu.SemaphoreType.DMA((8,)),
            pltpu.SemaphoreType.DMA((2,)),
        ]

    def peers(self):
        row, across, core, plane = neighbours()
        found = {}
        if "core" in self.ops:
            found["core"] = dict(row=core)
        if "x" in self.ops:
            found["across"] = dict(row=across)
        slots = (2, 4, 6) if "z" in self.ops else ()
        if {"y", "sum", "swap"} & set(self.ops):
            slots += (1,)
        for slot in slots:
            found[SLOTS[slot]] = slot_device(slot)
        return found

    def phase(self, number, src, out, *scratch):
        scratch = list(scratch)
        held = {
            name: [scratch.pop(0) for _ in range(length)]
            for name, length in zip(self.names, self.lengths)
        }
        send, recv, local = scratch
        row, across, core, plane = neighbours()
        x, c = row // 2, lax.rem(row, 2)
        if self.ops[0] == "z":
            x = 0
        dp, col = lax.axis_index("dp"), lax.axis_index("col")
        total = held["total"][0]
        span = pl.ds(self.first, self.count)
        start = dp * self.part if "y" in self.ops else 0
        part, rest = pl.ds(start, self.part), pl.ds((1 - dp) * self.part, self.part)
        if self.take is not None:
            loads = []
        elif self.ops[0] == "core":
            loads = [Within(src.at[2 * i + c, :, span], total.at[i], local.at[i]) for i in range(2)]
        elif self.ops[0] == "z":
            loads = [Within(src.at[:, span], total.at[0], local.at[0])]
        else:
            loads = [Within(src.at[:, :, span], total, local.at[0])]

        def copies(op):
            if op == "core":
                near = held["near"][0] if self.take is None else total
                return [
                    remote(src.at[2 * i + 1 - c, :, span], near.at[i], send, recv, i, row=core)
                    for i in range(2)
                ]
            begun = op == self.ops[0]
            if op == "y":
                view = total.at[:, :, rest]
                if begun:
                    view = src.at[:, :, pl.ds(self.first + (1 - dp) * self.part, self.part)]
                return [remote(view, held["y"][0], send, recv, 2, dp=plane)]
            if op == "x":
                view = src.at[1 - x, :, span] if begun else total.at[1 - x, :, part]
                return [remote(view, held["x"][0], send, recv, 3, row=across)]
            if op == "z":
                found = []
                for b in (2, 3, 1):
                    device = slot_device(2 * b)
                    view = total.at[x, device["col"], part]
                    if begun:
                        view = src.at[device["col"], span]
                    found.append(remote(view, held["z"][0].at[b - 1], send, recv, 3 + b, **device))
                return found
            return [remote(held["z"][1], held["end"][0], send, recv, 7, dp=plane)]

        wide = lambda value: value.astype(F32)
        count, cols, size = self.count, self.cols, self.part
        if number > 0:
            op = self.ops[number - 1]
            last = number == len(self.ops)
            if number == 1:
                for load in loads:
                    load.wait()
            for copy in copies(op):
                copy.wait_recv()
            if op == "core":

                def add(i):
                    at = (i // (cols * count), lax.rem(i // count, cols), lax.rem(i, count))
                    if self.take is None:
                        more = held["near"][0][at]
                    else:
                        more = src[2 * at[0] + c, at[1], self.first + at[2]]
                    total[at] = (wide(total[at]) + wide(more)).astype(LOW)

                each(2 * cols * count, add)
            elif op == "y":

                def add(i):
                    at = (i // (cols * size), lax.rem(i // size, cols))
                    k = lax.rem(i, size)
                    kept = at + (start + k,)
                    value = wide(total[kept]) + wide(held["y"][0][at + (k,)])
                    if last:
                        out[at + (k,)] = value.astype(LOW)
                    else:
                        total[kept] = value.astype(LOW)

                each(2 * cols * size, add)
            elif op == "x":

                def add(i):
                    z, k = i // size, lax.rem(i, size)
                    value = wide(total[x, z, start + k]) + wide(held["x"][0][z, k])
                    if last and cols == 1:
                        out[k] = value
                    elif last:
                        out[z, k] = value.astype(LOW)
                    else:
                        total[x, z, start + k] = value.astype(LOW)

                each(cols * size, add)
            elif op == "z":

                def add(k):
                    value = wide(total[x, col, start + k])
                    for b in range(cols - 1):
                        value = value + wide(held["z"][0][b, k])
                    held["z"][1][k] = value.astype(LOW)

                each(size, add)
            else:

                def add(k):
                    mine, other = wide(held["z"][1][k]), wide(held["end"][0][k])
                    if op == "sum":
                        out[k] = mine + other
                    else:
                        out[dp * size + k] = mine
                        out[(1 - dp) * size + k] = other

                each(size, add)
        if number < len(self.ops):
            op = self.ops[number]
            for copy in copies(op):
                copy.start()
            if number == 0:
                for load in loads:
                    load.start()
        else:
            for op in self.ops:
                for copy in copies(op):
                    copy.wait_send()


class CoreSum:
    phases = 6

    def __init__(self, shape, cols, take):
        self.take, self.cols = take, cols
        self.result = jax.ShapeDtypeStruct((2, cols, 8) + shape, LOW)
        self.spec = once(self.result.shape)
        self.scratch = [
            pltpu.VMEM(self.result.shape, LOW),
            pltpu.SemaphoreType.DMA((10,)),
            pltpu.SemaphoreType.DMA((10,)),
        ]

    def peers(self):
        row, across, core, plane = neighbours()
        return dict(core=dict(row=core))

    def phase(self, number, src, out, near, send, recv):
        row, across, core, plane = neighbours()
        c = lax.rem(row, 2)

        def inner(j, i):
            at = (slice(None), 4 + j)
            view = src.at[2 * i + 1 - c].at[at]
            return remote(view, near.at[i].at[at], send, recv, 2 * j + i, row=core)

        def outer(i):
            at = (slice(None), pl.ds(0, 4))
            view = src.at[2 * i + 1 - c].at[at]
            return remote(view, near.at[i].at[at], send, recv, 8 + i, row=core)

        def begin(j):
            for i in range(2):
                inner(j, i).start()
            if j % 2 == 1:
                outer(j // 2).start()

        def add(i, z, k):
            out[i, z, k] = (src[2 * i + c, z, k].astype(F32) + near[i, z, k].astype(F32)).astype(LOW)

        def end(j):
            for i in range(2):
                inner(j, i).wait_recv()
            each(2 * self.cols, lambda n: add(n // self.cols, lax.rem(n, self.cols), 4 + j))
            if j % 2 == 1:
                outer(j // 2).wait_recv()
                each(4 * self.cols, lambda n: add(j // 2, n // 4, lax.rem(n, 4)))

        if 1 <= number <= 4:
            begin(number - 1)
        if number in (3, 4):
            end(number - 3)
        if number == 5:
            end(2)
            end(3)
            for j in range(4):
                for i in range(2):
                    inner(j, i).wait_send()
            for i in range(2):
                outer(i).wait_send()


class Total:
    def __init__(self, shape, take=None, short=False):
        self.take, self.short = take, short
        self.phases = 3 if short else 5
        hops, arrivals = (2, 10) if short else (4, 6)
        self.result = jax.ShapeDtypeStruct(shape, F32)
        self.spec = once(shape)
        self.scratch = [
            pltpu.VMEM((hops,) + shape, LOW),
            pltpu.VMEM((arrivals,) + shape, LOW),
            pltpu.SemaphoreType.DMA((arrivals,)),
            pltpu.SemaphoreType.DMA((arrivals,)),
            pltpu.SemaphoreType.DMA((1,)),
        ]

    def hops(self):
        row, across, core, plane = neighbours()
        if self.short:
            first = [dict(row=across), dict(row=lax.rem(core + 2, 4)), dict(row=core)]
            return [first, [slot_device(slot) for slot in (4, 5, 6, 7, 2, 3, 1)]]
        found = [[dict(row=core)], [dict(row=across)], [dict(dp=plane)]]
        return found + [[slot_device(2 * b) for b in (1, 2, 3)]]

    def peers(self):
        row, across, core, plane = neighbours()
        found = dict(across=dict(row=across), core=dict(row=core))
        if self.short:
            found["far"] = dict(row=lax.rem(core + 2, 4))
        for slot in range(1, 8) if self.short else (1, 2, 4, 6):
            found[SLOTS[slot]] = slot_device(slot)
        return found

    def phase(self, number, src, out, mine, other, send, recv, local):
        hops = self.hops()
        starts = [sum(len(hop) for hop in hops[:i]) for i in range(len(hops))]

        def copies(hop):
            return [
                remote(mine.at[hop], other.at[starts[hop] + i], send, recv, starts[hop] + i, **device)
                for i, device in enumerate(hops[hop])
            ]

        if number == 0:
            load = Within(src, mine.at[0], local.at[0])
            load.start()
            load.wait()
        else:
            value = mine[number - 1].astype(F32)
            for i, copy in enumerate(copies(number - 1)):
                copy.wait_recv()
                value = value + other[starts[number - 1] + i].astype(F32)
            if number < len(hops):
                mine[number] = value.astype(LOW)
            else:
                out[...] = value
        if number < len(hops):
            for copy in copies(number):
                copy.start()
        else:
            for hop in range(len(hops)):
                for copy in copies(hop):
                    copy.wait_send()


def greet(flows):
    barrier = pltpu.get_barrier_semaphore()
    devices = {}
    for flow in flows:
        devices.update(flow.peers())
    for device in devices.values():
        pl.semaphore_signal(barrier, inc=1, device_id=device, device_id_type=MESH)
    pl.semaphore_wait(barrier, len(devices))


LATE = 99


def layer(flow, index):
    flow.view = lambda ref: ref.at[index]
    return flow


def carry(body, moves, grid, in_specs, out_specs, out_shape, scratch_shapes, mib, name, after=()):
    inputs, outputs, extras = len(in_specs), len(out_specs), len(scratch_shapes)
    steps = grid[0]
    hbm = pl.BlockSpec(memory_space=pl.ANY)
    flows = [flow for flow, _ in moves]
    used = [at for _, marks in moves for at in marks] + [at for at, _ in after]
    given = [flow for flow in flows if flow.take is None]
    shared = [flow for flow in flows if getattr(flow, "into", None) is not None]
    kept = [flow for flow in flows if getattr(flow, "keep", False)]
    shown = [flow for flow in flows if flow not in shared and flow not in kept]

    def kernel(*refs):
        refs = list(refs)
        take = lambda count: [refs.pop(0) for _ in range(count)]
        own_in = take(inputs)
        sources = {flow: refs.pop(0) for flow in given}
        own_out = take(outputs)
        results = {flow: refs.pop(0) for flow in shown}
        own_extra = take(extras)
        packs = {}
        for flow in flows:
            if flow in kept:
                results[flow] = refs.pop(0)
            elif flow in shared:
                results[flow] = results[flow.into]
            if flow not in sources:
                sources[flow] = flow.take(own_out, own_extra)
            source_of = getattr(flow, "view", None)
            if source_of is not None:
                sources[flow] = source_of(sources[flow])
            packs[flow] = [sources[flow], results[flow]] + take(len(flow.scratch))
        step = pl.program_id(0)

        def run(low, high):
            plan = []
            for index, (flow, marks) in enumerate(moves):
                for number in range(flow.phases):
                    if low <= marks[number] < high:
                        call = functools.partial(flow.phase, number, *packs[flow])
                        plan.append((marks[number], number, index, call))
            for mark, function in after:
                if low <= mark < high:
                    call = functools.partial(
                        function, own_in, own_out, own_extra, [results[flow] for flow in flows]
                    )
                    plan.append((mark, 0, len(moves), call))
            for entry in sorted(plan, key=lambda entry: entry[:3]):
                entry[3]()

        for mark in range(steps):
            if mark == 0 or any(mark <= at < mark + 1 for at in used):

                @pl.when(step == mark)
                def _():
                    if mark == 0:
                        greet(flows)
                    run(mark, mark + 1)

        if body is not None:
            body(*own_in, *own_out, *own_extra)

        @pl.when(step == steps - 1)
        def _():
            run(LATE - 1, LATE + 100)

    scratch = list(scratch_shapes)
    for flow in flows:
        if flow in kept:
            scratch.append(pltpu.VMEM(flow.result.shape, flow.result.dtype))
        scratch += flow.scratch

    def call(*args):
        return pl.pallas_call(
            kernel,
            grid=grid,
            out_shape=tuple(out_shape) + tuple(flow.result for flow in shown),
            in_specs=list(in_specs) + [hbm] * len(given),
            out_specs=tuple(out_specs) + tuple(flow.spec for flow in shown),
            scratch_shapes=scratch,
            compiler_params=pltpu.CompilerParams(
                vmem_limit_bytes=mib * MIB,
                dimension_semantics=("arbitrary",),
                collective_id=name,
                has_side_effects=True,
            ),
        )(*args)

    return call


def bias_table(buckets, rel):
    place = jnp.arange(WRAP, dtype=jnp.int32)
    dist = jnp.where(place <= PLEN, PLEN - place, PLEN + WRAP - place)
    read = (place <= PLEN) | (place > KEYS)
    index = jnp.take(buckets, jnp.clip(dist, 0, KEYS - 1), axis=0)
    hot = ((index[:, None] == jnp.arange(BUCKETS)[None, :]) & read[:, None]).astype(LOW)
    floor = jnp.where(read, 0.0, NEG).astype(F32)
    return hot, floor


def fill_strip(strip, table, head):
    @pl.when(pl.program_id(0) == 0)
    def _():
        strip[:, KEYS:] = jnp.full((128, STRIP - KEYS), NEG, F32)

    line = jnp.broadcast_to(table[pl.ds(head, 1), :], (128, WRAP))
    strip[:, :KEYS] = pltpu.roll(line, 0, 1, stride=1, stride_axis=0)[:, :KEYS]


def tiles_of(pslice):
    places = []
    for tile in range(pslice // 128):
        start = PLEN - (lax.axis_index("row") * pslice + tile * 128)
        places.append((tile * 128, pl.ds(pl.multiple_of(start, 128), PLEN), PLEN))
    places.append((pslice, pl.ds(0, KEYS), KEYS))
    return places


def attend_kernel(pslice, query, keys, values, table, mixed, total, strip, raw, weights):
    pair = pl.program_id(0)
    lane = lax.broadcasted_iota(jnp.int32, (1, 128), 1)

    @pl.when(pair == 0)
    def _():
        weights[:pslice, PLEN:] = jnp.zeros((pslice, CLEN), LOW)

    for half in range(2):
        mine = (lane < HDIM) if half == 0 else (lane >= HDIM)
        fill_strip(strip, table, 2 * pair + half)
        part = jnp.where(mine, query[...], 0) * HDIM ** (-0.5)
        raw[...] = dot_back(part.astype(LOW), keys[...])
        for row, place, count in tiles_of(pslice):
            rows = pl.ds(row, 128)
            scores = raw[rows, :count] + strip[:, place]
            top = jnp.max(scores, -1, keepdims=True)
            raised = jnp.exp(scores - top)
            summed = jnp.sum(raised, -1, keepdims=True)
            weights[rows, :count] = (raised * (1.0 / summed)).astype(LOW)
            log_total = jnp.broadcast_to(top + jnp.log(summed), (128, 128))
            if half == 0:
                total[rows, :] = log_total
            else:
                total[rows, :] = jnp.where(mine, log_total, total[rows, :])
        result = dot_low(weights[...], values[...]).astype(LOW)
        if half == 0:
            mixed[...] = result
        else:
            mixed[...] = jnp.where(mine, result, mixed[...])


def attend_forward(query, keys, values, table):
    tokens = query.shape[0]
    pslice = tokens - CLEN
    block = lambda rows: pl.BlockSpec((rows, 128), lambda i: (0, i))
    return pl.pallas_call(
        functools.partial(attend_kernel, pslice),
        grid=(HEADS // 2,),
        out_shape=(
            jax.ShapeDtypeStruct((tokens, D), LOW),
            jax.ShapeDtypeStruct((tokens, D), F32),
        ),
        in_specs=[block(tokens), block(KEYS), block(KEYS), whole(table.shape)],
        out_specs=(block(tokens), block(tokens)),
        scratch_shapes=[
            pltpu.VMEM((128, STRIP), F32),
            pltpu.VMEM((tokens, KEYS), F32),
            pltpu.VMEM((tokens, KEYS), LOW),
        ],
        compiler_params=params(32),
    )(query, keys, values, table)


def attend_back_kernel(
    pslice,
    query,
    keys,
    values,
    table,
    total,
    grad_mixed,
    grad_query,
    grad_keys,
    grad_values,
    grad_table,
    strip,
    raw,
    pulled,
    probs,
    grads,
    folded,
    sum_keys,
    sum_values,
):
    pair = pl.program_id(0)
    lane = lax.broadcasted_iota(jnp.int32, (1, 128), 1)
    across = lax.broadcasted_iota(jnp.int32, (128, 128), 0)
    along = lax.broadcasted_iota(jnp.int32, (128, 128), 1)
    mirror = (across + along == 127).astype(LOW)

    @pl.when(pair == 0)
    def _():
        probs[:pslice, PLEN:] = jnp.zeros((pslice, CLEN), LOW)
        grads[:pslice, PLEN:] = jnp.zeros((pslice, CLEN), LOW)

    for half in range(2):
        mine = (lane < HDIM) if half == 0 else (lane >= HDIM)
        fill_strip(strip, table, 2 * pair + half)
        part = (jnp.where(mine, query[...], 0) * HDIM ** (-0.5)).astype(LOW)
        upstream = jnp.where(mine, grad_mixed[...], 0).astype(LOW)
        raw[...] = dot_back(part, keys[...])
        pulled[...] = dot_back(upstream, values[...])
        folded[...] = jnp.zeros_like(folded)
        for row, place, count in tiles_of(pslice):
            rows = pl.ds(row, 128)
            log_total = total[rows, half * HDIM : half * HDIM + 1]
            chance = jnp.exp(raw[rows, :count] + strip[:, place] - log_total)
            product = chance * pulled[rows, :count]
            centre = jnp.sum(product, -1, keepdims=True)
            slope = (product - chance * centre).astype(LOW)
            probs[rows, :count] = chance.astype(LOW)
            grads[rows, :count] = slope
            folded[:, place] += dot_low(mirror, slope)
        result = dot_low(grads[...], keys[...]) * HDIM ** (-0.5)
        if half == 0:
            grad_query[...] = result.astype(LOW)
            sum_keys[...] = dot_over(part, grads[...])
            sum_values[...] = dot_over(upstream, probs[...])
        else:
            grad_query[...] = jnp.where(mine, result.astype(LOW), grad_query[...])
            sum_keys[...] += dot_over(part, grads[...])
            sum_values[...] += dot_over(upstream, probs[...])
        turned = pltpu.roll(folded[:, :WRAP], WRAP - 127, 1, stride=1, stride_axis=0)
        grad_table[pl.ds(2 * pair + half, 1), :] = jnp.sum(turned, 0, keepdims=True)
    grad_keys[...] = sum_keys[...].T.astype(LOW)
    grad_values[...] = sum_values[...].T.astype(LOW)


def attend_backward(query, keys, values, table, total, grad_mixed):
    tokens = query.shape[0]
    pslice = tokens - CLEN
    block = lambda rows: pl.BlockSpec((rows, 128), lambda i: (0, i))
    return pl.pallas_call(
        functools.partial(attend_back_kernel, pslice),
        grid=(HEADS // 2,),
        out_shape=(
            jax.ShapeDtypeStruct((tokens, D), LOW),
            jax.ShapeDtypeStruct((KEYS, D), LOW),
            jax.ShapeDtypeStruct((KEYS, D), LOW),
            jax.ShapeDtypeStruct(table.shape, F32),
        ),
        in_specs=[
            block(tokens),
            block(KEYS),
            block(KEYS),
            whole(table.shape),
            block(tokens),
            block(tokens),
        ],
        out_specs=(block(tokens), block(KEYS), block(KEYS), whole(table.shape)),
        scratch_shapes=[
            pltpu.VMEM((128, STRIP), F32),
            pltpu.VMEM((tokens, KEYS), F32),
            pltpu.VMEM((tokens, KEYS), F32),
            pltpu.VMEM((tokens, KEYS), LOW),
            pltpu.VMEM((tokens, KEYS), LOW),
            pltpu.VMEM((128, STRIP), F32),
            pltpu.VMEM((128, KEYS), F32),
            pltpu.VMEM((128, KEYS), F32),
        ],
        compiler_params=params(32),
    )(query, keys, values, table, total, grad_mixed)


def mlp_forward_kernel(state, gain, first, second, result, normed):
    step = pl.program_id(0)

    @pl.when(step == 0)
    def _():
        normed[...] = norm_rows(state[...], gain[...]).astype(LOW)
        result[...] = state[...]

    active = gelu(dot_low(normed[...], first[...])).astype(LOW)
    result[...] += dot_low(active, second[...])


def mlp_forward(state, gain, first, second):
    tokens = state.shape[0]
    part = 768
    return pl.pallas_call(
        mlp_forward_kernel,
        grid=(FF // part,),
        out_shape=(
            jax.ShapeDtypeStruct((tokens, D), F32),
            jax.ShapeDtypeStruct((tokens, D), LOW),
        ),
        in_specs=[
            whole((tokens, D)),
            whole((1, D)),
            pl.BlockSpec((D, part), lambda i: (0, i)),
            pl.BlockSpec((part, D), lambda i: (i, 0)),
        ],
        out_specs=(whole((tokens, D)), whole((tokens, D))),
        compiler_params=params(32),
    )(state, gain, first, second)


def mlp_backward_kernel(
    grad_next, state, normed, gain, first, second, result, grad_gain, grad_first, grad_second, low, total
):
    step = pl.program_id(0)

    @pl.when(step == 0)
    def _():
        low[...] = grad_next[...].astype(LOW)
        total[...] = jnp.zeros_like(total)

    active, slope = gelu_parts(dot_low(normed[...], first[...]))
    grad_hidden = (slope * dot_back(low[...], second[...])).astype(LOW)
    grad_second[...] = dot_over(active.astype(LOW), low[...]).astype(LOW)
    grad_first[...] = dot_over(normed[...], grad_hidden).astype(LOW)
    total[...] += dot_back(grad_hidden, first[...])

    @pl.when(step == pl.num_programs(0) - 1)
    def _():
        grad_state, grad_line = norm_back(state[...], gain[...], total[...])
        result[...] = grad_next[...] + grad_state
        grad_gain[...] = grad_line


def mlp_backward(grad_next, state, normed, gain, first, second):
    tokens = state.shape[0]
    part = 768
    return pl.pallas_call(
        mlp_backward_kernel,
        grid=(FF // part,),
        out_shape=(
            jax.ShapeDtypeStruct((tokens, D), F32),
            jax.ShapeDtypeStruct((1, D), F32),
            jax.ShapeDtypeStruct((D, FF), LOW),
            jax.ShapeDtypeStruct((FF, D), LOW),
        ),
        in_specs=[
            whole((tokens, D)),
            whole((tokens, D)),
            whole((tokens, D)),
            whole((1, D)),
            pl.BlockSpec((D, part), lambda i: (0, i)),
            pl.BlockSpec((part, D), lambda i: (i, 0)),
        ],
        out_specs=(
            whole((tokens, D)),
            whole((1, D)),
            pl.BlockSpec((D, part), lambda i: (0, i)),
            pl.BlockSpec((part, D), lambda i: (i, 0)),
        ),
        scratch_shapes=[pltpu.VMEM((tokens, D), LOW), pltpu.VMEM((tokens, D), F32)],
        compiler_params=params(48),
    )(grad_next, state, normed, gain, first, second)


def expert_kernel(
    rows, cotangent, gate, first, second, result, grad_rows, grad_gate, grad_first, grad_second, upstream, total, back
):
    step = pl.program_id(0)

    @pl.when(step == 0)
    def _():
        upstream[...] = (gate[:, :1] * cotangent[...].astype(F32)).astype(LOW)
        total[...] = jnp.zeros_like(total)
        back[...] = jnp.zeros_like(back)

    active, slope = gelu_parts(dot_low(rows[...], first[...]))
    active = active.astype(LOW)
    total[...] += dot_low(active, second[...])
    grad_hidden = (slope * dot_back(upstream[...], second[...])).astype(LOW)
    grad_second[...] = dot_over(active, upstream[...]).astype(LOW)
    grad_first[...] = dot_over(rows[...], grad_hidden).astype(LOW)
    back[...] += dot_back(grad_hidden, first[...])

    @pl.when(step == pl.num_programs(0) - 1)
    def _():
        low = total[...].astype(LOW)
        result[...] = low
        grad_rows[...] = back[...].astype(LOW)
        reach = jnp.sum(cotangent[...].astype(F32) * low.astype(F32), -1, keepdims=True)
        grad_gate[...] = jnp.broadcast_to(reach, grad_gate.shape)


def expert_pass(rows, cotangent, gate, first, second):
    count = rows.shape[0]
    shards, _, width = first.shape
    part = 256
    split = width // part
    inner = pl.BlockSpec((None, D, part), lambda i: (i // split, 0, i % split))
    outer = pl.BlockSpec((None, part, D), lambda i: (i // split, i % split, 0))
    return pl.pallas_call(
        expert_kernel,
        grid=(shards * split,),
        out_shape=(
            jax.ShapeDtypeStruct((count, D), LOW),
            jax.ShapeDtypeStruct((count, D), LOW),
            jax.ShapeDtypeStruct((count, 128), F32),
            jax.ShapeDtypeStruct(first.shape, LOW),
            jax.ShapeDtypeStruct(second.shape, LOW),
        ),
        in_specs=[whole((count, D)), whole((count, D)), whole((count, 128)), inner, outer],
        out_specs=(whole((count, D)), whole((count, D)), whole((count, 128)), inner, outer),
        scratch_shapes=[
            pltpu.VMEM((count, D), LOW),
            pltpu.VMEM((count, D), F32),
            pltpu.VMEM((count, D), F32),
        ],
        compiler_params=params(56),
    )(rows, cotangent, gate, first, second)


def split_low(values):
    high = values.astype(LOW)
    rest = values - high.astype(F32)
    middle = rest.astype(LOW)
    return high, middle, (rest - middle.astype(F32)).astype(LOW)


def exchange(block):
    return lax.all_to_all(block, ("dp", "col"), split_axis=0, concat_axis=0, tiled=True)


def attention_forward(state, gain, others, weight_in, weight_out, table, raw_others):
    tokens = state.shape[0]
    pslice = tokens - CLEN
    normed = norm_rows(state, gain).astype(LOW)
    if others is None:
        shared = lax.all_gather(normed[:pslice], "row", axis=0, tiled=True)
    else:
        shared = norm_rows(others.astype(F32), gain).astype(LOW)
    read = jnp.concatenate([shared, normed[pslice:]], 0)
    query = dot_low(normed, weight_in[:, :D]).astype(LOW)
    keys = dot_low(read, weight_in[:, D : 2 * D]).astype(LOW)
    values = dot_low(read, weight_in[:, 2 * D :]).astype(LOW)
    mixed, total = attend_forward(query, keys, values, table)
    return state + dot_low(mixed, weight_out), (state, normed, read, query, keys, values, mixed, total)


def attention_backward(grad_next, stash, gain, weight_in, weight_out, table, hot):
    state, normed, read, query, keys, values, mixed, total = stash
    pslice = state.shape[0] - CLEN
    branch = grad_next.astype(LOW)
    grad_out = dot_over(mixed, branch).astype(LOW)
    grad_mixed = dot_back(branch, weight_out).astype(LOW)
    grad_query, grad_keys, grad_values, grad_table = attend_backward(
        query, keys, values, table, total, grad_mixed
    )
    grad_in = jnp.concatenate(
        [dot_over(normed, grad_query), dot_over(read, grad_keys), dot_over(read, grad_values)], 1
    ).astype(LOW)
    grad_read = dot_back(grad_keys, weight_in[:, D : 2 * D]) + dot_back(
        grad_values, weight_in[:, 2 * D :]
    )
    own = lax.psum_scatter(
        grad_read[:PLEN].astype(LOW), "row", scatter_dimension=0, tiled=True
    ).astype(F32)
    grad_normed = dot_back(grad_query, weight_in[:, :D]) + jnp.concatenate(
        [own, grad_read[PLEN:]], 0
    )
    grad_state, grad_gain = norm_back(state, gain, grad_normed)
    grad_rel = jnp.dot(grad_table[:HEADS], hot.astype(F32), precision=HIGH).T
    return grad_next + grad_state, grad_in, grad_out, grad_rel, grad_gain


def general(
    inputs,
    cotangent,
    routes,
    buckets,
    norm_gains,
    attn_qkv,
    attn_out,
    rel_bias,
    mlp_in,
    mlp_out,
    router,
    expert_in,
    expert_out,
):
    grid = ("row", "col")
    places = lax.axis_size(grid)
    experts = lax.axis_size(("dp", "col"))
    tokens = inputs.shape[1]
    pslice = tokens - CLEN
    capacity = max(2, 3 * tokens // experts)

    small = [norm_gains.reshape(-1), rel_bias.reshape(-1), router.reshape(-1)]
    cuts = [part.shape[0] for part in small]
    packed = jnp.concatenate(small)
    packed = jnp.pad(packed, (0, -packed.shape[0] % 1024)).reshape(-1, 128)
    packed = lax.all_gather(packed, grid, axis=0, tiled=False).reshape(places, -1)
    gains = packed[:, : cuts[0]].reshape(places, 4, -1).transpose(1, 0, 2).reshape(4, 1, D).astype(F32)
    rel = packed[:, cuts[0] : cuts[0] + cuts[1]].reshape(places, 2, -1, HEADS)
    rel = rel.transpose(1, 0, 2, 3).reshape(2, BUCKETS, HEADS)
    route_w = packed[:, cuts[0] + cuts[1] : sum(cuts)].reshape(D, experts)

    qkv = [lax.all_gather(attn_qkv[i], grid, axis=0, tiled=True) for i in range(2)]
    out = [lax.all_gather(attn_out[i], grid, axis=0, tiled=True) for i in range(2)]
    dense_in = lax.all_gather(mlp_in, grid, axis=0, tiled=True)
    dense_out = lax.all_gather(mlp_out, grid, axis=0, tiled=True)
    first = lax.all_gather(expert_in[0], "row", axis=0, tiled=False)
    second = lax.all_gather(expert_out[0], "row", axis=0, tiled=False)

    hot, floor = bias_table(buckets, rel)
    tables = [
        jnp.pad(dot_low(rel[i].T, hot.T) + floor[None], ((0, 16 - HEADS), (0, 0))) for i in range(2)
    ]

    flat = routes[0].reshape(-1)
    levels = jnp.arange(experts, dtype=jnp.int32)
    choose = (routes[0][:, :, None] == levels[None, None, :]).astype(F32)
    hits = (flat[:, None] == levels[None, :]).astype(LOW)
    before = jnp.arange(2 * tokens)
    before = (before[:, None] > before[None, :]).astype(LOW)
    rank = jnp.sum(dot_low(before, hits) * hits.astype(F32), 1).astype(jnp.int32)
    place = (flat * capacity + rank).reshape(tokens, 2)
    slots = jnp.arange(experts * capacity, dtype=jnp.int32)
    picks = [(place[:, k][:, None] == slots[None, :]).astype(LOW) for k in range(2)]
    both = picks[0] + picks[1]
    sent_cotangent = dot_over(both, cotangent[0]).astype(LOW).reshape(experts, capacity, D)
    far_cotangent = exchange(sent_cotangent).reshape(experts * capacity, D)

    state0 = inputs[0].astype(F32)
    shared0 = lax.all_gather(inputs[0, :pslice], "row", axis=0, tiled=True)
    state1, stash1 = attention_forward(state0, gains[0], shared0, qkv[0], out[0], tables[0], None)
    state2, normed1 = mlp_forward(state1, gains[1], dense_in, dense_out)
    state3, stash3 = attention_forward(state2, gains[2], None, qkv[1], out[1], tables[1], None)

    normed3 = norm_rows(state3, gains[3]).astype(LOW)
    logits = dot_low(normed3, route_w)
    picked = jnp.sum(choose * logits[:, None, :], -1)
    raised = jnp.exp(picked - jnp.max(picked, -1, keepdims=True))
    gates = raised / jnp.sum(raised, -1, keepdims=True)
    parts = [split_low(gates[:, k]) for k in range(2)]
    spread = [
        dot_over(picks[k], jnp.pad(jnp.stack(parts[k], 1), ((0, 0), (0, 125)))) for k in range(2)
    ]
    sent = jnp.concatenate([dot_over(both, normed3), spread[0] + spread[1]], 1).astype(LOW)
    received = exchange(sent.reshape(experts, capacity, D + 128)).reshape(experts * capacity, D + 128)
    far_gate = jnp.sum(received[:, D : D + 3].astype(F32), 1, keepdims=True)
    far_gate = jnp.broadcast_to(far_gate, (experts * capacity, 128))
    result, grad_rows, grad_gate, grad_first, grad_second = expert_pass(
        received[:, :D], far_cotangent, far_gate, first, second
    )
    reach = jnp.pad(jnp.stack(split_low(grad_gate[:, 0]), 1), ((0, 0), (0, 125)))
    returned = exchange(
        jnp.concatenate([grad_rows, reach], 1).reshape(experts, capacity, D + 128)
    ).reshape(experts * capacity, D + 128)
    outcome = exchange(result.reshape(experts, capacity, D)).reshape(experts * capacity, D)
    output = state3 + sum(gates[:, k : k + 1] * dot_low(picks[k], outcome) for k in range(2))

    grad_gates = jnp.stack(
        [jnp.sum(dot_low(picks[k], returned[:, D:]), 1) for k in range(2)], 1
    )
    grad_picked = gates * (grad_gates - jnp.sum(gates * grad_gates, -1, keepdims=True))
    grad_logits = jnp.sum(choose * grad_picked[:, :, None], 1).astype(LOW)
    grad_route = dot_over(normed3, grad_logits)
    grad_normed3 = dot_low(both, returned[:, :D]) + dot_back(grad_logits, route_w)
    upstream = cotangent[0].astype(F32)
    grad_state3, gain_last = norm_back(state3, gains[3], grad_normed3)
    grad3 = upstream + grad_state3
    own_first = lax.psum_scatter(grad_first, "row", scatter_dimension=0, tiled=False)
    own_second = lax.psum_scatter(grad_second, "row", scatter_dimension=0, tiled=False)

    grad2, qkv_late, out_late, rel_late, gain_third = attention_backward(
        grad3, stash3, gains[2], qkv[1], out[1], tables[1], hot
    )
    grad1, gain_second, dense_grad_in, dense_grad_out = mlp_backward(
        grad2, state1, normed1, gains[1], dense_in, dense_out
    )
    grad0, qkv_early, out_early, rel_early, gain_first = attention_backward(
        grad1, stash1, gains[0], qkv[0], out[0], tables[0], hot
    )

    def share(block):
        block = lax.psum_scatter(block.astype(LOW), grid, scatter_dimension=0, tiled=True)
        return lax.psum(block, "dp").astype(F32)

    gain_grads = jnp.concatenate([gain_first, gain_second, gain_third, gain_last], 0)
    gain_grads = gain_grads.reshape(4, places, -1).transpose(1, 0, 2).reshape(places, -1)
    rel_grads = jnp.stack([rel_early, rel_late]).reshape(2, places, -1, HEADS)
    rel_grads = rel_grads.transpose(1, 0, 2, 3).reshape(places, -1)
    packed = jnp.concatenate([gain_grads, rel_grads, grad_route.reshape(places, -1)], 1)
    packed = jnp.pad(packed, ((0, 0), (0, -packed.shape[1] % 1024))).reshape(-1, 128)
    packed = share(packed).reshape(-1)
    gain_share = packed[: cuts[0]].reshape(4, -1)
    rel_share = packed[cuts[0] : cuts[0] + cuts[1]].reshape(2, -1, HEADS)
    route_share = packed[cuts[0] + cuts[1] : sum(cuts)].reshape(-1, experts)
    return (
        output[None],
        grad0[None],
        gain_share,
        jnp.stack([share(qkv_early), share(qkv_late)]),
        jnp.stack([share(out_early), share(out_late)]),
        rel_share,
        share(dense_grad_in),
        share(dense_grad_out),
        route_share,
        own_first.astype(F32)[None],
        own_second.astype(F32)[None],
    )


def once(shape):
    return pl.BlockSpec(shape, lambda *_: (0,) * len(shape), pipeline_mode=pl.Buffered(1))


def head_block(cols, piece, index):
    pair = lambda i: jnp.minimum(i, HEADS // 2 - 1)
    return pl.BlockSpec((4, cols, piece, 128), lambda i: (0, 0, 0, 6 * index + pair(i)))


def outer_block(cols, piece):
    return once((4, cols, piece, D))


def strip_block():
    return pl.BlockSpec((2, 128, STRIP), lambda i: (jnp.minimum(i, HEADS // 2 - 1), 0, 0))


def line_block(index, shape):
    return pl.BlockSpec(
        (None,) + shape, lambda i: (index,) + (0,) * len(shape), pipeline_mode=pl.Buffered(1)
    )


def up_kernel(
    raw_rows,
    pslice,
    state,
    own,
    shared,
    gain,
    table,
    wq,
    wk,
    wv,
    wo,
    result,
    normed,
    read,
    query,
    keys,
    values,
    mixed,
    total,
    strips,
    raw,
    weights,
    outer,
):
    pair = pl.program_id(0)
    lane = lax.broadcasted_iota(jnp.int32, (1, 128), 1)

    @pl.when(pair == 0)
    def _():
        weights[:pslice, PLEN:] = jnp.zeros((pslice, CLEN), LOW)
        outer[...] = wo[...].reshape(D, D)
        result[...] = state[...].astype(F32)
        if raw_rows:
            normed[...] = norm_rows(own[...].astype(F32), gain[...]).astype(LOW)
            for i in range(PLEN // pslice):
                rows = pl.ds(i * pslice, pslice)
                read[rows, :] = norm_rows(shared[i].astype(F32), gain[...]).astype(LOW)
        else:
            normed[...] = own[...]
            for i in range(PLEN // pslice):
                read[pl.ds(i * pslice, pslice), :] = shared[i]
        read[PLEN:, :] = normed[pslice:, :]

    query[...] = dot_low(normed[...], wq[...].reshape(D, 128)).astype(LOW)
    both = jnp.concatenate([wk[...].reshape(D, 128), wv[...].reshape(D, 128)], 1)
    both = dot_low(read[...], both).astype(LOW)
    keys[...] = both[:, :128]
    values[...] = both[:, 128:]

    for half in range(2):
        mine = (lane < HDIM) if half == 0 else (lane >= HDIM)
        line = jnp.broadcast_to(table[pl.ds(2 * pair + half, 1), :], (128, WRAP))
        line = pltpu.roll(line, 0, 1, stride=1, stride_axis=0)[:, :KEYS]
        strips[half, :, :KEYS] = line.astype(LOW)
        strips[half, :, KEYS:] = jnp.full((128, STRIP - KEYS), NEG, LOW)
        part = jnp.where(mine, query[...], 0) * HDIM ** (-0.5)
        raw[...] = dot_back(part.astype(LOW), keys[...])
        for row, place, count in tiles_of(pslice):
            rows = pl.ds(row, 128)
            scores = raw[rows, :count] + strips[half, :, place].astype(F32)
            top = jnp.max(scores, -1, keepdims=True)
            raised = jnp.exp(scores - top)
            summed = jnp.sum(raised, -1, keepdims=True)
            weights[rows, :count] = (raised * (1.0 / summed)).astype(LOW)
            log_total = jnp.broadcast_to(top + jnp.log(summed), (128, 128))
            if half == 0:
                total[rows, :] = log_total
            else:
                total[rows, :] = jnp.where(mine, log_total, total[rows, :])
        part = dot_low(weights[...], values[...]).astype(LOW)
        if half == 0:
            mixed[...] = part
        else:
            mixed[...] = jnp.where(mine, part, mixed[...])
    result[...] += dot_low(mixed[...], outer[pl.ds(pl.multiple_of(pair * 128, 128), 128), :])


def route_rows(routes, cotangent, picks, sent):
    tokens = routes.shape[0]
    slots, capacity, _ = sent.shape
    dp, col = lax.axis_index("dp"), lax.axis_index("col")
    lanes = lax.broadcasted_iota(jnp.int32, (tokens, 128), 1)
    slot, hot = [], []
    for k in range(2):
        expert = routes[:, k : k + 1]
        slot.append(2 * ((expert & 3) ^ col) + ((expert >> 2) ^ dp))
        hot.append(jnp.where(slot[k] == lanes, 1.0, 0.0))
    up = lax.broadcasted_iota(jnp.int32, (tokens, tokens), 0)
    along = lax.broadcasted_iota(jnp.int32, (tokens, tokens), 1)
    before = dot_low(jnp.where(up > along, 1.0, 0.0).astype(LOW), (hot[0] + hot[1]).astype(LOW))
    spots = lax.broadcasted_iota(jnp.int32, (tokens, slots * capacity), 1).astype(F32)
    for k in range(2):
        rank = jnp.sum(before * hot[k], -1, keepdims=True)
        place = slot[k].astype(F32) * capacity + rank
        picks[k] = jnp.where(place == spots, 1.0, 0.0).astype(LOW)
    both = picks[0] + picks[1]
    sent[...] = dot_over(both, cotangent[...]).astype(LOW).reshape(sent.shape)


def laid_lanes(columns, tokens):
    lanes = lax.broadcasted_iota(jnp.int32, (tokens, 128), 1)
    laid = jnp.zeros((tokens, 128), F32)
    for i, column in enumerate(columns):
        laid = jnp.where(lanes == i, column, laid)
    return laid


def chosen(routes):
    lanes = lax.broadcasted_iota(jnp.int32, (routes.shape[0], 128), 1)
    return [jnp.where(routes[:, k : k + 1] == lanes, 1.0, 0.0) for k in range(2)]


def send_rows(state, gain, route_w, routes, picks, normed, gates, line, sent):
    tokens = routes.shape[0]
    slots, capacity, _ = sent.shape
    shift = pl.multiple_of((pl.program_id(0) - (pl.num_programs(0) - 1)) * 8, 8)
    normed[...] = norm_rows(state[pl.ds(shift, tokens), :], gain[...]).astype(LOW)
    logits = dot_low(normed[...], route_w[...])
    picked = [jnp.sum(hot * logits, -1, keepdims=True) for hot in chosen(routes)]
    top = jnp.maximum(picked[0], picked[1])
    raised = [jnp.exp(value - top) for value in picked]
    gate = [value / (raised[0] + raised[1]) for value in raised]
    gates[...] = laid_lanes(gate, tokens)
    total = 0.0
    for k in range(2):
        parts = laid_lanes([part.astype(F32) for part in split_low(gate[k])], tokens).astype(LOW)
        total = total + jnp.sum(dot_over(parts, picks[k]), 0, keepdims=True)
    for slot in range(slots):
        part = total[:, slot * capacity : (slot + 1) * capacity]
        part = jnp.pad(part, ((0, 0), (0, line.shape[2] - capacity)))
        line[slot] = jnp.broadcast_to(part, line.shape[1:])
    sent[...] = dot_over(picks[0] + picks[1], normed[...]).astype(LOW).reshape(sent.shape)


def take_rows(
    cotangent, returned, reach, picks, gates, normed, routes, route_w, state, gain, grad_gain, grad_route, result
):
    tokens = routes.shape[0]
    capacity = picks.shape[2] // reach.shape[0]
    line = jnp.concatenate([reach[slot, :1, :capacity] for slot in range(reach.shape[0])], 1)
    gate = [gates[:, k : k + 1] for k in range(2)]
    met = [jnp.sum(picks[k].astype(F32) * line, -1, keepdims=True) for k in range(2)]
    centre = gate[0] * met[0] + gate[1] * met[1]
    hots = chosen(routes)
    slopes = sum(hots[k] * (gate[k] * (met[k] - centre)) for k in range(2)).astype(LOW)
    grad_route[...] = dot_over(slopes, normed[...])[: grad_route.shape[0]]
    grad_normed = dot_low(picks[0] + picks[1], returned[...]) + dot_back(slopes, route_w[...])
    grad_state, grad_line = norm_back(state[...], gain[...], grad_normed)
    result[...] = cotangent[...].astype(F32) + grad_state
    grad_gain[...] = grad_line


def attention_up(
    state,
    own,
    shared,
    layer_index,
    gains,
    tables,
    inner,
    output,
    moves,
    sources,
    name,
    more=(),
    extra=(),
    after=(),
):
    tokens = own.shape[0]
    pslice = tokens - CLEN
    _, cols, piece, _ = inner.shape
    raw_rows = layer_index == 0
    slots = lax.axis_size(("dp", "col"))
    capacity = 3 * tokens // slots
    more_specs = [once(block.shape) for block in more]
    if not raw_rows:
        more_specs[0] = line_block(3, (1, D))
    if raw_rows:
        more_out = [
            jax.ShapeDtypeStruct((2, tokens, slots * capacity), LOW),
            jax.ShapeDtypeStruct((tokens, D), LOW),
            jax.ShapeDtypeStruct((tokens, D), F32),
            jax.ShapeDtypeStruct((tokens, D), LOW),
            jax.ShapeDtypeStruct((slots, capacity, D), LOW),
        ]
        more_specs[2:] = [line_block(1, (1, D)), line_block(2, (1, D))]
    else:
        more_out = [
            jax.ShapeDtypeStruct((tokens, D), LOW),
            jax.ShapeDtypeStruct((tokens, 128), F32),
            jax.ShapeDtypeStruct((slots, 8, capacity + -capacity % 128), F32),
            jax.ShapeDtypeStruct((slots, capacity, D), LOW),
        ]

    def body(*refs):
        refs = list(refs)
        given = [refs.pop(9) for _ in more]
        found = [refs.pop(18) for _ in more_out]
        step = pl.program_id(0)
        for _ in extra:
            refs.pop()

        @pl.when(step < HEADS // 2)
        def _():
            up_kernel(raw_rows, pslice, *refs)

        @pl.when(step == (1 if raw_rows else HEADS // 2 - 1))
        def _():
            if raw_rows:
                route_rows(given[0], given[1], found[0], found[-1])
            else:
                send_rows(refs[9], *given, *found)
    block = lambda rows: pl.BlockSpec((rows, 128), lambda i: (0, jnp.minimum(i, HEADS // 2 - 1)))
    low = lambda rows: jax.ShapeDtypeStruct((rows, D), LOW)
    result, normed, read, query, keys, values, mixed, total, strips, *moved = carry(
        body,
        moves,
        grid=(HEADS // 2 + (4 if raw_rows else 0),),
        out_shape=(
            jax.ShapeDtypeStruct((tokens, D), F32),
            low(tokens),
            low(KEYS),
            low(tokens),
            low(KEYS),
            low(KEYS),
            low(tokens),
            jax.ShapeDtypeStruct((tokens, D), F32),
            jax.ShapeDtypeStruct((HEADS, 128, STRIP), LOW),
            *more_out,
        ),
        in_specs=[
            once((tokens, D)),
            once((tokens, D)),
            once(shared.shape),
            line_block(2 * layer_index, (1, D)),
            line_block(layer_index, tables.shape[1:]),
            head_block(cols, piece, 0),
            head_block(cols, piece, 1),
            head_block(cols, piece, 2),
            outer_block(cols, piece),
            *more_specs,
        ],
        out_specs=(
            whole((tokens, D)),
            whole((tokens, D)),
            whole((KEYS, D)),
            block(tokens),
            block(KEYS),
            block(KEYS),
            block(tokens),
            block(tokens),
            strip_block(),
            *[once(out.shape) for out in more_out],
        ),
        scratch_shapes=[
            pltpu.VMEM((tokens, KEYS), F32),
            pltpu.VMEM((tokens, KEYS), LOW),
            pltpu.VMEM((D, D), LOW),
            *extra,
        ],
        mib=60,
        name=name,
        after=after,
    )(state, own, shared, gains, tables, inner, inner, inner, output, *more, *sources)
    stash = (normed, read, query, keys, values, mixed, total, strips, inner, output)
    return result, stash, moved[: len(more_out)], moved[len(more_out) :]


def slide_sum(grid):
    rows = grid.shape[0]
    while rows > 8:
        rows = rows // 2
        grid = grid[:rows] + pltpu.roll(grid[rows:], WRAP - rows, 1)
    for step in (4, 2, 1):
        grid = grid + pltpu.roll(pltpu.roll(grid, 8 - step, 0), WRAP - step, 1)
    return grid[:1]


def down_kernel(
    pslice,
    grad_next,
    state,
    gain,
    normed,
    read,
    query,
    keys,
    values,
    mixed,
    total,
    strips,
    wq,
    wk,
    wv,
    wo,
    result,
    grad_gain,
    grads,
    grad_table,
    low,
    outer,
    grad_outer,
    sum_own,
    sum_read,
    spill,
    raw,
    pulled,
    probs,
    slopes,
    folded,
    sum_keys,
    sum_values,
):
    pair = pl.program_id(0)
    lane = lax.broadcasted_iota(jnp.int32, (1, 128), 1)
    here = pl.ds(pl.multiple_of(pair * 128, 128), 128)

    @pl.when(pair == 0)
    def _():
        probs[:pslice, PLEN:] = jnp.zeros((pslice, CLEN), LOW)
        slopes[:pslice, PLEN:] = jnp.zeros((pslice, CLEN), LOW)
        low[...] = grad_next[...].astype(LOW)
        outer[...] = wo[...].reshape(D, D)
        sum_own[...] = jnp.zeros_like(sum_own)
        sum_read[...] = jnp.zeros_like(sum_read)

    grad_outer[here, :] = dot_over(mixed[...], low[...]).astype(LOW)
    grad_mixed = dot_back(low[...], outer[here, :]).astype(LOW)
    for half in range(2):
        mine = (lane < HDIM) if half == 0 else (lane >= HDIM)
        part = (jnp.where(mine, query[...], 0) * HDIM ** (-0.5)).astype(LOW)
        upstream = jnp.where(mine, grad_mixed, 0).astype(LOW)
        raw[...] = dot_back(part, keys[...])
        pulled[...] = dot_back(upstream, values[...])
        for row, place, count in reversed(tiles_of(pslice)):
            rows = pl.ds(row, 128)
            log_total = total[rows, half * HDIM : half * HDIM + 1]
            scores = raw[rows, :count] + strips[half, :, place].astype(F32)
            chance = jnp.exp(scores - log_total)
            product = chance * pulled[rows, :count]
            centre = jnp.sum(product, -1, keepdims=True)
            slope = (product - chance * centre).astype(LOW)
            probs[rows, :count] = chance.astype(LOW)
            slopes[rows, :count] = slope
            if row == pslice:
                folded[:, :KEYS] = slope.astype(F32)
                folded[:, KEYS:] = jnp.zeros((128, STRIP - KEYS), F32)
            else:
                folded[:, place] += slope.astype(F32)
        step = (dot_low(slopes[...], keys[...]) * HDIM ** (-0.5)).astype(LOW)
        if half == 0:
            grad_query = step
            sum_keys[...] = dot_over(part, slopes[...])
            sum_values[...] = dot_over(upstream, probs[...])
        else:
            grad_query = jnp.where(mine, step, grad_query)
            sum_keys[...] += dot_over(part, slopes[...])
            sum_values[...] += dot_over(upstream, probs[...])
        grad_table[pl.ds(2 * pair + half, 1), :] = slide_sum(folded[:, :WRAP])

    shape = grads.shape[:2] + grads.shape[3:4] + (128,)

    def keep(index, turned):
        grads[:, :, index, :, here] = turned.T.astype(LOW).reshape(shape)

    keep(0, dot_over(grad_query, normed[...]))
    turned = jnp.concatenate([sum_keys[...], sum_values[...]], 0).astype(LOW)
    turned = dot_low(turned, read[...])
    keep(1, turned[:128])
    keep(2, turned[128:])
    sum_own[...] += dot_back(grad_query, wq[...].reshape(D, 128))
    pairs = jnp.concatenate([sum_keys[...].T, sum_values[...].T], 1).astype(LOW)
    both = jnp.concatenate([wk[...].reshape(D, 128), wv[...].reshape(D, 128)], 1)
    sum_read[...] += dot_back(pairs, both)

    @pl.when(pair == pl.num_programs(0) - 1)
    def _():
        grads[:, :, 3] = grad_outer[...].reshape(shape[:3] + (D,))
        spill[...] = sum_read[:PLEN, :].astype(LOW).reshape(spill.shape)


def down_after(pslice, fill, own_in, own_out, extras, results):
    grad_next, state, gain = own_in[:3]
    if not fill:
        grad_next = extras[-1]
    result, grad_gain = own_out[:2]
    sum_own, sum_read = extras[3:5]
    shift = (pl.program_id(0) - (pl.num_programs(0) - 1)) * 8
    lines = 0.0
    for row, count in ((0, pslice), (pslice, CLEN)):
        rows = pl.ds(pl.multiple_of(row + shift, 8), count)
        if row == 0:
            more = results[0][...].reshape(pslice, D)
        else:
            more = sum_read[pl.ds(pl.multiple_of(PLEN + shift, 8), CLEN), :]
        grad_state, line = norm_back(state[rows, :].astype(F32), gain[...], sum_own[rows, :] + more)
        result[rows, :] = grad_next[rows, :] + grad_state
        lines = lines + line
    grad_gain[...] = lines
    if fill:
        first = lax.broadcasted_iota(jnp.int32, (16, 1), 0) == 0
        extras[-1][...] = jnp.where(first, lines, 0.0).astype(LOW)


def attention_down(
    grad_next, state, gains, layer_index, stash, moves, sources, name, known=None
):
    normed, read, query, keys, values, mixed, total, strips, inner, output = stash
    tokens = normed.shape[0]
    pslice = tokens - CLEN
    _, cols, piece, _ = inner.shape
    table = jax.ShapeDtypeStruct((16, WRAP), F32)
    block = lambda rows: pl.BlockSpec((rows, 128), lambda i: (0, i))
    rows = Reduce(
        (pslice // 16, 16, D), ("core", "x"), take=lambda outs, extras: extras[5], keep=True
    )
    share = (4, cols, 4, piece, D)
    body, shown, extra = down_kernel, [jax.ShapeDtypeStruct(share, LOW)], []
    more, more_specs = [], []
    last = known is not None
    ends = []
    if not last:
        (grad_next, *ends) = grad_next

        def body(pslice, *refs):
            refs = list(refs)
            given = [refs.pop(15) for _ in ends]
            found = [refs.pop(19) for _ in range(2)]
            formed = refs.pop()

            @pl.when(pl.program_id(0) == 0)
            def _():
                take_rows(refs[0], *given, *found, formed)

            down_kernel(pslice, formed, *refs[1:])

        shown = [jax.ShapeDtypeStruct(share, LOW)]
        extra = [pltpu.VMEM((tokens, D), F32)]
        more, more_specs = list(ends), [once(block.shape) for block in ends]
        more_specs[-1] = line_block(3, (1, D))
    if last:
        def body(pslice, *refs):
            refs = list(refs)
            known_lines, small = refs.pop(15), refs[-2]
            down_kernel(pslice, *refs[:17], refs[-3], refs[17], *refs[18:-3])

            @pl.when(pl.program_id(0) == pl.num_programs(0) - 1)
            def _():
                small[:16, :] = refs[17][...].astype(LOW)
                small[16:, :] = known_lines[...]

        shown = []
        extra = [
            pltpu.VMEM(share, LOW),
            pltpu.VMEM((16 + known.shape[0], WRAP), LOW),
            pltpu.VMEM((16, D), LOW),
        ]
        more, more_specs = [known], [once(known.shape)]
    return carry(
        functools.partial(body, pslice),
        [(rows, (LATE, LATE + 2, LATE + 4))] + moves,
        grid=(HEADS // 2,),
        out_shape=(
            jax.ShapeDtypeStruct((tokens, D), F32),
            jax.ShapeDtypeStruct((1, D), F32),
            *shown,
            jax.ShapeDtypeStruct(table.shape, F32),
            *([] if last else [jax.ShapeDtypeStruct((1, D), F32), jax.ShapeDtypeStruct((8, D), F32)]),
        ),
        in_specs=[
            once((tokens, D)),
            once((tokens, D)),
            line_block(2 * layer_index, (1, D)),
            once((tokens, D)),
            once((KEYS, D)),
            block(tokens),
            block(KEYS),
            block(KEYS),
            block(tokens),
            block(tokens),
            strip_block(),
            head_block(cols, piece, 0),
            head_block(cols, piece, 1),
            head_block(cols, piece, 2),
            outer_block(cols, piece),
            *more_specs,
        ],
        out_specs=(
            once((tokens, D)),
            once((1, D)),
            *[once(share) for _ in shown],
            once(table.shape),
            *([] if last else [once((1, D)), once((8, D))]),
        ),
        scratch_shapes=[
            pltpu.VMEM((tokens, D), LOW),
            pltpu.VMEM((D, D), LOW),
            pltpu.VMEM((D, D), LOW),
            pltpu.VMEM((tokens, D), F32),
            pltpu.VMEM((KEYS, D), F32),
            pltpu.VMEM((4, 1, pslice // 16, 16, D), LOW),
            pltpu.VMEM((tokens, KEYS), F32),
            pltpu.VMEM((tokens, KEYS), F32),
            pltpu.VMEM((tokens, KEYS), LOW),
            pltpu.VMEM((tokens, KEYS), LOW),
            pltpu.VMEM((128, STRIP), F32),
            pltpu.VMEM((128, KEYS), F32),
            pltpu.VMEM((128, KEYS), F32),
            *extra,
        ],
        mib=62,
        name=name,
        after=[(LATE + 4.5, functools.partial(down_after, pslice, last))],
    )(
        grad_next,
        state,
        gains,
        normed,
        read,
        query,
        keys,
        values,
        mixed,
        total,
        strips,
        inner,
        inner,
        inner,
        output,
        *more,
        *sources,
    )


def mlp_blocks(cols, piece):
    return (
        pl.BlockSpec((4, cols, piece, D), lambda i: (0, 0, 0, i)),
        pl.BlockSpec((None, cols, 4 * piece, D), lambda i: (i, 0, 0, 0)),
    )


MLP_STEP = HEADS // 2


def mlp_load(extras, results):
    dense_in, dense_out = results[:2]
    inner, outer, arrived = extras[-3:]
    copies = []
    for j in range(4):
        source = dense_in.at[:, :, :, pl.ds(j * D, D)]
        copies.append((Within(source, inner.at[j], arrived.at[0, j]),))
        copies[j] += (Within(dense_out.at[j], outer.at[j], arrived.at[1, j]),)
    return copies


def mlp_part(j, own_in, own_out, extras, results):
    state, gain = own_out[0], own_in[-2]
    normed, result = own_out[10:12]
    inner, outer = extras[-3:-1]
    copies = mlp_load(extras, results)
    if j == 0:
        for pair in copies:
            for copy in pair:
                copy.start()
        normed[...] = norm_rows(state[...], gain[...]).astype(LOW)
        result[...] = state[...]
    for copy in copies[j]:
        copy.wait()
    active = gelu(dot_low(normed[...], inner[j].reshape(D, D))).astype(LOW)
    result[...] += dot_low(active, outer[j].reshape(D, D))


def mlp_end(own_in, own_out, extras, results):
    gain, result, normed = own_in[-1], own_out[11], own_out[12]
    shift = pl.multiple_of((pl.program_id(0) - (pl.num_programs(0) - 1)) * 8, 8)
    normed[...] = norm_rows(result[pl.ds(shift, normed.shape[0]), :], gain[...]).astype(LOW)


def mlp_down_kernel(
    grad_next,
    state,
    normed,
    gain,
    first,
    second,
    last_state,
    gates,
    picks,
    outcome,
    result,
    grad_gain,
    output,
    low,
    total,
    grads,
):
    step = pl.program_id(0)

    @pl.when(step == 0)
    def _():
        output[...] = last_state[...]

    @pl.when(step < 2)
    def _():
        gate = jnp.where(step == 0, gates[:, :1], gates[:, 1:2])
        output[...] += gate * dot_low(picks[step], outcome[...])

    @pl.when(step == 0)
    def _():
        low[...] = grad_next[...].astype(LOW)
        total[...] = jnp.zeros_like(total)

    inner, outer = first[...].reshape(D, D), second[...].reshape(D, D)
    active, slope = gelu_parts(dot_low(normed[...], inner))
    grad_hidden = (slope * dot_back(low[...], outer)).astype(LOW)
    _, cols, _, piece, _ = grads.shape
    grad_second = dot_over(active.astype(LOW), low[...]).astype(LOW)
    grads[step, :, :4] = grad_second.reshape(cols, 4, piece, D)
    grads[:, :, 4 + step] = dot_over(normed[...], grad_hidden).astype(LOW).reshape(4, cols, piece, D)
    total[...] += dot_back(grad_hidden, inner)

    @pl.when(step == pl.num_programs(0) - 1)
    def _():
        grad_state, grad_line = norm_back(state[...], gain[...], total[...])
        result[...] = grad_next[...] + grad_state
        grad_gain[...] = grad_line


def mlp_down(grad_next, state, normed, gains, dense_in, dense_out, ends, moves, sources, name):
    tokens = state.shape[0]
    _, cols, piece, _ = dense_in.shape
    pairs = CoreSum((piece, D), cols, lambda outs, extras: extras[2])
    return carry(
        mlp_down_kernel,
        [(pairs, (0, 1, 2, 3, LATE, LATE + 1))] + moves,
        grid=(4,),
        out_shape=(
            jax.ShapeDtypeStruct((tokens, D), F32),
            jax.ShapeDtypeStruct((1, D), F32),
            jax.ShapeDtypeStruct((tokens, D), F32),
        ),
        in_specs=[
            once((tokens, D)),
            once((tokens, D)),
            once((tokens, D)),
            line_block(1, (1, D)),
            *mlp_blocks(cols, piece),
            *[once(block.shape) for block in ends],
        ],
        out_specs=(once((tokens, D)), once((1, D)), once((tokens, D))),
        scratch_shapes=[
            pltpu.VMEM((tokens, D), LOW),
            pltpu.VMEM((tokens, D), F32),
            pltpu.VMEM((4, cols, 8, piece, D), LOW),
        ],
        mib=60,
        name=name,
    )(grad_next, state, normed, gains, dense_in, dense_out, *ends, *sources)


def routed_kernel(
    sent,
    sent_gates,
    sent_cotangent,
    first,
    second,
    outcome,
    returned,
    reach,
    grad_first,
    grad_second,
    rows,
    gates,
    cotangent,
    inner,
    outer,
    active_all,
    hidden_all,
    upstream,
    back,
    back_reach,
    turned,
    sum_up,
    sum_down,
    held,
    near,
    row_send,
    row_recv,
    gate_send,
    gate_recv,
    back_send,
    back_recv,
    reach_send,
    reach_recv,
    core_send,
    core_recv,
    local,
    store,
):
    capacity = rows.shape[1]
    barrier = pltpu.get_barrier_semaphore()
    others = range(1, len(SLOTS))
    row, across, core, plane = neighbours()
    c = lax.rem(row, 2)
    for slot in others:
        pl.semaphore_signal(barrier, inc=1, device_id=slot_device(slot), device_id_type=MESH)
    pl.semaphore_signal(barrier, inc=1, device_id=dict(row=core), device_id_type=MESH)
    loads = [
        Within(sent.at[0], rows.at[0], local.at[0]),
        Within(sent_gates.at[0], gates.at[0], local.at[1]),
        Within(sent_cotangent, cotangent, local.at[2]),
        Within(first, inner, local.at[3]),
        Within(second, outer, local.at[4]),
    ]
    for load in loads:
        load.start()
    pl.semaphore_wait(barrier, len(others) + 1)

    def there(slot):
        device = slot_device(slot)
        return (
            remote(sent_gates.at[slot], gates.at[slot], gate_send, gate_recv, slot, **device),
            remote(sent.at[slot], rows.at[slot], row_send, row_recv, slot, **device),
        )

    def home(slot):
        device = slot_device(slot)
        return (
            remote(back_reach.at[slot], reach.at[slot], reach_send, reach_recv, slot, **device),
            remote(back.at[slot], returned.at[slot], back_send, back_recv, slot, **device),
        )

    own_home = [
        Within(back_reach.at[0], reach.at[0], local.at[5]),
        Within(back.at[0], returned.at[0], local.at[6]),
    ]
    for slot in (4, 5, 1, 6, 7, 2, 3):
        for copy in there(slot):
            copy.start()
    for load in loads:
        load.wait()
    ones = jnp.ones((8, D), F32)
    count = 2 * capacity
    for b in (0, 2, 1, 3):
        for a in range(2):
            slot = 2 * b + a
            if slot:
                for copy in there(slot):
                    copy.wait_recv()
            gate = gates[slot].T[:capacity, :1]
            at = pl.ds(slot * capacity, capacity)
            upstream[at, :] = (gate * cotangent[slot].astype(F32)).astype(LOW)
        both = pl.ds(2 * b * capacity, count)
        block = rows[2 * b : 2 * b + 2].reshape(count, D)
        sum_up[...] = jnp.zeros_like(sum_up)
        sum_down[...] = jnp.zeros_like(sum_down)

        def part(j):
            active, slope = gelu_parts(dot_low(block, inner[j]))
            active = active.astype(LOW)
            active_all[j, both, :] = active
            sum_up[...] += dot_low(active, outer[j])
            hidden = (slope * dot_back(upstream[both, :], outer[j])).astype(LOW)
            hidden_all[j, both, :] = hidden
            sum_down[...] += dot_back(hidden, inner[j])

        each(4, part)
        back[2 * b : 2 * b + 2] = sum_down[...].astype(LOW).reshape(2, capacity, D)
        outcome[2 * b : 2 * b + 2] = sum_up[...].astype(LOW).reshape(2, capacity, D)
        for a in range(2):
            slot = 2 * b + a
            met = cotangent[slot].astype(F32) * outcome[slot].astype(F32)
            line = lax.dot_general(
                ones, met, (((1,), (1,)), ((), ())), precision=HIGH, preferred_element_type=F32
            )
            back_reach[slot] = jnp.pad(line, ((0, 0), (0, back_reach.shape[2] - capacity)))
            if slot:
                for copy in home(slot):
                    copy.start()
            else:
                for copy in own_home:
                    copy.start()
    turned[...] = rows[...].reshape(len(SLOTS) * capacity, D).T

    def formed(j):
        return dot_low(turned[...], hidden_all[j]), dot_over(active_all[j], upstream[...])

    def passed(i, k):
        return remote(held.at[i, k], near.at[i, k], core_send, core_recv, 2 * i + k, row=core)

    def stored(i, k):
        return Within(near.at[i, k], (grad_first, grad_second)[k].at[i], store.at[i, k])

    def give(i):
        for k, value in enumerate(formed(2 * i + 1 - c)):
            held[i, k] = value.astype(LOW)
            passed(i, k).start()

    def meet(i):
        for k, value in enumerate(formed(2 * i + c)):
            passed(i, k).wait_recv()
            near[i, k] = (value + near[i, k].astype(F32)).astype(LOW)
            stored(i, k).start()

    each(2, give)
    each(2, meet)
    for i in range(2):
        for k in range(2):
            stored(i, k).wait()
            passed(i, k).wait_send()
    for copy in own_home:
        copy.wait()
    for slot in (4, 5, 1, 6, 7, 2, 3):
        for copy in home(slot):
            copy.wait_recv()
    for slot in (4, 5, 1, 6, 7, 2, 3):
        for copy in there(slot) + home(slot):
            copy.wait_send()


def routed(sent, gates, cotangent, first, second, name):
    slots, capacity, _ = sent.shape
    hbm = pl.BlockSpec(memory_space=pl.ANY)
    count = slots * capacity
    low = jax.ShapeDtypeStruct(sent.shape, LOW)
    share = jax.ShapeDtypeStruct((2,) + first.shape[1:], LOW)
    pairs = [pltpu.SemaphoreType.DMA((slots,)) for _ in range(8)]
    return pl.pallas_call(
        routed_kernel,
        out_shape=(low, low, jax.ShapeDtypeStruct(gates.shape, F32), share, share),
        in_specs=[hbm] * 5,
        out_specs=(pl.BlockSpec(memory_space=pltpu.VMEM), hbm, hbm, hbm, hbm),
        scratch_shapes=[
            pltpu.VMEM(sent.shape, LOW),
            pltpu.VMEM(gates.shape, F32),
            pltpu.VMEM(sent.shape, LOW),
            pltpu.VMEM(first.shape, LOW),
            pltpu.VMEM(second.shape, LOW),
            pltpu.VMEM((4, count, D), LOW),
            pltpu.VMEM((4, count, D), LOW),
            pltpu.VMEM((count, D), LOW),
            pltpu.VMEM(sent.shape, LOW),
            pltpu.VMEM(gates.shape, F32),
            pltpu.VMEM((D, count), LOW),
            pltpu.VMEM((2 * capacity, D), F32),
            pltpu.VMEM((2 * capacity, D), F32),
            pltpu.VMEM((2, 2, D, D), LOW),
            pltpu.VMEM((2, 2, D, D), LOW),
            *pairs,
            pltpu.SemaphoreType.DMA((4,)),
            pltpu.SemaphoreType.DMA((4,)),
            pltpu.SemaphoreType.DMA((7,)),
            pltpu.SemaphoreType.DMA((2, 2)),
        ],
        compiler_params=pltpu.CompilerParams(
            vmem_limit_bytes=62 * MIB, collective_id=name, has_side_effects=True
        ),
    )(sent, gates, cotangent, first, second)


def finish_kernel(
    index,
    small,
    line,
    early_q,
    early_k,
    early_b,
    late_a,
    late_b,
    dense_b,
    dense_a,
    dense_rest,
    *moved,
):
    *moved, sems = moved
    ends, moved, staged = moved[:5], moved[5:-5], moved[-5:]
    (
    gain_share,
    rel_share,
    route_share,
    qkv,
    out,
    dense_in,
    dense_out,
    ) = moved[:7]
    targets = list(moved[7:10])
    half = ends[3].shape[0]
    targets += [moved[10].at[pl.ds(0, half)], moved[10].at[pl.ds(half, half)]]
    loads = [Within(end, to, sems.at[0, i]) for i, (end, to) in enumerate(zip(ends, staged))]
    copies = [Within(end, to, sems.at[1, i]) for i, (end, to) in enumerate(zip(staged, targets))]
    for load in loads:
        load.start()
    row, col = lax.axis_index("row"), lax.axis_index("col")
    place = row * 4 + col
    width = gain_share.shape[1]
    buckets = rel_share.shape[1]
    lines = jnp.concatenate([line[:8, :D], small[32:48, :D]], 0)
    lines = pltpu.roll(lines, lax.rem(D - place * width, D), 1)[:, :width]
    gain_share[...] = jnp.concatenate([lines[0:1], lines[10:11], lines[8:9], lines[9:10]], 0)
    route_share[...] = lines[11:19]
    wanted = place * buckets + lax.broadcasted_iota(jnp.int32, (8, 1), 0)
    hot = (index[...] == wanted).astype(F32)
    for i, block in enumerate((small[:16, :], small[16:32, :])):
        sums = lax.dot_general(
            hot, block, (((1,), (1,)), ((), ())), precision=HIGH, preferred_element_type=F32
        )
        rel_share[i] = sums[:buckets, :HEADS]
    for i, blocks in enumerate(
        ((early_q[0], early_k[0], early_b[0]), (late_a[0], late_a[1], late_b[0]))
    ):
        for k, block in enumerate(blocks):
            qkv[i, :, k * D : (k + 1) * D] = block
    out[0] = early_b[1]
    out[1] = late_b[1]
    for k in range(4):
        dense_in[:, k * D : (k + 1) * D] = dense_b[k]
    for k in range(2):
        dense_out[k] = dense_a[k]
        dense_out[2 + k] = dense_rest[k]
    for load, copy in zip(loads, copies):
        load.wait()
        copy.start()
    for copy in copies:
        copy.wait()


def finish(index, *blocks):
    piece = blocks[2].shape[1]
    hbm, near = pl.BlockSpec(memory_space=pl.ANY), pl.BlockSpec()
    ends = [block.shape for block in blocks[-5:]]
    ends = ends[:3] + [(2 * ends[3][0],) + ends[3][1:]]
    shapes = (
        (4, piece),
        (2, BUCKETS * piece // D, HEADS),
        (8, piece),
        (2, piece, 3 * D),
        (2, piece, D),
        (piece, FF),
        (4, piece, D),
    ) + tuple(ends)
    return pl.pallas_call(
        finish_kernel,
        in_specs=[near] * (len(blocks) - 4) + [hbm] * 5,
        out_specs=[near] * 7 + [hbm] * 4,
        scratch_shapes=[pltpu.VMEM(block.shape, F32) for block in blocks[-5:]]
        + [pltpu.SemaphoreType.DMA((2, 5))],
        out_shape=tuple(jax.ShapeDtypeStruct(shape, F32) for shape in shapes),
        compiler_params=pltpu.CompilerParams(vmem_limit_bytes=62 * MIB),
    )(index, *blocks)


def tiled(
    inputs,
    cotangent,
    routes,
    buckets,
    norm_gains,
    attn_qkv,
    attn_out,
    rel_bias,
    mlp_in,
    mlp_out,
    router,
    expert_in,
    expert_out,
):
    grid = ("row", "col")
    places = lax.axis_size(grid)
    cols, planes = lax.axis_size("col"), lax.axis_size("dp")
    experts = planes * cols
    tokens = inputs.shape[1]
    pslice = tokens - CLEN
    capacity = 3 * tokens // experts
    piece = D // places

    small = [norm_gains.reshape(-1), rel_bias.reshape(-1), router.reshape(-1)]
    cuts = [part.shape[0] for part in small]
    packed = jnp.concatenate(small)
    packed = jnp.pad(packed, (0, -packed.shape[0] % 2048)).reshape(1, -1, 128)

    pair, cut = (2, piece, D), (piece, 3 * D)
    early = (0, LATE, LATE, LATE, LATE)
    inner_a = layer(Gather(cut, False, cols, span=(0, 2 * D)), 0)
    inner_b = layer(Gather(cut, True, cols, span=(2 * D, D), into=inner_a), 0)
    packed, inner0, output0, shared0 = carry(
        None,
        [
            (Gather(packed.shape, False, cols), early),
            (inner_a, early),
            (inner_b, early),
            (layer(Gather((piece, D), True, cols), 0), early),
            (Rows((pslice, D)), (0, LATE, LATE)),
        ],
        (1,),
        [],
        [],
        [],
        [],
        60,
        1,
    )(packed, attn_qkv, attn_qkv, attn_out, inputs[0, :pslice])
    packed = packed.reshape(places, -1)
    gains = packed[:, : cuts[0]].reshape(places, 4, -1).transpose(1, 0, 2).reshape(4, 1, D).astype(F32)
    rel = packed[:, cuts[0] : cuts[0] + cuts[1]].reshape(places, 2, -1, HEADS)
    rel = rel.transpose(1, 3, 0, 2).reshape(2, HEADS, BUCKETS)
    route_w = packed[:, cuts[0] + cuts[1] : sum(cuts)].reshape(D, experts)

    gap = jnp.full((WRAP - KEYS,), -1, jnp.int32)
    index = jnp.concatenate([jnp.flip(buckets[: PLEN + 1]), gap, jnp.flip(buckets[PLEN + 1 :])])
    hot = (jnp.arange(BUCKETS, dtype=jnp.int32)[:, None] == index[None, :]).astype(LOW)
    floor = jnp.where(index < 0, NEG, 0.0).astype(F32)
    tables = jnp.pad(rel, ((0, 0), (0, 16 - HEADS), (0, 0))).reshape(32, BUCKETS)
    tables = (dot_low(tables, hot) + floor[None]).reshape(2, 16, WRAP)

    rows = Rows((pslice, D), take=lambda outs, extras: outs[12].at[pl.ds(0, pslice)])
    state1, stash1, (picks, normed1, state2, normed2, sent_cotangent), moved = attention_up(
        inputs[0],
        inputs[0],
        shared0,
        0,
        gains,
        tables,
        inner0,
        output0,
        [
            (Gather(mlp_in.shape, True, cols), (0, 2, 4, MLP_STEP, MLP_STEP + 0.1)),
            (Gather(mlp_out.shape, True, cols), (0, 2, 4, MLP_STEP, MLP_STEP + 0.1)),
            (Rows(expert_in.shape[1:]), (0, 4, LATE + 0.5)),
            (layer(Gather(cut, True, cols), 1), (3, 5, 7, LATE + 0.4, LATE + 0.5)),
            (layer(Gather((piece, D), True, cols), 1), (3, 5, 7, LATE + 0.4, LATE + 0.5)),
            (rows, (LATE + 0.1, LATE + 0.3, LATE + 0.5)),
        ],
        (mlp_in, mlp_out, expert_in[0], attn_qkv, attn_out),
        2,
        more=(routes[0], cotangent[0], gains, gains),
        extra=(
            pltpu.VMEM((4, 4, cols, piece, D), LOW),
            pltpu.VMEM((4, cols, 4 * piece, D), LOW),
            pltpu.SemaphoreType.DMA((2, 4)),
        ),
        after=[(MLP_STEP + j + 0.5, functools.partial(mlp_part, j)) for j in range(4)]
        + [(LATE, mlp_end)],
    )
    dense_in, dense_out, first, inner1, output1, shared2 = moved
    route_w = jnp.pad(route_w, ((0, 0), (0, 128 - experts)))
    state3, stash3, (normed3, gates, line, sent), (second, far_cotangent) = attention_up(
        state2,
        normed2,
        shared2,
        1,
        gains,
        tables,
        inner1,
        output1,
        [(Rows(expert_out.shape[1:]), (0, 5, LATE)), (Swap((capacity, D)), (0, LATE))],
        (expert_out[0], sent_cotangent),
        4,
        more=(gains, route_w, routes[0], picks),
    )

    outcome, returned, reach, grad_first, grad_second = routed(
        sent, line, far_cotangent, first, second, 5
    )
    returned = returned.reshape(experts * capacity, D)
    laid = (2, 1, places, piece, D)
    octet = (places // 2, piece, D)
    grad_first, grad_second = grad_first.reshape(laid), grad_second.reshape(laid)
    grad2, gain_third, late, table_late, gain_last, grad_route, own_first, own_second, outcome = (
        attention_down(
        (cotangent[0], returned, reach, picks, gates, normed3, routes[0], route_w, state3, gains),
        state2,
        gains,
        1,
        stash3,
        [
            (Reduce((places, piece, D), ("x",)), (0, 5)),
            (Reduce(octet, ("x",)), (1, LATE + 3)),
            (Swap((capacity, D)), (0, LATE + 5)),
        ],
        (grad_first, grad_second, outcome),
        6,
    ))
    outcome = outcome.reshape(experts * capacity, D)
    grad1, gain_second, output, dense_pairs, own_rest, late_a, late_b = mlp_down(
        grad2,
        state1,
        normed1,
        gains,
        dense_in,
        dense_out,
        (state3, gates, picks, outcome),
        [
            (Reduce(octet, ("x",), first=places // 2), (0, LATE)),
            (Reduce(pair, ("core", "x"), cols), (0, 1, LATE + 2)),
            (Reduce(pair, ("core", "y"), cols, first=2), (0, 1, LATE)),
        ],
        (grad_second, late, late),
        7,
    )
    lines = jnp.concatenate([gain_third, gain_last, gain_second, grad_route], 0)
    lines = jnp.pad(lines, ((0, 16 - lines.shape[0]), (0, WRAP - D)))
    known = jnp.concatenate([table_late, lines], 0).astype(LOW)
    quad = (4, piece, D)
    single = (1, piece, D)
    held = lambda outs, extras: extras[-3]
    (
        grad0,
        _,
        _,
        late_a,
        late_b,
        dense_a,
        dense_a_rest,
        dense_b,
        early_q,
        early_k,
        early_b,
        small,
        line,
    ) = attention_down(
        grad1,
        inputs[0],
        gains,
        0,
        stash1,
        [
            (Reduce(pair, ("z", "sum"), cols), (0, 2, 4)),
            (Reduce(single, ("x", "z", "swap"), cols), (0, 1, 3, 5)),
            (Reduce(pair, ("x", "z", "sum"), cols), (0, 2, 5, LATE + 3)),
            (Reduce(pair, ("x", "z", "sum"), cols, first=2), (2, 4, LATE + 1, LATE + 4)),
            (
                Reduce(quad, ("y", "x", "z", "swap"), cols, first=4),
                (0, 4, LATE + 0.2, LATE + 5, LATE + 7),
            ),
            (
                Reduce(single, ("core", "x", "z", "sum"), cols, take=held),
                (LATE, LATE + 2, LATE + 5, LATE + 8, LATE + 10),
            ),
            (
                Reduce(single, ("core", "x", "z", "sum"), cols, first=1, take=held),
                (LATE, LATE + 2, LATE + 6, LATE + 9, LATE + 10),
            ),
            (
                Reduce(pair, ("core", "y", "x", "z", "swap"), cols, first=2, take=held),
                (LATE, LATE + 2, LATE + 5, LATE + 7, LATE + 9, LATE + 10),
            ),
            (
                Total((16 + known.shape[0], WRAP), take=lambda outs, extras: extras[-2]),
                (LATE - 0.5, LATE + 0.5, LATE + 1.5, LATE + 2.5, LATE + 4.2),
            ),
            (
                Total((16, D), take=lambda outs, extras: extras[-1], short=True),
                (LATE + 4.6, LATE + 6.5, LATE + 9.5),
            ),
        ],
        (late_a, late_b, dense_pairs, dense_pairs, dense_pairs),
        8,
        known=known,
    )
    gain_share, rel_share, route_share, qkv_share, out_share, in_share, up_share, *ends = finish(
        index.reshape(1, -1),
        small,
        line,
        early_q,
        early_k,
        early_b,
        late_a,
        late_b,
        dense_b,
        dense_a,
        dense_a_rest,
        output,
        grad0,
        own_first,
        own_second,
        own_rest,
    )
    output, grad0, own_first, own_second = ends
    return (
        output[None],
        grad0[None],
        gain_share,
        qkv_share,
        out_share,
        rel_share,
        in_share,
        up_share.reshape(-1, D),
        route_share.T,
        own_first.reshape(1, D, D),
        own_second.reshape(1, D, D),
    )


def solution(mesh):
    in_specs = (
        P(("dp", "col"), "row", None),
        P(("dp", "col"), "row", None),
        P(("dp", "col"), "row", None),
        P(),
        P(None, ("row", "col")),
        P(None, ("row", "col"), None),
        P(None, ("row", "col"), None),
        P(None, ("row", "col"), None),
        P(("row", "col"), None),
        P(("row", "col"), None),
        P(("row", "col"), None),
        P(("dp", "col"), None, "row"),
        P(("dp", "col"), "row", None),
    )
    out_specs = (
        P(("dp", "col"), "row", None),
        P(("dp", "col"), "row", None),
        P(None, ("row", "col")),
        P(None, ("row", "col"), None),
        P(None, ("row", "col"), None),
        P(None, ("row", "col"), None),
        P(("row", "col"), None),
        P(("row", "col"), None),
        P(("row", "col"), None),
        P(("dp", "col"), None, "row"),
        P(("dp", "col"), "row", None),
    )
    sizes = dict(mesh.shape)
    piece = D // (sizes["row"] * sizes["col"])
    capacity = 3 * (PLEN // sizes["row"] + CLEN) // (sizes["dp"] * sizes["col"])
    whole_tiles = (sizes["dp"], sizes["row"], sizes["col"]) == (2, 4, 4) and piece % 16 == 0 and capacity % 16 == 0
    return jax.shard_map(
        tiled if whole_tiles else general, mesh=mesh, in_specs=in_specs, out_specs=out_specs, check_vma=False
    )
```
